32 devices in a mesh: wide: 8 (over y, x, core), narrow: 4 (over z).
Axes of the slice: x: 2, y: 2, z: 4, core: 2. Of those that a mesh axis runs over, the one named last changes fastest.
Arguments:
- volumes: bfloat16 [4, 1, 4, 32, 4096], P('narrow', None, None, 'wide'), may hold values from -6 to 6
- first_kernel: bfloat16 [27, 32, 4], replicated, may hold values from -0.625 to 0.625
- second_kernel: bfloat16 [27, 64, 32], replicated, may hold values from -0.21875 to 0.21875
- cotangent: bfloat16 [4, 1, 64, 16384], P('narrow', None, None, 'wide'), may hold values from -6 to 6
Outputs:
- activations: bfloat16 [4, 1, 64, 16384], P('narrow', None, None, 'wide')
- weight_grad: float32 [27, 64, 32], P(None, 'narrow')
The draws below stay inside these ranges and needn't reach their ends.
All inputs are finite; a program needn't handle non-finite values.
Results may differ from the reference program's by a relative error of at most 0.023.
The reference program's roundings to bfloat16 on the way (of `first_act` and `back`) count: a program that leaves them out, or rounds other values in their place, can miss the bound.
Values may be sent and summed in bfloat16 or wider, within the bound.
No kernel may reach another device: no remote copies, remote signals or barrier semaphores. Data moves between devices by JAX's collectives and lax.ppermute only.
A program may use at most 64 MiB of HBM per device.

```python
import math
import jax
import jax.numpy as jnp
from jax import lax

CIN = 4
C1 = 32
C2 = 64
SAMP = 1
YCELLS = 64
XCELLS = 64
NZ = 32
GROUPS = 4


def shard_levels(stream_key, shape, split, least, largest):
    loudness = 1.0
    for dim, parts in split:
        heights = jax.random.uniform(jax.random.fold_in(jax.random.fold_in(stream_key, 6), dim), (parts,), jnp.float32, least / len(split), largest / len(split))
        loudness = loudness * jnp.repeat(jnp.exp(heights), shape[dim] // parts).reshape((-1,) + (1,) * (len(shape) - 1 - dim))
    return loudness


def gaussian(stream_key, dims, deviation, reach, split=(), kind=jnp.bfloat16):
    result = deviation * jax.random.normal(stream_key, dims, jnp.float32)
    if split:
        result = result * shard_levels(stream_key, dims, split, -0.22, 0.18)
    return jnp.clip(result, -reach, reach).astype(kind)


def setup_inputs(seed: int = 0) -> dict:
    splits = jax.random.split(jax.random.key(seed), 5)
    volumes = gaussian(splits[0], (GROUPS, SAMP, CIN, NZ, YCELLS * XCELLS), 1.0, 6.0, ((0, 4), (3, 8)))
    first_kernel = gaussian(splits[1], (27, C1, CIN), (27 * CIN) ** -0.5, 0.625)
    second_kernel = gaussian(splits[2], (27, C2, C1), (27 * C1) ** -0.5, 0.21875)
    cotangent = gaussian(splits[3], (GROUPS, SAMP, C2, (NZ // 2) * (YCELLS // 2) * (XCELLS // 2)), 1.0, 6.0, ((0, 4), (3, 8)))
    return dict(volumes=volumes, first_kernel=first_kernel, second_kernel=second_kernel, cotangent=cotangent)


neg_slope = 0.3

def leaky_relu(value):
    return jnp.where(value > 0, value, neg_slope * value)

def kernel_layout(kernel):
    outs_n = kernel.shape[1]
    ins_n = kernel.shape[2]
    return kernel.reshape(3, 3, 3, outs_n, ins_n).transpose(3, 4, 0, 1, 2)

def convolve(inputs, kernel, stride, padding, precision):
    return lax.conv_general_dilated(inputs, kernel_layout(kernel), (stride, stride, stride), [padding, padding, padding], dimension_numbers=('NCDHW', 'OIDHW', 'NCDHW'), precision=precision, preferred_element_type=jnp.float32)

def reference(volumes, first_kernel, second_kernel, cotangent):
    samples = volumes.reshape(-1, CIN, NZ, YCELLS, XCELLS)
    cells_out = NZ // 2 * (YCELLS // 2) * (XCELLS // 2)
    cot_flat = cotangent.reshape(-1, C2, cells_out)

    def one_sample(grads, inputs):
        sample, cot = inputs
        first_pre = convolve(sample[None], first_kernel, 2, (1, 0), None)
        first_act = leaky_relu(first_pre).astype(jnp.bfloat16)
        second_pre = convolve(first_act, second_kernel, 1, (1, 1), None)
        pre = second_pre.reshape(C2, cells_out)
        output = leaky_relu(pre).astype(jnp.bfloat16)
        back = (cot.astype(jnp.float32) * jnp.where(pre > 0, 1.0, neg_slope)).astype(jnp.bfloat16)
        act_wide = first_act.astype(jnp.float32)

        def apply_kernel(kernel):
            return convolve(act_wide, kernel, 1, (1, 1), lax.Precision.HIGHEST)
        primal, pullback = jax.vjp(apply_kernel, second_kernel.astype(jnp.float32))
        back_grid = back.astype(jnp.float32).reshape(primal.shape)
        term = pullback(back_grid)[0]
        return (grads + term, output)
    start = jnp.zeros((27, C2, C1), jnp.float32)
    grads, outputs = lax.scan(one_sample, start, (samples, cot_flat))
    count = GROUPS * SAMP * cells_out
    weight_grad = grads * (1.0 / math.sqrt(count))
    return (outputs.reshape(GROUPS, SAMP, C2, cells_out), weight_grad)
```

```python
import functools
import math

import jax
import jax.numpy as jnp
import numpy as np
from jax import lax
from jax.experimental import pallas as pl
from jax.experimental.pallas import tpu as pltpu
from jax.sharding import PartitionSpec as P

CIN = 4
C1 = 32
C2 = 64
PLANES = 4
CELLS = 4096
HALF = 32
PLANE = 1024
LANES = 128
ROWS = 3 * CIN * PLANES
WINDOW = 640
PACKED = 7 * LANES
neg_slope = 0.3


def selection():
    table = np.zeros((WINDOW, 9, LANES), np.float32)
    for b in range(3):
        for c in range(3):
            for lane in range(LANES):
                row, col = divmod(lane, HALF)
                x = 2 * col + c - 1
                if x >= 0:
                    table[(2 * row + b + 1) * 64 + x, 3 * b + c, lane] = 1
    return table.reshape(WINDOW, 9 * LANES)


def placement():
    table = np.zeros((27, CIN, 4, 512), np.float32)
    for a in range(3):
        for bc in range(9):
            for i in range(CIN):
                for q in range(4):
                    src, zp = divmod(2 * q + a + 1, PLANES)
                    table[9 * a + bc, i, q, bc * ROWS + src * 16 + i * PLANES + zp] = 1
    return table.reshape(27 * CIN, 4 * 512)


def leaky_relu(value):
    return jnp.where(value > 0, value, neg_slope * value)


def slots():
    where = {}
    free = [(tile, 3) for tile in range(6)]
    for bc in range(9):
        for a in range(3):
            where[9 * a + bc] = (bc, a) if bc < 7 else free.pop(0)
    return where


def prepare_kernel(k1_ref, place_ref, k2_ref, w1_ref, w2_ref):
    spread = jnp.dot(k1_ref[...], place_ref[...], preferred_element_type=jnp.float32)
    for q in range(4):
        w1_ref[q * C1 : (q + 1) * C1, :] = spread[:, 512 * q : 512 * q + 9 * ROWS].astype(jnp.bfloat16)
    blank = jnp.zeros((C2, C1), jnp.bfloat16)
    for bc in range(9):
        taps = [k2_ref[9 * a + bc] for a in range(3)]
        here = slice(bc * LANES, (bc + 1) * LANES)
        w2_ref[0:C2, here] = jnp.concatenate(taps + [blank], axis=1)
        w2_ref[C2 : 2 * C2, here] = jnp.concatenate([blank] + taps, axis=1)


def main_kernel(
    wide, scale, before_ref, own_ref, after_ref, select_ref, w1_ref, w2_ref, cot_ref,
    out_ref, grad_ref, x_ref, window_ref, taps_ref, act_ref, shifted_ref, back_ref,
):
    for s, ref in enumerate((before_ref, own_ref, after_ref)):
        for i in range(CIN):
            row = 16 * s + PLANES * i
            x_ref[row : row + PLANES, :] = ref[0, 0, i].astype(jnp.float32)
    window_ref[0:ROWS, 0:LANES] = jnp.zeros((ROWS, LANES), jnp.bfloat16)
    for j in range(8):
        rows = slice(j * ROWS, (j + 1) * ROWS)
        if j:
            window_ref[rows, 0:LANES] = x_ref[:, 512 * j - LANES : 512 * j].astype(jnp.bfloat16)
        window_ref[rows, LANES:WINDOW] = x_ref[:, 512 * j : 512 * j + 512].astype(jnp.bfloat16)
    for first in range(0, 9, 2):
        count = min(2, 9 - first)
        picked = jnp.dot(
            window_ref[...], select_ref[:, first * LANES : (first + count) * LANES],
            preferred_element_type=jnp.float32,
        ).astype(jnp.bfloat16)
        for k in range(count):
            for j in range(8):
                taps_ref[(first + k) * ROWS : (first + k + 1) * ROWS, j * LANES : (j + 1) * LANES] = picked[
                    j * ROWS : (j + 1) * ROWS, k * LANES : (k + 1) * LANES
                ]
    inside = jnp.where(lax.axis_index("wide") < wide - 1, 1.0, 0.0)
    margin = jnp.zeros((4 * C1, LANES), jnp.bfloat16)
    act_ref[:, 0:LANES] = margin
    act_ref[:, LANES + PLANE :] = margin
    for n in range(4):
        first_pre = jnp.dot(w1_ref[...], taps_ref[:, 256 * n : 256 * n + 256], preferred_element_type=jnp.float32)
        first_act = leaky_relu(first_pre)
        here = slice(LANES + 256 * n, LANES + 256 * n + 256)
        act_ref[0 : 3 * C1, here] = first_act[0 : 3 * C1].astype(jnp.bfloat16)
        act_ref[3 * C1 :, here] = (first_act[3 * C1 :] * inside).astype(jnp.bfloat16)
    column = lax.broadcasted_iota(jnp.int32, (1, PLANE), 1) % HALF
    left_ok = jnp.where(column > 0, 1.0, 0.0).astype(jnp.bfloat16)
    right_ok = jnp.where(column < HALF - 1, 1.0, 0.0).astype(jnp.bfloat16)
    for b in range(3):
        for c in range(3):
            begin = LANES + (b - 1) * HALF + (c - 1)
            part = act_ref[:, begin : begin + PLANE]
            if c == 0:
                part = part * left_ok
            if c == 2:
                part = part * right_ok
            shifted_ref[(3 * b + c) * LANES : (3 * b + c + 1) * LANES, :] = part
    for n in range(4):
        here = slice(256 * n, 256 * n + 256)
        pre = jnp.dot(w2_ref[...], shifted_ref[:, here], preferred_element_type=jnp.float32)
        output = leaky_relu(pre).astype(jnp.bfloat16)
        slope = jnp.where(pre > 0, 1.0, neg_slope)
        for z in range(2):
            cells = slice(z * PLANE + 256 * n, z * PLANE + 256 * n + 256)
            rows = slice(z * C2, (z + 1) * C2)
            out_ref[0, 0, :, cells] = output[rows]
            back_ref[rows, here] = (cot_ref[0, 0, :, cells].astype(jnp.float32) * slope[rows]).astype(jnp.bfloat16)
    where = slots()
    group = lax.broadcasted_iota(jnp.int32, (C2, LANES), 1) // C1
    tiles = [None] * 9
    for first in range(0, 9, 2):
        count = min(2, 9 - first)
        sums = lax.dot_general(
            back_ref[...], shifted_ref[first * LANES : (first + count) * LANES, :],
            (((1,), (1,)), ((), ())), preferred_element_type=jnp.float32,
        )
        for k in range(count):
            tile = sums[:, k * LANES : (k + 1) * LANES]
            tiles[first + k] = (tile[0:C2] + pltpu.roll(tile[C2:], LANES - C1, 1)) * scale
    for bc in (7, 8):
        for a in range(3):
            tile, place = where[9 * a + bc]
            moved = pltpu.roll(tiles[bc], ((place - a) * C1) % LANES, 1)
            tiles[tile] = jnp.where(group == place, moved, tiles[tile])
    for tile in range(7):
        grad_ref[:, tile * LANES : (tile + 1) * LANES] = tiles[tile].astype(jnp.bfloat16)


def finish_kernel(parts_ref, grad_ref):
    total = parts_ref[0].astype(jnp.float32)
    for k in range(1, parts_ref.shape[0]):
        total = total + parts_ref[k].astype(jnp.float32)
    for tap, (tile, place) in slots().items():
        begin = tile * LANES + place * C1
        grad_ref[tap] = total[:, begin : begin + C1]


def body(volumes, first_kernel, second_kernel, cotangent):
    wide = lax.axis_size("wide")
    narrow = lax.axis_size("narrow")
    cells_out = cotangent.shape[3]
    scale = 1.0 / math.sqrt(wide * narrow * cells_out)
    before = lax.ppermute(volumes, "wide", [(k, k + 1) for k in range(wide - 1)])
    after = lax.ppermute(volumes, "wide", [(k + 1, k) for k in range(wide - 1)])
    k1 = first_kernel.transpose(1, 0, 2).reshape(C1, 27 * CIN)
    w1, w2 = pl.pallas_call(
        prepare_kernel,
        out_shape=(
            jax.ShapeDtypeStruct((4 * C1, 9 * ROWS), jnp.bfloat16),
            jax.ShapeDtypeStruct((2 * C2, 9 * LANES), jnp.bfloat16),
        ),
        name="prepare",
    )(k1, jnp.asarray(placement(), jnp.bfloat16), second_kernel)
    output, term = pl.pallas_call(
        functools.partial(main_kernel, wide, scale),
        out_shape=(
            jax.ShapeDtypeStruct((1, 1, C2, cells_out), jnp.bfloat16),
            jax.ShapeDtypeStruct((C2, PACKED), jnp.bfloat16),
        ),
        scratch_shapes=[
            pltpu.VMEM((ROWS, CELLS), jnp.float32),
            pltpu.VMEM((8 * ROWS, WINDOW), jnp.bfloat16),
            pltpu.VMEM((9 * ROWS, PLANE), jnp.bfloat16),
            pltpu.VMEM((4 * C1, PLANE + 2 * LANES), jnp.bfloat16),
            pltpu.VMEM((9 * LANES, PLANE), jnp.bfloat16),
            pltpu.VMEM((2 * C2, PLANE), jnp.bfloat16),
        ],
        compiler_params=pltpu.CompilerParams(vmem_limit_bytes=24 * 2**20),
        name="local",
    )(before, volumes, after, jnp.asarray(selection(), jnp.bfloat16), w1, w2, cotangent)
    rows = C2 // narrow
    owned = lax.all_to_all(term, "narrow", 0, 0, tiled=True)
    partial = jnp.sum(owned.reshape(narrow, rows, PACKED).astype(jnp.float32), axis=0).astype(jnp.bfloat16)
    copies = jnp.broadcast_to(partial[None], (wide, rows, PACKED))
    parts = lax.all_to_all(copies, "wide", 0, 0, tiled=True)
    weight_grad = pl.pallas_call(
        finish_kernel,
        out_shape=jax.ShapeDtypeStruct((27, rows, C1), jnp.float32),
        name="finish",
    )(parts)
    return (output, weight_grad)


def solution(mesh):
    return jax.shard_map(
        body,
        mesh=mesh,
        in_specs=(P("narrow", None, None, "wide", None), P(), P(), P("narrow", None, None, "wide")),
        out_specs=(P("narrow", None, None, "wide"), P(None, "narrow", None)),
        check_vma=False,
    )
```

```python
import functools
import math

import jax
import jax.numpy as jnp
import numpy as np
from jax import lax
from jax.experimental import pallas as pl
from jax.experimental.pallas import tpu as pltpu
from jax.sharding import PartitionSpec as P

CIN = 4
C1 = 32
C2 = 64
PLANES = 4
CELLS = 4096
HALF = 32
PLANE = 1024
LANES = 128
ROWS = 3 * CIN * PLANES
WINDOW = 640
PACKED = 7 * LANES
neg_slope = 0.3


def selection():
    table = np.zeros((WINDOW, 9, LANES), np.float32)
    for b in range(3):
        for c in range(3):
            for lane in range(LANES):
                row, col = divmod(lane, HALF)
                x = 2 * col + c - 1
                if x >= 0:
                    table[(2 * row + b + 1) * 64 + x, 3 * b + c, lane] = 1
    return table.reshape(WINDOW, 9 * LANES)


def placement():
    table = np.zeros((27, CIN, 4, 512), np.float32)
    for a in range(3):
        for bc in range(9):
            for i in range(CIN):
                for q in range(4):
                    src, zp = divmod(2 * q + a + 1, PLANES)
                    table[9 * a + bc, i, q, bc * ROWS + src * 16 + i * PLANES + zp] = 1
    return table.reshape(27 * CIN, 4 * 512)


def leaky_relu(value):
    return jnp.where(value > 0, value, neg_slope * value)


def slots():
    where = {}
    free = [(tile, 3) for tile in range(6)]
    for bc in range(9):
        for a in range(3):
            where[9 * a + bc] = (bc, a) if bc < 7 else free.pop(0)
    return where


def prepare_kernel(k1_ref, place_ref, k2_ref, w1_ref, w2_ref, rows_ref):
    for tap in range(27):
        rows_ref[CIN * tap : CIN * (tap + 1), :] = k1_ref[tap].astype(jnp.float32)
    spread = lax.dot_general(
        rows_ref[...].astype(jnp.bfloat16), place_ref[...],
        (((0,), (0,)), ((), ())), preferred_element_type=jnp.float32,
    )
    for q in range(4):
        w1_ref[q * C1 : (q + 1) * C1, :] = spread[:, 512 * q : 512 * q + 9 * ROWS].astype(jnp.bfloat16)
    blank = jnp.zeros((C1, C2), jnp.bfloat16)
    for bc in range(9):
        taps = [k2_ref[9 * a + bc] for a in range(3)]
        here = slice(bc * LANES, (bc + 1) * LANES)
        lower = jnp.concatenate(taps + [blank], axis=0)
        upper = jnp.concatenate([blank] + taps, axis=0)
        w2_ref[:, here] = jnp.concatenate([lower, upper], axis=1).T


def main_kernel(
    wide, scale, before_ref, own_ref, after_ref, select_ref, w1_ref, w2_ref, cot_hbm,
    out_hbm, grad_ref, x_ref, window_ref, taps_ref, act_ref, shifted_ref, back_ref, cot_ref, out_ref, cot_sem, out_sem,
):
    cot_copy = pltpu.make_async_copy(cot_hbm, cot_ref, cot_sem)
    cot_copy.start()
    for s, ref in enumerate((before_ref, own_ref, after_ref)):
        for i in range(CIN):
            row = 16 * s + PLANES * i
            x_ref[row : row + PLANES, :] = ref[0, 0, i].astype(jnp.float32)
    window_ref[0:ROWS, 0:LANES] = jnp.zeros((ROWS, LANES), jnp.bfloat16)
    for j in range(8):
        rows = slice(j * ROWS, (j + 1) * ROWS)
        if j:
            window_ref[rows, 0:LANES] = x_ref[:, 512 * j - LANES : 512 * j].astype(jnp.bfloat16)
        window_ref[rows, LANES:WINDOW] = x_ref[:, 512 * j : 512 * j + 512].astype(jnp.bfloat16)
    for first in range(0, 9, 2):
        count = min(2, 9 - first)
        picked = jnp.dot(
            window_ref[...], select_ref[:, first * LANES : (first + count) * LANES],
            preferred_element_type=jnp.float32,
        ).astype(jnp.bfloat16)
        for k in range(count):
            for j in range(8):
                taps_ref[(first + k) * ROWS : (first + k + 1) * ROWS, j * LANES : (j + 1) * LANES] = picked[
                    j * ROWS : (j + 1) * ROWS, k * LANES : (k + 1) * LANES
                ]
    inside = jnp.where(lax.axis_index("wide") < wide - 1, 1.0, 0.0)
    margin = jnp.zeros((4 * C1, LANES), jnp.bfloat16)
    act_ref[:, 0:LANES] = margin
    act_ref[:, LANES + PLANE :] = margin
    for n in range(4):
        first_pre = jnp.dot(w1_ref[...], taps_ref[:, 256 * n : 256 * n + 256], preferred_element_type=jnp.float32)
        first_act = leaky_relu(first_pre)
        here = slice(LANES + 256 * n, LANES + 256 * n + 256)
        act_ref[0 : 3 * C1, here] = first_act[0 : 3 * C1].astype(jnp.bfloat16)
        act_ref[3 * C1 :, here] = (first_act[3 * C1 :] * inside).astype(jnp.bfloat16)
    column = lax.broadcasted_iota(jnp.int32, (1, PLANE), 1) % HALF
    left_ok = jnp.where(column > 0, 1.0, 0.0).astype(jnp.bfloat16)
    right_ok = jnp.where(column < HALF - 1, 1.0, 0.0).astype(jnp.bfloat16)
    for b in range(3):
        for c in range(3):
            begin = LANES + (b - 1) * HALF + (c - 1)
            part = act_ref[:, begin : begin + PLANE]
            if c == 0:
                part = part * left_ok
            if c == 2:
                part = part * right_ok
            shifted_ref[(3 * b + c) * LANES : (3 * b + c + 1) * LANES, :] = part
    cot_copy.wait()
    for n in range(4):
        here = slice(256 * n, 256 * n + 256)
        pre = jnp.dot(w2_ref[...], shifted_ref[:, here], preferred_element_type=jnp.float32)
        output = leaky_relu(pre).astype(jnp.bfloat16)
        slope = jnp.where(pre > 0, 1.0, neg_slope)
        for z in range(2):
            cells = slice(z * PLANE + 256 * n, z * PLANE + 256 * n + 256)
            rows = slice(z * C2, (z + 1) * C2)
            out_ref[0, 0, :, cells] = output[rows]
            back_ref[rows, here] = (cot_ref[0, 0, :, cells].astype(jnp.float32) * slope[rows]).astype(jnp.bfloat16)
    out_copy = pltpu.make_async_copy(out_ref, out_hbm, out_sem)
    out_copy.start()
    where = slots()
    group = lax.broadcasted_iota(jnp.int32, (C2, LANES), 1) // C1
    tiles = [None] * 9
    for first in range(0, 9, 2):
        count = min(2, 9 - first)
        sums = lax.dot_general(
            back_ref[...], shifted_ref[first * LANES : (first + count) * LANES, :],
            (((1,), (1,)), ((), ())), preferred_element_type=jnp.float32,
        )
        for k in range(count):
            tile = sums[:, k * LANES : (k + 1) * LANES]
            tiles[first + k] = (tile[0:C2] + pltpu.roll(tile[C2:], LANES - C1, 1)) * scale
    for bc in (7, 8):
        for a in range(3):
            tile, place = where[9 * a + bc]
            moved = pltpu.roll(tiles[bc], ((place - a) * C1) % LANES, 1)
            tiles[tile] = jnp.where(group == place, moved, tiles[tile])
    for tile in range(7):
        grad_ref[:, tile * LANES : (tile + 1) * LANES] = tiles[tile].astype(jnp.bfloat16)
    out_copy.wait()


def finish_kernel(parts_ref, grad_ref):
    total = parts_ref[0].astype(jnp.float32)
    for k in range(1, parts_ref.shape[0]):
        total = total + parts_ref[k].astype(jnp.float32)
    for tap, (tile, place) in slots().items():
        begin = tile * LANES + place * C1
        grad_ref[tap] = total[:, begin : begin + C1]


def body(volumes, first_kernel, second_kernel, cotangent):
    wide = lax.axis_size("wide")
    narrow = lax.axis_size("narrow")
    cells_out = cotangent.shape[3]
    scale = 1.0 / math.sqrt(wide * narrow * cells_out)
    before = lax.ppermute(volumes, "wide", [(k, k + 1) for k in range(wide - 1)])
    after = lax.ppermute(volumes, "wide", [(k + 1, k) for k in range(wide - 1)])
    w1, w2 = pl.pallas_call(
        prepare_kernel,
        out_shape=(
            jax.ShapeDtypeStruct((4 * C1, 9 * ROWS), jnp.bfloat16),
            jax.ShapeDtypeStruct((2 * C2, 9 * LANES), jnp.bfloat16),
        ),
        scratch_shapes=[pltpu.VMEM((27 * CIN, C1), jnp.float32)],
        compiler_params=pltpu.CompilerParams(vmem_limit_bytes=8 * 2**20),
        name="prepare",
    )(first_kernel.transpose(0, 2, 1), jnp.asarray(placement(), jnp.bfloat16), second_kernel.transpose(0, 2, 1))
    output, term = pl.pallas_call(
        functools.partial(main_kernel, wide, scale),
        in_specs=[pl.BlockSpec(memory_space=pltpu.VMEM)] * 6 + [pl.BlockSpec(memory_space=pl.ANY)],
        out_specs=(pl.BlockSpec(memory_space=pl.ANY), pl.BlockSpec(memory_space=pltpu.VMEM)),
        out_shape=(
            jax.ShapeDtypeStruct((1, 1, C2, cells_out), jnp.bfloat16),
            jax.ShapeDtypeStruct((C2, PACKED), jnp.bfloat16),
        ),
        scratch_shapes=[
            pltpu.VMEM((ROWS, CELLS), jnp.float32),
            pltpu.VMEM((8 * ROWS, WINDOW), jnp.bfloat16),
            pltpu.VMEM((9 * ROWS, PLANE), jnp.bfloat16),
            pltpu.VMEM((4 * C1, PLANE + 2 * LANES), jnp.bfloat16),
            pltpu.VMEM((9 * LANES, PLANE), jnp.bfloat16),
            pltpu.VMEM((2 * C2, PLANE), jnp.bfloat16),
            pltpu.VMEM((1, 1, C2, cells_out), jnp.bfloat16),
            pltpu.VMEM((1, 1, C2, cells_out), jnp.bfloat16),
            pltpu.SemaphoreType.DMA,
            pltpu.SemaphoreType.DMA,
        ],
        compiler_params=pltpu.CompilerParams(vmem_limit_bytes=24 * 2**20),
        name="local",
    )(before, volumes, after, jnp.asarray(selection(), jnp.bfloat16), w1, w2, cotangent)
    rows = C2 // narrow
    owned = lax.all_to_all(term, "narrow", 0, 0, tiled=True)
    partial = jnp.sum(owned.reshape(narrow, rows, PACKED).astype(jnp.float32), axis=0).astype(jnp.bfloat16)
    copies = jnp.broadcast_to(partial[None], (wide, rows, PACKED))
    parts = lax.all_to_all(copies, "wide", 0, 0, tiled=True)
    weight_grad = pl.pallas_call(
        finish_kernel,
        out_shape=jax.ShapeDtypeStruct((27, rows, C1), jnp.float32),
        compiler_params=pltpu.CompilerParams(vmem_limit_bytes=8 * 2**20),
        name="finish",
    )(parts)
    return (output, weight_grad)


def solution(mesh):
    return jax.shard_map(
        body,
        mesh=mesh,
        in_specs=(P("narrow", None, None, "wide", None), P(), P(), P("narrow", None, None, "wide")),
        out_specs=(P("narrow", None, None, "wide"), P(None, "narrow", None)),
        check_vma=False,
    )
```

```python
import functools
import math

import jax
import jax.numpy as jnp
import numpy as np
from jax import lax
from jax.experimental import pallas as pl
from jax.experimental.pallas import tpu as pltpu
from jax.sharding import PartitionSpec as P

CIN = 4
C1 = 32
C2 = 64
PLANES = 4
CELLS = 4096
HALF = 32
PLANE = 1024
LANES = 128
ROWS = 3 * CIN * PLANES
WINDOW = 640
PACKED = 8 * LANES
MIB = 2**20
neg_slope = 0.3


def selection():
    table = np.zeros((WINDOW, 9, LANES), np.float32)
    for b in range(3):
        for c in range(3):
            for lane in range(LANES):
                row, col = divmod(lane, HALF)
                x = 2 * col + c - 1
                if x >= 0:
                    table[(2 * row + b + 1) * 64 + x, 3 * b + c, lane] = 1
    return table.reshape(WINDOW, 9 * LANES)


def placement():
    table = np.zeros((27, CIN, 4, 512), np.float32)
    for a in range(3):
        for bc in range(9):
            for i in range(CIN):
                for q in range(4):
                    src, zp = divmod(2 * q + a + 1, PLANES)
                    table[9 * a + bc, i, q, bc * ROWS + src * 16 + i * PLANES + zp] = 1
    return table.reshape(27 * CIN, 4 * 512)


def leaky_relu(value):
    return jnp.where(value > 0, value, neg_slope * value)


def slots():
    return {9 * a + bc: (bc, a) if bc < 8 else (a, 3) for a in range(3) for bc in range(9)}


def plane_rows(volume_ref, rows_ref):
    for i in range(CIN):
        rows_ref[PLANES * i : PLANES * (i + 1), :] = volume_ref[0, 0, i].astype(jnp.float32)
    return rows_ref[...].astype(jnp.bfloat16)


def prepare_kernel(
    k1_hbm, place_hbm, k2_hbm, own_hbm, select_hbm, cot_hbm, w1_ref, w2_ref, mine_ref, select_ref, cot_ref,
    k1_ref, place_ref, k2_ref, own_ref, k1_rows_ref, rows_ref, sems,
):
    moves = ((k2_hbm, k2_ref), (own_hbm, own_ref), (k1_hbm, k1_ref), (place_hbm, place_ref), (select_hbm, select_ref), (cot_hbm, cot_ref))
    copies = [pltpu.make_async_copy(src, dst, sems.at[k]) for k, (src, dst) in enumerate(moves)]
    for copy in copies:
        copy.start()
    copies[0].wait()
    blank = jnp.zeros((C1, C2), jnp.bfloat16)
    for bc in range(9):
        taps = [k2_ref[9 * a + bc] for a in range(3)]
        here = slice(bc * LANES, (bc + 1) * LANES)
        lower = jnp.concatenate(taps + [blank], axis=0)
        upper = jnp.concatenate([blank] + taps, axis=0)
        w2_ref[:, here] = jnp.concatenate([lower, upper], axis=1).T
    copies[1].wait()
    mine_ref[...] = plane_rows(own_ref, rows_ref)
    copies[2].wait()
    for tap in range(27):
        k1_rows_ref[CIN * tap : CIN * (tap + 1), :] = k1_ref[tap].astype(jnp.float32)
    copies[3].wait()
    spread = lax.dot_general(
        k1_rows_ref[...].astype(jnp.bfloat16), place_ref[...],
        (((0,), (0,)), ((), ())), preferred_element_type=jnp.float32,
    )
    for q in range(4):
        w1_ref[q * C1 : (q + 1) * C1, :] = spread[:, 512 * q : 512 * q + 9 * ROWS].astype(jnp.bfloat16)
    copies[4].wait()
    copies[5].wait()


def main_kernel(
    wide, scale, before_ref, mine_ref, after_ref, select_ref, w1_ref, w2_ref, cot_ref, out_hbm, grad_ref,
    rows_ref, window_ref, taps_ref, act_ref, shifted_ref, back_ref, out_ref, out_sem,
):
    sources = (plane_rows(before_ref, rows_ref.at[0]), mine_ref[...], plane_rows(after_ref, rows_ref.at[1]))
    for s, rows in enumerate(sources):
        for j in range(8):
            top = j * ROWS + 16 * s
            if j:
                window_ref[top : top + 16, 0:LANES] = rows[:, 512 * j - LANES : 512 * j]
            else:
                window_ref[top : top + 16, 0:LANES] = jnp.zeros((16, LANES), jnp.bfloat16)
            window_ref[top : top + 16, LANES:WINDOW] = rows[:, 512 * j : 512 * j + 512]
    for first in range(0, 9, 2):
        count = min(2, 9 - first)
        picked = jnp.dot(
            window_ref[...], select_ref[:, first * LANES : (first + count) * LANES],
            preferred_element_type=jnp.float32,
        ).astype(jnp.bfloat16)
        for k in range(count):
            for j in range(8):
                taps_ref[(first + k) * ROWS : (first + k + 1) * ROWS, j * LANES : (j + 1) * LANES] = picked[
                    j * ROWS : (j + 1) * ROWS, k * LANES : (k + 1) * LANES
                ]
    inside = jnp.where(lax.axis_index("wide") < wide - 1, 1.0, 0.0)
    margin = jnp.zeros((4 * C1, LANES), jnp.bfloat16)
    act_ref[:, 0:LANES] = margin
    act_ref[:, LANES + PLANE :] = margin
    for n in range(4):
        first_pre = jnp.dot(w1_ref[...], taps_ref[:, 256 * n : 256 * n + 256], preferred_element_type=jnp.float32)
        first_act = leaky_relu(first_pre)
        here = slice(LANES + 256 * n, LANES + 256 * n + 256)
        act_ref[0 : 3 * C1, here] = first_act[0 : 3 * C1].astype(jnp.bfloat16)
        act_ref[3 * C1 :, here] = (first_act[3 * C1 :] * inside).astype(jnp.bfloat16)
    column = lax.broadcasted_iota(jnp.int32, (1, PLANE), 1) % HALF
    left_ok = jnp.where(column > 0, 1.0, 0.0).astype(jnp.bfloat16)
    right_ok = jnp.where(column < HALF - 1, 1.0, 0.0).astype(jnp.bfloat16)
    for b in range(3):
        for c in range(3):
            begin = LANES + (b - 1) * HALF + (c - 1)
            part = act_ref[:, begin : begin + PLANE]
            if c == 0:
                part = part * left_ok
            if c == 2:
                part = part * right_ok
            shifted_ref[(3 * b + c) * LANES : (3 * b + c + 1) * LANES, :] = part
    for n in range(4):
        here = slice(256 * n, 256 * n + 256)
        pre = jnp.dot(w2_ref[...], shifted_ref[:, here], preferred_element_type=jnp.float32)
        output = leaky_relu(pre).astype(jnp.bfloat16)
        slope = jnp.where(pre > 0, 1.0, neg_slope)
        for z in range(2):
            cells = slice(z * PLANE + 256 * n, z * PLANE + 256 * n + 256)
            rows = slice(z * C2, (z + 1) * C2)
            out_ref[0, 0, :, cells] = output[rows]
            back_ref[rows, here] = (cot_ref[0, 0, :, cells].astype(jnp.float32) * slope[rows]).astype(jnp.bfloat16)
    out_copy = pltpu.make_async_copy(out_ref, out_hbm, out_sem)
    out_copy.start()
    group = lax.broadcasted_iota(jnp.int32, (C2, LANES), 1) // C1
    tiles = []
    for first in range(0, 9, 2):
        count = min(2, 9 - first)
        sums = lax.dot_general(
            back_ref[...], shifted_ref[first * LANES : (first + count) * LANES, :],
            (((1,), (1,)), ((), ())), preferred_element_type=jnp.float32,
        )
        for k in range(count):
            tile = sums[:, k * LANES : (k + 1) * LANES]
            tiles.append((tile[0:C2] + pltpu.roll(tile[C2:], LANES - C1, 1)) * scale)
    last = tiles.pop()
    for a in range(3):
        tiles[a] = jnp.where(group == 3, pltpu.roll(last, (3 - a) * C1, 1), tiles[a])
    pieces, rows, lanes = grad_ref.shape
    narrow = C2 // rows
    for tile in range(8):
        rounded = tiles[tile].astype(jnp.bfloat16)
        for n in range(narrow):
            part = rounded[n * rows : (n + 1) * rows]
            if pieces > 1:
                grad_ref[tile * narrow + n] = part
            else:
                grad_ref[0, n * rows : (n + 1) * rows, tile * LANES : (tile + 1) * LANES] = part
    out_copy.wait()


def finish_kernel(parts_ref, grad_ref):
    for tap, (tile, place) in slots().items():
        grad_ref[tap] = parts_ref[tile, :, place * C1 : (place + 1) * C1]


def body(volumes, first_kernel, second_kernel, cotangent):
    wide = lax.axis_size("wide")
    narrow = lax.axis_size("narrow")
    cells_out = cotangent.shape[3]
    scale = 1.0 / math.sqrt(wide * narrow * cells_out)
    before = lax.ppermute(volumes, "wide", [(k, k + 1) for k in range(wide - 1)])
    after = lax.ppermute(volumes, "wide", [(k + 1, k) for k in range(wide - 1)])
    pinned = pl.BlockSpec(memory_space=pltpu.HBM)
    fast = pl.BlockSpec(memory_space=pltpu.VMEM)
    w1, w2, mine, select, cot = pl.pallas_call(
        prepare_kernel,
        in_specs=[pinned] * 6,
        out_specs=(fast,) * 5,
        out_shape=(
            jax.ShapeDtypeStruct((4 * C1, 9 * ROWS), jnp.bfloat16),
            jax.ShapeDtypeStruct((2 * C2, 9 * LANES), jnp.bfloat16),
            jax.ShapeDtypeStruct((CIN * PLANES, CELLS), jnp.bfloat16),
            jax.ShapeDtypeStruct((WINDOW, 9 * LANES), jnp.bfloat16),
            jax.ShapeDtypeStruct(cotangent.shape, jnp.bfloat16),
        ),
        scratch_shapes=[
            pltpu.VMEM((27, CIN, C1), jnp.bfloat16),
            pltpu.VMEM((27 * CIN, 4 * 512), jnp.bfloat16),
            pltpu.VMEM((27, C1, C2), jnp.bfloat16),
            pltpu.VMEM(volumes.shape, jnp.bfloat16),
            pltpu.VMEM((27 * CIN, C1), jnp.float32),
            pltpu.VMEM((CIN * PLANES, CELLS), jnp.float32),
            pltpu.SemaphoreType.DMA((6,)),
        ],
        compiler_params=pltpu.CompilerParams(vmem_limit_bytes=16 * MIB),
        cost_estimate=pl.CostEstimate(flops=10**9, bytes_accessed=4 * MIB, transcendentals=0),
        name="prepare",
    )(*(pltpu.with_memory_space_constraint(x, pltpu.HBM) for x in (
        first_kernel.transpose(0, 2, 1), jnp.asarray(placement(), jnp.bfloat16), second_kernel.transpose(0, 2, 1),
        volumes, jnp.asarray(selection(), jnp.bfloat16), cotangent,
    )))
    rows = C2 // narrow
    direct = rows % 16 == 0 and wide * LANES == PACKED
    pieces = (wide * narrow, rows, LANES) if direct else (1, C2, PACKED)
    output, term = pl.pallas_call(
        functools.partial(main_kernel, wide, scale),
        in_specs=[fast] * 7,
        out_specs=(pl.BlockSpec(memory_space=pl.ANY), fast),
        out_shape=(
            jax.ShapeDtypeStruct((1, 1, C2, cells_out), jnp.bfloat16),
            jax.ShapeDtypeStruct(pieces, jnp.bfloat16),
        ),
        scratch_shapes=[
            pltpu.VMEM((2, CIN * PLANES, CELLS), jnp.float32),
            pltpu.VMEM((8 * ROWS, WINDOW), jnp.bfloat16),
            pltpu.VMEM((9 * ROWS, PLANE), jnp.bfloat16),
            pltpu.VMEM((4 * C1, PLANE + 2 * LANES), jnp.bfloat16),
            pltpu.VMEM((9 * LANES, PLANE), jnp.bfloat16),
            pltpu.VMEM((2 * C2, PLANE), jnp.bfloat16),
            pltpu.VMEM((1, 1, C2, cells_out), jnp.bfloat16),
            pltpu.SemaphoreType.DMA,
        ],
        compiler_params=pltpu.CompilerParams(vmem_limit_bytes=24 * MIB),
        name="local",
    )(before, mine, after, select, w1, w2, cot)
    lanes = PACKED // wide
    if not direct:
        term = term.reshape(narrow, rows, wide, lanes).transpose(2, 0, 1, 3).reshape(wide * narrow, rows, lanes)
    received = lax.all_to_all(term, ("wide", "narrow"), 0, 0, tiled=True)
    owned = jnp.sum(received.astype(jnp.float32), axis=0)
    parts = lax.all_to_all(jnp.broadcast_to(owned[None], (wide, rows, lanes)), "wide", 0, 0, tiled=True)
    if not direct:
        parts = parts.transpose(1, 0, 2).reshape(rows, PACKED // LANES, LANES).transpose(1, 0, 2)
    weight_grad = pl.pallas_call(
        finish_kernel,
        out_shape=jax.ShapeDtypeStruct((27, rows, C1), jnp.float32),
        compiler_params=pltpu.CompilerParams(vmem_limit_bytes=8 * MIB),
        name="finish",
    )(parts)
    return (output, weight_grad)


def solution(mesh):
    return jax.shard_map(
        body,
        mesh=mesh,
        in_specs=(P("narrow", None, None, "wide", None), P(), P(), P("narrow", None, None, "wide")),
        out_specs=(P("narrow", None, None, "wide"), P(None, "narrow", None)),
        check_vma=False,
    )
```

```python
import functools
import math

import jax
import jax.numpy as jnp
import numpy as np
from jax import lax
from jax.experimental import pallas as pl
from jax.experimental.pallas import tpu as pltpu
from jax.sharding import PartitionSpec as P

CIN = 4
C1 = 32
C2 = 64
PLANES = 4
CELLS = 4096
HALF = 32
PLANE = 1024
LANES = 128
ROWS = 3 * CIN * PLANES
WINDOW = 640
PACKED = 7 * LANES
MIB = 2**20
neg_slope = 0.3


def selection():
    table = np.zeros((WINDOW, 9, LANES), np.float32)
    for b in range(3):
        for c in range(3):
            for lane in range(LANES):
                row, col = divmod(lane, HALF)
                x = 2 * col + c - 1
                if x >= 0:
                    table[(2 * row + b + 1) * 64 + x, 3 * b + c, lane] = 1
    return table.reshape(WINDOW, 9 * LANES)


def placement():
    table = np.zeros((27, CIN, 4, 512), np.float32)
    for a in range(3):
        for bc in range(9):
            for i in range(CIN):
                for q in range(4):
                    src, zp = divmod(2 * q + a + 1, PLANES)
                    table[9 * a + bc, i, q, bc * ROWS + src * 16 + i * PLANES + zp] = 1
    return table.reshape(27 * CIN, 4 * 512)


def leaky_relu(value):
    return jnp.where(value > 0, value, neg_slope * value)


def slots():
    where = {}
    free = [(tile, 3) for tile in range(6)]
    for bc in range(9):
        for a in range(3):
            where[9 * a + bc] = (bc, a) if bc < 7 else free.pop(0)
    return where


def plane_rows(volume_ref, rows_ref):
    for i in range(CIN):
        rows_ref[PLANES * i : PLANES * (i + 1), :] = volume_ref[0, 0, i].astype(jnp.float32)


def prepare_kernel(
    k1_hbm, place_hbm, k2_hbm, own_hbm, select_hbm, cot_hbm, w1_ref, w2_ref, mine_ref, select_ref, cot_ref,
    k1_ref, place_ref, k2_ref, own_ref, k1_rows_ref, rows_ref, sems,
):
    moves = ((k2_hbm, k2_ref), (own_hbm, own_ref), (k1_hbm, k1_ref), (place_hbm, place_ref), (select_hbm, select_ref), (cot_hbm, cot_ref))
    copies = [pltpu.make_async_copy(src, dst, sems.at[k]) for k, (src, dst) in enumerate(moves)]
    for copy in copies:
        copy.start()
    copies[0].wait()
    blank = jnp.zeros((C1, C2), jnp.bfloat16)
    for bc in range(9):
        taps = [k2_ref[9 * a + bc] for a in range(3)]
        here = slice(bc * LANES, (bc + 1) * LANES)
        lower = jnp.concatenate(taps + [blank], axis=0)
        upper = jnp.concatenate([blank] + taps, axis=0)
        w2_ref[:, here] = jnp.concatenate([lower, upper], axis=1).T
    copies[1].wait()
    plane_rows(own_ref, rows_ref)
    mine_ref[...] = rows_ref[...].astype(jnp.bfloat16)
    copies[2].wait()
    for tap in range(27):
        k1_rows_ref[CIN * tap : CIN * (tap + 1), :] = k1_ref[tap].astype(jnp.float32)
    copies[3].wait()
    spread = lax.dot_general(
        k1_rows_ref[...].astype(jnp.bfloat16), place_ref[...],
        (((0,), (0,)), ((), ())), preferred_element_type=jnp.float32,
    )
    for q in range(4):
        w1_ref[q * C1 : (q + 1) * C1, :] = spread[:, 512 * q : 512 * q + 9 * ROWS].astype(jnp.bfloat16)
    copies[4].wait()
    copies[5].wait()


def main_kernel(
    wide, scale, across_ref, mine_ref, within_ref, select_ref, w1_ref, w2_ref, cot_ref, out_hbm, grad_ref,
    rows_ref, window_ref, taps_ref, act_ref, shifted_ref, back_ref, out_ref, out_sem,
):
    place = lax.axis_index("wide")
    odd = lax.rem(place, 2)
    plane_rows(across_ref, rows_ref.at[odd])
    plane_rows(within_ref, rows_ref.at[1 - odd])
    sources = (rows_ref[0].astype(jnp.bfloat16), mine_ref[...], rows_ref[1].astype(jnp.bfloat16))
    for s, rows in enumerate(sources):
        for j in range(8):
            top = j * ROWS + 16 * s
            if j:
                window_ref[top : top + 16, 0:LANES] = rows[:, 512 * j - LANES : 512 * j]
            else:
                window_ref[top : top + 16, 0:LANES] = jnp.zeros((16, LANES), jnp.bfloat16)
            window_ref[top : top + 16, LANES:WINDOW] = rows[:, 512 * j : 512 * j + 512]
    for first in range(0, 9, 2):
        count = min(2, 9 - first)
        picked = jnp.dot(
            window_ref[...], select_ref[:, first * LANES : (first + count) * LANES],
            preferred_element_type=jnp.float32,
        ).astype(jnp.bfloat16)
        for k in range(count):
            for j in range(8):
                taps_ref[(first + k) * ROWS : (first + k + 1) * ROWS, j * LANES : (j + 1) * LANES] = picked[
                    j * ROWS : (j + 1) * ROWS, k * LANES : (k + 1) * LANES
                ]
    inside = jnp.where(place < wide - 1, 1.0, 0.0)
    margin = jnp.zeros((4 * C1, LANES), jnp.bfloat16)
    act_ref[:, 0:LANES] = margin
    act_ref[:, LANES + PLANE :] = margin
    for n in range(4):
        first_pre = jnp.dot(w1_ref[...], taps_ref[:, 256 * n : 256 * n + 256], preferred_element_type=jnp.float32)
        first_act = leaky_relu(first_pre)
        here = slice(LANES + 256 * n, LANES + 256 * n + 256)
        act_ref[0 : 3 * C1, here] = first_act[0 : 3 * C1].astype(jnp.bfloat16)
        act_ref[3 * C1 :, here] = (first_act[3 * C1 :] * inside).astype(jnp.bfloat16)
    column = lax.broadcasted_iota(jnp.int32, (1, PLANE), 1) % HALF
    left_ok = jnp.where(column > 0, 1.0, 0.0).astype(jnp.bfloat16)
    right_ok = jnp.where(column < HALF - 1, 1.0, 0.0).astype(jnp.bfloat16)
    for b in range(3):
        for c in range(3):
            begin = LANES + (b - 1) * HALF + (c - 1)
            part = act_ref[:, begin : begin + PLANE]
            if c == 0:
                part = part * left_ok
            if c == 2:
                part = part * right_ok
            shifted_ref[(3 * b + c) * LANES : (3 * b + c + 1) * LANES, :] = part
    for n in range(4):
        here = slice(256 * n, 256 * n + 256)
        pre = jnp.dot(w2_ref[...], shifted_ref[:, here], preferred_element_type=jnp.float32)
        output = leaky_relu(pre).astype(jnp.bfloat16)
        slope = jnp.where(pre > 0, 1.0, neg_slope)
        for z in range(2):
            cells = slice(z * PLANE + 256 * n, z * PLANE + 256 * n + 256)
            rows = slice(z * C2, (z + 1) * C2)
            out_ref[0, 0, :, cells] = output[rows]
            back_ref[rows, here] = (cot_ref[0, 0, :, cells].astype(jnp.float32) * slope[rows]).astype(jnp.bfloat16)
    out_copy = pltpu.make_async_copy(out_ref, out_hbm, out_sem)
    out_copy.start()
    group = lax.broadcasted_iota(jnp.int32, (C2, LANES), 1) // C1
    tiles = []
    for first in range(0, 9, 2):
        count = min(2, 9 - first)
        sums = lax.dot_general(
            back_ref[...], shifted_ref[first * LANES : (first + count) * LANES, :],
            (((1,), (1,)), ((), ())), preferred_element_type=jnp.float32,
        )
        for k in range(count):
            tile = sums[:, k * LANES : (k + 1) * LANES]
            tiles.append((tile[0:C2] + pltpu.roll(tile[C2:], LANES - C1, 1)) * scale)
    where = slots()
    for bc in (7, 8):
        for a in range(3):
            tile, slot = where[9 * a + bc]
            tiles[tile] = jnp.where(group == slot, pltpu.roll(tiles[bc], (slot - a) * C1, 1), tiles[tile])
    for tile in range(7):
        grad_ref[:, tile * LANES : (tile + 1) * LANES] = tiles[tile].astype(jnp.bfloat16)
    out_copy.wait()


def finish_kernel(parts_ref, grad_ref):
    total = parts_ref[0].astype(jnp.float32)
    for k in range(1, parts_ref.shape[0]):
        total = total + parts_ref[k].astype(jnp.float32)
    for tap, (tile, slot) in slots().items():
        begin = tile * LANES + slot * C1
        grad_ref[tap] = total[:, begin : begin + C1]


def body(volumes, first_kernel, second_kernel, cotangent):
    wide = lax.axis_size("wide")
    narrow = lax.axis_size("narrow")
    cells_out = cotangent.shape[3]
    scale = 1.0 / math.sqrt(wide * narrow * cells_out)
    across = lax.ppermute(volumes, "wide", [p for k in range(1, wide - 1, 2) for p in ((k, k + 1), (k + 1, k))])
    within = lax.ppermute(volumes, "wide", [p for k in range(0, wide - 1, 2) for p in ((k, k + 1), (k + 1, k))])
    pinned = pl.BlockSpec(memory_space=pltpu.HBM)
    fast = pl.BlockSpec(memory_space=pltpu.VMEM)
    w1, w2, mine, select, cot = pl.pallas_call(
        prepare_kernel,
        in_specs=[pinned] * 6,
        out_specs=(fast,) * 5,
        out_shape=(
            jax.ShapeDtypeStruct((4 * C1, 9 * ROWS), jnp.bfloat16),
            jax.ShapeDtypeStruct((2 * C2, 9 * LANES), jnp.bfloat16),
            jax.ShapeDtypeStruct((CIN * PLANES, CELLS), jnp.bfloat16),
            jax.ShapeDtypeStruct((WINDOW, 9 * LANES), jnp.bfloat16),
            jax.ShapeDtypeStruct(cotangent.shape, jnp.bfloat16),
        ),
        scratch_shapes=[
            pltpu.VMEM((27, CIN, C1), jnp.bfloat16),
            pltpu.VMEM((27 * CIN, 4 * 512), jnp.bfloat16),
            pltpu.VMEM((27, C1, C2), jnp.bfloat16),
            pltpu.VMEM(volumes.shape, jnp.bfloat16),
            pltpu.VMEM((27 * CIN, C1), jnp.float32),
            pltpu.VMEM((CIN * PLANES, CELLS), jnp.float32),
            pltpu.SemaphoreType.DMA((6,)),
        ],
        compiler_params=pltpu.CompilerParams(vmem_limit_bytes=16 * MIB),
        cost_estimate=pl.CostEstimate(flops=10**9, bytes_accessed=4 * MIB, transcendentals=0),
        name="prepare",
    )(*(pltpu.with_memory_space_constraint(x, pltpu.HBM) for x in (
        first_kernel.transpose(0, 2, 1), jnp.asarray(placement(), jnp.bfloat16), second_kernel.transpose(0, 2, 1),
        volumes, jnp.asarray(selection(), jnp.bfloat16), cotangent,
    )))
    rows = C2 // narrow
    output, term = pl.pallas_call(
        functools.partial(main_kernel, wide, scale),
        in_specs=[fast] * 7,
        out_specs=(pl.BlockSpec(memory_space=pl.ANY), fast),
        out_shape=(
            jax.ShapeDtypeStruct((1, 1, C2, cells_out), jnp.bfloat16),
            jax.ShapeDtypeStruct((C2, PACKED), jnp.bfloat16),
        ),
        scratch_shapes=[
            pltpu.VMEM((2, CIN * PLANES, CELLS), jnp.float32),
            pltpu.VMEM((8 * ROWS, WINDOW), jnp.bfloat16),
            pltpu.VMEM((9 * ROWS, PLANE), jnp.bfloat16),
            pltpu.VMEM((4 * C1, PLANE + 2 * LANES), jnp.bfloat16),
            pltpu.VMEM((9 * LANES, PLANE), jnp.bfloat16),
            pltpu.VMEM((2 * C2, PLANE), jnp.bfloat16),
            pltpu.VMEM((1, 1, C2, cells_out), jnp.bfloat16),
            pltpu.SemaphoreType.DMA,
        ],
        compiler_params=pltpu.CompilerParams(vmem_limit_bytes=24 * MIB),
        name="local",
    )(across, mine, within, select, w1, w2, cot)
    received = lax.all_to_all(term, "narrow", 0, 0, tiled=True)
    owned = jnp.sum(received.reshape(narrow, rows, PACKED).astype(jnp.float32), axis=0).astype(jnp.bfloat16)
    parts = lax.all_to_all(jnp.broadcast_to(owned[None], (wide, rows, PACKED)), "wide", 0, 0, tiled=True)
    weight_grad = pl.pallas_call(
        finish_kernel,
        out_shape=jax.ShapeDtypeStruct((27, rows, C1), jnp.float32),
        compiler_params=pltpu.CompilerParams(vmem_limit_bytes=8 * MIB),
        name="finish",
    )(parts)
    return (output, weight_grad)


def solution(mesh):
    return jax.shard_map(
        body,
        mesh=mesh,
        in_specs=(P("narrow", None, None, "wide", None), P(), P(), P("narrow", None, None, "wide")),
        out_specs=(P("narrow", None, None, "wide"), P(None, "narrow", None)),
        check_vma=False,
    )
```

```python
import functools
import math

import jax
import jax.numpy as jnp
import numpy as np
from jax import lax
from jax.experimental import pallas as pl
from jax.experimental.pallas import tpu as pltpu
from jax.sharding import PartitionSpec as P

CIN = 4
C1 = 32
C2 = 64
PLANES = 4
CELLS = 4096
HALF = 32
PLANE = 1024
LANES = 128
ROWS = 3 * CIN * PLANES
WINDOW = 640
PACKED = 7 * LANES
MIB = 2**20
WIDE = ("chip", "core")
neg_slope = 0.3


def selection():
    table = np.zeros((WINDOW, 9, LANES), np.float32)
    for b in range(3):
        for c in range(3):
            for lane in range(LANES):
                row, col = divmod(lane, HALF)
                x = 2 * col + c - 1
                if x >= 0:
                    table[(2 * row + b + 1) * 64 + x, 3 * b + c, lane] = 1
    return table.reshape(WINDOW, 9 * LANES)


def placement():
    table = np.zeros((27, CIN, 4, 512), np.float32)
    for a in range(3):
        for bc in range(9):
            for i in range(CIN):
                for q in range(4):
                    src, zp = divmod(2 * q + a + 1, PLANES)
                    table[9 * a + bc, i, q, bc * ROWS + src * 16 + i * PLANES + zp] = 1
    return table.reshape(27 * CIN, 4 * 512)


def leaky_relu(value):
    return jnp.where(value > 0, value, neg_slope * value)


def slots():
    where = {}
    free = [(tile, 3) for tile in range(6)]
    for bc in range(9):
        for a in range(3):
            where[9 * a + bc] = (bc, a) if bc < 7 else free.pop(0)
    return where


def plane_rows(volume_ref, rows_ref):
    for i in range(CIN):
        rows_ref[PLANES * i : PLANES * (i + 1), :] = volume_ref[0, 0, i].astype(jnp.float32)


def prepare_kernel(
    k1_hbm, place_hbm, k2_hbm, own_hbm, select_hbm, cot_hbm, w1_ref, w2_ref, mine_ref, select_ref, cot_ref,
    k1_ref, place_ref, k2_ref, own_ref, k1_rows_ref, rows_ref, sems,
):
    moves = ((k2_hbm, k2_ref), (own_hbm, own_ref), (k1_hbm, k1_ref), (place_hbm, place_ref), (select_hbm, select_ref), (cot_hbm, cot_ref))
    copies = [pltpu.make_async_copy(src, dst, sems.at[k]) for k, (src, dst) in enumerate(moves)]
    for copy in copies:
        copy.start()
    copies[0].wait()
    blank = jnp.zeros((C1, C2), jnp.bfloat16)
    for bc in range(9):
        taps = [k2_ref[9 * a + bc] for a in range(3)]
        here = slice(bc * LANES, (bc + 1) * LANES)
        lower = jnp.concatenate(taps + [blank], axis=0)
        upper = jnp.concatenate([blank] + taps, axis=0)
        w2_ref[:, here] = jnp.concatenate([lower, upper], axis=1).T
    copies[1].wait()
    plane_rows(own_ref, rows_ref)
    mine_ref[...] = rows_ref[...].astype(jnp.bfloat16)
    copies[2].wait()
    for tap in range(27):
        k1_rows_ref[CIN * tap : CIN * (tap + 1), :] = k1_ref[tap].astype(jnp.float32)
    copies[3].wait()
    spread = lax.dot_general(
        k1_rows_ref[...].astype(jnp.bfloat16), place_ref[...],
        (((0,), (0,)), ((), ())), preferred_element_type=jnp.float32,
    )
    for q in range(4):
        w1_ref[q * C1 : (q + 1) * C1, :] = spread[:, 512 * q : 512 * q + 9 * ROWS].astype(jnp.bfloat16)
    copies[4].wait()
    copies[5].wait()


def main_kernel(
    wide, scale, across_ref, mine_ref, within_ref, select_ref, w1_ref, w2_ref, cot_ref, out_hbm, grad_ref,
    rows_ref, window_ref, taps_ref, act_ref, shifted_ref, back_ref, out_ref, out_sem,
):
    place = 2 * lax.axis_index("chip") + lax.axis_index("core")
    odd = lax.axis_index("core")
    plane_rows(across_ref, rows_ref.at[odd])
    plane_rows(within_ref, rows_ref.at[1 - odd])
    sources = (rows_ref[0].astype(jnp.bfloat16), mine_ref[...], rows_ref[1].astype(jnp.bfloat16))
    for s, rows in enumerate(sources):
        for j in range(8):
            top = j * ROWS + 16 * s
            if j:
                window_ref[top : top + 16, 0:LANES] = rows[:, 512 * j - LANES : 512 * j]
            else:
                window_ref[top : top + 16, 0:LANES] = jnp.zeros((16, LANES), jnp.bfloat16)
            window_ref[top : top + 16, LANES:WINDOW] = rows[:, 512 * j : 512 * j + 512]
    for first in range(0, 9, 2):
        count = min(2, 9 - first)
        picked = jnp.dot(
            window_ref[...], select_ref[:, first * LANES : (first + count) * LANES],
            preferred_element_type=jnp.float32,
        ).astype(jnp.bfloat16)
        for k in range(count):
            for j in range(8):
                taps_ref[(first + k) * ROWS : (first + k + 1) * ROWS, j * LANES : (j + 1) * LANES] = picked[
                    j * ROWS : (j + 1) * ROWS, k * LANES : (k + 1) * LANES
                ]
    inside = jnp.where(place < wide - 1, 1.0, 0.0)
    margin = jnp.zeros((4 * C1, LANES), jnp.bfloat16)
    act_ref[:, 0:LANES] = margin
    act_ref[:, LANES + PLANE :] = margin
    for n in range(4):
        first_pre = jnp.dot(w1_ref[...], taps_ref[:, 256 * n : 256 * n + 256], preferred_element_type=jnp.float32)
        first_act = leaky_relu(first_pre)
        here = slice(LANES + 256 * n, LANES + 256 * n + 256)
        act_ref[0 : 3 * C1, here] = first_act[0 : 3 * C1].astype(jnp.bfloat16)
        act_ref[3 * C1 :, here] = (first_act[3 * C1 :] * inside).astype(jnp.bfloat16)
    column = lax.broadcasted_iota(jnp.int32, (1, PLANE), 1) % HALF
    left_ok = jnp.where(column > 0, 1.0, 0.0).astype(jnp.bfloat16)
    right_ok = jnp.where(column < HALF - 1, 1.0, 0.0).astype(jnp.bfloat16)
    for b in range(3):
        for c in range(3):
            begin = LANES + (b - 1) * HALF + (c - 1)
            part = act_ref[:, begin : begin + PLANE]
            if c == 0:
                part = part * left_ok
            if c == 2:
                part = part * right_ok
            shifted_ref[(3 * b + c) * LANES : (3 * b + c + 1) * LANES, :] = part
    for n in range(4):
        here = slice(256 * n, 256 * n + 256)
        pre = jnp.dot(w2_ref[...], shifted_ref[:, here], preferred_element_type=jnp.float32)
        output = leaky_relu(pre).astype(jnp.bfloat16)
        slope = jnp.where(pre > 0, 1.0, neg_slope)
        for z in range(2):
            cells = slice(z * PLANE + 256 * n, z * PLANE + 256 * n + 256)
            rows = slice(z * C2, (z + 1) * C2)
            out_ref[0, 0, :, cells] = output[rows]
            back_ref[rows, here] = (cot_ref[0, 0, :, cells].astype(jnp.float32) * slope[rows]).astype(jnp.bfloat16)
    out_copy = pltpu.make_async_copy(out_ref, out_hbm, out_sem)
    out_copy.start()
    group = lax.broadcasted_iota(jnp.int32, (C2, LANES), 1) // C1
    tiles = []
    for first in range(0, 9, 2):
        count = min(2, 9 - first)
        sums = lax.dot_general(
            back_ref[...], shifted_ref[first * LANES : (first + count) * LANES, :],
            (((1,), (1,)), ((), ())), preferred_element_type=jnp.float32,
        )
        for k in range(count):
            tile = sums[:, k * LANES : (k + 1) * LANES]
            tiles.append((tile[0:C2] + pltpu.roll(tile[C2:], LANES - C1, 1)) * scale)
    where = slots()
    for bc in (7, 8):
        for a in range(3):
            tile, slot = where[9 * a + bc]
            tiles[tile] = jnp.where(group == slot, pltpu.roll(tiles[bc], (slot - a) * C1, 1), tiles[tile])
    for tile in range(7):
        grad_ref[:, tile * LANES : (tile + 1) * LANES] = tiles[tile].astype(jnp.bfloat16)
    out_copy.wait()


def finish_kernel(parts_ref, grad_ref):
    wide, half, _ = parts_ref.shape
    for core in range(2):
        total = parts_ref[core].astype(jnp.float32)
        for k in range(core + 2, wide, 2):
            total = total + parts_ref[k].astype(jnp.float32)
        for tap, (tile, slot) in slots().items():
            begin = tile * LANES + slot * C1
            grad_ref[tap, core * half : (core + 1) * half, :] = total[:, begin : begin + C1]


def body(volumes, first_kernel, second_kernel, cotangent):
    wide = lax.axis_size(WIDE)
    narrow = lax.axis_size("narrow")
    cells_out = cotangent.shape[3]
    scale = 1.0 / math.sqrt(wide * narrow * cells_out)
    across = lax.ppermute(volumes, WIDE, [p for k in range(1, wide - 1, 2) for p in ((k, k + 1), (k + 1, k))])
    within = lax.ppermute(volumes, WIDE, [p for k in range(0, wide - 1, 2) for p in ((k, k + 1), (k + 1, k))])
    pinned = pl.BlockSpec(memory_space=pltpu.HBM)
    fast = pl.BlockSpec(memory_space=pltpu.VMEM)
    w1, w2, mine, select, cot = pl.pallas_call(
        prepare_kernel,
        in_specs=[pinned] * 6,
        out_specs=(fast,) * 5,
        out_shape=(
            jax.ShapeDtypeStruct((4 * C1, 9 * ROWS), jnp.bfloat16),
            jax.ShapeDtypeStruct((2 * C2, 9 * LANES), jnp.bfloat16),
            jax.ShapeDtypeStruct((CIN * PLANES, CELLS), jnp.bfloat16),
            jax.ShapeDtypeStruct((WINDOW, 9 * LANES), jnp.bfloat16),
            jax.ShapeDtypeStruct(cotangent.shape, jnp.bfloat16),
        ),
        scratch_shapes=[
            pltpu.VMEM((27, CIN, C1), jnp.bfloat16),
            pltpu.VMEM((27 * CIN, 4 * 512), jnp.bfloat16),
            pltpu.VMEM((27, C1, C2), jnp.bfloat16),
            pltpu.VMEM(volumes.shape, jnp.bfloat16),
            pltpu.VMEM((27 * CIN, C1), jnp.float32),
            pltpu.VMEM((CIN * PLANES, CELLS), jnp.float32),
            pltpu.SemaphoreType.DMA((6,)),
        ],
        compiler_params=pltpu.CompilerParams(vmem_limit_bytes=16 * MIB),
        cost_estimate=pl.CostEstimate(flops=10**9, bytes_accessed=4 * MIB, transcendentals=0),
        name="prepare",
    )(*(pltpu.with_memory_space_constraint(x, pltpu.HBM) for x in (
        first_kernel.transpose(0, 2, 1), jnp.asarray(placement(), jnp.bfloat16), second_kernel.transpose(0, 2, 1),
        volumes, jnp.asarray(selection(), jnp.bfloat16), cotangent,
    )))
    rows = C2 // narrow
    output, term = pl.pallas_call(
        functools.partial(main_kernel, wide, scale),
        in_specs=[fast] * 7,
        out_specs=(pl.BlockSpec(memory_space=pl.ANY), fast),
        out_shape=(
            jax.ShapeDtypeStruct((1, 1, C2, cells_out), jnp.bfloat16),
            jax.ShapeDtypeStruct((C2, PACKED), jnp.bfloat16),
        ),
        scratch_shapes=[
            pltpu.VMEM((2, CIN * PLANES, CELLS), jnp.float32),
            pltpu.VMEM((8 * ROWS, WINDOW), jnp.bfloat16),
            pltpu.VMEM((9 * ROWS, PLANE), jnp.bfloat16),
            pltpu.VMEM((4 * C1, PLANE + 2 * LANES), jnp.bfloat16),
            pltpu.VMEM((9 * LANES, PLANE), jnp.bfloat16),
            pltpu.VMEM((2 * C2, PLANE), jnp.bfloat16),
            pltpu.VMEM((1, 1, C2, cells_out), jnp.bfloat16),
            pltpu.SemaphoreType.DMA,
        ],
        compiler_params=pltpu.CompilerParams(vmem_limit_bytes=24 * MIB),
        name="local",
    )(across, mine, within, select, w1, w2, cot)
    half = rows // 2
    received = lax.all_to_all(term, ("narrow", "core"), 0, 0, tiled=True)
    owned = jnp.sum(received.reshape(2 * narrow, half, PACKED).astype(jnp.float32), axis=0).astype(jnp.bfloat16)
    parts = lax.all_to_all(jnp.broadcast_to(owned[None], (wide, half, PACKED)), WIDE, 0, 0, tiled=True)
    weight_grad = pl.pallas_call(
        finish_kernel,
        out_shape=jax.ShapeDtypeStruct((27, rows, C1), jnp.float32),
        compiler_params=pltpu.CompilerParams(vmem_limit_bytes=8 * MIB),
        name="finish",
    )(parts)
    return (output, weight_grad)


def solution(mesh):
    wide, narrow = mesh.devices.shape
    split = jax.sharding.Mesh(mesh.devices.reshape(wide // 2, 2, narrow), ("chip", "core", "narrow"))
    return jax.shard_map(
        body,
        mesh=split,
        in_specs=(P("narrow", None, None, WIDE, None), P(), P(), P("narrow", None, None, WIDE)),
        out_specs=(P("narrow", None, None, WIDE), P(None, "narrow", None)),
        check_vma=False,
    )
```

```python
import functools
import math

import jax
import jax.numpy as jnp
import numpy as np
from jax import lax
from jax.experimental import pallas as pl
from jax.experimental.pallas import tpu as pltpu
from jax.sharding import PartitionSpec as P

CIN = 4
C1 = 32
C2 = 64
PLANES = 4
CELLS = 4096
HALF = 32
PLANE = 1024
LANES = 128
ROWS = CIN * PLANES
CHUNK = 512
PACKED = 7 * LANES
MIB = 2**20
WIDE = ("chip", "core")
neg_slope = 0.3


def selection():
    table = np.zeros((CHUNK, 2, 2, 4, HALF), np.float32)
    for py in range(2):
        for px in range(2):
            for row in range(4):
                for col in range(HALF):
                    table[(2 * row + py) * 64 + 2 * col + px, py, px, row, col] = 1
    return table.reshape(CHUNK, CHUNK)


def placement():
    table = np.zeros((2, 27, CIN, 4, CHUNK), np.float32)
    for odd in range(2):
        for a in range(3):
            for bc in range(9):
                for i in range(CIN):
                    for q in range(4):
                        slab, plane = divmod(2 * q + a + 1, PLANES)
                        inner = i * PLANES + plane
                        if slab == 1:
                            column = bc * 2 * ROWS + inner
                        elif (slab == 0) == (odd == 1):
                            column = bc * 2 * ROWS + ROWS + inner
                        else:
                            column = 18 * ROWS + bc * ROWS + inner
                        table[odd, 9 * a + bc, i, q, column] = 1
    return table.reshape(2, 27 * CIN, 4 * CHUNK)


def leaky_relu(value):
    return jnp.where(value > 0, value, neg_slope * value)


def plane_rows(volume_ref, rows_ref):
    for i in range(CIN):
        rows_ref[PLANES * i : PLANES * (i + 1), :] = volume_ref[0, 0, i].astype(jnp.float32)


def column_masks():
    column = lax.broadcasted_iota(jnp.int32, (1, PLANE), 1) % HALF
    left_ok = jnp.where(column > 0, 1.0, 0.0).astype(jnp.bfloat16)
    right_ok = jnp.where(column < HALF - 1, 1.0, 0.0).astype(jnp.bfloat16)
    return left_ok, right_ok


def strided_taps(rows, select_ref, parity_ref, taps_ref):
    count = rows.shape[0]
    left_ok, _ = column_masks()
    chunks = jnp.concatenate([rows[:, CHUNK * j : CHUNK * (j + 1)] for j in range(8)], axis=0)
    for p in range(4):
        parity_ref[p, :, 0:LANES] = jnp.zeros((count, LANES), jnp.bfloat16)
    for py in range(2):
        parts = jnp.dot(
            chunks, select_ref[:, 256 * py : 256 * py + 256], preferred_element_type=jnp.float32
        ).astype(jnp.bfloat16)
        for px in range(2):
            for j in range(8):
                parity_ref[2 * py + px, :, LANES * (j + 1) : LANES * (j + 2)] = parts[
                    j * count : (j + 1) * count, px * LANES : (px + 1) * LANES
                ]
    for b in range(3):
        for c in range(3):
            begin = LANES - HALF * (b == 0) - (c == 0)
            part = parity_ref[2 * (b != 1) + (c != 1), :, begin : begin + PLANE]
            if c == 0:
                part = part * left_ok
            taps_ref[(3 * b + c) * count : (3 * b + c + 1) * count, :] = part


def shifted_taps(act_ref, shifted_ref):
    left_ok, right_ok = column_masks()
    for b in range(3):
        for c in range(3):
            begin = LANES + (b - 1) * HALF + (c - 1)
            part = act_ref[:, begin : begin + PLANE]
            if c == 0:
                part = part * left_ok
            if c == 2:
                part = part * right_ok
            shifted_ref[(3 * b + c) * 2 * C1 : (3 * b + c + 1) * 2 * C1, :] = part


def clear_margins(act_ref):
    margin = jnp.zeros((2 * C1, LANES), jnp.bfloat16)
    act_ref[:, 0:LANES] = margin
    act_ref[:, LANES + PLANE :] = margin


def prepare_kernel(
    k1_hbm, place_hbm, k2_hbm, select_hbm, cot_hbm, w1_near_ref, w1_far_ref, w2_ref, select_ref, cot_ref,
    k1_ref, place_ref, k2_ref, k1_rows_ref, sems,
):
    odd = lax.axis_index("core")
    moves = ((k1_hbm, k1_ref), (k2_hbm, k2_ref), (place_hbm.at[odd], place_ref), (select_hbm, select_ref), (cot_hbm, cot_ref))
    copies = [pltpu.make_async_copy(src, dst, sems.at[k]) for k, (src, dst) in enumerate(moves)]
    for copy in copies:
        copy.start()
    copies[0].wait()
    for tap in range(27):
        k1_rows_ref[CIN * tap : CIN * (tap + 1), :] = k1_ref[tap].astype(jnp.float32)
    copies[1].wait()
    blank = jnp.zeros((C1, C2), jnp.bfloat16)

    def stacked(bc, pair):
        k = [blank] + [k2_ref[9 * a + bc] for a in range(3)] + [blank]
        lower = jnp.concatenate(k[1 + 2 * pair : 3 + 2 * pair], axis=0)
        upper = jnp.concatenate(k[2 * pair : 2 + 2 * pair], axis=0)
        return jnp.concatenate([lower, upper], axis=1)

    for pair in range(2):
        for bc in range(0, 8, 2):
            both = jnp.concatenate([stacked(bc, pair), stacked(bc + 1, pair)], axis=0)
            w2_ref[pair, :, C2 * bc : C2 * bc + LANES] = both.T
        alone = jnp.concatenate([stacked(8, pair), jnp.zeros((2 * C1, LANES), jnp.bfloat16)], axis=0)
        w2_ref[pair, :, C2 * 8 : C2 * 9] = alone.T[:, 0 : 2 * C1]
    copies[2].wait()
    spread = lax.dot_general(
        k1_rows_ref[...].astype(jnp.bfloat16), place_ref[...],
        (((0,), (0,)), ((), ())), preferred_element_type=jnp.float32,
    ).astype(jnp.bfloat16)
    for q in range(4):
        rows = slice(q % 2 * C1, (q % 2 + 1) * C1)
        w1_near_ref[q // 2, rows, :] = spread[:, CHUNK * q : CHUNK * q + 18 * ROWS]
        w1_far_ref[q // 2, rows, :] = spread[:, CHUNK * q + 18 * ROWS : CHUNK * q + 27 * ROWS]
    copies[3].wait()
    copies[4].wait()


def near_kernel(
    own_ref, within_ref, select_ref, w1_ref, w2_ref, first_ref, shifted_ref, pre_ref, rows_ref, parity_ref, taps_ref, act_ref,
):
    odd = lax.axis_index("core")
    plane_rows(own_ref, rows_ref.at[0:ROWS])
    plane_rows(within_ref, rows_ref.at[ROWS : 2 * ROWS])
    strided_taps(rows_ref[...].astype(jnp.bfloat16), select_ref, parity_ref, taps_ref)
    clear_margins(act_ref)
    for n in range(4):
        here = slice(256 * n, 256 * n + 256)
        first_ref[:, here] = jnp.dot(w1_ref[odd], taps_ref[:, here], preferred_element_type=jnp.float32)
        complete = jnp.dot(w1_ref[1 - odd], taps_ref[:, here], preferred_element_type=jnp.float32)
        act_ref[:, LANES + 256 * n : LANES + 256 * n + 256] = leaky_relu(complete).astype(jnp.bfloat16)
    shifted_taps(act_ref, shifted_ref)
    for n in range(4):
        here = slice(256 * n, 256 * n + 256)
        pre_ref[:, here] = jnp.dot(w2_ref[1 - odd], shifted_ref[:, here], preferred_element_type=jnp.float32)


def far_kernel(
    chips, scale, across_ref, select_ref, w1_ref, w2_ref, cot_ref, first_ref, near_ref, pre_ref, out_hbm, grad_ref,
    rows_ref, parity_ref, taps_ref, act_ref, shifted_ref, back_ref, sums_ref, out_ref, out_sem,
):
    odd = lax.axis_index("core")
    last = (lax.axis_index("chip") == chips - 1) & (odd == 1)
    inside = jnp.where(last, 0.0, 1.0)
    plane_rows(across_ref, rows_ref)
    strided_taps(rows_ref[...].astype(jnp.bfloat16), select_ref, parity_ref, taps_ref)
    clear_margins(act_ref)
    for n in range(4):
        here = slice(256 * n, 256 * n + 256)
        first_pre = first_ref[:, here] + jnp.dot(w1_ref[odd], taps_ref[:, here], preferred_element_type=jnp.float32)
        first_act = leaky_relu(first_pre)
        there = slice(LANES + 256 * n, LANES + 256 * n + 256)
        act_ref[0:C1, there] = first_act[0:C1].astype(jnp.bfloat16)
        act_ref[C1:, there] = (first_act[C1:] * inside).astype(jnp.bfloat16)
    shifted_taps(act_ref, shifted_ref)
    for n in range(4):
        here = slice(256 * n, 256 * n + 256)
        pre = pre_ref[:, here] + jnp.dot(w2_ref[odd], shifted_ref[:, here], preferred_element_type=jnp.float32)
        output = leaky_relu(pre).astype(jnp.bfloat16)
        slope = jnp.where(pre > 0, 1.0, neg_slope)
        for z in range(2):
            cells = slice(z * PLANE + 256 * n, z * PLANE + 256 * n + 256)
            rows = slice(z * C2, (z + 1) * C2)
            out_ref[0, 0, :, cells] = output[rows]
            back_ref[rows, here] = (cot_ref[0, 0, :, cells].astype(jnp.float32) * slope[rows]).astype(jnp.bfloat16)
    out_copy = pltpu.make_async_copy(out_ref, out_hbm, out_sem)
    out_copy.start()
    for pair, ref in ((1 - odd, near_ref), (odd, shifted_ref)):
        sums_ref[pair] = lax.dot_general(
            ref[...], back_ref[...], (((1,), (1,)), ((), ())), preferred_element_type=jnp.float32
        )
    low = lax.broadcasted_iota(jnp.int32, (C1, LANES), 1) < C2

    def plane_sums(bc, q):
        begin = 2 * C1 * bc + C1 * (q % 2)
        return sums_ref[q // 2, begin : begin + C1, :]

    def two_taps(first, second):
        a, bc = divmod(first, 9)
        here, above = plane_sums(bc, a), pltpu.roll(plane_sums(bc, a + 1), C2, 1)
        if second > 26:
            return here + above
        a, bc = divmod(second, 9)
        there, beyond = pltpu.roll(plane_sums(bc, a), C2, 1), plane_sums(bc, a + 1)
        return jnp.where(low, here, there) + jnp.where(low, above, beyond)

    for block in range(4):
        tall = jnp.concatenate([two_taps(min(8 * block + g, 26), 8 * block + 4 + g) for g in range(4)], axis=0)
        flat = (tall * scale).T.astype(jnp.bfloat16)
        grad_ref[:, 2 * block * LANES : (2 * block + 1) * LANES] = flat[0:C2]
        if block < 3:
            grad_ref[:, (2 * block + 1) * LANES : (2 * block + 2) * LANES] = flat[C2:]
    out_copy.wait()


def finish_kernel(parts_ref, grad_ref):
    wide, half, _ = parts_ref.shape
    for core in range(2):
        total = parts_ref[core].astype(jnp.float32)
        for k in range(core + 2, wide, 2):
            total = total + parts_ref[k].astype(jnp.float32)
        for tap in range(27):
            grad_ref[tap, core * half : (core + 1) * half, :] = total[:, tap * C1 : (tap + 1) * C1]


def body(volumes, first_kernel, second_kernel, cotangent):
    wide = lax.axis_size(WIDE)
    narrow = lax.axis_size("narrow")
    cells_out = cotangent.shape[3]
    scale = 1.0 / math.sqrt(wide * narrow * cells_out)
    across = lax.ppermute(volumes, WIDE, [p for k in range(1, wide - 1, 2) for p in ((k, k + 1), (k + 1, k))])
    within = lax.ppermute(volumes, WIDE, [p for k in range(0, wide - 1, 2) for p in ((k, k + 1), (k + 1, k))])
    pinned = pl.BlockSpec(memory_space=pltpu.HBM)
    fast = pl.BlockSpec(memory_space=pltpu.VMEM)
    bf16 = functools.partial(jax.ShapeDtypeStruct, dtype=jnp.bfloat16)
    f32 = functools.partial(jax.ShapeDtypeStruct, dtype=jnp.float32)
    stored = (
        first_kernel.transpose(0, 2, 1), jnp.asarray(placement(), jnp.bfloat16), second_kernel.transpose(0, 2, 1),
        jnp.asarray(selection(), jnp.bfloat16), cotangent,
    )
    w1_near, w1_far, w2, select, cot = pl.pallas_call(
        prepare_kernel,
        in_specs=[pinned] * 5,
        out_specs=(fast,) * 5,
        out_shape=(
            bf16((2, 2 * C1, 18 * ROWS)), bf16((2, 2 * C1, 9 * ROWS)), bf16((2, 2 * C2, 18 * C1)),
            bf16((CHUNK, CHUNK)), bf16(cotangent.shape),
        ),
        scratch_shapes=[
            pltpu.VMEM((27, CIN, C1), jnp.bfloat16),
            pltpu.VMEM((27 * CIN, 4 * CHUNK), jnp.bfloat16),
            pltpu.VMEM((27, C1, C2), jnp.bfloat16),
            pltpu.VMEM((27 * CIN, C1), jnp.float32),
            pltpu.SemaphoreType.DMA((5,)),
        ],
        compiler_params=pltpu.CompilerParams(vmem_limit_bytes=12 * MIB),
        cost_estimate=pl.CostEstimate(flops=10**9, bytes_accessed=4 * MIB, transcendentals=0),
        name="prepare",
    )(*(pltpu.with_memory_space_constraint(x, pltpu.HBM) for x in stored))
    first, near, pre = pl.pallas_call(
        near_kernel,
        in_specs=[fast] * 5,
        out_specs=(fast,) * 3,
        out_shape=(f32((2 * C1, PLANE)), bf16((18 * C1, PLANE)), f32((2 * C2, PLANE))),
        scratch_shapes=[
            pltpu.VMEM((2 * ROWS, CELLS), jnp.float32),
            pltpu.VMEM((4, 2 * ROWS, LANES + PLANE), jnp.bfloat16),
            pltpu.VMEM((18 * ROWS, PLANE), jnp.bfloat16),
            pltpu.VMEM((2 * C1, PLANE + 2 * LANES), jnp.bfloat16),
        ],
        compiler_params=pltpu.CompilerParams(vmem_limit_bytes=16 * MIB),
        cost_estimate=pl.CostEstimate(flops=10**9, bytes_accessed=4 * MIB, transcendentals=0),
        name="near",
    )(volumes, within, select, w1_near, w2)
    rows = C2 // narrow
    output, term = pl.pallas_call(
        functools.partial(far_kernel, wide // 2, scale),
        in_specs=[fast] * 8,
        out_specs=(pl.BlockSpec(memory_space=pl.ANY), fast),
        out_shape=(bf16((1, 1, C2, cells_out)), bf16((C2, PACKED))),
        scratch_shapes=[
            pltpu.VMEM((ROWS, CELLS), jnp.float32),
            pltpu.VMEM((4, ROWS, LANES + PLANE), jnp.bfloat16),
            pltpu.VMEM((9 * ROWS, PLANE), jnp.bfloat16),
            pltpu.VMEM((2 * C1, PLANE + 2 * LANES), jnp.bfloat16),
            pltpu.VMEM((18 * C1, PLANE), jnp.bfloat16),
            pltpu.VMEM((2 * C2, PLANE), jnp.bfloat16),
            pltpu.VMEM((2, 18 * C1, LANES), jnp.float32),
            pltpu.VMEM((1, 1, C2, cells_out), jnp.bfloat16),
            pltpu.SemaphoreType.DMA,
        ],
        compiler_params=pltpu.CompilerParams(vmem_limit_bytes=16 * MIB),
        name="far",
    )(across, select, w1_far, w2, cot, first, near, pre)
    half = rows // 2
    received = lax.all_to_all(term, ("narrow", "core"), 0, 0, tiled=True)
    owned = jnp.sum(received.reshape(2 * narrow, half, PACKED).astype(jnp.float32), axis=0).astype(jnp.bfloat16)
    parts = lax.all_to_all(jnp.broadcast_to(owned[None], (wide, half, PACKED)), WIDE, 0, 0, tiled=True)
    weight_grad = pl.pallas_call(
        finish_kernel,
        out_shape=jax.ShapeDtypeStruct((27, rows, C1), jnp.float32),
        compiler_params=pltpu.CompilerParams(vmem_limit_bytes=8 * MIB),
        name="finish",
    )(parts)
    return (output, weight_grad)


def solution(mesh):
    wide, narrow = mesh.devices.shape
    split = jax.sharding.Mesh(mesh.devices.reshape(wide // 2, 2, narrow), ("chip", "core", "narrow"))
    return jax.shard_map(
        body,
        mesh=split,
        in_specs=(P("narrow", None, None, WIDE, None), P(), P(), P("narrow", None, None, WIDE)),
        out_specs=(P("narrow", None, None, WIDE), P(None, "narrow", None)),
        check_vma=False,
    )
```

```python
import functools
import math

import jax
import jax.numpy as jnp
import numpy as np
from jax import lax
from jax.experimental import pallas as pl
from jax.experimental.pallas import tpu as pltpu
from jax.sharding import PartitionSpec as P

CIN = 4
C1 = 32
C2 = 64
PLANES = 4
CELLS = 4096
HALF = 32
PLANE = 1024
LANES = 128
ROWS = CIN * PLANES
CHUNK = 512
PACKED = 7 * LANES
MIB = 2**20
WIDE = ("chip", "core")
neg_slope = 0.3


def selection():
    table = np.zeros((CHUNK, 2, 2, 4, HALF), np.float32)
    for py in range(2):
        for px in range(2):
            for row in range(4):
                for col in range(HALF):
                    table[(2 * row + py) * 64 + 2 * col + px, py, px, row, col] = 1
    return table.reshape(CHUNK, CHUNK)


def placement():
    table = np.zeros((2, 27, CIN, 4, CHUNK), np.float32)
    for odd in range(2):
        for a in range(3):
            for bc in range(9):
                for i in range(CIN):
                    for q in range(4):
                        slab, plane = divmod(2 * q + a + 1, PLANES)
                        inner = i * PLANES + plane
                        if slab == 1:
                            column = bc * 2 * ROWS + inner
                        elif (slab == 0) == (odd == 1):
                            column = bc * 2 * ROWS + ROWS + inner
                        else:
                            column = 18 * ROWS + bc * ROWS + inner
                        table[odd, 9 * a + bc, i, q, column] = 1
    return table.reshape(2, 27 * CIN, 4 * CHUNK)


def leaky_relu(value):
    return jnp.where(value > 0, value, neg_slope * value)


def plane_rows(volume_ref, rows_ref):
    for i in range(CIN):
        rows_ref[PLANES * i : PLANES * (i + 1), :] = volume_ref[0, 0, i].astype(jnp.float32)


def column_masks():
    column = lax.broadcasted_iota(jnp.int32, (1, PLANE), 1) % HALF
    left_ok = jnp.where(column > 0, 1.0, 0.0).astype(jnp.bfloat16)
    right_ok = jnp.where(column < HALF - 1, 1.0, 0.0).astype(jnp.bfloat16)
    return left_ok, right_ok


def strided_taps(rows, select_ref, parity_ref, taps_ref):
    count = rows.shape[0]
    left_ok, _ = column_masks()
    chunks = jnp.concatenate([rows[:, CHUNK * j : CHUNK * (j + 1)] for j in range(8)], axis=0)
    for p in range(4):
        parity_ref[p, :, 0:LANES] = jnp.zeros((count, LANES), jnp.bfloat16)
    for py in range(2):
        parts = jnp.dot(
            chunks, select_ref[:, 256 * py : 256 * py + 256], preferred_element_type=jnp.float32
        ).astype(jnp.bfloat16)
        for px in range(2):
            for j in range(8):
                parity_ref[2 * py + px, :, LANES * (j + 1) : LANES * (j + 2)] = parts[
                    j * count : (j + 1) * count, px * LANES : (px + 1) * LANES
                ]
    for b in range(3):
        for c in range(3):
            begin = LANES - HALF * (b == 0) - (c == 0)
            part = parity_ref[2 * (b != 1) + (c != 1), :, begin : begin + PLANE]
            if c == 0:
                part = part * left_ok
            taps_ref[(3 * b + c) * count : (3 * b + c + 1) * count, :] = part


def shifted_columns(act_ref, columns_ref):
    left_ok, right_ok = column_masks()
    for c in range(3):
        begin = LANES + c - 1
        part = act_ref[:, begin : begin + PLANE]
        if c == 0:
            part = part * left_ok
        if c == 2:
            part = part * right_ok
        columns_ref[c * 2 * C1 : (c + 1) * 2 * C1, :] = part


def second_layer(w2, columns_ref, rowed_ref):
    blank = jnp.zeros((2 * C2, LANES), jnp.float32)
    for b in (0, 2):
        rowed_ref[b, :, 0:LANES] = blank
        rowed_ref[b, :, LANES + PLANE :] = blank
    for n in range(4):
        sums = jnp.dot(w2, columns_ref[:, 256 * n : 256 * n + 256], preferred_element_type=jnp.float32)
        for b in range(3):
            rowed_ref[b, :, LANES + 256 * n : LANES + 256 * n + 256] = sums[b * 2 * C2 : (b + 1) * 2 * C2]


def row_sum(rowed_ref, n):
    total = rowed_ref[1, :, LANES + 256 * n : LANES + 256 * n + 256]
    for b in (0, 2):
        begin = LANES + HALF * (b - 1) + 256 * n
        total = total + rowed_ref[b, :, begin : begin + 256]
    return total


def clear_margins(act_ref):
    margin = jnp.zeros((2 * C1, LANES), jnp.bfloat16)
    act_ref[:, 0:LANES] = margin
    act_ref[:, LANES + PLANE :] = margin


def prepare_kernel(
    k1_hbm, place_hbm, k2_hbm, select_hbm, cot_hbm, w1_near_ref, w1_far_ref, w2_ref, select_ref, cot_ref,
    k1_ref, place_ref, k2_ref, k1_rows_ref, sems,
):
    odd = lax.axis_index("core")
    moves = ((k1_hbm, k1_ref), (k2_hbm, k2_ref), (place_hbm.at[odd], place_ref), (select_hbm, select_ref), (cot_hbm, cot_ref))
    copies = [pltpu.make_async_copy(src, dst, sems.at[k]) for k, (src, dst) in enumerate(moves)]
    for copy in copies:
        copy.start()
    copies[0].wait()
    for tap in range(27):
        k1_rows_ref[CIN * tap : CIN * (tap + 1), :] = k1_ref[tap].astype(jnp.float32)
    copies[1].wait()
    blank = jnp.zeros((C1, C2), jnp.bfloat16)

    def stacked(bc, pair):
        k = [blank] + [k2_ref[9 * a + bc] for a in range(3)] + [blank]
        lower = jnp.concatenate(k[1 + 2 * pair : 3 + 2 * pair], axis=0)
        upper = jnp.concatenate(k[2 * pair : 2 + 2 * pair], axis=0)
        return jnp.concatenate([lower, upper], axis=1)

    for b in range(3):
        rows = slice(b * 2 * C2, (b + 1) * 2 * C2)
        for pair in range(2):
            both = jnp.concatenate([stacked(3 * b, pair), stacked(3 * b + 1, pair)], axis=0)
            w2_ref[pair, rows, 0:LANES] = both.T
        both = jnp.concatenate([stacked(3 * b + 2, 0), stacked(3 * b + 2, 1)], axis=0).T
        for pair in range(2):
            w2_ref[pair, rows, LANES : LANES + 2 * C1] = both[:, pair * 2 * C1 : (pair + 1) * 2 * C1]
    copies[2].wait()
    spread = lax.dot_general(
        k1_rows_ref[...].astype(jnp.bfloat16), place_ref[...],
        (((0,), (0,)), ((), ())), preferred_element_type=jnp.float32,
    ).astype(jnp.bfloat16)
    for q in range(4):
        rows = slice(q % 2 * C1, (q % 2 + 1) * C1)
        w1_near_ref[q // 2, rows, :] = spread[:, CHUNK * q : CHUNK * q + 18 * ROWS]
        w1_far_ref[q // 2, rows, :] = spread[:, CHUNK * q + 18 * ROWS : CHUNK * q + 27 * ROWS]
    copies[3].wait()
    copies[4].wait()


def near_kernel(
    own_ref, within_ref, select_ref, w1_ref, w2_ref, first_ref, columns_ref, pre_ref,
    rows_ref, parity_ref, taps_ref, act_ref, rowed_ref,
):
    odd = lax.axis_index("core")
    plane_rows(own_ref, rows_ref.at[0:ROWS])
    plane_rows(within_ref, rows_ref.at[ROWS : 2 * ROWS])
    strided_taps(rows_ref[...].astype(jnp.bfloat16), select_ref, parity_ref, taps_ref)
    clear_margins(act_ref)
    for n in range(4):
        here = slice(256 * n, 256 * n + 256)
        first_ref[:, here] = jnp.dot(w1_ref[odd], taps_ref[:, here], preferred_element_type=jnp.float32)
        complete = jnp.dot(w1_ref[1 - odd], taps_ref[:, here], preferred_element_type=jnp.float32)
        act_ref[:, LANES + 256 * n : LANES + 256 * n + 256] = leaky_relu(complete).astype(jnp.bfloat16)
    shifted_columns(act_ref, columns_ref)
    second_layer(w2_ref[1 - odd], columns_ref, rowed_ref)
    for n in range(4):
        pre_ref[:, 256 * n : 256 * n + 256] = row_sum(rowed_ref, n)


def far_kernel(
    chips, scale, across_ref, select_ref, w1_ref, w2_ref, cot_ref, first_ref, near_ref, pre_ref, out_hbm, grad_ref,
    rows_ref, parity_ref, taps_ref, act_ref, columns_ref, rowed_ref, back_ref, sums_ref, out_ref, out_sem,
):
    odd = lax.axis_index("core")
    last = (lax.axis_index("chip") == chips - 1) & (odd == 1)
    inside = jnp.where(last, 0.0, 1.0)
    plane_rows(across_ref, rows_ref)
    strided_taps(rows_ref[...].astype(jnp.bfloat16), select_ref, parity_ref, taps_ref)
    clear_margins(act_ref)
    for n in range(4):
        here = slice(256 * n, 256 * n + 256)
        first_pre = first_ref[:, here] + jnp.dot(w1_ref[odd], taps_ref[:, here], preferred_element_type=jnp.float32)
        first_act = leaky_relu(first_pre)
        there = slice(LANES + 256 * n, LANES + 256 * n + 256)
        act_ref[0:C1, there] = first_act[0:C1].astype(jnp.bfloat16)
        act_ref[C1:, there] = (first_act[C1:] * inside).astype(jnp.bfloat16)
    shifted_columns(act_ref, columns_ref)
    second_layer(w2_ref[odd], columns_ref, rowed_ref)
    margin = jnp.zeros((HALF, LANES), jnp.bfloat16)
    back_ref[0:HALF, :] = margin
    back_ref[HALF + PLANE :, :] = margin
    for n in range(4):
        pre = pre_ref[:, 256 * n : 256 * n + 256] + row_sum(rowed_ref, n)
        output = leaky_relu(pre).astype(jnp.bfloat16)
        slope = jnp.where(pre > 0, 1.0, neg_slope)
        backs = []
        for z in range(2):
            cells = slice(z * PLANE + 256 * n, z * PLANE + 256 * n + 256)
            rows = slice(z * C2, (z + 1) * C2)
            out_ref[0, 0, :, cells] = output[rows]
            backs.append((cot_ref[0, 0, :, cells].astype(jnp.float32) * slope[rows]).astype(jnp.bfloat16))
        back_ref[HALF + 256 * n : HALF + 256 * n + 256, :] = jnp.concatenate(backs, axis=0).T
    out_copy = pltpu.make_async_copy(out_ref, out_hbm, out_sem)
    out_copy.start()
    columns = jnp.concatenate([near_ref[...], columns_ref[...]], axis=0)
    rowed_back = jnp.concatenate([back_ref[(2 - b) * HALF : (2 - b) * HALF + PLANE, :] for b in range(3)], axis=1)
    sums = jnp.dot(columns, rowed_back, preferred_element_type=jnp.float32)
    sums_ref[1 - odd] = sums[0 : 6 * C1]
    sums_ref[odd] = sums[6 * C1 :]
    low = lax.broadcasted_iota(jnp.int32, (C1, LANES), 1) < C2

    def plane_sums(bc, q):
        b, c = divmod(bc, 3)
        begin = 2 * C1 * c + C1 * (q % 2)
        return sums_ref[q // 2, begin : begin + C1, b * LANES : (b + 1) * LANES]

    def two_taps(first, second):
        a, bc = divmod(first, 9)
        here, above = plane_sums(bc, a), pltpu.roll(plane_sums(bc, a + 1), C2, 1)
        if second > 26:
            return here + above
        a, bc = divmod(second, 9)
        there, beyond = pltpu.roll(plane_sums(bc, a), C2, 1), plane_sums(bc, a + 1)
        return jnp.where(low, here, there) + jnp.where(low, above, beyond)

    for block in range(4):
        tall = jnp.concatenate([two_taps(min(8 * block + g, 26), 8 * block + 4 + g) for g in range(4)], axis=0)
        flat = (tall * scale).T.astype(jnp.bfloat16)
        grad_ref[:, 2 * block * LANES : (2 * block + 1) * LANES] = flat[0:C2]
        if block < 3:
            grad_ref[:, (2 * block + 1) * LANES : (2 * block + 2) * LANES] = flat[C2:]
    out_copy.wait()


def finish_kernel(parts_ref, grad_ref):
    wide, half, _ = parts_ref.shape
    for core in range(2):
        total = parts_ref[core].astype(jnp.float32)
        for k in range(core + 2, wide, 2):
            total = total + parts_ref[k].astype(jnp.float32)
        for tap in range(27):
            grad_ref[tap, core * half : (core + 1) * half, :] = total[:, tap * C1 : (tap + 1) * C1]


def body(volumes, first_kernel, second_kernel, cotangent):
    wide = lax.axis_size(WIDE)
    narrow = lax.axis_size("narrow")
    cells_out = cotangent.shape[3]
    scale = 1.0 / math.sqrt(wide * narrow * cells_out)
    across = lax.ppermute(volumes, WIDE, [p for k in range(1, wide - 1, 2) for p in ((k, k + 1), (k + 1, k))])
    within = lax.ppermute(volumes, WIDE, [p for k in range(0, wide - 1, 2) for p in ((k, k + 1), (k + 1, k))])
    pinned = pl.BlockSpec(memory_space=pltpu.HBM)
    fast = pl.BlockSpec(memory_space=pltpu.VMEM)
    bf16 = functools.partial(jax.ShapeDtypeStruct, dtype=jnp.bfloat16)
    f32 = functools.partial(jax.ShapeDtypeStruct, dtype=jnp.float32)
    stored = (
        first_kernel.transpose(0, 2, 1), jnp.asarray(placement(), jnp.bfloat16), second_kernel.transpose(0, 2, 1),
        jnp.asarray(selection(), jnp.bfloat16), cotangent,
    )
    w1_near, w1_far, w2, select, cot = pl.pallas_call(
        prepare_kernel,
        in_specs=[pinned] * 5,
        out_specs=(fast,) * 5,
        out_shape=(
            bf16((2, 2 * C1, 18 * ROWS)), bf16((2, 2 * C1, 9 * ROWS)), bf16((2, 6 * C2, 6 * C1)),
            bf16((CHUNK, CHUNK)), bf16(cotangent.shape),
        ),
        scratch_shapes=[
            pltpu.VMEM((27, CIN, C1), jnp.bfloat16),
            pltpu.VMEM((27 * CIN, 4 * CHUNK), jnp.bfloat16),
            pltpu.VMEM((27, C1, C2), jnp.bfloat16),
            pltpu.VMEM((27 * CIN, C1), jnp.float32),
            pltpu.SemaphoreType.DMA((5,)),
        ],
        compiler_params=pltpu.CompilerParams(vmem_limit_bytes=12 * MIB),
        cost_estimate=pl.CostEstimate(flops=10**9, bytes_accessed=4 * MIB, transcendentals=0),
        name="prepare",
    )(*(pltpu.with_memory_space_constraint(x, pltpu.HBM) for x in stored))
    first, near, pre = pl.pallas_call(
        near_kernel,
        in_specs=[fast] * 5,
        out_specs=(fast,) * 3,
        out_shape=(f32((2 * C1, PLANE)), bf16((6 * C1, PLANE)), f32((2 * C2, PLANE))),
        scratch_shapes=[
            pltpu.VMEM((2 * ROWS, CELLS), jnp.float32),
            pltpu.VMEM((4, 2 * ROWS, LANES + PLANE), jnp.bfloat16),
            pltpu.VMEM((18 * ROWS, PLANE), jnp.bfloat16),
            pltpu.VMEM((2 * C1, PLANE + 2 * LANES), jnp.bfloat16),
            pltpu.VMEM((3, 2 * C2, PLANE + 2 * LANES), jnp.float32),
        ],
        compiler_params=pltpu.CompilerParams(vmem_limit_bytes=16 * MIB),
        cost_estimate=pl.CostEstimate(flops=10**9, bytes_accessed=4 * MIB, transcendentals=0),
        name="near",
    )(volumes, within, select, w1_near, w2)
    rows = C2 // narrow
    output, term = pl.pallas_call(
        functools.partial(far_kernel, wide // 2, scale),
        in_specs=[fast] * 8,
        out_specs=(pl.BlockSpec(memory_space=pl.ANY), fast),
        out_shape=(bf16((1, 1, C2, cells_out)), bf16((C2, PACKED))),
        scratch_shapes=[
            pltpu.VMEM((ROWS, CELLS), jnp.float32),
            pltpu.VMEM((4, ROWS, LANES + PLANE), jnp.bfloat16),
            pltpu.VMEM((9 * ROWS, PLANE), jnp.bfloat16),
            pltpu.VMEM((2 * C1, PLANE + 2 * LANES), jnp.bfloat16),
            pltpu.VMEM((6 * C1, PLANE), jnp.bfloat16),
            pltpu.VMEM((3, 2 * C2, PLANE + 2 * LANES), jnp.float32),
            pltpu.VMEM((PLANE + 2 * HALF, LANES), jnp.bfloat16),
            pltpu.VMEM((2, 6 * C1, 3 * LANES), jnp.float32),
            pltpu.VMEM((1, 1, C2, cells_out), jnp.bfloat16),
            pltpu.SemaphoreType.DMA,
        ],
        compiler_params=pltpu.CompilerParams(vmem_limit_bytes=16 * MIB),
        name="far",
    )(across, select, w1_far, w2, cot, first, near, pre)
    half = rows // 2
    received = lax.all_to_all(term, ("narrow", "core"), 0, 0, tiled=True)
    owned = jnp.sum(received.reshape(2 * narrow, half, PACKED).astype(jnp.float32), axis=0).astype(jnp.bfloat16)
    parts = lax.all_to_all(jnp.broadcast_to(owned[None], (wide, half, PACKED)), WIDE, 0, 0, tiled=True)
    weight_grad = pl.pallas_call(
        finish_kernel,
        out_shape=jax.ShapeDtypeStruct((27, rows, C1), jnp.float32),
        compiler_params=pltpu.CompilerParams(vmem_limit_bytes=8 * MIB),
        name="finish",
    )(parts)
    return (output, weight_grad)


def solution(mesh):
    wide, narrow = mesh.devices.shape
    split = jax.sharding.Mesh(mesh.devices.reshape(wide // 2, 2, narrow), ("chip", "core", "narrow"))
    return jax.shard_map(
        body,
        mesh=split,
        in_specs=(P("narrow", None, None, WIDE, None), P(), P(), P("narrow", None, None, WIDE)),
        out_specs=(P("narrow", None, None, WIDE), P(None, "narrow", None)),
        check_vma=False,
    )
```

```python
import functools
import math

import jax
import jax.numpy as jnp
import numpy as np
from jax import lax
from jax.experimental import pallas as pl
from jax.experimental.pallas import tpu as pltpu
from jax.sharding import PartitionSpec as P

CIN = 4
C1 = 32
C2 = 64
PLANES = 4
CELLS = 4096
HALF = 32
PLANE = 1024
LANES = 128
ROWS = CIN * PLANES
CHUNK = 512
PACKED = 7 * LANES
MIB = 2**20
WIDE = ("chip", "core")
neg_slope = 0.3


def selection():
    table = np.zeros((CHUNK, 2, 2, 4, HALF), np.float32)
    for py in range(2):
        for px in range(2):
            for row in range(4):
                for col in range(HALF):
                    table[(2 * row + py) * 64 + 2 * col + px, py, px, row, col] = 1
    return table.reshape(CHUNK, CHUNK)


def placement():
    table = np.zeros((2, 27, CIN, 4, CHUNK), np.float32)
    for odd in range(2):
        for a in range(3):
            for bc in range(9):
                for i in range(CIN):
                    for q in range(4):
                        slab, plane = divmod(2 * q + a + 1, PLANES)
                        inner = i * PLANES + plane
                        if slab == 1:
                            column = bc * 2 * ROWS + inner
                        elif (slab == 0) == (odd == 1):
                            column = bc * 2 * ROWS + ROWS + inner
                        else:
                            column = 18 * ROWS + bc * ROWS + inner
                        table[odd, 9 * a + bc, i, q, column] = 1
    return table.reshape(2, 27 * CIN, 4 * CHUNK)


def leaky_relu(value):
    return jnp.where(value > 0, value, neg_slope * value)


def plane_rows(volume_ref, rows_ref):
    for i in range(CIN):
        rows_ref[PLANES * i : PLANES * (i + 1), :] = volume_ref[0, 0, i].astype(jnp.float32)


def column_masks():
    column = lax.broadcasted_iota(jnp.int32, (1, PLANE), 1) % HALF
    left_ok = jnp.where(column > 0, 1.0, 0.0).astype(jnp.bfloat16)
    right_ok = jnp.where(column < HALF - 1, 1.0, 0.0).astype(jnp.bfloat16)
    return left_ok, right_ok


def strided_taps(rows, select_ref, parity_ref, taps_ref):
    count = rows.shape[0]
    left_ok, _ = column_masks()
    chunks = jnp.concatenate([rows[:, CHUNK * j : CHUNK * (j + 1)] for j in range(8)], axis=0)
    for p in range(4):
        parity_ref[p, :, 0:LANES] = jnp.zeros((count, LANES), jnp.bfloat16)
    for py in range(2):
        parts = jnp.dot(
            chunks, select_ref[:, 256 * py : 256 * py + 256], preferred_element_type=jnp.float32
        ).astype(jnp.bfloat16)
        for px in range(2):
            for j in range(8):
                parity_ref[2 * py + px, :, LANES * (j + 1) : LANES * (j + 2)] = parts[
                    j * count : (j + 1) * count, px * LANES : (px + 1) * LANES
                ]
    for b in range(3):
        for c in range(3):
            begin = LANES - HALF * (b == 0) - (c == 0)
            part = parity_ref[2 * (b != 1) + (c != 1), :, begin : begin + PLANE]
            if c == 0:
                part = part * left_ok
            taps_ref[(3 * b + c) * count : (3 * b + c + 1) * count, :] = part


def shifted_columns(act_ref, columns_ref):
    left_ok, right_ok = column_masks()
    for c in range(3):
        begin = LANES + c - 1
        part = act_ref[:, begin : begin + PLANE]
        if c == 0:
            part = part * left_ok
        if c == 2:
            part = part * right_ok
        columns_ref[c * 2 * C1 : (c + 1) * 2 * C1, :] = part


def second_layer(w2, columns_ref, rowed_ref):
    blank = jnp.zeros((2 * C2, LANES), jnp.float32)
    for b in (0, 2):
        rowed_ref[b, :, 0:LANES] = blank
        rowed_ref[b, :, LANES + PLANE :] = blank
    for n in range(4):
        sums = jnp.dot(w2, columns_ref[:, 256 * n : 256 * n + 256], preferred_element_type=jnp.float32)
        for b in range(3):
            rowed_ref[b, :, LANES + 256 * n : LANES + 256 * n + 256] = sums[b * 2 * C2 : (b + 1) * 2 * C2]


def row_sum(rowed_ref, n):
    total = rowed_ref[1, :, LANES + 256 * n : LANES + 256 * n + 256]
    for b in (0, 2):
        begin = LANES + HALF * (b - 1) + 256 * n
        total = total + rowed_ref[b, :, begin : begin + 256]
    return total


def clear_margins(act_ref):
    margin = jnp.zeros((2 * C1, LANES), jnp.bfloat16)
    act_ref[:, 0:LANES] = margin
    act_ref[:, LANES + PLANE :] = margin


def prepare_kernel(
    k1_hbm, place_hbm, k2_hbm, select_hbm, cot_hbm, w1_near_ref, w1_far_ref, w2_ref, select_ref, cot_ref,
    k1_ref, place_ref, k2_ref, k1_rows_ref, sems,
):
    odd = lax.axis_index("core")
    moves = ((k1_hbm, k1_ref), (k2_hbm, k2_ref), (place_hbm.at[odd], place_ref), (select_hbm, select_ref), (cot_hbm, cot_ref))
    copies = [pltpu.make_async_copy(src, dst, sems.at[k]) for k, (src, dst) in enumerate(moves)]
    for copy in copies:
        copy.start()
    copies[0].wait()
    for tap in range(27):
        k1_rows_ref[CIN * tap : CIN * (tap + 1), :] = k1_ref[tap].astype(jnp.float32)
    copies[1].wait()
    blank = jnp.zeros((C1, C2), jnp.bfloat16)

    def stacked(bc, pair):
        k = [blank] + [k2_ref[9 * a + bc] for a in range(3)] + [blank]
        lower = jnp.concatenate(k[1 + 2 * pair : 3 + 2 * pair], axis=0)
        upper = jnp.concatenate(k[2 * pair : 2 + 2 * pair], axis=0)
        return jnp.concatenate([lower, upper], axis=1)

    for b in range(3):
        rows = slice(b * 2 * C2, (b + 1) * 2 * C2)
        for pair in range(2):
            both = jnp.concatenate([stacked(3 * b, pair), stacked(3 * b + 1, pair)], axis=0)
            w2_ref[pair, rows, 0:LANES] = both.T
        both = jnp.concatenate([stacked(3 * b + 2, 0), stacked(3 * b + 2, 1)], axis=0).T
        for pair in range(2):
            w2_ref[pair, rows, LANES : LANES + 2 * C1] = both[:, pair * 2 * C1 : (pair + 1) * 2 * C1]
    copies[2].wait()
    spread = lax.dot_general(
        k1_rows_ref[...].astype(jnp.bfloat16), place_ref[...],
        (((0,), (0,)), ((), ())), preferred_element_type=jnp.float32,
    ).astype(jnp.bfloat16)
    for q in range(4):
        rows = slice(q % 2 * C1, (q % 2 + 1) * C1)
        w1_near_ref[q // 2, rows, :] = spread[:, CHUNK * q : CHUNK * q + 18 * ROWS]
        w1_far_ref[q // 2, rows, :] = spread[:, CHUNK * q + 18 * ROWS : CHUNK * q + 27 * ROWS]
    copies[3].wait()
    copies[4].wait()


def near_kernel(
    own_ref, within_ref, select_ref, w1_ref, w2_ref, first_ref, columns_ref, pre_ref,
    rows_ref, parity_ref, taps_ref, act_ref, rowed_ref,
):
    odd = lax.axis_index("core")
    plane_rows(own_ref, rows_ref.at[0:ROWS])
    plane_rows(within_ref, rows_ref.at[ROWS : 2 * ROWS])
    strided_taps(rows_ref[...].astype(jnp.bfloat16), select_ref, parity_ref, taps_ref)
    clear_margins(act_ref)
    for n in range(4):
        here = slice(256 * n, 256 * n + 256)
        first_ref[:, here] = jnp.dot(w1_ref[odd], taps_ref[:, here], preferred_element_type=jnp.float32)
        complete = jnp.dot(w1_ref[1 - odd], taps_ref[:, here], preferred_element_type=jnp.float32)
        act_ref[:, LANES + 256 * n : LANES + 256 * n + 256] = leaky_relu(complete).astype(jnp.bfloat16)
    shifted_columns(act_ref, columns_ref)
    second_layer(w2_ref[1 - odd], columns_ref, rowed_ref)
    for n in range(4):
        pre_ref[:, 256 * n : 256 * n + 256] = row_sum(rowed_ref, n)


def far_kernel(
    chips, narrow, scale, across_ref, select_ref, w1_ref, w2_ref, cot_ref, first_ref, near_ref, pre_ref, out_hbm, keep_ref, give_ref,
    rows_ref, parity_ref, taps_ref, act_ref, columns_ref, rowed_ref, back_ref, sums_ref, out_ref, out_sem,
):
    odd = lax.axis_index("core")
    last = (lax.axis_index("chip") == chips - 1) & (odd == 1)
    inside = jnp.where(last, 0.0, 1.0)
    plane_rows(across_ref, rows_ref)
    strided_taps(rows_ref[...].astype(jnp.bfloat16), select_ref, parity_ref, taps_ref)
    clear_margins(act_ref)
    for n in range(4):
        here = slice(256 * n, 256 * n + 256)
        first_pre = first_ref[:, here] + jnp.dot(w1_ref[odd], taps_ref[:, here], preferred_element_type=jnp.float32)
        first_act = leaky_relu(first_pre)
        there = slice(LANES + 256 * n, LANES + 256 * n + 256)
        act_ref[0:C1, there] = first_act[0:C1].astype(jnp.bfloat16)
        act_ref[C1:, there] = (first_act[C1:] * inside).astype(jnp.bfloat16)
    shifted_columns(act_ref, columns_ref)
    second_layer(w2_ref[odd], columns_ref, rowed_ref)
    margin = jnp.zeros((HALF, LANES), jnp.bfloat16)
    back_ref[0:HALF, :] = margin
    back_ref[HALF + PLANE :, :] = margin
    for n in range(4):
        pre = pre_ref[:, 256 * n : 256 * n + 256] + row_sum(rowed_ref, n)
        output = leaky_relu(pre).astype(jnp.bfloat16)
        slope = jnp.where(pre > 0, 1.0, neg_slope)
        backs = []
        for z in range(2):
            cells = slice(z * PLANE + 256 * n, z * PLANE + 256 * n + 256)
            rows = slice(z * C2, (z + 1) * C2)
            out_ref[0, 0, :, cells] = output[rows]
            backs.append((cot_ref[0, 0, :, cells].astype(jnp.float32) * slope[rows]).astype(jnp.bfloat16))
        back_ref[HALF + 256 * n : HALF + 256 * n + 256, :] = jnp.concatenate(backs, axis=0).T
    out_copy = pltpu.make_async_copy(out_ref, out_hbm, out_sem)
    out_copy.start()
    columns = jnp.concatenate([near_ref[...], columns_ref[...]], axis=0)
    rowed_back = jnp.concatenate([back_ref[(2 - b) * HALF : (2 - b) * HALF + PLANE, :] for b in range(3)], axis=1)
    sums = jnp.dot(columns, rowed_back, preferred_element_type=jnp.float32)
    sums_ref[1 - odd] = sums[0 : 6 * C1]
    sums_ref[odd] = sums[6 * C1 :]
    low = lax.broadcasted_iota(jnp.int32, (C1, LANES), 1) < C2

    def plane_sums(bc, q):
        b, c = divmod(bc, 3)
        begin = 2 * C1 * c + C1 * (q % 2)
        return sums_ref[q // 2, begin : begin + C1, b * LANES : (b + 1) * LANES]

    def two_taps(first, second):
        a, bc = divmod(first, 9)
        here, above = plane_sums(bc, a), pltpu.roll(plane_sums(bc, a + 1), C2, 1)
        if second > 26:
            return here + above
        a, bc = divmod(second, 9)
        there, beyond = pltpu.roll(plane_sums(bc, a), C2, 1), plane_sums(bc, a + 1)
        return jnp.where(low, here, there) + jnp.where(low, above, beyond)

    half = C2 // (2 * narrow)

    def put(tile, sums):
        here = slice(tile * LANES, (tile + 1) * LANES)
        for n in range(narrow):
            lower = sums[2 * n * half : (2 * n + 1) * half]
            upper = sums[(2 * n + 1) * half : (2 * n + 2) * half]
            rows = slice(n * half, (n + 1) * half)
            keep_ref[rows, here] = jnp.where(odd == 1, upper, lower).astype(jnp.bfloat16)
            give_ref[rows, here] = jnp.where(odd == 1, lower, upper).astype(jnp.bfloat16)

    for block in range(4):
        tall = jnp.concatenate([two_taps(min(8 * block + g, 26), 8 * block + 4 + g) for g in range(4)], axis=0)
        flat = (tall * scale).T
        put(2 * block, flat[0:C2])
        if block < 3:
            put(2 * block + 1, flat[C2:])
    out_copy.wait()


def finish_kernel(parts_ref, grad_ref):
    wide, half, _ = parts_ref.shape
    for core in range(2):
        total = parts_ref[core].astype(jnp.float32)
        for k in range(core + 2, wide, 2):
            total = total + parts_ref[k].astype(jnp.float32)
        for tap in range(27):
            grad_ref[tap, core * half : (core + 1) * half, :] = total[:, tap * C1 : (tap + 1) * C1]


def body(volumes, first_kernel, second_kernel, cotangent):
    wide = lax.axis_size(WIDE)
    narrow = lax.axis_size("narrow")
    cells_out = cotangent.shape[3]
    scale = 1.0 / math.sqrt(wide * narrow * cells_out)
    across = lax.ppermute(volumes, WIDE, [p for k in range(1, wide - 1, 2) for p in ((k, k + 1), (k + 1, k))])
    pairs = [p for k in range(0, wide - 1, 2) for p in ((k, k + 1), (k + 1, k))]
    within = lax.ppermute(volumes, WIDE, pairs)
    pinned = pl.BlockSpec(memory_space=pltpu.HBM)
    fast = pl.BlockSpec(memory_space=pltpu.VMEM)
    bf16 = functools.partial(jax.ShapeDtypeStruct, dtype=jnp.bfloat16)
    f32 = functools.partial(jax.ShapeDtypeStruct, dtype=jnp.float32)
    stored = (
        first_kernel.transpose(0, 2, 1), jnp.asarray(placement(), jnp.bfloat16), second_kernel.transpose(0, 2, 1),
        jnp.asarray(selection(), jnp.bfloat16), cotangent,
    )
    w1_near, w1_far, w2, select, cot = pl.pallas_call(
        prepare_kernel,
        in_specs=[pinned] * 5,
        out_specs=(fast,) * 5,
        out_shape=(
            bf16((2, 2 * C1, 18 * ROWS)), bf16((2, 2 * C1, 9 * ROWS)), bf16((2, 6 * C2, 6 * C1)),
            bf16((CHUNK, CHUNK)), bf16(cotangent.shape),
        ),
        scratch_shapes=[
            pltpu.VMEM((27, CIN, C1), jnp.bfloat16),
            pltpu.VMEM((27 * CIN, 4 * CHUNK), jnp.bfloat16),
            pltpu.VMEM((27, C1, C2), jnp.bfloat16),
            pltpu.VMEM((27 * CIN, C1), jnp.float32),
            pltpu.SemaphoreType.DMA((5,)),
        ],
        compiler_params=pltpu.CompilerParams(vmem_limit_bytes=12 * MIB),
        cost_estimate=pl.CostEstimate(flops=10**9, bytes_accessed=4 * MIB, transcendentals=0),
        name="prepare",
    )(*(pltpu.with_memory_space_constraint(x, pltpu.HBM) for x in stored))
    first, near, pre = pl.pallas_call(
        near_kernel,
        in_specs=[fast] * 5,
        out_specs=(fast,) * 3,
        out_shape=(f32((2 * C1, PLANE)), bf16((6 * C1, PLANE)), f32((2 * C2, PLANE))),
        scratch_shapes=[
            pltpu.VMEM((2 * ROWS, CELLS), jnp.float32),
            pltpu.VMEM((4, 2 * ROWS, LANES + PLANE), jnp.bfloat16),
            pltpu.VMEM((18 * ROWS, PLANE), jnp.bfloat16),
            pltpu.VMEM((2 * C1, PLANE + 2 * LANES), jnp.bfloat16),
            pltpu.VMEM((3, 2 * C2, PLANE + 2 * LANES), jnp.float32),
        ],
        compiler_params=pltpu.CompilerParams(vmem_limit_bytes=16 * MIB),
        cost_estimate=pl.CostEstimate(flops=10**9, bytes_accessed=4 * MIB, transcendentals=0),
        name="near",
    )(volumes, within, select, w1_near, w2)
    rows = C2 // narrow
    output, keep, give = pl.pallas_call(
        functools.partial(far_kernel, wide // 2, narrow, scale),
        in_specs=[fast] * 8,
        out_specs=(pl.BlockSpec(memory_space=pl.ANY), fast, fast),
        out_shape=(bf16((1, 1, C2, cells_out)), bf16((C2 // 2, PACKED)), bf16((C2 // 2, PACKED))),
        scratch_shapes=[
            pltpu.VMEM((ROWS, CELLS), jnp.float32),
            pltpu.VMEM((4, ROWS, LANES + PLANE), jnp.bfloat16),
            pltpu.VMEM((9 * ROWS, PLANE), jnp.bfloat16),
            pltpu.VMEM((2 * C1, PLANE + 2 * LANES), jnp.bfloat16),
            pltpu.VMEM((6 * C1, PLANE), jnp.bfloat16),
            pltpu.VMEM((3, 2 * C2, PLANE + 2 * LANES), jnp.float32),
            pltpu.VMEM((PLANE + 2 * HALF, LANES), jnp.bfloat16),
            pltpu.VMEM((2, 6 * C1, 3 * LANES), jnp.float32),
            pltpu.VMEM((1, 1, C2, cells_out), jnp.bfloat16),
            pltpu.SemaphoreType.DMA,
        ],
        compiler_params=pltpu.CompilerParams(vmem_limit_bytes=16 * MIB),
        name="far",
    )(across, select, w1_far, w2, cot, first, near, pre)
    half = rows // 2
    got = lax.ppermute(give, WIDE, pairs)
    term = (keep.astype(jnp.float32) + got.astype(jnp.float32)).astype(jnp.bfloat16)
    received = lax.all_to_all(term, "narrow", 0, 0, tiled=True)
    owned = jnp.sum(received.reshape(narrow, half, PACKED).astype(jnp.float32), axis=0).astype(jnp.bfloat16)
    parts = lax.all_to_all(jnp.broadcast_to(owned[None], (wide, half, PACKED)), WIDE, 0, 0, tiled=True)
    weight_grad = pl.pallas_call(
        finish_kernel,
        out_shape=jax.ShapeDtypeStruct((27, rows, C1), jnp.float32),
        compiler_params=pltpu.CompilerParams(vmem_limit_bytes=8 * MIB),
        name="finish",
    )(parts)
    return (output, weight_grad)


def solution(mesh):
    wide, narrow = mesh.devices.shape
    split = jax.sharding.Mesh(mesh.devices.reshape(wide // 2, 2, narrow), ("chip", "core", "narrow"))
    return jax.shard_map(
        body,
        mesh=split,
        in_specs=(P("narrow", None, None, WIDE, None), P(), P(), P("narrow", None, None, WIDE)),
        out_specs=(P("narrow", None, None, WIDE), P(None, "narrow", None)),
        check_vma=False,
    )
```

```python
import functools
import math

import jax
import jax.numpy as jnp
import numpy as np
from jax import lax
from jax.experimental import pallas as pl
from jax.experimental.pallas import tpu as pltpu
from jax.sharding import PartitionSpec as P

CIN = 4
C1 = 32
C2 = 64
PLANES = 4
CELLS = 4096
HALF = 32
PLANE = 1024
LANES = 128
ROWS = CIN * PLANES
CHUNK = 512
PACKED = 7 * LANES
MIB = 2**20
WIDE = ("chip", "core")
neg_slope = 0.3


def selection():
    table = np.zeros((CHUNK, 2, 2, 4, HALF), np.float32)
    for py in range(2):
        for px in range(2):
            for row in range(4):
                for col in range(HALF):
                    table[(2 * row + py) * 64 + 2 * col + px, py, px, row, col] = 1
    return table.reshape(CHUNK, CHUNK)


def placement():
    table = np.zeros((2, 27, CIN, 4, CHUNK), np.float32)
    for odd in range(2):
        for a in range(3):
            for bc in range(9):
                for i in range(CIN):
                    for q in range(4):
                        slab, plane = divmod(2 * q + a + 1, PLANES)
                        inner = i * PLANES + plane
                        if slab == 1:
                            column = bc * 2 * ROWS + inner
                        elif (slab == 0) == (odd == 1):
                            column = bc * 2 * ROWS + ROWS + inner
                        else:
                            column = 18 * ROWS + bc * ROWS + inner
                        table[odd, 9 * a + bc, i, q, column] = 1
    return table.reshape(2, 27 * CIN, 4 * CHUNK)


def leaky_relu(value):
    return jnp.where(value > 0, value, neg_slope * value)


def plane_rows(volume_ref, rows_ref):
    for i in range(CIN):
        rows_ref[PLANES * i : PLANES * (i + 1), :] = volume_ref[0, 0, i].astype(jnp.float32)


def column_masks():
    column = lax.broadcasted_iota(jnp.int32, (1, PLANE), 1) % HALF
    left_ok = jnp.where(column > 0, 1.0, 0.0).astype(jnp.bfloat16)
    right_ok = jnp.where(column < HALF - 1, 1.0, 0.0).astype(jnp.bfloat16)
    return left_ok, right_ok


def strided_taps(rows, select_ref, parity_ref, taps_ref):
    count = rows.shape[0]
    left_ok, _ = column_masks()
    chunks = jnp.concatenate([rows[:, CHUNK * j : CHUNK * (j + 1)] for j in range(8)], axis=0)
    for p in range(4):
        parity_ref[p, :, 0:LANES] = jnp.zeros((count, LANES), jnp.bfloat16)
    for py in range(2):
        parts = jnp.dot(
            chunks, select_ref[:, 256 * py : 256 * py + 256], preferred_element_type=jnp.float32
        ).astype(jnp.bfloat16)
        for px in range(2):
            for j in range(8):
                parity_ref[2 * py + px, :, LANES * (j + 1) : LANES * (j + 2)] = parts[
                    j * count : (j + 1) * count, px * LANES : (px + 1) * LANES
                ]
    for b in range(3):
        for c in range(3):
            begin = LANES - HALF * (b == 0) - (c == 0)
            part = parity_ref[2 * (b != 1) + (c != 1), :, begin : begin + PLANE]
            if c == 0:
                part = part * left_ok
            taps_ref[(3 * b + c) * count : (3 * b + c + 1) * count, :] = part


def shifted_columns(act_ref, columns_ref):
    left_ok, right_ok = column_masks()
    for c in range(3):
        begin = LANES + c - 1
        part = act_ref[:, begin : begin + PLANE]
        if c == 0:
            part = part * left_ok
        if c == 2:
            part = part * right_ok
        columns_ref[c * 2 * C1 : (c + 1) * 2 * C1, :] = part


def second_layer(w2, columns_ref, rowed_ref):
    blank = jnp.zeros((2 * C2, LANES), jnp.float32)
    for b in (0, 2):
        rowed_ref[b, :, 0:LANES] = blank
        rowed_ref[b, :, LANES + PLANE :] = blank
    for n in range(4):
        sums = jnp.dot(w2, columns_ref[:, 256 * n : 256 * n + 256], preferred_element_type=jnp.float32)
        for b in range(3):
            rowed_ref[b, :, LANES + 256 * n : LANES + 256 * n + 256] = sums[b * 2 * C2 : (b + 1) * 2 * C2]


def row_sum(rowed_ref, n):
    total = rowed_ref[1, :, LANES + 256 * n : LANES + 256 * n + 256]
    for b in (0, 2):
        begin = LANES + HALF * (b - 1) + 256 * n
        total = total + rowed_ref[b, :, begin : begin + 256]
    return total


def clear_margins(act_ref):
    margin = jnp.zeros((2 * C1, LANES), jnp.bfloat16)
    act_ref[:, 0:LANES] = margin
    act_ref[:, LANES + PLANE :] = margin


def prepare_kernel(
    k1_hbm, place_hbm, k2_hbm, select_hbm, cot_hbm, w1_near_ref, w1_far_ref, w2_ref, select_ref, cot_ref,
    k1_ref, place_ref, k2_ref, k1_rows_ref, sems,
):
    odd = lax.axis_index("core")
    moves = ((k1_hbm, k1_ref), (k2_hbm, k2_ref), (place_hbm.at[odd], place_ref), (select_hbm, select_ref), (cot_hbm, cot_ref))
    copies = [pltpu.make_async_copy(src, dst, sems.at[k]) for k, (src, dst) in enumerate(moves)]
    for copy in copies:
        copy.start()
    copies[0].wait()
    for tap in range(27):
        k1_rows_ref[CIN * tap : CIN * (tap + 1), :] = k1_ref[tap].astype(jnp.float32)
    copies[1].wait()
    blank = jnp.zeros((C1, C2), jnp.bfloat16)

    def stacked(bc, pair):
        k = [blank] + [k2_ref[9 * a + bc] for a in range(3)] + [blank]
        lower = jnp.concatenate(k[1 + 2 * pair : 3 + 2 * pair], axis=0)
        upper = jnp.concatenate(k[2 * pair : 2 + 2 * pair], axis=0)
        return jnp.concatenate([lower, upper], axis=1)

    for b in range(3):
        rows = slice(b * 2 * C2, (b + 1) * 2 * C2)
        for pair in range(2):
            both = jnp.concatenate([stacked(3 * b, pair), stacked(3 * b + 1, pair)], axis=0)
            w2_ref[pair, rows, 0:LANES] = both.T
        both = jnp.concatenate([stacked(3 * b + 2, 0), stacked(3 * b + 2, 1)], axis=0).T
        for pair in range(2):
            w2_ref[pair, rows, LANES : LANES + 2 * C1] = both[:, pair * 2 * C1 : (pair + 1) * 2 * C1]
    copies[2].wait()
    spread = lax.dot_general(
        k1_rows_ref[...].astype(jnp.bfloat16), place_ref[...],
        (((0,), (0,)), ((), ())), preferred_element_type=jnp.float32,
    ).astype(jnp.bfloat16)
    for q in range(4):
        rows = slice(q % 2 * C1, (q % 2 + 1) * C1)
        w1_near_ref[q // 2, rows, :] = spread[:, CHUNK * q : CHUNK * q + 18 * ROWS]
        w1_far_ref[q // 2, rows, :] = spread[:, CHUNK * q + 18 * ROWS : CHUNK * q + 27 * ROWS]
    copies[3].wait()
    copies[4].wait()


def near_kernel(
    own_ref, within_ref, select_ref, w1_ref, w2_ref, first_ref, columns_ref, pre_ref,
    rows_ref, parity_ref, taps_ref, act_ref, rowed_ref,
):
    odd = lax.axis_index("core")
    plane_rows(own_ref, rows_ref.at[0:ROWS])
    plane_rows(within_ref, rows_ref.at[ROWS : 2 * ROWS])
    strided_taps(rows_ref[...].astype(jnp.bfloat16), select_ref, parity_ref, taps_ref)
    clear_margins(act_ref)
    for n in range(4):
        here = slice(256 * n, 256 * n + 256)
        first_ref[:, here] = jnp.dot(w1_ref[odd], taps_ref[:, here], preferred_element_type=jnp.float32)
        complete = jnp.dot(w1_ref[1 - odd], taps_ref[:, here], preferred_element_type=jnp.float32)
        act_ref[:, LANES + 256 * n : LANES + 256 * n + 256] = leaky_relu(complete).astype(jnp.bfloat16)
    shifted_columns(act_ref, columns_ref)
    second_layer(w2_ref[1 - odd], columns_ref, rowed_ref)
    for n in range(4):
        pre_ref[:, 256 * n : 256 * n + 256] = row_sum(rowed_ref, n)


def far_kernel(
    chips, scale, across_ref, select_ref, w1_ref, w2_ref, cot_ref, first_ref, near_ref, pre_ref, out_hbm, grad_ref,
    rows_ref, parity_ref, taps_ref, act_ref, columns_ref, rowed_ref, back_ref, sums_ref, out_ref, out_sem,
):
    odd = lax.axis_index("core")
    last = (lax.axis_index("chip") == chips - 1) & (odd == 1)
    inside = jnp.where(last, 0.0, 1.0)
    plane_rows(across_ref, rows_ref)
    strided_taps(rows_ref[...].astype(jnp.bfloat16), select_ref, parity_ref, taps_ref)
    clear_margins(act_ref)
    for n in range(4):
        here = slice(256 * n, 256 * n + 256)
        first_pre = first_ref[:, here] + jnp.dot(w1_ref[odd], taps_ref[:, here], preferred_element_type=jnp.float32)
        first_act = leaky_relu(first_pre)
        there = slice(LANES + 256 * n, LANES + 256 * n + 256)
        act_ref[0:C1, there] = first_act[0:C1].astype(jnp.bfloat16)
        act_ref[C1:, there] = (first_act[C1:] * inside).astype(jnp.bfloat16)
    shifted_columns(act_ref, columns_ref)
    second_layer(w2_ref[odd], columns_ref, rowed_ref)
    margin = jnp.zeros((HALF, LANES), jnp.bfloat16)
    back_ref[0:HALF, :] = margin
    back_ref[HALF + PLANE :, :] = margin
    for n in range(4):
        pre = pre_ref[:, 256 * n : 256 * n + 256] + row_sum(rowed_ref, n)
        output = leaky_relu(pre).astype(jnp.bfloat16)
        slope = jnp.where(pre > 0, 1.0, neg_slope)
        backs = []
        for z in range(2):
            cells = slice(z * PLANE + 256 * n, z * PLANE + 256 * n + 256)
            rows = slice(z * C2, (z + 1) * C2)
            out_ref[0, 0, :, cells] = output[rows]
            backs.append((cot_ref[0, 0, :, cells].astype(jnp.float32) * slope[rows]).astype(jnp.bfloat16))
        back_ref[HALF + 256 * n : HALF + 256 * n + 256, :] = jnp.concatenate(backs, axis=0).T
    out_copy = pltpu.make_async_copy(out_ref, out_hbm, out_sem)
    out_copy.start()
    columns = jnp.concatenate([near_ref[...], columns_ref[...]], axis=0)
    rowed_back = jnp.concatenate([back_ref[(2 - b) * HALF : (2 - b) * HALF + PLANE, :] for b in range(3)], axis=1)
    sums = jnp.dot(columns, rowed_back, preferred_element_type=jnp.float32)
    sums_ref[1 - odd] = sums[0 : 6 * C1]
    sums_ref[odd] = sums[6 * C1 :]
    low = lax.broadcasted_iota(jnp.int32, (C1, LANES), 1) < C2

    def plane_sums(bc, q):
        b, c = divmod(bc, 3)
        begin = 2 * C1 * c + C1 * (q % 2)
        return sums_ref[q // 2, begin : begin + C1, b * LANES : (b + 1) * LANES]

    def two_taps(first, second):
        a, bc = divmod(first, 9)
        here, above = plane_sums(bc, a), pltpu.roll(plane_sums(bc, a + 1), C2, 1)
        if second > 26:
            return here + above
        a, bc = divmod(second, 9)
        there, beyond = pltpu.roll(plane_sums(bc, a), C2, 1), plane_sums(bc, a + 1)
        return jnp.where(low, here, there) + jnp.where(low, above, beyond)

    for block in range(4):
        tall = jnp.concatenate([two_taps(min(8 * block + g, 26), 8 * block + 4 + g) for g in range(4)], axis=0)
        flat = (tall * scale).T.astype(jnp.bfloat16)
        grad_ref[:, 2 * block * LANES : (2 * block + 1) * LANES] = flat[0:C2]
        if block < 3:
            grad_ref[:, (2 * block + 1) * LANES : (2 * block + 2) * LANES] = flat[C2:]
    out_copy.wait()


def finish_kernel(parts_ref, grad_ref):
    wide, half, _ = parts_ref.shape
    for core in range(2):
        total = parts_ref[core].astype(jnp.float32)
        for k in range(core + 2, wide, 2):
            total = total + parts_ref[k].astype(jnp.float32)
        for tap in range(27):
            grad_ref[tap, core * half : (core + 1) * half, :] = total[:, tap * C1 : (tap + 1) * C1]


def body(volumes, first_kernel, second_kernel, cotangent):
    wide = lax.axis_size(WIDE)
    narrow = lax.axis_size("narrow")
    cells_out = cotangent.shape[3]
    scale = 1.0 / math.sqrt(wide * narrow * cells_out)
    across = lax.ppermute(volumes, WIDE, [p for k in range(1, wide - 1, 2) for p in ((k, k + 1), (k + 1, k))])
    within = lax.ppermute(volumes, WIDE, [p for k in range(0, wide - 1, 2) for p in ((k, k + 1), (k + 1, k))])
    pinned = pl.BlockSpec(memory_space=pltpu.HBM)
    fast = pl.BlockSpec(memory_space=pltpu.VMEM)
    bf16 = functools.partial(jax.ShapeDtypeStruct, dtype=jnp.bfloat16)
    f32 = functools.partial(jax.ShapeDtypeStruct, dtype=jnp.float32)
    stored = (
        first_kernel.transpose(0, 2, 1), jnp.asarray(placement(), jnp.bfloat16), second_kernel.transpose(0, 2, 1),
        jnp.asarray(selection(), jnp.bfloat16), cotangent,
    )
    w1_near, w1_far, w2, select, cot = pl.pallas_call(
        prepare_kernel,
        in_specs=[pinned] * 5,
        out_specs=(fast,) * 5,
        out_shape=(
            bf16((2, 2 * C1, 18 * ROWS)), bf16((2, 2 * C1, 9 * ROWS)), bf16((2, 6 * C2, 6 * C1)),
            bf16((CHUNK, CHUNK)), bf16(cotangent.shape),
        ),
        scratch_shapes=[
            pltpu.VMEM((27, CIN, C1), jnp.bfloat16),
            pltpu.VMEM((27 * CIN, 4 * CHUNK), jnp.bfloat16),
            pltpu.VMEM((27, C1, C2), jnp.bfloat16),
            pltpu.VMEM((27 * CIN, C1), jnp.float32),
            pltpu.SemaphoreType.DMA((5,)),
        ],
        compiler_params=pltpu.CompilerParams(vmem_limit_bytes=12 * MIB),
        cost_estimate=pl.CostEstimate(flops=10**9, bytes_accessed=4 * MIB, transcendentals=0),
        name="prepare",
    )(*(pltpu.with_memory_space_constraint(x, pltpu.HBM) for x in stored))
    first, near, pre = pl.pallas_call(
        near_kernel,
        in_specs=[fast] * 5,
        out_specs=(fast,) * 3,
        out_shape=(f32((2 * C1, PLANE)), bf16((6 * C1, PLANE)), f32((2 * C2, PLANE))),
        scratch_shapes=[
            pltpu.VMEM((2 * ROWS, CELLS), jnp.float32),
            pltpu.VMEM((4, 2 * ROWS, LANES + PLANE), jnp.bfloat16),
            pltpu.VMEM((18 * ROWS, PLANE), jnp.bfloat16),
            pltpu.VMEM((2 * C1, PLANE + 2 * LANES), jnp.bfloat16),
            pltpu.VMEM((3, 2 * C2, PLANE + 2 * LANES), jnp.float32),
        ],
        compiler_params=pltpu.CompilerParams(vmem_limit_bytes=16 * MIB),
        cost_estimate=pl.CostEstimate(flops=10**9, bytes_accessed=4 * MIB, transcendentals=0),
        name="near",
    )(volumes, within, select, w1_near, w2)
    rows = C2 // narrow
    output, term = pl.pallas_call(
        functools.partial(far_kernel, wide // 2, scale),
        in_specs=[fast] * 8,
        out_specs=(pl.BlockSpec(memory_space=pl.ANY), fast),
        out_shape=(bf16((1, 1, C2, cells_out)), bf16((C2, PACKED))),
        scratch_shapes=[
            pltpu.VMEM((ROWS, CELLS), jnp.float32),
            pltpu.VMEM((4, ROWS, LANES + PLANE), jnp.bfloat16),
            pltpu.VMEM((9 * ROWS, PLANE), jnp.bfloat16),
            pltpu.VMEM((2 * C1, PLANE + 2 * LANES), jnp.bfloat16),
            pltpu.VMEM((6 * C1, PLANE), jnp.bfloat16),
            pltpu.VMEM((3, 2 * C2, PLANE + 2 * LANES), jnp.float32),
            pltpu.VMEM((PLANE + 2 * HALF, LANES), jnp.bfloat16),
            pltpu.VMEM((2, 6 * C1, 3 * LANES), jnp.float32),
            pltpu.VMEM((1, 1, C2, cells_out), jnp.bfloat16),
            pltpu.SemaphoreType.DMA,
        ],
        compiler_params=pltpu.CompilerParams(vmem_limit_bytes=16 * MIB),
        name="far",
    )(across, select, w1_far, w2, cot, first, near, pre)
    half = rows // 2
    received = lax.all_to_all(term, ("narrow", "core"), 0, 0, tiled=True)
    owned = jnp.sum(received.reshape(2 * narrow, half, PACKED).astype(jnp.float32), axis=0).astype(jnp.bfloat16)
    parts = lax.all_gather(owned, WIDE)
    weight_grad = pl.pallas_call(
        finish_kernel,
        out_shape=jax.ShapeDtypeStruct((27, rows, C1), jnp.float32),
        compiler_params=pltpu.CompilerParams(vmem_limit_bytes=8 * MIB),
        name="finish",
    )(parts)
    return (output, weight_grad)


def solution(mesh):
    wide, narrow = mesh.devices.shape
    split = jax.sharding.Mesh(mesh.devices.reshape(wide // 2, 2, narrow), ("chip", "core", "narrow"))
    return jax.shard_map(
        body,
        mesh=split,
        in_specs=(P("narrow", None, None, WIDE, None), P(), P(), P("narrow", None, None, WIDE)),
        out_specs=(P("narrow", None, None, WIDE), P(None, "narrow", None)),
        check_vma=False,
    )
```

```python
import functools
import math

import jax
import jax.numpy as jnp
import numpy as np
from jax import lax
from jax.experimental import pallas as pl
from jax.experimental.pallas import tpu as pltpu
from jax.sharding import PartitionSpec as P

CIN = 4
C1 = 32
C2 = 64
PLANES = 4
CELLS = 4096
HALF = 32
PLANE = 1024
LANES = 128
ROWS = CIN * PLANES
CHUNK = 512
PACKED = 7 * LANES
MIB = 2**20
WIDE = ("chip", "core")
neg_slope = 0.3


def selection():
    table = np.zeros((CHUNK, 2, 2, 4, HALF), np.float32)
    for py in range(2):
        for px in range(2):
            for row in range(4):
                for col in range(HALF):
                    table[(2 * row + py) * 64 + 2 * col + px, py, px, row, col] = 1
    return table.reshape(CHUNK, CHUNK)


def placement():
    table = np.zeros((2, 27, CIN, 4, CHUNK), np.float32)
    for odd in range(2):
        for a in range(3):
            for bc in range(9):
                for i in range(CIN):
                    for q in range(4):
                        slab, plane = divmod(2 * q + a + 1, PLANES)
                        inner = i * PLANES + plane
                        if slab == 1:
                            column = bc * 2 * ROWS + inner
                        elif (slab == 0) == (odd == 1):
                            column = bc * 2 * ROWS + ROWS + inner
                        else:
                            column = 18 * ROWS + bc * ROWS + inner
                        table[odd, 9 * a + bc, i, q, column] = 1
    return table.reshape(2, 27 * CIN, 4 * CHUNK)


def leaky_relu(value):
    return jnp.where(value > 0, value, neg_slope * value)


def plane_rows(volume_ref, rows_ref):
    for i in range(CIN):
        rows_ref[PLANES * i : PLANES * (i + 1), :] = volume_ref[0, 0, i].astype(jnp.float32)


def column_masks():
    column = lax.broadcasted_iota(jnp.int32, (1, PLANE), 1) % HALF
    left_ok = jnp.where(column > 0, 1.0, 0.0).astype(jnp.bfloat16)
    right_ok = jnp.where(column < HALF - 1, 1.0, 0.0).astype(jnp.bfloat16)
    return left_ok, right_ok


def strided_taps(rows, select_ref, parity_ref, taps_ref):
    count = rows.shape[0]
    left_ok, _ = column_masks()
    chunks = jnp.concatenate([rows[:, CHUNK * j : CHUNK * (j + 1)] for j in range(8)], axis=0)
    for p in range(4):
        parity_ref[p, :, 0:LANES] = jnp.zeros((count, LANES), jnp.bfloat16)
    for py in range(2):
        parts = jnp.dot(
            chunks, select_ref[:, 256 * py : 256 * py + 256], preferred_element_type=jnp.float32
        ).astype(jnp.bfloat16)
        for px in range(2):
            for j in range(8):
                parity_ref[2 * py + px, :, LANES * (j + 1) : LANES * (j + 2)] = parts[
                    j * count : (j + 1) * count, px * LANES : (px + 1) * LANES
                ]
    for b in range(3):
        for c in range(3):
            begin = LANES - HALF * (b == 0) - (c == 0)
            part = parity_ref[2 * (b != 1) + (c != 1), :, begin : begin + PLANE]
            if c == 0:
                part = part * left_ok
            taps_ref[(3 * b + c) * count : (3 * b + c + 1) * count, :] = part


def shifted_columns(act_ref, columns_ref):
    left_ok, right_ok = column_masks()
    for c in range(3):
        begin = LANES + c - 1
        part = act_ref[:, begin : begin + PLANE]
        if c == 0:
            part = part * left_ok
        if c == 2:
            part = part * right_ok
        columns_ref[c * 2 * C1 : (c + 1) * 2 * C1, :] = part


def second_layer(w2, columns_ref, rowed_ref):
    blank = jnp.zeros((2 * C2, LANES), jnp.float32)
    for b in (0, 2):
        rowed_ref[b, :, 0:LANES] = blank
        rowed_ref[b, :, LANES + PLANE :] = blank
    for n in range(4):
        sums = jnp.dot(w2, columns_ref[:, 256 * n : 256 * n + 256], preferred_element_type=jnp.float32)
        for b in range(3):
            rowed_ref[b, :, LANES + 256 * n : LANES + 256 * n + 256] = sums[b * 2 * C2 : (b + 1) * 2 * C2]


def row_sum(rowed_ref, n):
    total = rowed_ref[1, :, LANES + 256 * n : LANES + 256 * n + 256]
    for b in (0, 2):
        begin = LANES + HALF * (b - 1) + 256 * n
        total = total + rowed_ref[b, :, begin : begin + 256]
    return total


def clear_margins(act_ref):
    margin = jnp.zeros((2 * C1, LANES), jnp.bfloat16)
    act_ref[:, 0:LANES] = margin
    act_ref[:, LANES + PLANE :] = margin


def prepare_kernel(
    k1_hbm, place_hbm, k2_hbm, select_hbm, cot_hbm, w1_near_ref, w1_far_ref, w2_ref, select_ref, cot_ref,
    k1_ref, place_ref, k2_ref, k1_rows_ref, sems,
):
    odd = lax.axis_index("core")
    moves = ((k1_hbm, k1_ref), (k2_hbm, k2_ref), (place_hbm.at[odd], place_ref), (select_hbm, select_ref), (cot_hbm, cot_ref))
    copies = [pltpu.make_async_copy(src, dst, sems.at[k]) for k, (src, dst) in enumerate(moves)]
    for copy in copies:
        copy.start()
    copies[0].wait()
    for tap in range(27):
        k1_rows_ref[CIN * tap : CIN * (tap + 1), :] = k1_ref[tap].astype(jnp.float32)
    copies[1].wait()
    blank = jnp.zeros((C1, C2), jnp.bfloat16)

    def stacked(bc, pair):
        k = [blank] + [k2_ref[9 * a + bc] for a in range(3)] + [blank]
        lower = jnp.concatenate(k[1 + 2 * pair : 3 + 2 * pair], axis=0)
        upper = jnp.concatenate(k[2 * pair : 2 + 2 * pair], axis=0)
        return jnp.concatenate([lower, upper], axis=1)

    for b in range(3):
        rows = slice(b * 2 * C2, (b + 1) * 2 * C2)
        for pair in range(2):
            both = jnp.concatenate([stacked(3 * b, pair), stacked(3 * b + 1, pair)], axis=0)
            w2_ref[pair, rows, 0:LANES] = both.T
        both = jnp.concatenate([stacked(3 * b + 2, 0), stacked(3 * b + 2, 1)], axis=0).T
        for pair in range(2):
            w2_ref[pair, rows, LANES : LANES + 2 * C1] = both[:, pair * 2 * C1 : (pair + 1) * 2 * C1]
    copies[2].wait()
    spread = lax.dot_general(
        k1_rows_ref[...].astype(jnp.bfloat16), place_ref[...],
        (((0,), (0,)), ((), ())), preferred_element_type=jnp.float32,
    ).astype(jnp.bfloat16)
    for q in range(4):
        rows = slice(q % 2 * C1, (q % 2 + 1) * C1)
        w1_near_ref[q // 2, rows, :] = spread[:, CHUNK * q : CHUNK * q + 18 * ROWS]
        w1_far_ref[q // 2, rows, :] = spread[:, CHUNK * q + 18 * ROWS : CHUNK * q + 27 * ROWS]
    copies[3].wait()
    copies[4].wait()


def near_kernel(
    own_ref, within_ref, select_ref, w1_ref, w2_ref, first_ref, columns_ref, pre_ref,
    rows_ref, parity_ref, taps_ref, act_ref, rowed_ref,
):
    odd = lax.axis_index("core")
    plane_rows(own_ref, rows_ref.at[0:ROWS])
    plane_rows(within_ref, rows_ref.at[ROWS : 2 * ROWS])
    strided_taps(rows_ref[...].astype(jnp.bfloat16), select_ref, parity_ref, taps_ref)
    clear_margins(act_ref)
    for n in range(4):
        here = slice(256 * n, 256 * n + 256)
        first_ref[:, here] = jnp.dot(w1_ref[odd], taps_ref[:, here], preferred_element_type=jnp.float32)
        complete = jnp.dot(w1_ref[1 - odd], taps_ref[:, here], preferred_element_type=jnp.float32)
        act_ref[:, LANES + 256 * n : LANES + 256 * n + 256] = leaky_relu(complete).astype(jnp.bfloat16)
    shifted_columns(act_ref, columns_ref)
    second_layer(w2_ref[1 - odd], columns_ref, rowed_ref)
    for n in range(4):
        pre_ref[:, 256 * n : 256 * n + 256] = row_sum(rowed_ref, n)


def far_kernel(
    chips, scale, across_ref, select_ref, w1_ref, w2_ref, cot_ref, first_ref, near_ref, pre_ref, out_hbm, grad_ref,
    rows_ref, parity_ref, taps_ref, act_ref, columns_ref, rowed_ref, back_ref, sums_ref, out_ref, out_sem,
):
    odd = lax.axis_index("core")
    last = (lax.axis_index("chip") == chips - 1) & (odd == 1)
    inside = jnp.where(last, 0.0, 1.0)
    plane_rows(across_ref, rows_ref)
    strided_taps(rows_ref[...].astype(jnp.bfloat16), select_ref, parity_ref, taps_ref)
    clear_margins(act_ref)
    for n in range(4):
        here = slice(256 * n, 256 * n + 256)
        first_pre = first_ref[:, here] + jnp.dot(w1_ref[odd], taps_ref[:, here], preferred_element_type=jnp.float32)
        first_act = leaky_relu(first_pre)
        there = slice(LANES + 256 * n, LANES + 256 * n + 256)
        act_ref[0:C1, there] = first_act[0:C1].astype(jnp.bfloat16)
        act_ref[C1:, there] = (first_act[C1:] * inside).astype(jnp.bfloat16)
    shifted_columns(act_ref, columns_ref)
    second_layer(w2_ref[odd], columns_ref, rowed_ref)
    margin = jnp.zeros((HALF, LANES), jnp.bfloat16)
    back_ref[0:HALF, :] = margin
    back_ref[HALF + PLANE :, :] = margin
    for n in range(4):
        pre = pre_ref[:, 256 * n : 256 * n + 256] + row_sum(rowed_ref, n)
        output = leaky_relu(pre).astype(jnp.bfloat16)
        slope = jnp.where(pre > 0, 1.0, neg_slope)
        backs = []
        for z in range(2):
            cells = slice(z * PLANE + 256 * n, z * PLANE + 256 * n + 256)
            rows = slice(z * C2, (z + 1) * C2)
            out_ref[0, 0, :, cells] = output[rows]
            backs.append((cot_ref[0, 0, :, cells].astype(jnp.float32) * slope[rows]).astype(jnp.bfloat16))
        back_ref[HALF + 256 * n : HALF + 256 * n + 256, :] = jnp.concatenate(backs, axis=0).T
    out_copy = pltpu.make_async_copy(out_ref, out_hbm, out_sem)
    out_copy.start()
    columns = jnp.concatenate([near_ref[...], columns_ref[...]], axis=0)
    rowed_back = jnp.concatenate([back_ref[(2 - b) * HALF : (2 - b) * HALF + PLANE, :] for b in range(3)], axis=1)
    sums = jnp.dot(columns, rowed_back, preferred_element_type=jnp.float32)
    sums_ref[1 - odd] = sums[0 : 6 * C1]
    sums_ref[odd] = sums[6 * C1 :]
    low = lax.broadcasted_iota(jnp.int32, (C1, LANES), 1) < C2

    def plane_sums(bc, q):
        b, c = divmod(bc, 3)
        begin = 2 * C1 * c + C1 * (q % 2)
        return sums_ref[q // 2, begin : begin + C1, b * LANES : (b + 1) * LANES]

    def two_taps(first, second):
        a, bc = divmod(first, 9)
        here, above = plane_sums(bc, a), pltpu.roll(plane_sums(bc, a + 1), C2, 1)
        if second > 26:
            return here + above
        a, bc = divmod(second, 9)
        there, beyond = pltpu.roll(plane_sums(bc, a), C2, 1), plane_sums(bc, a + 1)
        return jnp.where(low, here, there) + jnp.where(low, above, beyond)

    for block in range(4):
        tall = jnp.concatenate([two_taps(min(8 * block + g, 26), 8 * block + 4 + g) for g in range(4)], axis=0)
        flat = (tall * scale).T.astype(jnp.bfloat16)
        grad_ref[:, 2 * block * LANES : (2 * block + 1) * LANES] = flat[0:C2]
        if block < 3:
            grad_ref[:, (2 * block + 1) * LANES : (2 * block + 2) * LANES] = flat[C2:]
    out_copy.wait()


def finish_kernel(mine_ref, other_ref, grad_ref):
    total = mine_ref[...].astype(jnp.float32) + other_ref[...].astype(jnp.float32)
    for tap in range(27):
        grad_ref[tap] = total[:, tap * C1 : (tap + 1) * C1]


def body(volumes, first_kernel, second_kernel, cotangent):
    wide = lax.axis_size(WIDE)
    narrow = lax.axis_size("narrow")
    cells_out = cotangent.shape[3]
    scale = 1.0 / math.sqrt(wide * narrow * cells_out)
    across = lax.ppermute(volumes, WIDE, [p for k in range(1, wide - 1, 2) for p in ((k, k + 1), (k + 1, k))])
    pairs = [p for k in range(0, wide - 1, 2) for p in ((k, k + 1), (k + 1, k))]
    within = lax.ppermute(volumes, WIDE, pairs)
    pinned = pl.BlockSpec(memory_space=pltpu.HBM)
    fast = pl.BlockSpec(memory_space=pltpu.VMEM)
    bf16 = functools.partial(jax.ShapeDtypeStruct, dtype=jnp.bfloat16)
    f32 = functools.partial(jax.ShapeDtypeStruct, dtype=jnp.float32)
    stored = (
        first_kernel.transpose(0, 2, 1), jnp.asarray(placement(), jnp.bfloat16), second_kernel.transpose(0, 2, 1),
        jnp.asarray(selection(), jnp.bfloat16), cotangent,
    )
    w1_near, w1_far, w2, select, cot = pl.pallas_call(
        prepare_kernel,
        in_specs=[pinned] * 5,
        out_specs=(fast,) * 5,
        out_shape=(
            bf16((2, 2 * C1, 18 * ROWS)), bf16((2, 2 * C1, 9 * ROWS)), bf16((2, 6 * C2, 6 * C1)),
            bf16((CHUNK, CHUNK)), bf16(cotangent.shape),
        ),
        scratch_shapes=[
            pltpu.VMEM((27, CIN, C1), jnp.bfloat16),
            pltpu.VMEM((27 * CIN, 4 * CHUNK), jnp.bfloat16),
            pltpu.VMEM((27, C1, C2), jnp.bfloat16),
            pltpu.VMEM((27 * CIN, C1), jnp.float32),
            pltpu.SemaphoreType.DMA((5,)),
        ],
        compiler_params=pltpu.CompilerParams(vmem_limit_bytes=12 * MIB),
        cost_estimate=pl.CostEstimate(flops=10**9, bytes_accessed=4 * MIB, transcendentals=0),
        name="prepare",
    )(*(pltpu.with_memory_space_constraint(x, pltpu.HBM) for x in stored))
    first, near, pre = pl.pallas_call(
        near_kernel,
        in_specs=[fast] * 5,
        out_specs=(fast,) * 3,
        out_shape=(f32((2 * C1, PLANE)), bf16((6 * C1, PLANE)), f32((2 * C2, PLANE))),
        scratch_shapes=[
            pltpu.VMEM((2 * ROWS, CELLS), jnp.float32),
            pltpu.VMEM((4, 2 * ROWS, LANES + PLANE), jnp.bfloat16),
            pltpu.VMEM((18 * ROWS, PLANE), jnp.bfloat16),
            pltpu.VMEM((2 * C1, PLANE + 2 * LANES), jnp.bfloat16),
            pltpu.VMEM((3, 2 * C2, PLANE + 2 * LANES), jnp.float32),
        ],
        compiler_params=pltpu.CompilerParams(vmem_limit_bytes=16 * MIB),
        cost_estimate=pl.CostEstimate(flops=10**9, bytes_accessed=4 * MIB, transcendentals=0),
        name="near",
    )(volumes, within, select, w1_near, w2)
    rows = C2 // narrow
    output, term = pl.pallas_call(
        functools.partial(far_kernel, wide // 2, scale),
        in_specs=[fast] * 8,
        out_specs=(pl.BlockSpec(memory_space=pl.ANY), fast),
        out_shape=(bf16((1, 1, C2, cells_out)), bf16((C2, PACKED))),
        scratch_shapes=[
            pltpu.VMEM((ROWS, CELLS), jnp.float32),
            pltpu.VMEM((4, ROWS, LANES + PLANE), jnp.bfloat16),
            pltpu.VMEM((9 * ROWS, PLANE), jnp.bfloat16),
            pltpu.VMEM((2 * C1, PLANE + 2 * LANES), jnp.bfloat16),
            pltpu.VMEM((6 * C1, PLANE), jnp.bfloat16),
            pltpu.VMEM((3, 2 * C2, PLANE + 2 * LANES), jnp.float32),
            pltpu.VMEM((PLANE + 2 * HALF, LANES), jnp.bfloat16),
            pltpu.VMEM((2, 6 * C1, 3 * LANES), jnp.float32),
            pltpu.VMEM((1, 1, C2, cells_out), jnp.bfloat16),
            pltpu.SemaphoreType.DMA,
        ],
        compiler_params=pltpu.CompilerParams(vmem_limit_bytes=16 * MIB),
        name="far",
    )(across, select, w1_far, w2, cot, first, near, pre)
    received = lax.all_to_all(term, "narrow", 0, 0, tiled=True)
    owned = jnp.sum(received.reshape(narrow, rows, PACKED).astype(jnp.float32), axis=0).astype(jnp.bfloat16)
    copies = jnp.broadcast_to(owned[None], (wide // 2, rows, PACKED))
    parts = lax.all_to_all(copies, "chip", 0, 0, tiled=True)
    mine = jnp.sum(parts.astype(jnp.float32), axis=0).astype(jnp.bfloat16)
    other = lax.ppermute(mine, WIDE, pairs)
    weight_grad = pl.pallas_call(
        finish_kernel,
        out_shape=jax.ShapeDtypeStruct((27, rows, C1), jnp.float32),
        compiler_params=pltpu.CompilerParams(vmem_limit_bytes=8 * MIB),
        name="finish",
    )(mine, other)
    return (output, weight_grad)


def solution(mesh):
    wide, narrow = mesh.devices.shape
    split = jax.sharding.Mesh(mesh.devices.reshape(wide // 2, 2, narrow), ("chip", "core", "narrow"))
    return jax.shard_map(
        body,
        mesh=split,
        in_specs=(P("narrow", None, None, WIDE, None), P(), P(), P("narrow", None, None, WIDE)),
        out_specs=(P("narrow", None, None, WIDE), P(None, "narrow", None)),
        check_vma=False,
    )
```

```python
import functools
import math

import jax
import jax.numpy as jnp
import numpy as np
from jax import lax
from jax.experimental import pallas as pl
from jax.experimental.pallas import tpu as pltpu
from jax.sharding import PartitionSpec as P

CIN = 4
C1 = 32
C2 = 64
PLANES = 4
CELLS = 4096
HALF = 32
PLANE = 1024
LANES = 128
ROWS = CIN * PLANES
CHUNK = 512
PACKED = 7 * LANES
MIB = 2**20
WIDE = ("chip", "core")
neg_slope = 0.3


def selection():
    table = np.zeros((CHUNK, 2, 2, 4, HALF), np.float32)
    for py in range(2):
        for px in range(2):
            for row in range(4):
                for col in range(HALF):
                    table[(2 * row + py) * 64 + 2 * col + px, py, px, row, col] = 1
    return table.reshape(CHUNK, CHUNK)


def placement():
    table = np.zeros((2, 27, CIN, 4, CHUNK), np.float32)
    for odd in range(2):
        for a in range(3):
            for bc in range(9):
                for i in range(CIN):
                    for q in range(4):
                        slab, plane = divmod(2 * q + a + 1, PLANES)
                        inner = i * PLANES + plane
                        if slab == 1:
                            column = bc * 2 * ROWS + inner
                        elif (slab == 0) == (odd == 1):
                            column = bc * 2 * ROWS + ROWS + inner
                        else:
                            column = 18 * ROWS + bc * ROWS + inner
                        table[odd, 9 * a + bc, i, q, column] = 1
    return table.reshape(2, 27 * CIN, 4 * CHUNK)


def leaky_relu(value):
    return jnp.where(value > 0, value, neg_slope * value)


def plane_rows(volume_ref, rows_ref):
    for i in range(CIN):
        rows_ref[PLANES * i : PLANES * (i + 1), :] = volume_ref[0, 0, i].astype(jnp.float32)


def column_masks():
    column = lax.broadcasted_iota(jnp.int32, (1, PLANE), 1) % HALF
    left_ok = jnp.where(column > 0, 1.0, 0.0).astype(jnp.bfloat16)
    right_ok = jnp.where(column < HALF - 1, 1.0, 0.0).astype(jnp.bfloat16)
    return left_ok, right_ok


def strided_taps(rows, select_ref, parity_ref, taps_ref):
    count = rows.shape[0]
    left_ok, _ = column_masks()
    chunks = jnp.concatenate([rows[:, CHUNK * j : CHUNK * (j + 1)] for j in range(8)], axis=0)
    for p in range(4):
        parity_ref[p, :, 0:LANES] = jnp.zeros((count, LANES), jnp.bfloat16)
    for py in range(2):
        parts = jnp.dot(
            chunks, select_ref[:, 256 * py : 256 * py + 256], preferred_element_type=jnp.float32
        ).astype(jnp.bfloat16)
        for px in range(2):
            for j in range(8):
                parity_ref[2 * py + px, :, LANES * (j + 1) : LANES * (j + 2)] = parts[
                    j * count : (j + 1) * count, px * LANES : (px + 1) * LANES
                ]
    for b in range(3):
        for c in range(3):
            begin = LANES - HALF * (b == 0) - (c == 0)
            part = parity_ref[2 * (b != 1) + (c != 1), :, begin : begin + PLANE]
            if c == 0:
                part = part * left_ok
            taps_ref[(3 * b + c) * count : (3 * b + c + 1) * count, :] = part


def shifted_columns(act_ref, columns_ref):
    left_ok, right_ok = column_masks()
    for c in range(3):
        begin = LANES + c - 1
        part = act_ref[:, begin : begin + PLANE]
        if c == 0:
            part = part * left_ok
        if c == 2:
            part = part * right_ok
        columns_ref[c * 2 * C1 : (c + 1) * 2 * C1, :] = part


def second_layer(w2, columns_ref, rowed_ref):
    blank = jnp.zeros((2 * C2, LANES), jnp.float32)
    for b in (0, 2):
        rowed_ref[b, :, 0:LANES] = blank
        rowed_ref[b, :, LANES + PLANE :] = blank
    for n in range(4):
        sums = jnp.dot(w2, columns_ref[:, 256 * n : 256 * n + 256], preferred_element_type=jnp.float32)
        for b in range(3):
            rowed_ref[b, :, LANES + 256 * n : LANES + 256 * n + 256] = sums[b * 2 * C2 : (b + 1) * 2 * C2]


def row_sum(rowed_ref, n):
    total = rowed_ref[1, :, LANES + 256 * n : LANES + 256 * n + 256]
    for b in (0, 2):
        begin = LANES + HALF * (b - 1) + 256 * n
        total = total + rowed_ref[b, :, begin : begin + 256]
    return total


def clear_margins(act_ref):
    margin = jnp.zeros((2 * C1, LANES), jnp.bfloat16)
    act_ref[:, 0:LANES] = margin
    act_ref[:, LANES + PLANE :] = margin


def prepare_kernel(
    k1_hbm, place_hbm, k2_hbm, select_hbm, cot_hbm, slab_hbm,
    w1_near_ref, w1_far_ref, w2_ref, select_ref, cot_ref, slab_ref,
    k1_ref, place_ref, k2_ref, k1_rows_ref, sems,
):
    odd = lax.axis_index("core")
    moves = (
        (k1_hbm, k1_ref), (k2_hbm, k2_ref), (place_hbm.at[odd], place_ref),
        (select_hbm, select_ref), (cot_hbm, cot_ref), (slab_hbm, slab_ref),
    )
    copies = [pltpu.make_async_copy(src, dst, sems.at[k]) for k, (src, dst) in enumerate(moves)]
    for copy in copies:
        copy.start()
    copies[0].wait()
    for tap in range(27):
        k1_rows_ref[CIN * tap : CIN * (tap + 1), :] = k1_ref[tap].astype(jnp.float32)
    copies[1].wait()
    blank = jnp.zeros((C1, C2), jnp.bfloat16)

    def stacked(bc, pair):
        k = [blank] + [k2_ref[9 * a + bc] for a in range(3)] + [blank]
        lower = jnp.concatenate(k[1 + 2 * pair : 3 + 2 * pair], axis=0)
        upper = jnp.concatenate(k[2 * pair : 2 + 2 * pair], axis=0)
        return jnp.concatenate([lower, upper], axis=1)

    for b in range(3):
        rows = slice(b * 2 * C2, (b + 1) * 2 * C2)
        for pair in range(2):
            both = jnp.concatenate([stacked(3 * b, pair), stacked(3 * b + 1, pair)], axis=0)
            w2_ref[pair, rows, 0:LANES] = both.T
        both = jnp.concatenate([stacked(3 * b + 2, 0), stacked(3 * b + 2, 1)], axis=0).T
        for pair in range(2):
            w2_ref[pair, rows, LANES : LANES + 2 * C1] = both[:, pair * 2 * C1 : (pair + 1) * 2 * C1]
    copies[2].wait()
    spread = lax.dot_general(
        k1_rows_ref[...].astype(jnp.bfloat16), place_ref[...],
        (((0,), (0,)), ((), ())), preferred_element_type=jnp.float32,
    ).astype(jnp.bfloat16)
    for q in range(4):
        rows = slice(q % 2 * C1, (q % 2 + 1) * C1)
        w1_near_ref[q // 2, rows, :] = spread[:, CHUNK * q : CHUNK * q + 18 * ROWS]
        w1_far_ref[q // 2, rows, :] = spread[:, CHUNK * q + 18 * ROWS : CHUNK * q + 27 * ROWS]
    copies[3].wait()
    copies[4].wait()
    copies[5].wait()


def near_kernel(
    own_ref, within_ref, select_ref, w1_ref, w2_ref, first_ref, columns_ref, pre_ref,
    rows_ref, parity_ref, taps_ref, act_ref, rowed_ref,
):
    odd = lax.axis_index("core")
    plane_rows(own_ref, rows_ref.at[0:ROWS])
    plane_rows(within_ref, rows_ref.at[ROWS : 2 * ROWS])
    strided_taps(rows_ref[...].astype(jnp.bfloat16), select_ref, parity_ref, taps_ref)
    clear_margins(act_ref)
    for n in range(4):
        here = slice(256 * n, 256 * n + 256)
        first_ref[:, here] = jnp.dot(w1_ref[odd], taps_ref[:, here], preferred_element_type=jnp.float32)
        complete = jnp.dot(w1_ref[1 - odd], taps_ref[:, here], preferred_element_type=jnp.float32)
        act_ref[:, LANES + 256 * n : LANES + 256 * n + 256] = leaky_relu(complete).astype(jnp.bfloat16)
    shifted_columns(act_ref, columns_ref)
    second_layer(w2_ref[1 - odd], columns_ref, rowed_ref)
    for n in range(4):
        pre_ref[:, 256 * n : 256 * n + 256] = row_sum(rowed_ref, n)


def far_kernel(
    chips, scale, hop_ref, turn_ref, select_ref, w1_ref, w2_ref, cot_ref, first_ref, near_ref, pre_ref, out_hbm, grad_ref,
    rows_ref, parity_ref, taps_ref, act_ref, columns_ref, rowed_ref, back_ref, sums_ref, out_ref, out_sem,
):
    odd = lax.axis_index("core")
    chip = lax.axis_index("chip")
    inside = jnp.where((chip == chips - 1) & (odd == 1), 0.0, 1.0)
    turned = lax.rem(chip + odd, 2) == 0
    pl.when(turned)(lambda: plane_rows(turn_ref, rows_ref))
    pl.when(jnp.logical_not(turned))(lambda: plane_rows(hop_ref, rows_ref))
    strided_taps(rows_ref[...].astype(jnp.bfloat16), select_ref, parity_ref, taps_ref)
    clear_margins(act_ref)
    for n in range(4):
        here = slice(256 * n, 256 * n + 256)
        first_pre = first_ref[:, here] + jnp.dot(w1_ref[odd], taps_ref[:, here], preferred_element_type=jnp.float32)
        first_act = leaky_relu(first_pre)
        there = slice(LANES + 256 * n, LANES + 256 * n + 256)
        act_ref[0:C1, there] = first_act[0:C1].astype(jnp.bfloat16)
        act_ref[C1:, there] = (first_act[C1:] * inside).astype(jnp.bfloat16)
    shifted_columns(act_ref, columns_ref)
    second_layer(w2_ref[odd], columns_ref, rowed_ref)
    margin = jnp.zeros((HALF, LANES), jnp.bfloat16)
    back_ref[0:HALF, :] = margin
    back_ref[HALF + PLANE :, :] = margin
    for n in range(4):
        pre = pre_ref[:, 256 * n : 256 * n + 256] + row_sum(rowed_ref, n)
        output = leaky_relu(pre).astype(jnp.bfloat16)
        slope = jnp.where(pre > 0, 1.0, neg_slope)
        backs = []
        for z in range(2):
            cells = slice(z * PLANE + 256 * n, z * PLANE + 256 * n + 256)
            rows = slice(z * C2, (z + 1) * C2)
            out_ref[0, 0, :, cells] = output[rows]
            backs.append((cot_ref[0, 0, :, cells].astype(jnp.float32) * slope[rows]).astype(jnp.bfloat16))
        back_ref[HALF + 256 * n : HALF + 256 * n + 256, :] = jnp.concatenate(backs, axis=0).T
    out_copy = pltpu.make_async_copy(out_ref, out_hbm, out_sem)
    out_copy.start()
    columns = jnp.concatenate([near_ref[...], columns_ref[...]], axis=0)
    rowed_back = jnp.concatenate([back_ref[(2 - b) * HALF : (2 - b) * HALF + PLANE, :] for b in range(3)], axis=1)
    sums = jnp.dot(columns, rowed_back, preferred_element_type=jnp.float32)
    sums_ref[1 - odd] = sums[0 : 6 * C1]
    sums_ref[odd] = sums[6 * C1 :]
    low = lax.broadcasted_iota(jnp.int32, (C1, LANES), 1) < C2

    def plane_sums(bc, q):
        b, c = divmod(bc, 3)
        begin = 2 * C1 * c + C1 * (q % 2)
        return sums_ref[q // 2, begin : begin + C1, b * LANES : (b + 1) * LANES]

    def two_taps(first, second):
        a, bc = divmod(first, 9)
        here, above = plane_sums(bc, a), pltpu.roll(plane_sums(bc, a + 1), C2, 1)
        if second > 26:
            return here + above
        a, bc = divmod(second, 9)
        there, beyond = pltpu.roll(plane_sums(bc, a), C2, 1), plane_sums(bc, a + 1)
        return jnp.where(low, here, there) + jnp.where(low, above, beyond)

    for block in range(4):
        tall = jnp.concatenate([two_taps(min(8 * block + g, 26), 8 * block + 4 + g) for g in range(4)], axis=0)
        flat = (tall * scale).T.astype(jnp.bfloat16)
        grad_ref[:, 2 * block * LANES : (2 * block + 1) * LANES] = flat[0:C2]
        if block < 3:
            grad_ref[:, (2 * block + 1) * LANES : (2 * block + 2) * LANES] = flat[C2:]
    out_copy.wait()


def finish_kernel(parts_ref, grad_ref):
    wide, half, _ = parts_ref.shape
    for core in range(2):
        total = parts_ref[core].astype(jnp.float32)
        for k in range(core + 2, wide, 2):
            total = total + parts_ref[k].astype(jnp.float32)
        for tap in range(27):
            grad_ref[tap, core * half : (core + 1) * half, :] = total[:, tap * C1 : (tap + 1) * C1]


def body(volumes, first_kernel, second_kernel, cotangent):
    wide = lax.axis_size(WIDE)
    narrow = lax.axis_size("narrow")
    cells_out = cotangent.shape[3]
    scale = 1.0 / math.sqrt(wide * narrow * cells_out)
    within, turn, hop = ([p for k in range(first, wide - 1, step) for p in ((k, k + 1), (k + 1, k))] for first, step in ((0, 2), (3, 4), (1, 4)))
    within = lax.ppermute(volumes, WIDE, within)
    turn = lax.ppermute(volumes, WIDE, turn)
    pinned = pl.BlockSpec(memory_space=pltpu.HBM)
    fast = pl.BlockSpec(memory_space=pltpu.VMEM)
    bf16 = functools.partial(jax.ShapeDtypeStruct, dtype=jnp.bfloat16)
    f32 = functools.partial(jax.ShapeDtypeStruct, dtype=jnp.float32)
    stored = (
        first_kernel.transpose(0, 2, 1), jnp.asarray(placement(), jnp.bfloat16), second_kernel.transpose(0, 2, 1),
        jnp.asarray(selection(), jnp.bfloat16), cotangent, volumes,
    )
    w1_near, w1_far, w2, select, cot, slab = pl.pallas_call(
        prepare_kernel,
        in_specs=[pinned] * 6,
        out_specs=(fast,) * 6,
        out_shape=(
            bf16((2, 2 * C1, 18 * ROWS)), bf16((2, 2 * C1, 9 * ROWS)), bf16((2, 6 * C2, 6 * C1)),
            bf16((CHUNK, CHUNK)), bf16(cotangent.shape), bf16(volumes.shape),
        ),
        scratch_shapes=[
            pltpu.VMEM((27, CIN, C1), jnp.bfloat16),
            pltpu.VMEM((27 * CIN, 4 * CHUNK), jnp.bfloat16),
            pltpu.VMEM((27, C1, C2), jnp.bfloat16),
            pltpu.VMEM((27 * CIN, C1), jnp.float32),
            pltpu.SemaphoreType.DMA((6,)),
        ],
        compiler_params=pltpu.CompilerParams(vmem_limit_bytes=12 * MIB),
        cost_estimate=pl.CostEstimate(flops=10**9, bytes_accessed=4 * MIB, transcendentals=0),
        name="prepare",
    )(*(pltpu.with_memory_space_constraint(x, pltpu.HBM) for x in stored))
    hop = lax.ppermute(slab, WIDE, hop)
    first, near, pre = pl.pallas_call(
        near_kernel,
        in_specs=[fast] * 5,
        out_specs=(fast,) * 3,
        out_shape=(f32((2 * C1, PLANE)), bf16((6 * C1, PLANE)), f32((2 * C2, PLANE))),
        scratch_shapes=[
            pltpu.VMEM((2 * ROWS, CELLS), jnp.float32),
            pltpu.VMEM((4, 2 * ROWS, LANES + PLANE), jnp.bfloat16),
            pltpu.VMEM((18 * ROWS, PLANE), jnp.bfloat16),
            pltpu.VMEM((2 * C1, PLANE + 2 * LANES), jnp.bfloat16),
            pltpu.VMEM((3, 2 * C2, PLANE + 2 * LANES), jnp.float32),
        ],
        compiler_params=pltpu.CompilerParams(vmem_limit_bytes=16 * MIB),
        cost_estimate=pl.CostEstimate(flops=10**9, bytes_accessed=4 * MIB, transcendentals=0),
        name="near",
    )(slab, within, select, w1_near, w2)
    rows = C2 // narrow
    output, term = pl.pallas_call(
        functools.partial(far_kernel, wide // 2, scale),
        in_specs=[fast] * 9,
        out_specs=(pl.BlockSpec(memory_space=pl.ANY), fast),
        out_shape=(bf16((1, 1, C2, cells_out)), bf16((C2, PACKED))),
        scratch_shapes=[
            pltpu.VMEM((ROWS, CELLS), jnp.float32),
            pltpu.VMEM((4, ROWS, LANES + PLANE), jnp.bfloat16),
            pltpu.VMEM((9 * ROWS, PLANE), jnp.bfloat16),
            pltpu.VMEM((2 * C1, PLANE + 2 * LANES), jnp.bfloat16),
            pltpu.VMEM((6 * C1, PLANE), jnp.bfloat16),
            pltpu.VMEM((3, 2 * C2, PLANE + 2 * LANES), jnp.float32),
            pltpu.VMEM((PLANE + 2 * HALF, LANES), jnp.bfloat16),
            pltpu.VMEM((2, 6 * C1, 3 * LANES), jnp.float32),
            pltpu.VMEM((1, 1, C2, cells_out), jnp.bfloat16),
            pltpu.SemaphoreType.DMA,
        ],
        compiler_params=pltpu.CompilerParams(vmem_limit_bytes=16 * MIB),
        name="far",
    )(hop, turn, select, w1_far, w2, cot, first, near, pre)
    half = rows // 2
    received = lax.all_to_all(term, ("narrow", "core"), 0, 0, tiled=True)
    owned = jnp.sum(received.reshape(2 * narrow, half, PACKED).astype(jnp.float32), axis=0).astype(jnp.bfloat16)
    parts = lax.all_to_all(jnp.broadcast_to(owned[None], (wide, half, PACKED)), WIDE, 0, 0, tiled=True)
    weight_grad = pl.pallas_call(
        finish_kernel,
        out_shape=jax.ShapeDtypeStruct((27, rows, C1), jnp.float32),
        compiler_params=pltpu.CompilerParams(vmem_limit_bytes=8 * MIB),
        name="finish",
    )(parts)
    return (output, weight_grad)


def solution(mesh):
    wide, narrow = mesh.devices.shape
    split = jax.sharding.Mesh(mesh.devices.reshape(wide // 2, 2, narrow), ("chip", "core", "narrow"))
    return jax.shard_map(
        body,
        mesh=split,
        in_specs=(P("narrow", None, None, WIDE, None), P(), P(), P("narrow", None, None, WIDE)),
        out_specs=(P("narrow", None, None, WIDE), P(None, "narrow", None)),
        check_vma=False,
    )
```

```python
import functools
import math

import jax
import jax.numpy as jnp
import numpy as np
from jax import lax
from jax.experimental import pallas as pl
from jax.experimental.pallas import tpu as pltpu
from jax.sharding import PartitionSpec as P

CIN = 4
C1 = 32
C2 = 64
PLANES = 4
CELLS = 4096
HALF = 32
PLANE = 1024
LANES = 128
ROWS = CIN * PLANES
CHUNK = 512
PACKED = 7 * LANES
MIB = 2**20
WIDE = ("chip", "core")
neg_slope = 0.3


def selection():
    table = np.zeros((CHUNK, 2, 2, 4, HALF), np.float32)
    for py in range(2):
        for px in range(2):
            for row in range(4):
                for col in range(HALF):
                    table[(2 * row + py) * 64 + 2 * col + px, py, px, row, col] = 1
    return table.reshape(CHUNK, CHUNK)


def placement():
    table = np.zeros((2, 27, CIN, 4, CHUNK), np.float32)
    for odd in range(2):
        for a in range(3):
            for bc in range(9):
                for i in range(CIN):
                    for q in range(4):
                        slab, plane = divmod(2 * q + a + 1, PLANES)
                        inner = i * PLANES + plane
                        if slab == 1:
                            column = bc * 2 * ROWS + inner
                        elif (slab == 0) == (odd == 1):
                            column = bc * 2 * ROWS + ROWS + inner
                        else:
                            column = 18 * ROWS + bc * ROWS + inner
                        table[odd, 9 * a + bc, i, q, column] = 1
    return table.reshape(2, 27 * CIN, 4 * CHUNK)


def leaky_relu(value):
    return jnp.where(value > 0, value, neg_slope * value)


def plane_rows(volume_ref, rows_ref):
    for i in range(CIN):
        rows_ref[PLANES * i : PLANES * (i + 1), :] = volume_ref[0, 0, i].astype(jnp.float32)


def column_masks():
    column = lax.broadcasted_iota(jnp.int32, (1, PLANE), 1) % HALF
    left_ok = jnp.where(column > 0, 1.0, 0.0).astype(jnp.bfloat16)
    right_ok = jnp.where(column < HALF - 1, 1.0, 0.0).astype(jnp.bfloat16)
    return left_ok, right_ok


def strided_taps(rows, select_ref, parity_ref, taps_ref):
    count = rows.shape[0]
    left_ok, _ = column_masks()
    chunks = jnp.concatenate([rows[:, CHUNK * j : CHUNK * (j + 1)] for j in range(8)], axis=0)
    for p in range(4):
        parity_ref[p, :, 0:LANES] = jnp.zeros((count, LANES), jnp.bfloat16)
    for py in range(2):
        parts = jnp.dot(
            chunks, select_ref[:, 256 * py : 256 * py + 256], preferred_element_type=jnp.float32
        ).astype(jnp.bfloat16)
        for px in range(2):
            for j in range(8):
                parity_ref[2 * py + px, :, LANES * (j + 1) : LANES * (j + 2)] = parts[
                    j * count : (j + 1) * count, px * LANES : (px + 1) * LANES
                ]
    for b in range(3):
        for c in range(3):
            begin = LANES - HALF * (b == 0) - (c == 0)
            part = parity_ref[2 * (b != 1) + (c != 1), :, begin : begin + PLANE]
            if c == 0:
                part = part * left_ok
            taps_ref[(3 * b + c) * count : (3 * b + c + 1) * count, :] = part


def shifted_columns(act_ref, columns_ref):
    left_ok, right_ok = column_masks()
    for c in range(3):
        begin = LANES + c - 1
        part = act_ref[:, begin : begin + PLANE]
        if c == 0:
            part = part * left_ok
        if c == 2:
            part = part * right_ok
        columns_ref[c * 2 * C1 : (c + 1) * 2 * C1, :] = part


def second_layer(w2, columns_ref, rowed_ref):
    blank = jnp.zeros((2 * C2, LANES), jnp.float32)
    for b in (0, 2):
        rowed_ref[b, :, 0:LANES] = blank
        rowed_ref[b, :, LANES + PLANE :] = blank
    for n in range(4):
        sums = jnp.dot(w2, columns_ref[:, 256 * n : 256 * n + 256], preferred_element_type=jnp.float32)
        for b in range(3):
            rowed_ref[b, :, LANES + 256 * n : LANES + 256 * n + 256] = sums[b * 2 * C2 : (b + 1) * 2 * C2]


def row_sum(rowed_ref, n):
    total = rowed_ref[1, :, LANES + 256 * n : LANES + 256 * n + 256]
    for b in (0, 2):
        begin = LANES + HALF * (b - 1) + 256 * n
        total = total + rowed_ref[b, :, begin : begin + 256]
    return total


def clear_margins(act_ref):
    margin = jnp.zeros((2 * C1, LANES), jnp.bfloat16)
    act_ref[:, 0:LANES] = margin
    act_ref[:, LANES + PLANE :] = margin


def prepare_kernel(
    k1_hbm, place_hbm, k2_hbm, select_hbm, cot_hbm,
    w1_near_ref, w1_far_ref, w2_ref, select_ref, cot_ref,
    k1_ref, place_ref, k2_ref, k1_rows_ref, sems,
):
    odd = lax.axis_index("core")
    moves = (
        (k1_hbm, k1_ref), (k2_hbm, k2_ref), (place_hbm.at[odd], place_ref),
        (select_hbm, select_ref), (cot_hbm, cot_ref),
    )
    copies = [pltpu.make_async_copy(src, dst, sems.at[k]) for k, (src, dst) in enumerate(moves)]
    for copy in copies:
        copy.start()
    copies[0].wait()
    for tap in range(27):
        k1_rows_ref[CIN * tap : CIN * (tap + 1), :] = k1_ref[tap].astype(jnp.float32)
    copies[1].wait()
    blank = jnp.zeros((C1, C2), jnp.bfloat16)

    def stacked(bc, pair):
        k = [blank] + [k2_ref[9 * a + bc] for a in range(3)] + [blank]
        lower = jnp.concatenate(k[1 + 2 * pair : 3 + 2 * pair], axis=0)
        upper = jnp.concatenate(k[2 * pair : 2 + 2 * pair], axis=0)
        return jnp.concatenate([lower, upper], axis=1)

    for b in range(3):
        rows = slice(b * 2 * C2, (b + 1) * 2 * C2)
        for pair in range(2):
            both = jnp.concatenate([stacked(3 * b, pair), stacked(3 * b + 1, pair)], axis=0)
            w2_ref[pair, rows, 0:LANES] = both.T
        both = jnp.concatenate([stacked(3 * b + 2, 0), stacked(3 * b + 2, 1)], axis=0).T
        for pair in range(2):
            w2_ref[pair, rows, LANES : LANES + 2 * C1] = both[:, pair * 2 * C1 : (pair + 1) * 2 * C1]
    copies[2].wait()
    spread = lax.dot_general(
        k1_rows_ref[...].astype(jnp.bfloat16), place_ref[...],
        (((0,), (0,)), ((), ())), preferred_element_type=jnp.float32,
    ).astype(jnp.bfloat16)
    for q in range(4):
        rows = slice(q % 2 * C1, (q % 2 + 1) * C1)
        w1_near_ref[q // 2, rows, :] = spread[:, CHUNK * q : CHUNK * q + 18 * ROWS]
        w1_far_ref[q // 2, rows, :] = spread[:, CHUNK * q + 18 * ROWS : CHUNK * q + 27 * ROWS]
    copies[3].wait()
    copies[4].wait()


def near_kernel(
    own_ref, within_ref, select_ref, w1_ref, w2_ref, first_ref, columns_ref, pre_ref,
    rows_ref, parity_ref, taps_ref, act_ref, rowed_ref,
):
    odd = lax.axis_index("core")
    plane_rows(own_ref, rows_ref.at[0:ROWS])
    plane_rows(within_ref, rows_ref.at[ROWS : 2 * ROWS])
    strided_taps(rows_ref[...].astype(jnp.bfloat16), select_ref, parity_ref, taps_ref)
    clear_margins(act_ref)
    for n in range(4):
        here = slice(256 * n, 256 * n + 256)
        first_ref[:, here] = jnp.dot(w1_ref[odd], taps_ref[:, here], preferred_element_type=jnp.float32)
        complete = jnp.dot(w1_ref[1 - odd], taps_ref[:, here], preferred_element_type=jnp.float32)
        act_ref[:, LANES + 256 * n : LANES + 256 * n + 256] = leaky_relu(complete).astype(jnp.bfloat16)
    shifted_columns(act_ref, columns_ref)
    second_layer(w2_ref[1 - odd], columns_ref, rowed_ref)
    for n in range(4):
        pre_ref[:, 256 * n : 256 * n + 256] = row_sum(rowed_ref, n)


def far_kernel(
    chips, scale, hop_ref, turn_ref, select_ref, w1_ref, w2_ref, cot_ref, first_ref, near_ref, pre_ref, out_hbm, grad_ref,
    rows_ref, parity_ref, taps_ref, act_ref, columns_ref, rowed_ref, back_ref, sums_ref, out_ref, out_sem,
):
    odd = lax.axis_index("core")
    chip = lax.axis_index("chip")
    inside = jnp.where((chip == chips - 1) & (odd == 1), 0.0, 1.0)
    turned = lax.rem(chip + odd, 2) == 0
    pl.when(turned)(lambda: plane_rows(turn_ref, rows_ref))
    pl.when(jnp.logical_not(turned))(lambda: plane_rows(hop_ref, rows_ref))
    strided_taps(rows_ref[...].astype(jnp.bfloat16), select_ref, parity_ref, taps_ref)
    clear_margins(act_ref)
    for n in range(4):
        here = slice(256 * n, 256 * n + 256)
        first_pre = first_ref[:, here] + jnp.dot(w1_ref[odd], taps_ref[:, here], preferred_element_type=jnp.float32)
        first_act = leaky_relu(first_pre)
        there = slice(LANES + 256 * n, LANES + 256 * n + 256)
        act_ref[0:C1, there] = first_act[0:C1].astype(jnp.bfloat16)
        act_ref[C1:, there] = (first_act[C1:] * inside).astype(jnp.bfloat16)
    shifted_columns(act_ref, columns_ref)
    second_layer(w2_ref[odd], columns_ref, rowed_ref)
    margin = jnp.zeros((HALF, LANES), jnp.bfloat16)
    back_ref[0:HALF, :] = margin
    back_ref[HALF + PLANE :, :] = margin
    for n in range(4):
        pre = pre_ref[:, 256 * n : 256 * n + 256] + row_sum(rowed_ref, n)
        output = leaky_relu(pre).astype(jnp.bfloat16)
        slope = jnp.where(pre > 0, 1.0, neg_slope)
        backs = []
        for z in range(2):
            cells = slice(z * PLANE + 256 * n, z * PLANE + 256 * n + 256)
            rows = slice(z * C2, (z + 1) * C2)
            out_ref[0, 0, :, cells] = output[rows]
            backs.append((cot_ref[0, 0, :, cells].astype(jnp.float32) * slope[rows]).astype(jnp.bfloat16))
        back_ref[HALF + 256 * n : HALF + 256 * n + 256, :] = jnp.concatenate(backs, axis=0).T
    out_copy = pltpu.make_async_copy(out_ref, out_hbm, out_sem)
    out_copy.start()
    columns = jnp.concatenate([near_ref[...], columns_ref[...]], axis=0)
    rowed_back = jnp.concatenate([back_ref[(2 - b) * HALF : (2 - b) * HALF + PLANE, :] for b in range(3)], axis=1)
    sums = jnp.dot(columns, rowed_back, preferred_element_type=jnp.float32)
    sums_ref[1 - odd] = sums[0 : 6 * C1]
    sums_ref[odd] = sums[6 * C1 :]
    low = lax.broadcasted_iota(jnp.int32, (C1, LANES), 1) < C2

    def plane_sums(bc, q):
        b, c = divmod(bc, 3)
        begin = 2 * C1 * c + C1 * (q % 2)
        return sums_ref[q // 2, begin : begin + C1, b * LANES : (b + 1) * LANES]

    def two_taps(first, second):
        a, bc = divmod(first, 9)
        here, above = plane_sums(bc, a), pltpu.roll(plane_sums(bc, a + 1), C2, 1)
        if second > 26:
            return here + above
        a, bc = divmod(second, 9)
        there, beyond = pltpu.roll(plane_sums(bc, a), C2, 1), plane_sums(bc, a + 1)
        return jnp.where(low, here, there) + jnp.where(low, above, beyond)

    for block in range(4):
        tall = jnp.concatenate([two_taps(min(8 * block + g, 26), 8 * block + 4 + g) for g in range(4)], axis=0)
        flat = (tall * scale).T.astype(jnp.bfloat16)
        grad_ref[:, 2 * block * LANES : (2 * block + 1) * LANES] = flat[0:C2]
        if block < 3:
            grad_ref[:, (2 * block + 1) * LANES : (2 * block + 2) * LANES] = flat[C2:]
    out_copy.wait()


def finish_kernel(parts_ref, grad_ref):
    wide, half, _ = parts_ref.shape
    for core in range(2):
        total = parts_ref[core].astype(jnp.float32)
        for k in range(core + 2, wide, 2):
            total = total + parts_ref[k].astype(jnp.float32)
        for tap in range(27):
            grad_ref[tap, core * half : (core + 1) * half, :] = total[:, tap * C1 : (tap + 1) * C1]


def body(volumes, first_kernel, second_kernel, cotangent):
    wide = lax.axis_size(WIDE)
    narrow = lax.axis_size("narrow")
    cells_out = cotangent.shape[3]
    scale = 1.0 / math.sqrt(wide * narrow * cells_out)
    swaps = [[p for k in range(first, wide - 1, step) for p in ((k, k + 1), (k + 1, k))] for first, step in ((0, 2), (3, 4), (1, 4))]
    within, turn, hop = swaps
    within = lax.ppermute(volumes, WIDE, within)
    turn = lax.ppermute(volumes, WIDE, turn)
    hop = lax.ppermute(volumes, WIDE, hop)
    pinned = pl.BlockSpec(memory_space=pltpu.HBM)
    fast = pl.BlockSpec(memory_space=pltpu.VMEM)
    bf16 = functools.partial(jax.ShapeDtypeStruct, dtype=jnp.bfloat16)
    f32 = functools.partial(jax.ShapeDtypeStruct, dtype=jnp.float32)
    stored = (
        first_kernel.transpose(0, 2, 1), jnp.asarray(placement(), jnp.bfloat16), second_kernel.transpose(0, 2, 1),
        jnp.asarray(selection(), jnp.bfloat16), cotangent,
    )
    w1_near, w1_far, w2, select, cot = pl.pallas_call(
        prepare_kernel,
        in_specs=[pinned] * 5,
        out_specs=(fast,) * 5,
        out_shape=(
            bf16((2, 2 * C1, 18 * ROWS)), bf16((2, 2 * C1, 9 * ROWS)), bf16((2, 6 * C2, 6 * C1)),
            bf16((CHUNK, CHUNK)), bf16(cotangent.shape),
        ),
        scratch_shapes=[
            pltpu.VMEM((27, CIN, C1), jnp.bfloat16),
            pltpu.VMEM((27 * CIN, 4 * CHUNK), jnp.bfloat16),
            pltpu.VMEM((27, C1, C2), jnp.bfloat16),
            pltpu.VMEM((27 * CIN, C1), jnp.float32),
            pltpu.SemaphoreType.DMA((5,)),
        ],
        compiler_params=pltpu.CompilerParams(vmem_limit_bytes=12 * MIB),
        cost_estimate=pl.CostEstimate(flops=10**9, bytes_accessed=4 * MIB, transcendentals=0),
        name="prepare",
    )(*(pltpu.with_memory_space_constraint(x, pltpu.HBM) for x in stored))
    first, near, pre = pl.pallas_call(
        near_kernel,
        in_specs=[fast] * 5,
        out_specs=(fast,) * 3,
        out_shape=(f32((2 * C1, PLANE)), bf16((6 * C1, PLANE)), f32((2 * C2, PLANE))),
        scratch_shapes=[
            pltpu.VMEM((2 * ROWS, CELLS), jnp.float32),
            pltpu.VMEM((4, 2 * ROWS, LANES + PLANE), jnp.bfloat16),
            pltpu.VMEM((18 * ROWS, PLANE), jnp.bfloat16),
            pltpu.VMEM((2 * C1, PLANE + 2 * LANES), jnp.bfloat16),
            pltpu.VMEM((3, 2 * C2, PLANE + 2 * LANES), jnp.float32),
        ],
        compiler_params=pltpu.CompilerParams(vmem_limit_bytes=16 * MIB),
        cost_estimate=pl.CostEstimate(flops=10**9, bytes_accessed=4 * MIB, transcendentals=0),
        name="near",
    )(volumes, within, select, w1_near, w2)
    rows = C2 // narrow
    output, term = pl.pallas_call(
        functools.partial(far_kernel, wide // 2, scale),
        in_specs=[fast] * 9,
        out_specs=(pl.BlockSpec(memory_space=pl.ANY), fast),
        out_shape=(bf16((1, 1, C2, cells_out)), bf16((C2, PACKED))),
        scratch_shapes=[
            pltpu.VMEM((ROWS, CELLS), jnp.float32),
            pltpu.VMEM((4, ROWS, LANES + PLANE), jnp.bfloat16),
            pltpu.VMEM((9 * ROWS, PLANE), jnp.bfloat16),
            pltpu.VMEM((2 * C1, PLANE + 2 * LANES), jnp.bfloat16),
            pltpu.VMEM((6 * C1, PLANE), jnp.bfloat16),
            pltpu.VMEM((3, 2 * C2, PLANE + 2 * LANES), jnp.float32),
            pltpu.VMEM((PLANE + 2 * HALF, LANES), jnp.bfloat16),
            pltpu.VMEM((2, 6 * C1, 3 * LANES), jnp.float32),
            pltpu.VMEM((1, 1, C2, cells_out), jnp.bfloat16),
            pltpu.SemaphoreType.DMA,
        ],
        compiler_params=pltpu.CompilerParams(vmem_limit_bytes=16 * MIB),
        name="far",
    )(hop, turn, select, w1_far, w2, cot, first, near, pre)
    half = rows // 2
    received = lax.all_to_all(term, ("narrow", "core"), 0, 0, tiled=True)
    owned = jnp.sum(received.reshape(2 * narrow, half, PACKED).astype(jnp.float32), axis=0).astype(jnp.bfloat16)
    parts = lax.all_to_all(jnp.broadcast_to(owned[None], (wide, half, PACKED)), WIDE, 0, 0, tiled=True)
    weight_grad = pl.pallas_call(
        finish_kernel,
        out_shape=jax.ShapeDtypeStruct((27, rows, C1), jnp.float32),
        compiler_params=pltpu.CompilerParams(vmem_limit_bytes=8 * MIB),
        name="finish",
    )(parts)
    return (output, weight_grad)


def solution(mesh):
    wide, narrow = mesh.devices.shape
    split = jax.sharding.Mesh(mesh.devices.reshape(wide // 2, 2, narrow), ("chip", "core", "narrow"))
    return jax.shard_map(
        body,
        mesh=split,
        in_specs=(P("narrow", None, None, WIDE, None), P(), P(), P("narrow", None, None, WIDE)),
        out_specs=(P("narrow", None, None, WIDE), P(None, "narrow", None)),
        check_vma=False,
    )
```

```python
import functools
import math

import jax
import jax.numpy as jnp
import numpy as np
from jax import lax
from jax.experimental import pallas as pl
from jax.experimental.pallas import tpu as pltpu
from jax.sharding import PartitionSpec as P

CIN = 4
C1 = 32
C2 = 64
PLANES = 4
CELLS = 4096
HALF = 32
PLANE = 1024
LANES = 128
ROWS = CIN * PLANES
CHUNK = 512
PACKED = 7 * LANES
MIB = 2**20
WIDE = ("chip", "core")
neg_slope = 0.3


def selection():
    table = np.zeros((CHUNK, 2, 2, 4, HALF), np.float32)
    for py in range(2):
        for px in range(2):
            for row in range(4):
                for col in range(HALF):
                    table[(2 * row + py) * 64 + 2 * col + px, py, px, row, col] = 1
    return table.reshape(CHUNK, CHUNK)


def placement():
    table = np.zeros((2, 27, CIN, 4, CHUNK), np.float32)
    for odd in range(2):
        for a in range(3):
            for bc in range(9):
                for i in range(CIN):
                    for q in range(4):
                        slab, plane = divmod(2 * q + a + 1, PLANES)
                        inner = i * PLANES + plane
                        if slab == 1:
                            column = bc * 2 * ROWS + inner
                        elif (slab == 0) == (odd == 1):
                            column = bc * 2 * ROWS + ROWS + inner
                        else:
                            column = 18 * ROWS + bc * ROWS + inner
                        table[odd, 9 * a + bc, i, q, column] = 1
    return table.reshape(2, 27 * CIN, 4 * CHUNK)


def leaky_relu(value):
    return jnp.where(value > 0, value, neg_slope * value)


def plane_rows(volume_ref, rows_ref):
    for i in range(CIN):
        rows_ref[PLANES * i : PLANES * (i + 1), :] = volume_ref[0, 0, i].astype(jnp.float32)


def column_masks():
    column = lax.broadcasted_iota(jnp.int32, (1, PLANE), 1) % HALF
    left_ok = jnp.where(column > 0, 1.0, 0.0).astype(jnp.bfloat16)
    right_ok = jnp.where(column < HALF - 1, 1.0, 0.0).astype(jnp.bfloat16)
    return left_ok, right_ok


def strided_taps(rows, select_ref, parity_ref, taps_ref):
    count = rows.shape[0]
    left_ok, _ = column_masks()
    chunks = jnp.concatenate([rows[:, CHUNK * j : CHUNK * (j + 1)] for j in range(8)], axis=0)
    for p in range(4):
        parity_ref[p, :, 0:LANES] = jnp.zeros((count, LANES), jnp.bfloat16)
    for py in range(2):
        parts = jnp.dot(
            chunks, select_ref[:, 256 * py : 256 * py + 256], preferred_element_type=jnp.float32
        ).astype(jnp.bfloat16)
        for px in range(2):
            for j in range(8):
                parity_ref[2 * py + px, :, LANES * (j + 1) : LANES * (j + 2)] = parts[
                    j * count : (j + 1) * count, px * LANES : (px + 1) * LANES
                ]
    for b in range(3):
        for c in range(3):
            begin = LANES - HALF * (b == 0) - (c == 0)
            part = parity_ref[2 * (b != 1) + (c != 1), :, begin : begin + PLANE]
            if c == 0:
                part = part * left_ok
            taps_ref[(3 * b + c) * count : (3 * b + c + 1) * count, :] = part


def shifted_columns(act_ref, columns_ref):
    left_ok, right_ok = column_masks()
    for c in range(3):
        begin = LANES + c - 1
        part = act_ref[:, begin : begin + PLANE]
        if c == 0:
            part = part * left_ok
        if c == 2:
            part = part * right_ok
        columns_ref[c * 2 * C1 : (c + 1) * 2 * C1, :] = part


def second_layer(w2, columns_ref, rowed_ref):
    blank = jnp.zeros((2 * C2, LANES), jnp.float32)
    for b in (0, 2):
        rowed_ref[b, :, 0:LANES] = blank
        rowed_ref[b, :, LANES + PLANE :] = blank
    for n in range(4):
        sums = jnp.dot(w2, columns_ref[:, 256 * n : 256 * n + 256], preferred_element_type=jnp.float32)
        for b in range(3):
            rowed_ref[b, :, LANES + 256 * n : LANES + 256 * n + 256] = sums[b * 2 * C2 : (b + 1) * 2 * C2]


def row_sum(rowed_ref, n):
    total = rowed_ref[1, :, LANES + 256 * n : LANES + 256 * n + 256]
    for b in (0, 2):
        begin = LANES + HALF * (b - 1) + 256 * n
        total = total + rowed_ref[b, :, begin : begin + 256]
    return total


def clear_margins(act_ref):
    margin = jnp.zeros((2 * C1, LANES), jnp.bfloat16)
    act_ref[:, 0:LANES] = margin
    act_ref[:, LANES + PLANE :] = margin


def prepare_kernel(
    k1_hbm, place_hbm, k2_hbm, select_hbm, cot_hbm, w1_near_ref, w1_far_ref, w2_ref, select_ref, cot_ref,
    k1_ref, place_ref, k2_ref, k1_rows_ref, sems,
):
    odd = lax.axis_index("core")
    moves = ((k1_hbm, k1_ref), (k2_hbm, k2_ref), (place_hbm.at[odd], place_ref), (select_hbm, select_ref), (cot_hbm, cot_ref))
    copies = [pltpu.make_async_copy(src, dst, sems.at[k]) for k, (src, dst) in enumerate(moves)]
    for copy in copies:
        copy.start()
    copies[0].wait()
    for tap in range(27):
        k1_rows_ref[CIN * tap : CIN * (tap + 1), :] = k1_ref[tap].astype(jnp.float32)
    copies[1].wait()
    blank = jnp.zeros((C1, C2), jnp.bfloat16)

    def stacked(bc, pair):
        k = [blank] + [k2_ref[9 * a + bc] for a in range(3)] + [blank]
        lower = jnp.concatenate(k[1 + 2 * pair : 3 + 2 * pair], axis=0)
        upper = jnp.concatenate(k[2 * pair : 2 + 2 * pair], axis=0)
        return jnp.concatenate([lower, upper], axis=1)

    for b in range(3):
        rows = slice(b * 2 * C2, (b + 1) * 2 * C2)
        for pair in range(2):
            both = jnp.concatenate([stacked(3 * b, pair), stacked(3 * b + 1, pair)], axis=0)
            w2_ref[pair, rows, 0:LANES] = both.T
        both = jnp.concatenate([stacked(3 * b + 2, 0), stacked(3 * b + 2, 1)], axis=0).T
        for pair in range(2):
            w2_ref[pair, rows, LANES : LANES + 2 * C1] = both[:, pair * 2 * C1 : (pair + 1) * 2 * C1]
    copies[2].wait()
    spread = lax.dot_general(
        k1_rows_ref[...].astype(jnp.bfloat16), place_ref[...],
        (((0,), (0,)), ((), ())), preferred_element_type=jnp.float32,
    ).astype(jnp.bfloat16)
    for q in range(4):
        rows = slice(q % 2 * C1, (q % 2 + 1) * C1)
        w1_near_ref[q // 2, rows, :] = spread[:, CHUNK * q : CHUNK * q + 18 * ROWS]
        w1_far_ref[q // 2, rows, :] = spread[:, CHUNK * q + 18 * ROWS : CHUNK * q + 27 * ROWS]
    copies[3].wait()
    copies[4].wait()


def near_kernel(
    own_ref, within_ref, select_ref, w1_ref, w2_ref, first_ref, columns_ref, pre_ref,
    rows_ref, parity_ref, taps_ref, act_ref, rowed_ref,
):
    odd = lax.axis_index("core")
    plane_rows(own_ref, rows_ref.at[0:ROWS])
    plane_rows(within_ref, rows_ref.at[ROWS : 2 * ROWS])
    strided_taps(rows_ref[...].astype(jnp.bfloat16), select_ref, parity_ref, taps_ref)
    clear_margins(act_ref)
    for n in range(4):
        here = slice(256 * n, 256 * n + 256)
        first_ref[:, here] = jnp.dot(w1_ref[odd], taps_ref[:, here], preferred_element_type=jnp.float32)
        complete = jnp.dot(w1_ref[1 - odd], taps_ref[:, here], preferred_element_type=jnp.float32)
        act_ref[:, LANES + 256 * n : LANES + 256 * n + 256] = leaky_relu(complete).astype(jnp.bfloat16)
    shifted_columns(act_ref, columns_ref)
    second_layer(w2_ref[1 - odd], columns_ref, rowed_ref)
    for n in range(4):
        pre_ref[:, 256 * n : 256 * n + 256] = row_sum(rowed_ref, n)


def slots():
    where = {}
    for a in range(3):
        for b in range(3):
            for c in range(3):
                slot, side = divmod(3 * a + c, 2)
                where[9 * a + 3 * b + c] = (2 * b + side, slot) if slot < 4 else (6, (0, 2, 1)[b])
    return where


def group_of_lane():
    return lax.broadcasted_iota(jnp.int32, (C1, LANES), 1) // C1


def paired_terms(sums_ref, tile):
    even = group_of_lane() % 2 == 0

    def plane(q, c):
        begin = 2 * C1 * c + C1 * (q % 2)
        return sums_ref[q // 2, begin : begin + C1, tile * LANES : (tile + 1) * LANES]

    terms = [plane(a, c) + pltpu.roll(plane(a + 1, c), 3 * C1, 1) for a in range(3) for c in range(3)]
    return [jnp.where(even, terms[k], pltpu.roll(terms[k + 1], C1, 1)) for k in range(0, 8, 2)] + [terms[8]]


def turned_groups(blocks, scale):
    flat = (jnp.concatenate(blocks, axis=0) * scale).T
    return [flat[g * C1 : (g + 1) * C1] for g in range(4)]


def gradient_sums(odd, near_ref, far_ref, backs, sums_ref):
    columns = jnp.concatenate([near_ref[...], far_ref[...]], axis=0)
    sums = jnp.dot(columns, backs, preferred_element_type=jnp.float32)
    sums_ref[1 - odd] = sums[0 : 6 * C1]
    sums_ref[odd] = sums[6 * C1 :]


def far_kernel(
    chips, narrow, scale, across_ref, select_ref, w1_ref, w2_ref, cot_ref, first_ref, near_ref, pre_ref,
    out_ref, give_ref, keep_ref, columns_ref, kept_ref,
    rows_ref, parity_ref, taps_ref, act_ref, rowed_ref, given_ref, mixed_ref, sums_ref,
):
    odd = lax.axis_index("core")
    last = (lax.axis_index("chip") == chips - 1) & (odd == 1)
    inside = jnp.where(last, 0.0, 1.0)
    plane_rows(across_ref, rows_ref)
    strided_taps(rows_ref[...].astype(jnp.bfloat16), select_ref, parity_ref, taps_ref)
    clear_margins(act_ref)
    for n in range(4):
        here = slice(256 * n, 256 * n + 256)
        first_pre = first_ref[:, here] + jnp.dot(w1_ref[odd], taps_ref[:, here], preferred_element_type=jnp.float32)
        first_act = leaky_relu(first_pre)
        there = slice(LANES + 256 * n, LANES + 256 * n + 256)
        act_ref[0:C1, there] = first_act[0:C1].astype(jnp.bfloat16)
        act_ref[C1:, there] = (first_act[C1:] * inside).astype(jnp.bfloat16)
    shifted_columns(act_ref, columns_ref)
    second_layer(w2_ref[odd], columns_ref, rowed_ref)

    margin = jnp.zeros((HALF, LANES), jnp.bfloat16)
    for ref in (given_ref, mixed_ref, kept_ref):
        ref[HALF : 2 * HALF, :] = margin
        ref[PLANE : PLANE + HALF, :] = margin
    half = C2 // (2 * narrow)

    def halves(x):
        lower = [x[2 * n * half : (2 * n + 1) * half] for n in range(narrow)]
        upper = [x[(2 * n + 1) * half : (2 * n + 2) * half] for n in range(narrow)]
        give = jnp.concatenate([jnp.where(odd == 1, l, u) for l, u in zip(lower, upper)], axis=0)
        keep = jnp.concatenate([jnp.where(odd == 1, u, l) for l, u in zip(lower, upper)], axis=0)
        return give, keep

    for n in range(4):
        pre = pre_ref[:, 256 * n : 256 * n + 256] + row_sum(rowed_ref, n)
        output = leaky_relu(pre).astype(jnp.bfloat16)
        slope = jnp.where(pre > 0, 1.0, neg_slope)
        parts = []
        for z in range(2):
            cells = slice(z * PLANE + 256 * n, z * PLANE + 256 * n + 256)
            rows = slice(z * C2, (z + 1) * C2)
            out_ref[0, 0, :, cells] = output[rows]
            parts.append(halves(cot_ref[0, 0, :, cells].astype(jnp.float32) * slope[rows]))
        order = jnp.concatenate([parts[0][0], parts[1][0], parts[0][1], parts[1][1]], axis=0)
        back = order.astype(jnp.bfloat16).T
        other = jnp.concatenate([back[:, C2:], back[:, 0:C2]], axis=1)
        rows = [slice(256 * n + HALF * b, 256 * n + HALF * b + 256) for b in range(3)]
        given_ref[rows[0], 0:C2] = back[:, 0:C2]
        given_ref[rows[1], C2:] = other[:, C2:]
        mixed_ref[rows[2], :] = back
        kept_ref[rows[0], 0:C2] = other[:, 0:C2]
        kept_ref[rows[1], C2:] = back[:, C2:]
    middle = slice(HALF, HALF + PLANE)
    gradient_sums(odd, near_ref, columns_ref, jnp.concatenate([given_ref[middle, :], mixed_ref[middle, :]], axis=1), sums_ref)
    given, mixed = paired_terms(sums_ref, 0), paired_terms(sums_ref, 1)
    first = turned_groups(given[0:4], scale)
    second = turned_groups(mixed[0:4], scale)
    third = turned_groups([given[4], mixed[4], given[4], mixed[4]], scale)
    group = group_of_lane()
    tiles = first + second[0:2] + [jnp.where(group < 2, third[0], pltpu.roll(third[2], C2, 1))]
    for k, tile in enumerate(tiles):
        give_ref[:, k * LANES : (k + 1) * LANES] = tile.astype(jnp.bfloat16)
    for k, tile in enumerate((second[2], second[3], third[2])):
        keep_ref[:, k * LANES : (k + 1) * LANES] = tile


def rest_kernel(scale, out_ref, near_ref, far_ref, kept_ref, mixed_ref, out_hbm, keep_ref, sums_ref, out_sem):
    out_copy = pltpu.make_async_copy(out_ref, out_hbm, out_sem)
    out_copy.start()
    odd = lax.axis_index("core")
    gradient_sums(odd, near_ref, far_ref, kept_ref[HALF : HALF + PLANE, :], sums_ref)
    kept = paired_terms(sums_ref, 0)
    first = turned_groups(kept[0:4], scale)
    third = turned_groups([kept[4]] * 4, scale)
    group = group_of_lane()
    mixed = [mixed_ref[:, k * LANES : (k + 1) * LANES] for k in range(3)]
    ends = jnp.where(group == 1, mixed[2], jnp.where(group == 0, third[0], pltpu.roll(third[2], C2, 1)))
    for k, tile in enumerate(first + mixed[0:2] + [ends]):
        keep_ref[:, k * LANES : (k + 1) * LANES] = tile
    out_copy.wait()


def finish_kernel(parts_ref, grad_ref):
    wide, half, _ = parts_ref.shape
    for core in range(2):
        total = parts_ref[core].astype(jnp.float32)
        for k in range(core + 2, wide, 2):
            total = total + parts_ref[k].astype(jnp.float32)
        for tap, (tile, slot) in slots().items():
            begin = tile * LANES + slot * C1
            grad_ref[tap, core * half : (core + 1) * half, :] = total[:, begin : begin + C1]


def body(volumes, first_kernel, second_kernel, cotangent):
    wide = lax.axis_size(WIDE)
    narrow = lax.axis_size("narrow")
    cells_out = cotangent.shape[3]
    scale = 1.0 / math.sqrt(wide * narrow * cells_out)
    across = lax.ppermute(volumes, WIDE, [p for k in range(1, wide - 1, 2) for p in ((k, k + 1), (k + 1, k))])
    pairs = [p for k in range(0, wide - 1, 2) for p in ((k, k + 1), (k + 1, k))]
    within = lax.ppermute(volumes, WIDE, pairs)
    pinned = pl.BlockSpec(memory_space=pltpu.HBM)
    fast = pl.BlockSpec(memory_space=pltpu.VMEM)
    bf16 = functools.partial(jax.ShapeDtypeStruct, dtype=jnp.bfloat16)
    f32 = functools.partial(jax.ShapeDtypeStruct, dtype=jnp.float32)
    stored = (
        first_kernel.transpose(0, 2, 1), jnp.asarray(placement(), jnp.bfloat16), second_kernel.transpose(0, 2, 1),
        jnp.asarray(selection(), jnp.bfloat16), cotangent,
    )
    w1_near, w1_far, w2, select, cot = pl.pallas_call(
        prepare_kernel,
        in_specs=[pinned] * 5,
        out_specs=(fast,) * 5,
        out_shape=(
            bf16((2, 2 * C1, 18 * ROWS)), bf16((2, 2 * C1, 9 * ROWS)), bf16((2, 6 * C2, 6 * C1)),
            bf16((CHUNK, CHUNK)), bf16(cotangent.shape),
        ),
        scratch_shapes=[
            pltpu.VMEM((27, CIN, C1), jnp.bfloat16),
            pltpu.VMEM((27 * CIN, 4 * CHUNK), jnp.bfloat16),
            pltpu.VMEM((27, C1, C2), jnp.bfloat16),
            pltpu.VMEM((27 * CIN, C1), jnp.float32),
            pltpu.SemaphoreType.DMA((5,)),
        ],
        compiler_params=pltpu.CompilerParams(vmem_limit_bytes=12 * MIB),
        cost_estimate=pl.CostEstimate(flops=10**9, bytes_accessed=4 * MIB, transcendentals=0),
        name="prepare",
    )(*(pltpu.with_memory_space_constraint(x, pltpu.HBM) for x in stored))
    first, near, pre = pl.pallas_call(
        near_kernel,
        in_specs=[fast] * 5,
        out_specs=(fast,) * 3,
        out_shape=(f32((2 * C1, PLANE)), bf16((6 * C1, PLANE)), f32((2 * C2, PLANE))),
        scratch_shapes=[
            pltpu.VMEM((2 * ROWS, CELLS), jnp.float32),
            pltpu.VMEM((4, 2 * ROWS, LANES + PLANE), jnp.bfloat16),
            pltpu.VMEM((18 * ROWS, PLANE), jnp.bfloat16),
            pltpu.VMEM((2 * C1, PLANE + 2 * LANES), jnp.bfloat16),
            pltpu.VMEM((3, 2 * C2, PLANE + 2 * LANES), jnp.float32),
        ],
        compiler_params=pltpu.CompilerParams(vmem_limit_bytes=16 * MIB),
        cost_estimate=pl.CostEstimate(flops=10**9, bytes_accessed=4 * MIB, transcendentals=0),
        name="near",
    )(volumes, within, select, w1_near, w2)
    rows = C2 // narrow
    acts, give, mixed, far, kept = pl.pallas_call(
        functools.partial(far_kernel, wide // 2, narrow, scale),
        in_specs=[fast] * 8,
        out_specs=(fast,) * 5,
        out_shape=(
            bf16((1, 1, C2, cells_out)), bf16((C2 // 2, PACKED)), f32((C2 // 2, 3 * LANES)),
            bf16((6 * C1, PLANE)), bf16((PLANE + 2 * HALF, LANES)),
        ),
        scratch_shapes=[
            pltpu.VMEM((ROWS, CELLS), jnp.float32),
            pltpu.VMEM((4, ROWS, LANES + PLANE), jnp.bfloat16),
            pltpu.VMEM((9 * ROWS, PLANE), jnp.bfloat16),
            pltpu.VMEM((2 * C1, PLANE + 2 * LANES), jnp.bfloat16),
            pltpu.VMEM((3, 2 * C2, PLANE + 2 * LANES), jnp.float32),
            pltpu.VMEM((PLANE + 2 * HALF, LANES), jnp.bfloat16),
            pltpu.VMEM((PLANE + 2 * HALF, LANES), jnp.bfloat16),
            pltpu.VMEM((2, 6 * C1, 2 * LANES), jnp.float32),
        ],
        compiler_params=pltpu.CompilerParams(vmem_limit_bytes=16 * MIB),
        cost_estimate=pl.CostEstimate(flops=10**9, bytes_accessed=4 * MIB, transcendentals=0),
        name="far",
    )(across, select, w1_far, w2, cot, first, near, pre)
    got = lax.ppermute(give, WIDE, pairs)
    output, keep = pl.pallas_call(
        functools.partial(rest_kernel, scale),
        in_specs=[fast] * 5,
        out_specs=(pl.BlockSpec(memory_space=pl.ANY), fast),
        out_shape=(bf16((1, 1, C2, cells_out)), f32((C2 // 2, PACKED))),
        scratch_shapes=[pltpu.VMEM((2, 6 * C1, LANES), jnp.float32), pltpu.SemaphoreType.DMA],
        compiler_params=pltpu.CompilerParams(vmem_limit_bytes=8 * MIB),
        cost_estimate=pl.CostEstimate(flops=10**9, bytes_accessed=4 * MIB, transcendentals=0),
        name="rest",
    )(acts, near, far, kept, mixed)
    half = rows // 2
    term = (keep + got.astype(jnp.float32)).astype(jnp.bfloat16)
    received = lax.all_to_all(term, "narrow", 0, 0, tiled=True)
    owned = jnp.sum(received.reshape(narrow, half, PACKED).astype(jnp.float32), axis=0).astype(jnp.bfloat16)
    parts = lax.all_to_all(jnp.broadcast_to(owned[None], (wide, half, PACKED)), WIDE, 0, 0, tiled=True)
    weight_grad = pl.pallas_call(
        finish_kernel,
        out_shape=jax.ShapeDtypeStruct((27, rows, C1), jnp.float32),
        compiler_params=pltpu.CompilerParams(vmem_limit_bytes=8 * MIB),
        name="finish",
    )(parts)
    return (output, weight_grad)


def solution(mesh):
    wide, narrow = mesh.devices.shape
    split = jax.sharding.Mesh(mesh.devices.reshape(wide // 2, 2, narrow), ("chip", "core", "narrow"))
    return jax.shard_map(
        body,
        mesh=split,
        in_specs=(P("narrow", None, None, WIDE, None), P(), P(), P("narrow", None, None, WIDE)),
        out_specs=(P("narrow", None, None, WIDE), P(None, "narrow", None)),
        check_vma=False,
    )
```

```python
import functools
import math

import jax
import jax.numpy as jnp
import numpy as np
from jax import lax
from jax.experimental import pallas as pl
from jax.experimental.pallas import tpu as pltpu
from jax.sharding import PartitionSpec as P

CIN = 4
C1 = 32
C2 = 64
PLANES = 4
CELLS = 4096
HALF = 32
PLANE = 1024
LANES = 128
ROWS = CIN * PLANES
CHUNK = 512
PACKED = 7 * LANES
MIB = 2**20
WIDE = ("chip", "core")
neg_slope = 0.3


def selection():
    table = np.zeros((CHUNK, 2, 2, 4, HALF), np.float32)
    for py in range(2):
        for px in range(2):
            for row in range(4):
                for col in range(HALF):
                    table[(2 * row + py) * 64 + 2 * col + px, py, px, row, col] = 1
    return table.reshape(CHUNK, CHUNK)


def placement():
    table = np.zeros((2, 27, CIN, 4, CHUNK), np.float32)
    for odd in range(2):
        for a in range(3):
            for bc in range(9):
                for i in range(CIN):
                    for q in range(4):
                        slab, plane = divmod(2 * q + a + 1, PLANES)
                        inner = i * PLANES + plane
                        if slab == 1:
                            column = bc * 2 * ROWS + inner
                        elif (slab == 0) == (odd == 1):
                            column = bc * 2 * ROWS + ROWS + inner
                        else:
                            column = 18 * ROWS + bc * ROWS + inner
                        table[odd, 9 * a + bc, i, q, column] = 1
    return table.reshape(2, 27 * CIN, 4 * CHUNK)


def channel_order(narrow):
    half = C2 // (2 * narrow)
    table = np.zeros((2, 2 * C2, 2 * C2), np.float32)
    for odd in range(2):
        for z in range(2):
            for o in range(C2):
                owner, inner = divmod(o, 2 * half)
                side, row = divmod(inner, half)
                table[odd, z * C2 + o, (side == odd) * C2 + z * C1 + owner * half + row] = 1
    return table


def leaky_relu(value):
    return jnp.where(value > 0, value, neg_slope * value)


def plane_rows(volume_ref, rows_ref):
    for i in range(CIN):
        rows_ref[PLANES * i : PLANES * (i + 1), :] = volume_ref[0, 0, i].astype(jnp.float32)


def column_masks():
    column = lax.broadcasted_iota(jnp.int32, (1, PLANE), 1) % HALF
    left_ok = jnp.where(column > 0, 1.0, 0.0).astype(jnp.bfloat16)
    right_ok = jnp.where(column < HALF - 1, 1.0, 0.0).astype(jnp.bfloat16)
    return left_ok, right_ok


def strided_taps(rows, select_ref, parity_ref, taps_ref):
    count = rows.shape[0]
    left_ok, _ = column_masks()
    chunks = jnp.concatenate([rows[:, CHUNK * j : CHUNK * (j + 1)] for j in range(8)], axis=0)
    for p in range(4):
        parity_ref[p, :, 0:LANES] = jnp.zeros((count, LANES), jnp.bfloat16)
    for py in range(2):
        parts = jnp.dot(
            chunks, select_ref[:, 256 * py : 256 * py + 256], preferred_element_type=jnp.float32
        ).astype(jnp.bfloat16)
        for px in range(2):
            for j in range(8):
                parity_ref[2 * py + px, :, LANES * (j + 1) : LANES * (j + 2)] = parts[
                    j * count : (j + 1) * count, px * LANES : (px + 1) * LANES
                ]
    for b in range(3):
        for c in range(3):
            begin = LANES - HALF * (b == 0) - (c == 0)
            part = parity_ref[2 * (b != 1) + (c != 1), :, begin : begin + PLANE]
            if c == 0:
                part = part * left_ok
            taps_ref[(3 * b + c) * count : (3 * b + c + 1) * count, :] = part


def shifted_columns(act_ref, columns_ref):
    left_ok, right_ok = column_masks()
    for c in range(3):
        begin = LANES + c - 1
        part = act_ref[:, begin : begin + PLANE]
        if c == 0:
            part = part * left_ok
        if c == 2:
            part = part * right_ok
        columns_ref[c * 2 * C1 : (c + 1) * 2 * C1, :] = part


def second_layer(w2, columns_ref, turned_ref, rowed_ref):
    blank = jnp.zeros((HALF, LANES), jnp.float32)
    for b in (0, 2):
        rowed_ref[b, 0:HALF, :] = blank
        rowed_ref[b, HALF + PLANE :, :] = blank
    for n in range(4):
        cells = slice(256 * n, 256 * n + 256)
        turned_ref[cells, :] = columns_ref[:, cells].T
    for n in range(4):
        sums = jnp.dot(turned_ref[256 * n : 256 * n + 256, :], w2, preferred_element_type=jnp.float32)
        for b in range(3):
            rowed_ref[b, HALF + 256 * n : HALF + 256 * n + 256, :] = sums[:, b * LANES : (b + 1) * LANES]


def row_sum(rowed_ref, n):
    begins = [HALF * b + 256 * n for b in range(3)]
    first, second, third = (rowed_ref[b, begin : begin + 256, :] for b, begin in enumerate(begins))
    return first + second + third


def clear_margins(act_ref):
    margin = jnp.zeros((2 * C1, LANES), jnp.bfloat16)
    act_ref[:, 0:LANES] = margin
    act_ref[:, LANES + PLANE :] = margin


def prepare_kernel(
    k1_hbm, place_hbm, k2_hbm, select_hbm, cot_hbm, order_hbm,
    w1_near_ref, w1_far_ref, w2_ref, select_ref, turned_ref, order_ref,
    k1_ref, place_ref, k2_ref, cot_ref, k1_rows_ref, k2_rows_ref, sems,
):
    odd = lax.axis_index("core")
    moves = (
        (k1_hbm, k1_ref), (k2_hbm, k2_ref), (order_hbm.at[odd], order_ref),
        (place_hbm.at[odd], place_ref), (cot_hbm, cot_ref), (select_hbm, select_ref),
    )
    copies = [pltpu.make_async_copy(src, dst, sems.at[k]) for k, (src, dst) in enumerate(moves)]
    for copy in copies:
        copy.start()
    copies[0].wait()
    for tap in range(27):
        k1_rows_ref[CIN * tap : CIN * (tap + 1), :] = k1_ref[tap].astype(jnp.float32)
    copies[1].wait()
    blank = jnp.zeros((C1, C2), jnp.bfloat16)

    def stacked(bc, pair):
        k = [blank] + [k2_ref[9 * a + bc] for a in range(3)] + [blank]
        lower = jnp.concatenate(k[1 + 2 * pair : 3 + 2 * pair], axis=0)
        upper = jnp.concatenate(k[2 * pair : 2 + 2 * pair], axis=0)
        return jnp.concatenate([lower, upper], axis=1)

    for pair in range(2):
        for bc in range(9):
            begin = (9 * pair + bc) * 2 * C1
            k2_rows_ref[begin : begin + 2 * C1, :] = stacked(bc, pair)
    copies[2].wait()
    ordered = jnp.dot(k2_rows_ref[...], order_ref[...], preferred_element_type=jnp.float32).astype(jnp.bfloat16)
    for pair in range(2):
        for b in range(3):
            for c in range(3):
                begin = (9 * pair + 3 * b + c) * 2 * C1
                w2_ref[pair, c * 2 * C1 : (c + 1) * 2 * C1, b * LANES : (b + 1) * LANES] = ordered[begin : begin + 2 * C1]
    copies[3].wait()
    spread = lax.dot_general(
        k1_rows_ref[...].astype(jnp.bfloat16), place_ref[...],
        (((0,), (0,)), ((), ())), preferred_element_type=jnp.float32,
    ).astype(jnp.bfloat16)
    for q in range(4):
        rows = slice(q % 2 * C1, (q % 2 + 1) * C1)
        w1_near_ref[q // 2, rows, :] = spread[:, CHUNK * q : CHUNK * q + 18 * ROWS]
        w1_far_ref[q // 2, rows, :] = spread[:, CHUNK * q + 18 * ROWS : CHUNK * q + 27 * ROWS]
    copies[4].wait()
    for n in range(4):
        planes = [cot_ref[0, 0, :, z * PLANE + 256 * n : z * PLANE + 256 * n + 256] for z in range(2)]
        turned = jnp.concatenate(planes, axis=0).T
        turned_ref[256 * n : 256 * n + 256, :] = jnp.dot(
            turned, order_ref[...], preferred_element_type=jnp.float32
        ).astype(jnp.bfloat16)
    copies[5].wait()


def near_kernel(
    own_ref, within_ref, select_ref, w1_ref, w2_ref, first_ref, columns_ref, pre_ref,
    rows_ref, parity_ref, taps_ref, act_ref, turned_ref, rowed_ref,
):
    odd = lax.axis_index("core")
    plane_rows(own_ref, rows_ref.at[0:ROWS])
    plane_rows(within_ref, rows_ref.at[ROWS : 2 * ROWS])
    strided_taps(rows_ref[...].astype(jnp.bfloat16), select_ref, parity_ref, taps_ref)
    clear_margins(act_ref)
    for n in range(4):
        here = slice(256 * n, 256 * n + 256)
        first_ref[:, here] = jnp.dot(w1_ref[odd], taps_ref[:, here], preferred_element_type=jnp.float32)
        complete = jnp.dot(w1_ref[1 - odd], taps_ref[:, here], preferred_element_type=jnp.float32)
        act_ref[:, LANES + 256 * n : LANES + 256 * n + 256] = leaky_relu(complete).astype(jnp.bfloat16)
    shifted_columns(act_ref, columns_ref)
    second_layer(w2_ref[1 - odd], columns_ref, turned_ref, rowed_ref)
    for n in range(4):
        pre_ref[256 * n : 256 * n + 256, :] = row_sum(rowed_ref, n)


def slots():
    where = {}
    for a in range(3):
        for b in range(3):
            for c in range(3):
                slot, side = divmod(3 * a + c, 2)
                where[9 * a + 3 * b + c] = (2 * b + side, slot) if slot < 4 else (6, (0, 2, 1)[b])
    return where


def group_of_lane():
    return lax.broadcasted_iota(jnp.int32, (C1, LANES), 1) // C1


def paired_terms(sums_ref, tile):
    even = group_of_lane() % 2 == 0

    def plane(q, c):
        begin = 2 * C1 * c + C1 * (q % 2)
        return sums_ref[q // 2, begin : begin + C1, tile * LANES : (tile + 1) * LANES]

    terms = [plane(a, c) + pltpu.roll(plane(a + 1, c), 3 * C1, 1) for a in range(3) for c in range(3)]
    return [jnp.where(even, terms[k], pltpu.roll(terms[k + 1], C1, 1)) for k in range(0, 8, 2)] + [terms[8]]


def turned_groups(blocks, scale):
    flat = (jnp.concatenate(blocks, axis=0) * scale).T
    return [flat[g * C1 : (g + 1) * C1] for g in range(4)]


def gradient_sums(odd, near_ref, far_ref, backs, sums_ref):
    columns = jnp.concatenate([near_ref[...], far_ref[...]], axis=0)
    sums = jnp.dot(columns, backs, preferred_element_type=jnp.float32)
    sums_ref[1 - odd] = sums[0 : 6 * C1]
    sums_ref[odd] = sums[6 * C1 :]


def far_kernel(
    chips, scale, across_ref, select_ref, w1_ref, w2_ref, cot_ref, first_ref, near_ref, near_pre_ref,
    pre_ref, give_ref, keep_ref, columns_ref, kept_ref,
    rows_ref, parity_ref, taps_ref, act_ref, turned_ref, rowed_ref, given_ref, mixed_ref, sums_ref,
):
    odd = lax.axis_index("core")
    last = (lax.axis_index("chip") == chips - 1) & (odd == 1)
    inside = jnp.where(last, 0.0, 1.0)
    plane_rows(across_ref, rows_ref)
    strided_taps(rows_ref[...].astype(jnp.bfloat16), select_ref, parity_ref, taps_ref)
    clear_margins(act_ref)
    for n in range(4):
        here = slice(256 * n, 256 * n + 256)
        first_pre = first_ref[:, here] + jnp.dot(w1_ref[odd], taps_ref[:, here], preferred_element_type=jnp.float32)
        first_act = leaky_relu(first_pre)
        there = slice(LANES + 256 * n, LANES + 256 * n + 256)
        act_ref[0:C1, there] = first_act[0:C1].astype(jnp.bfloat16)
        act_ref[C1:, there] = (first_act[C1:] * inside).astype(jnp.bfloat16)
    shifted_columns(act_ref, columns_ref)
    second_layer(w2_ref[odd], columns_ref, turned_ref, rowed_ref)

    margin = jnp.zeros((HALF, LANES), jnp.bfloat16)
    for ref in (given_ref, mixed_ref, kept_ref):
        ref[HALF : 2 * HALF, :] = margin
        ref[PLANE : PLANE + HALF, :] = margin
    for n in range(4):
        cells = slice(256 * n, 256 * n + 256)
        pre = near_pre_ref[cells, :] + row_sum(rowed_ref, n)
        pre_ref[cells, :] = pre
        back = (cot_ref[cells, :].astype(jnp.float32) * jnp.where(pre > 0, 1.0, neg_slope)).astype(jnp.bfloat16)
        other = jnp.concatenate([back[:, C2:], back[:, 0:C2]], axis=1)
        rows = [slice(256 * n + HALF * b, 256 * n + HALF * b + 256) for b in range(3)]
        given_ref[rows[0], 0:C2] = back[:, 0:C2]
        given_ref[rows[1], C2:] = other[:, C2:]
        mixed_ref[rows[2], :] = back
        kept_ref[rows[0], 0:C2] = other[:, 0:C2]
        kept_ref[rows[1], C2:] = back[:, C2:]
    middle = slice(HALF, HALF + PLANE)
    gradient_sums(odd, near_ref, columns_ref, jnp.concatenate([given_ref[middle, :], mixed_ref[middle, :]], axis=1), sums_ref)
    given, mixed = paired_terms(sums_ref, 0), paired_terms(sums_ref, 1)
    first = turned_groups(given[0:4], scale)
    second = turned_groups(mixed[0:4], scale)
    third = turned_groups([given[4], mixed[4], given[4], mixed[4]], scale)
    group = group_of_lane()
    tiles = first + second[0:2] + [jnp.where(group < 2, third[0], pltpu.roll(third[2], C2, 1))]
    for k, tile in enumerate(tiles):
        give_ref[:, k * LANES : (k + 1) * LANES] = tile.astype(jnp.bfloat16)
    for k, tile in enumerate((second[2], second[3], third[2])):
        keep_ref[:, k * LANES : (k + 1) * LANES] = tile


def rest_kernel(
    scale, pre_ref, order_ref, near_ref, far_ref, kept_ref, mixed_ref, out_hbm, keep_ref, sums_ref, out_ref, out_sem,
):
    for n in range(4):
        output = leaky_relu(pre_ref[256 * n : 256 * n + 256, :]).astype(jnp.bfloat16)
        ordered = lax.dot_general(
            order_ref[...], output, (((1,), (1,)), ((), ())), preferred_element_type=jnp.float32
        ).astype(jnp.bfloat16)
        for z in range(2):
            out_ref[0, 0, :, z * PLANE + 256 * n : z * PLANE + 256 * n + 256] = ordered[z * C2 : (z + 1) * C2]
    out_copy = pltpu.make_async_copy(out_ref, out_hbm, out_sem)
    out_copy.start()
    odd = lax.axis_index("core")
    gradient_sums(odd, near_ref, far_ref, kept_ref[HALF : HALF + PLANE, :], sums_ref)
    kept = paired_terms(sums_ref, 0)
    first = turned_groups(kept[0:4], scale)
    third = turned_groups([kept[4]] * 4, scale)
    group = group_of_lane()
    mixed = [mixed_ref[:, k * LANES : (k + 1) * LANES] for k in range(3)]
    ends = jnp.where(group == 1, mixed[2], jnp.where(group == 0, third[0], pltpu.roll(third[2], C2, 1)))
    for k, tile in enumerate(first + mixed[0:2] + [ends]):
        keep_ref[:, k * LANES : (k + 1) * LANES] = tile
    out_copy.wait()


def finish_kernel(parts_ref, grad_ref):
    wide, half, _ = parts_ref.shape
    for core in range(2):
        total = parts_ref[core].astype(jnp.float32)
        for k in range(core + 2, wide, 2):
            total = total + parts_ref[k].astype(jnp.float32)
        for tap, (tile, slot) in slots().items():
            begin = tile * LANES + slot * C1
            grad_ref[tap, core * half : (core + 1) * half, :] = total[:, begin : begin + C1]


def body(volumes, first_kernel, second_kernel, cotangent):
    wide = lax.axis_size(WIDE)
    narrow = lax.axis_size("narrow")
    cells_out = cotangent.shape[3]
    scale = 1.0 / math.sqrt(wide * narrow * cells_out)
    across = lax.ppermute(volumes, WIDE, [p for k in range(1, wide - 1, 2) for p in ((k, k + 1), (k + 1, k))])
    pairs = [p for k in range(0, wide - 1, 2) for p in ((k, k + 1), (k + 1, k))]
    within = lax.ppermute(volumes, WIDE, pairs)
    pinned = pl.BlockSpec(memory_space=pltpu.HBM)
    fast = pl.BlockSpec(memory_space=pltpu.VMEM)
    bf16 = functools.partial(jax.ShapeDtypeStruct, dtype=jnp.bfloat16)
    f32 = functools.partial(jax.ShapeDtypeStruct, dtype=jnp.float32)
    stored = (
        first_kernel.transpose(0, 2, 1), jnp.asarray(placement(), jnp.bfloat16), second_kernel.transpose(0, 2, 1),
        jnp.asarray(selection(), jnp.bfloat16), cotangent, jnp.asarray(channel_order(narrow), jnp.bfloat16),
    )
    w1_near, w1_far, w2, select, cot, order = pl.pallas_call(
        prepare_kernel,
        in_specs=[pinned] * 6,
        out_specs=(fast,) * 6,
        out_shape=(
            bf16((2, 2 * C1, 18 * ROWS)), bf16((2, 2 * C1, 9 * ROWS)), bf16((2, 6 * C1, 6 * C2)),
            bf16((CHUNK, CHUNK)), bf16((PLANE, 2 * C2)), bf16((2 * C2, 2 * C2)),
        ),
        scratch_shapes=[
            pltpu.VMEM((27, CIN, C1), jnp.bfloat16),
            pltpu.VMEM((27 * CIN, 4 * CHUNK), jnp.bfloat16),
            pltpu.VMEM((27, C1, C2), jnp.bfloat16),
            pltpu.VMEM(cotangent.shape, jnp.bfloat16),
            pltpu.VMEM((27 * CIN, C1), jnp.float32),
            pltpu.VMEM((36 * C1, 2 * C2), jnp.bfloat16),
            pltpu.SemaphoreType.DMA((6,)),
        ],
        compiler_params=pltpu.CompilerParams(vmem_limit_bytes=12 * MIB),
        cost_estimate=pl.CostEstimate(flops=10**9, bytes_accessed=4 * MIB, transcendentals=0),
        name="prepare",
    )(*(pltpu.with_memory_space_constraint(x, pltpu.HBM) for x in stored))
    first, near, pre = pl.pallas_call(
        near_kernel,
        in_specs=[fast] * 5,
        out_specs=(fast,) * 3,
        out_shape=(f32((2 * C1, PLANE)), bf16((6 * C1, PLANE)), f32((PLANE, 2 * C2))),
        scratch_shapes=[
            pltpu.VMEM((2 * ROWS, CELLS), jnp.float32),
            pltpu.VMEM((4, 2 * ROWS, LANES + PLANE), jnp.bfloat16),
            pltpu.VMEM((18 * ROWS, PLANE), jnp.bfloat16),
            pltpu.VMEM((2 * C1, PLANE + 2 * LANES), jnp.bfloat16),
            pltpu.VMEM((PLANE, 6 * C1), jnp.bfloat16),
            pltpu.VMEM((3, PLANE + 2 * HALF, LANES), jnp.float32),
        ],
        compiler_params=pltpu.CompilerParams(vmem_limit_bytes=16 * MIB),
        cost_estimate=pl.CostEstimate(flops=10**9, bytes_accessed=4 * MIB, transcendentals=0),
        name="near",
    )(volumes, within, select, w1_near, w2)
    rows = C2 // narrow
    pre, give, mixed, far, kept = pl.pallas_call(
        functools.partial(far_kernel, wide // 2, scale),
        in_specs=[fast] * 8,
        out_specs=(fast,) * 5,
        out_shape=(
            f32((PLANE, 2 * C2)), bf16((C2 // 2, PACKED)), f32((C2 // 2, 3 * LANES)),
            bf16((6 * C1, PLANE)), bf16((PLANE + 2 * HALF, LANES)),
        ),
        scratch_shapes=[
            pltpu.VMEM((ROWS, CELLS), jnp.float32),
            pltpu.VMEM((4, ROWS, LANES + PLANE), jnp.bfloat16),
            pltpu.VMEM((9 * ROWS, PLANE), jnp.bfloat16),
            pltpu.VMEM((2 * C1, PLANE + 2 * LANES), jnp.bfloat16),
            pltpu.VMEM((PLANE, 6 * C1), jnp.bfloat16),
            pltpu.VMEM((3, PLANE + 2 * HALF, LANES), jnp.float32),
            pltpu.VMEM((PLANE + 2 * HALF, LANES), jnp.bfloat16),
            pltpu.VMEM((PLANE + 2 * HALF, LANES), jnp.bfloat16),
            pltpu.VMEM((2, 6 * C1, 2 * LANES), jnp.float32),
        ],
        compiler_params=pltpu.CompilerParams(vmem_limit_bytes=16 * MIB),
        cost_estimate=pl.CostEstimate(flops=10**9, bytes_accessed=4 * MIB, transcendentals=0),
        name="far",
    )(across, select, w1_far, w2, cot, first, near, pre)
    got = lax.ppermute(give, WIDE, pairs)
    output, keep = pl.pallas_call(
        functools.partial(rest_kernel, scale),
        in_specs=[fast] * 6,
        out_specs=(pl.BlockSpec(memory_space=pl.ANY), fast),
        out_shape=(bf16((1, 1, C2, cells_out)), f32((C2 // 2, PACKED))),
        scratch_shapes=[
            pltpu.VMEM((2, 6 * C1, LANES), jnp.float32),
            pltpu.VMEM((1, 1, C2, cells_out), jnp.bfloat16),
            pltpu.SemaphoreType.DMA,
        ],
        compiler_params=pltpu.CompilerParams(vmem_limit_bytes=8 * MIB),
        cost_estimate=pl.CostEstimate(flops=10**9, bytes_accessed=4 * MIB, transcendentals=0),
        name="rest",
    )(pre, order, near, far, kept, mixed)
    half = rows // 2
    term = (keep + got.astype(jnp.float32)).astype(jnp.bfloat16)
    received = lax.all_to_all(term, "narrow", 0, 0, tiled=True)
    owned = jnp.sum(received.reshape(narrow, half, PACKED).astype(jnp.float32), axis=0).astype(jnp.bfloat16)
    parts = lax.all_to_all(jnp.broadcast_to(owned[None], (wide, half, PACKED)), WIDE, 0, 0, tiled=True)
    weight_grad = pl.pallas_call(
        finish_kernel,
        out_shape=jax.ShapeDtypeStruct((27, rows, C1), jnp.float32),
        compiler_params=pltpu.CompilerParams(vmem_limit_bytes=8 * MIB),
        name="finish",
    )(parts)
    return (output, weight_grad)


def solution(mesh):
    wide, narrow = mesh.devices.shape
    split = jax.sharding.Mesh(mesh.devices.reshape(wide // 2, 2, narrow), ("chip", "core", "narrow"))
    return jax.shard_map(
        body,
        mesh=split,
        in_specs=(P("narrow", None, None, WIDE, None), P(), P(), P("narrow", None, None, WIDE)),
        out_specs=(P("narrow", None, None, WIDE), P(None, "narrow", None)),
        check_vma=False,
    )
```

```python
import functools
import math

import jax
import jax.numpy as jnp
import numpy as np
from jax import lax
from jax.experimental import pallas as pl
from jax.experimental.pallas import tpu as pltpu
from jax.sharding import PartitionSpec as P

CIN = 4
C1 = 32
C2 = 64
PLANES = 4
CELLS = 4096
HALF = 32
PLANE = 1024
LANES = 128
ROWS = CIN * PLANES
CHUNK = 256
TABLE = 512
PACKED = 7 * LANES
MIB = 2**20
WIDE = ("chip", "core")
neg_slope = 0.3


def selection():
    table = np.zeros((CHUNK, 2, 2, 2, HALF), np.float32)
    for py in range(2):
        for px in range(2):
            for row in range(2):
                for col in range(HALF):
                    table[(2 * row + py) * 64 + 2 * col + px, py, px, row, col] = 1
    return table.reshape(CHUNK, CHUNK)


def placement():
    table = np.zeros((2, 27, CIN, 4, TABLE), np.float32)
    for odd in range(2):
        for a in range(3):
            for bc in range(9):
                for i in range(CIN):
                    for q in range(4):
                        slab, plane = divmod(2 * q + a + 1, PLANES)
                        inner = i * PLANES + plane
                        if slab == 1:
                            column = bc * 2 * ROWS + inner
                        elif (slab == 0) == (odd == 1):
                            column = bc * 2 * ROWS + ROWS + inner
                        else:
                            column = 18 * ROWS + bc * ROWS + inner
                        table[odd, 9 * a + bc, i, q, column] = 1
    return table.reshape(2, 27 * CIN, 4 * TABLE)


def channel_order(narrow):
    half = C2 // (2 * narrow)
    table = np.zeros((2, 2 * C2, 2 * C2), np.float32)
    for odd in range(2):
        for z in range(2):
            for o in range(C2):
                owner, inner = divmod(o, 2 * half)
                side, row = divmod(inner, half)
                table[odd, z * C2 + o, (side == odd) * C2 + z * C1 + owner * half + row] = 1
    return table


def leaky_relu(value):
    return jnp.where(value > 0, value, neg_slope * value)


def plane_rows(volume_ref, rows_ref):
    for i in range(CIN):
        rows_ref[PLANES * i : PLANES * (i + 1), :] = volume_ref[0, 0, i].astype(jnp.float32)


def column_masks():
    column = lax.broadcasted_iota(jnp.int32, (1, PLANE), 1) % HALF
    left_ok = jnp.where(column > 0, 1.0, 0.0).astype(jnp.bfloat16)
    right_ok = jnp.where(column < HALF - 1, 1.0, 0.0).astype(jnp.bfloat16)
    return left_ok, right_ok


def strided_taps(rows, select_ref, parity_ref, taps_ref):
    count = rows.shape[0]
    left_ok, _ = column_masks()
    chunks = jnp.concatenate([rows[:, CHUNK * j : CHUNK * (j + 1)] for j in range(16)], axis=0)
    for p in range(4):
        parity_ref[p, :, 0:LANES] = jnp.zeros((count, LANES), jnp.bfloat16)
    parts = jnp.dot(chunks, select_ref[...], preferred_element_type=jnp.float32).astype(jnp.bfloat16)
    for j in range(16):
        for p in range(4):
            begin = LANES + j * LANES // 2
            parity_ref[p, :, begin : begin + LANES // 2] = parts[
                j * count : (j + 1) * count, p * LANES // 2 : (p + 1) * LANES // 2
            ]
    for b in range(3):
        for c in range(3):
            begin = LANES - HALF * (b == 0) - (c == 0)
            part = parity_ref[2 * (b != 1) + (c != 1), :, begin : begin + PLANE]
            if c == 0:
                part = part * left_ok
            taps_ref[(3 * b + c) * count : (3 * b + c + 1) * count, :] = part


def shifted_columns(act_ref, columns_ref):
    left_ok, right_ok = column_masks()
    for c in range(3):
        begin = LANES + c - 1
        part = act_ref[:, begin : begin + PLANE]
        if c == 0:
            part = part * left_ok
        if c == 2:
            part = part * right_ok
        columns_ref[c * 2 * C1 : (c + 1) * 2 * C1, :] = part


def second_layer(w2, columns_ref, turned_ref, rowed_ref):
    blank = jnp.zeros((HALF, LANES), jnp.float32)
    for b in (0, 2):
        rowed_ref[b, 0:HALF, :] = blank
        rowed_ref[b, HALF + PLANE :, :] = blank
    for n in range(4):
        cells = slice(256 * n, 256 * n + 256)
        turned_ref[cells, :] = columns_ref[:, cells].T
    for n in range(4):
        sums = jnp.dot(turned_ref[256 * n : 256 * n + 256, :], w2, preferred_element_type=jnp.float32)
        for b in range(3):
            rowed_ref[b, HALF + 256 * n : HALF + 256 * n + 256, :] = sums[:, b * LANES : (b + 1) * LANES]


def row_sum(rowed_ref, n):
    begins = [HALF * b + 256 * n for b in range(3)]
    first, second, third = (rowed_ref[b, begin : begin + 256, :] for b, begin in enumerate(begins))
    return first + second + third


def clear_margins(act_ref):
    margin = jnp.zeros((2 * C1, LANES), jnp.bfloat16)
    act_ref[:, 0:LANES] = margin
    act_ref[:, LANES + PLANE :] = margin


def prepare_kernel(
    k1_hbm, place_hbm, k2_hbm, select_hbm, cot_hbm, order_hbm,
    w1_near_ref, w1_far_ref, w2_ref, select_ref, turned_ref, order_ref,
    k1_ref, place_ref, k2_ref, cot_ref, k1_rows_ref, k2_rows_ref, sems,
):
    odd = lax.axis_index("core")
    moves = (
        (k1_hbm, k1_ref), (k2_hbm, k2_ref), (order_hbm.at[odd], order_ref),
        (place_hbm.at[odd], place_ref), (cot_hbm, cot_ref), (select_hbm, select_ref),
    )
    copies = [pltpu.make_async_copy(src, dst, sems.at[k]) for k, (src, dst) in enumerate(moves)]
    for copy in copies:
        copy.start()
    copies[0].wait()
    for tap in range(27):
        k1_rows_ref[CIN * tap : CIN * (tap + 1), :] = k1_ref[tap].astype(jnp.float32)
    copies[1].wait()
    blank = jnp.zeros((C1, C2), jnp.bfloat16)

    def stacked(bc, pair):
        k = [blank] + [k2_ref[9 * a + bc] for a in range(3)] + [blank]
        lower = jnp.concatenate(k[1 + 2 * pair : 3 + 2 * pair], axis=0)
        upper = jnp.concatenate(k[2 * pair : 2 + 2 * pair], axis=0)
        return jnp.concatenate([lower, upper], axis=1)

    for pair in range(2):
        for bc in range(9):
            begin = (9 * pair + bc) * 2 * C1
            k2_rows_ref[begin : begin + 2 * C1, :] = stacked(bc, pair)
    copies[2].wait()
    ordered = jnp.dot(k2_rows_ref[...], order_ref[...], preferred_element_type=jnp.float32).astype(jnp.bfloat16)
    for pair in range(2):
        for b in range(3):
            for c in range(3):
                begin = (9 * pair + 3 * b + c) * 2 * C1
                w2_ref[pair, c * 2 * C1 : (c + 1) * 2 * C1, b * LANES : (b + 1) * LANES] = ordered[begin : begin + 2 * C1]
    copies[3].wait()
    spread = lax.dot_general(
        k1_rows_ref[...].astype(jnp.bfloat16), place_ref[...],
        (((0,), (0,)), ((), ())), preferred_element_type=jnp.float32,
    ).astype(jnp.bfloat16)
    for q in range(4):
        rows = slice(q % 2 * C1, (q % 2 + 1) * C1)
        w1_near_ref[q // 2, rows, :] = spread[:, TABLE * q : TABLE * q + 18 * ROWS]
        w1_far_ref[q // 2, rows, :] = spread[:, TABLE * q + 18 * ROWS : TABLE * q + 27 * ROWS]
    copies[4].wait()
    for n in range(4):
        planes = [cot_ref[0, 0, :, z * PLANE + 256 * n : z * PLANE + 256 * n + 256] for z in range(2)]
        turned = jnp.concatenate(planes, axis=0).T
        turned_ref[256 * n : 256 * n + 256, :] = jnp.dot(
            turned, order_ref[...], preferred_element_type=jnp.float32
        ).astype(jnp.bfloat16)
    copies[5].wait()


def near_kernel(
    own_ref, within_ref, select_ref, w1_ref, w2_ref, first_ref, columns_ref, pre_ref,
    rows_ref, parity_ref, taps_ref, act_ref, turned_ref, rowed_ref,
):
    odd = lax.axis_index("core")
    plane_rows(own_ref, rows_ref.at[0:ROWS])
    plane_rows(within_ref, rows_ref.at[ROWS : 2 * ROWS])
    strided_taps(rows_ref[...].astype(jnp.bfloat16), select_ref, parity_ref, taps_ref)
    clear_margins(act_ref)
    for n in range(4):
        here = slice(256 * n, 256 * n + 256)
        first_ref[:, here] = jnp.dot(w1_ref[odd], taps_ref[:, here], preferred_element_type=jnp.float32)
        complete = jnp.dot(w1_ref[1 - odd], taps_ref[:, here], preferred_element_type=jnp.float32)
        act_ref[:, LANES + 256 * n : LANES + 256 * n + 256] = leaky_relu(complete).astype(jnp.bfloat16)
    shifted_columns(act_ref, columns_ref)
    second_layer(w2_ref[1 - odd], columns_ref, turned_ref, rowed_ref)
    for n in range(4):
        pre_ref[256 * n : 256 * n + 256, :] = row_sum(rowed_ref, n)


def slots():
    where = {}
    for a in range(3):
        for b in range(3):
            for c in range(3):
                slot, side = divmod(3 * a + c, 2)
                where[9 * a + 3 * b + c] = (2 * b + side, slot) if slot < 4 else (6, (0, 2, 1)[b])
    return where


def group_of_lane():
    return lax.broadcasted_iota(jnp.int32, (C1, LANES), 1) // C1


def paired_terms(sums_ref, tile):
    even = group_of_lane() % 2 == 0

    def plane(q, c):
        begin = 2 * C1 * c + C1 * (q % 2)
        return sums_ref[q // 2, begin : begin + C1, tile * LANES : (tile + 1) * LANES]

    terms = [plane(a, c) + pltpu.roll(plane(a + 1, c), 3 * C1, 1) for a in range(3) for c in range(3)]
    return [jnp.where(even, terms[k], pltpu.roll(terms[k + 1], C1, 1)) for k in range(0, 8, 2)] + [terms[8]]


def turned_groups(blocks, scale):
    flat = (jnp.concatenate(blocks, axis=0) * scale).T
    return [flat[g * C1 : (g + 1) * C1] for g in range(4)]


def gradient_sums(odd, near_ref, far_ref, backs, sums_ref):
    columns = jnp.concatenate([near_ref[...], far_ref[...]], axis=0)
    sums = jnp.dot(columns, backs, preferred_element_type=jnp.float32)
    sums_ref[1 - odd] = sums[0 : 6 * C1]
    sums_ref[odd] = sums[6 * C1 :]


def far_kernel(
    chips, scale, across_ref, select_ref, w1_ref, w2_ref, cot_ref, first_ref, near_ref, near_pre_ref,
    pre_ref, give_ref, keep_ref, columns_ref, kept_ref,
    rows_ref, parity_ref, taps_ref, act_ref, turned_ref, rowed_ref, given_ref, mixed_ref, sums_ref,
):
    odd = lax.axis_index("core")
    last = (lax.axis_index("chip") == chips - 1) & (odd == 1)
    inside = jnp.where(last, 0.0, 1.0)
    plane_rows(across_ref, rows_ref)
    strided_taps(rows_ref[...].astype(jnp.bfloat16), select_ref, parity_ref, taps_ref)
    clear_margins(act_ref)
    for n in range(4):
        here = slice(256 * n, 256 * n + 256)
        first_pre = first_ref[:, here] + jnp.dot(w1_ref[odd], taps_ref[:, here], preferred_element_type=jnp.float32)
        first_act = leaky_relu(first_pre)
        there = slice(LANES + 256 * n, LANES + 256 * n + 256)
        act_ref[0:C1, there] = first_act[0:C1].astype(jnp.bfloat16)
        act_ref[C1:, there] = (first_act[C1:] * inside).astype(jnp.bfloat16)
    shifted_columns(act_ref, columns_ref)
    second_layer(w2_ref[odd], columns_ref, turned_ref, rowed_ref)

    margin = jnp.zeros((HALF, LANES), jnp.bfloat16)
    for ref in (given_ref, mixed_ref, kept_ref):
        ref[HALF : 2 * HALF, :] = margin
        ref[PLANE : PLANE + HALF, :] = margin
    for n in range(4):
        cells = slice(256 * n, 256 * n + 256)
        pre = near_pre_ref[cells, :] + row_sum(rowed_ref, n)
        pre_ref[cells, :] = pre
        back = (cot_ref[cells, :].astype(jnp.float32) * jnp.where(pre > 0, 1.0, neg_slope)).astype(jnp.bfloat16)
        other = jnp.concatenate([back[:, C2:], back[:, 0:C2]], axis=1)
        rows = [slice(256 * n + HALF * b, 256 * n + HALF * b + 256) for b in range(3)]
        given_ref[rows[0], 0:C2] = back[:, 0:C2]
        given_ref[rows[1], C2:] = other[:, C2:]
        mixed_ref[rows[2], :] = back
        kept_ref[rows[0], 0:C2] = other[:, 0:C2]
        kept_ref[rows[1], C2:] = back[:, C2:]
    middle = slice(HALF, HALF + PLANE)
    gradient_sums(odd, near_ref, columns_ref, jnp.concatenate([given_ref[middle, :], mixed_ref[middle, :]], axis=1), sums_ref)
    given, mixed = paired_terms(sums_ref, 0), paired_terms(sums_ref, 1)
    first = turned_groups(given[0:4], scale)
    second = turned_groups(mixed[0:4], scale)
    third = turned_groups([given[4], mixed[4], given[4], mixed[4]], scale)
    group = group_of_lane()
    tiles = first + second[0:2] + [jnp.where(group < 2, third[0], pltpu.roll(third[2], C2, 1))]
    for k, tile in enumerate(tiles):
        give_ref[:, k * LANES : (k + 1) * LANES] = tile.astype(jnp.bfloat16)
    for k, tile in enumerate((second[2], second[3], third[2])):
        keep_ref[:, k * LANES : (k + 1) * LANES] = tile


def rest_kernel(
    scale, pre_ref, order_ref, near_ref, far_ref, kept_ref, mixed_ref, out_hbm, keep_ref, sums_ref, out_ref, out_sem,
):
    for n in range(4):
        output = leaky_relu(pre_ref[256 * n : 256 * n + 256, :]).astype(jnp.bfloat16)
        ordered = lax.dot_general(
            order_ref[...], output, (((1,), (1,)), ((), ())), preferred_element_type=jnp.float32
        ).astype(jnp.bfloat16)
        for z in range(2):
            out_ref[0, 0, :, z * PLANE + 256 * n : z * PLANE + 256 * n + 256] = ordered[z * C2 : (z + 1) * C2]
    out_copy = pltpu.make_async_copy(out_ref, out_hbm, out_sem)
    out_copy.start()
    odd = lax.axis_index("core")
    gradient_sums(odd, near_ref, far_ref, kept_ref[HALF : HALF + PLANE, :], sums_ref)
    kept = paired_terms(sums_ref, 0)
    first = turned_groups(kept[0:4], scale)
    third = turned_groups([kept[4]] * 4, scale)
    group = group_of_lane()
    mixed = [mixed_ref[:, k * LANES : (k + 1) * LANES] for k in range(3)]
    ends = jnp.where(group == 1, mixed[2], jnp.where(group == 0, third[0], pltpu.roll(third[2], C2, 1)))
    for k, tile in enumerate(first + mixed[0:2] + [ends]):
        keep_ref[:, k * LANES : (k + 1) * LANES] = tile
    out_copy.wait()


def finish_kernel(total_ref, grad_ref):
    for tap, (tile, slot) in slots().items():
        begin = tile * LANES + slot * C1
        grad_ref[tap] = total_ref[:, begin : begin + C1]


def body(volumes, first_kernel, second_kernel, cotangent):
    wide = lax.axis_size(WIDE)
    narrow = lax.axis_size("narrow")
    cells_out = cotangent.shape[3]
    scale = 1.0 / math.sqrt(wide * narrow * cells_out)
    across = lax.ppermute(volumes, WIDE, [p for k in range(1, wide - 1, 2) for p in ((k, k + 1), (k + 1, k))])
    pairs = [p for k in range(0, wide - 1, 2) for p in ((k, k + 1), (k + 1, k))]
    within = lax.ppermute(volumes, WIDE, pairs)
    pinned = pl.BlockSpec(memory_space=pltpu.HBM)
    fast = pl.BlockSpec(memory_space=pltpu.VMEM)
    bf16 = functools.partial(jax.ShapeDtypeStruct, dtype=jnp.bfloat16)
    f32 = functools.partial(jax.ShapeDtypeStruct, dtype=jnp.float32)
    stored = (
        first_kernel.transpose(0, 2, 1), jnp.asarray(placement(), jnp.bfloat16), second_kernel.transpose(0, 2, 1),
        jnp.asarray(selection(), jnp.bfloat16), cotangent, jnp.asarray(channel_order(narrow), jnp.bfloat16),
    )
    w1_near, w1_far, w2, select, cot, order = pl.pallas_call(
        prepare_kernel,
        in_specs=[pinned] * 6,
        out_specs=(fast,) * 6,
        out_shape=(
            bf16((2, 2 * C1, 18 * ROWS)), bf16((2, 2 * C1, 9 * ROWS)), bf16((2, 6 * C1, 6 * C2)),
            bf16((CHUNK, CHUNK)), bf16((PLANE, 2 * C2)), bf16((2 * C2, 2 * C2)),
        ),
        scratch_shapes=[
            pltpu.VMEM((27, CIN, C1), jnp.bfloat16),
            pltpu.VMEM((27 * CIN, 4 * TABLE), jnp.bfloat16),
            pltpu.VMEM((27, C1, C2), jnp.bfloat16),
            pltpu.VMEM(cotangent.shape, jnp.bfloat16),
            pltpu.VMEM((27 * CIN, C1), jnp.float32),
            pltpu.VMEM((36 * C1, 2 * C2), jnp.bfloat16),
            pltpu.SemaphoreType.DMA((6,)),
        ],
        compiler_params=pltpu.CompilerParams(vmem_limit_bytes=12 * MIB),
        cost_estimate=pl.CostEstimate(flops=10**9, bytes_accessed=4 * MIB, transcendentals=0),
        name="prepare",
    )(*(pltpu.with_memory_space_constraint(x, pltpu.HBM) for x in stored))
    first, near, pre = pl.pallas_call(
        near_kernel,
        in_specs=[fast] * 5,
        out_specs=(fast,) * 3,
        out_shape=(f32((2 * C1, PLANE)), bf16((6 * C1, PLANE)), f32((PLANE, 2 * C2))),
        scratch_shapes=[
            pltpu.VMEM((2 * ROWS, CELLS), jnp.float32),
            pltpu.VMEM((4, 2 * ROWS, LANES + PLANE), jnp.bfloat16),
            pltpu.VMEM((18 * ROWS, PLANE), jnp.bfloat16),
            pltpu.VMEM((2 * C1, PLANE + 2 * LANES), jnp.bfloat16),
            pltpu.VMEM((PLANE, 6 * C1), jnp.bfloat16),
            pltpu.VMEM((3, PLANE + 2 * HALF, LANES), jnp.float32),
        ],
        compiler_params=pltpu.CompilerParams(vmem_limit_bytes=16 * MIB),
        cost_estimate=pl.CostEstimate(flops=10**9, bytes_accessed=4 * MIB, transcendentals=0),
        name="near",
    )(volumes, within, select, w1_near, w2)
    rows = C2 // narrow
    pre, give, mixed, far, kept = pl.pallas_call(
        functools.partial(far_kernel, wide // 2, scale),
        in_specs=[fast] * 8,
        out_specs=(fast,) * 5,
        out_shape=(
            f32((PLANE, 2 * C2)), bf16((C2 // 2, PACKED)), f32((C2 // 2, 3 * LANES)),
            bf16((6 * C1, PLANE)), bf16((PLANE + 2 * HALF, LANES)),
        ),
        scratch_shapes=[
            pltpu.VMEM((ROWS, CELLS), jnp.float32),
            pltpu.VMEM((4, ROWS, LANES + PLANE), jnp.bfloat16),
            pltpu.VMEM((9 * ROWS, PLANE), jnp.bfloat16),
            pltpu.VMEM((2 * C1, PLANE + 2 * LANES), jnp.bfloat16),
            pltpu.VMEM((PLANE, 6 * C1), jnp.bfloat16),
            pltpu.VMEM((3, PLANE + 2 * HALF, LANES), jnp.float32),
            pltpu.VMEM((PLANE + 2 * HALF, LANES), jnp.bfloat16),
            pltpu.VMEM((PLANE + 2 * HALF, LANES), jnp.bfloat16),
            pltpu.VMEM((2, 6 * C1, 2 * LANES), jnp.float32),
        ],
        compiler_params=pltpu.CompilerParams(vmem_limit_bytes=16 * MIB),
        cost_estimate=pl.CostEstimate(flops=10**9, bytes_accessed=4 * MIB, transcendentals=0),
        name="far",
    )(across, select, w1_far, w2, cot, first, near, pre)
    got = lax.ppermute(give, WIDE, pairs)
    output, keep = pl.pallas_call(
        functools.partial(rest_kernel, scale),
        in_specs=[fast] * 6,
        out_specs=(pl.BlockSpec(memory_space=pl.ANY), fast),
        out_shape=(bf16((1, 1, C2, cells_out)), f32((C2 // 2, PACKED))),
        scratch_shapes=[
            pltpu.VMEM((2, 6 * C1, LANES), jnp.float32),
            pltpu.VMEM((1, 1, C2, cells_out), jnp.bfloat16),
            pltpu.SemaphoreType.DMA,
        ],
        compiler_params=pltpu.CompilerParams(vmem_limit_bytes=8 * MIB),
        cost_estimate=pl.CostEstimate(flops=10**9, bytes_accessed=4 * MIB, transcendentals=0),
        name="rest",
    )(pre, order, near, far, kept, mixed)
    half = rows // 2
    term = (keep + got.astype(jnp.float32)).astype(jnp.bfloat16)
    received = lax.all_to_all(term, "narrow", 0, 0, tiled=True)
    owned = jnp.sum(received.reshape(narrow, half, PACKED).astype(jnp.float32), axis=0).astype(jnp.bfloat16)
    parts = lax.all_to_all(jnp.broadcast_to(owned[None], (wide, half, PACKED)), WIDE, 0, 0, tiled=True)
    total = jnp.sum(parts.reshape(wide // 2, rows, PACKED).astype(jnp.float32), axis=0)
    weight_grad = pl.pallas_call(
        finish_kernel,
        out_shape=jax.ShapeDtypeStruct((27, rows, C1), jnp.float32),
        compiler_params=pltpu.CompilerParams(vmem_limit_bytes=8 * MIB),
        name="finish",
    )(total)
    return (output, weight_grad)


def solution(mesh):
    wide, narrow = mesh.devices.shape
    split = jax.sharding.Mesh(mesh.devices.reshape(wide // 2, 2, narrow), ("chip", "core", "narrow"))
    return jax.shard_map(
        body,
        mesh=split,
        in_specs=(P("narrow", None, None, WIDE, None), P(), P(), P("narrow", None, None, WIDE)),
        out_specs=(P("narrow", None, None, WIDE), P(None, "narrow", None)),
        check_vma=False,
    )
```

```python
import functools
import math

import jax
import jax.numpy as jnp
import numpy as np
from jax import lax
from jax.experimental import pallas as pl
from jax.experimental.pallas import tpu as pltpu
from jax.sharding import PartitionSpec as P

CIN = 4
C1 = 32
C2 = 64
PLANES = 4
CELLS = 4096
HALF = 32
PLANE = 1024
LANES = 128
ROWS = CIN * PLANES
CHUNK = 512
PACKED = 7 * LANES
MIB = 2**20
WIDE = ("chip", "core")
neg_slope = 0.3


def selection():
    table = np.zeros((CHUNK, 2, 2, 4, HALF), np.float32)
    for py in range(2):
        for px in range(2):
            for row in range(4):
                for col in range(HALF):
                    table[(2 * row + py) * 64 + 2 * col + px, py, px, row, col] = 1
    return table.reshape(CHUNK, CHUNK)


def placement():
    table = np.zeros((2, 27, CIN, 4, CHUNK), np.float32)
    for odd in range(2):
        for a in range(3):
            for bc in range(9):
                for i in range(CIN):
                    for q in range(4):
                        slab, plane = divmod(2 * q + a + 1, PLANES)
                        inner = i * PLANES + plane
                        if slab == 1:
                            column = bc * 2 * ROWS + inner
                        elif (slab == 0) == (odd == 1):
                            column = bc * 2 * ROWS + ROWS + inner
                        else:
                            column = 18 * ROWS + bc * ROWS + inner
                        table[odd, 9 * a + bc, i, q, column] = 1
    return table.reshape(2, 27 * CIN, 4 * CHUNK)


def channel_order(narrow):
    half = C2 // (2 * narrow)
    table = np.zeros((2, 2 * C2, 2 * C2), np.float32)
    for odd in range(2):
        for z in range(2):
            for o in range(C2):
                owner, inner = divmod(o, 2 * half)
                side, row = divmod(inner, half)
                table[odd, z * C2 + o, (side == odd) * C2 + z * C1 + owner * half + row] = 1
    return table


def leaky_relu(value):
    return jnp.where(value > 0, value, neg_slope * value)


def plane_rows(volume_ref):
    return jnp.concatenate([volume_ref[0, 0, i] for i in range(CIN)], axis=0)


def column_masks():
    column = lax.broadcasted_iota(jnp.int32, (1, PLANE), 1) % HALF
    left_ok = jnp.where(column > 0, 1.0, 0.0).astype(jnp.bfloat16)
    right_ok = jnp.where(column < HALF - 1, 1.0, 0.0).astype(jnp.bfloat16)
    return left_ok, right_ok


def strided_taps(rows, select_ref, parity_ref, taps_ref):
    count = rows.shape[0]
    left_ok, _ = column_masks()
    chunks = jnp.concatenate([rows[:, CHUNK * j : CHUNK * (j + 1)] for j in range(8)], axis=0)
    for p in range(4):
        parity_ref[p, :, 0:LANES] = jnp.zeros((count, LANES), jnp.bfloat16)
    for py in range(2):
        parts = jnp.dot(
            chunks, select_ref[:, 256 * py : 256 * py + 256], preferred_element_type=jnp.float32
        ).astype(jnp.bfloat16)
        for px in range(2):
            for j in range(8):
                parity_ref[2 * py + px, :, LANES * (j + 1) : LANES * (j + 2)] = parts[
                    j * count : (j + 1) * count, px * LANES : (px + 1) * LANES
                ]
    for b in range(3):
        for c in range(3):
            begin = LANES - HALF * (b == 0) - (c == 0)
            part = parity_ref[2 * (b != 1) + (c != 1), :, begin : begin + PLANE]
            if c == 0:
                part = part * left_ok
            taps_ref[(3 * b + c) * count : (3 * b + c + 1) * count, :] = part


def shifted_columns(act_ref, columns_ref):
    left_ok, right_ok = column_masks()
    for c in range(3):
        begin = LANES + c - 1
        part = act_ref[:, begin : begin + PLANE]
        if c == 0:
            part = part * left_ok
        if c == 2:
            part = part * right_ok
        columns_ref[c * 2 * C1 : (c + 1) * 2 * C1, :] = part


def second_layer(w2, columns_ref, turned_ref, rowed_ref):
    blank = jnp.zeros((HALF, LANES), jnp.float32)
    for b in (0, 2):
        rowed_ref[b, 0:HALF, :] = blank
        rowed_ref[b, HALF + PLANE :, :] = blank
    for n in range(4):
        cells = slice(256 * n, 256 * n + 256)
        turned_ref[cells, :] = columns_ref[:, cells].T
    for n in range(4):
        sums = jnp.dot(turned_ref[256 * n : 256 * n + 256, :], w2, preferred_element_type=jnp.float32)
        for b in range(3):
            rowed_ref[b, HALF + 256 * n : HALF + 256 * n + 256, :] = sums[:, b * LANES : (b + 1) * LANES]


def row_sum(rowed_ref, n):
    begins = [HALF * b + 256 * n for b in range(3)]
    first, second, third = (rowed_ref[b, begin : begin + 256, :] for b, begin in enumerate(begins))
    return first + second + third


def clear_margins(act_ref):
    margin = jnp.zeros((2 * C1, LANES), jnp.bfloat16)
    act_ref[:, 0:LANES] = margin
    act_ref[:, LANES + PLANE :] = margin


def prepare_kernel(
    k1_hbm, place_hbm, k2_hbm, select_hbm, cot_hbm, order_hbm,
    w1_near_ref, w1_far_ref, w2_ref, select_ref, turned_ref, order_ref,
    k1_ref, place_ref, k2_ref, cot_ref, k1_rows_ref, k2_rows_ref, sems,
):
    odd = lax.axis_index("core")
    moves = (
        (k1_hbm, k1_ref), (k2_hbm, k2_ref), (order_hbm.at[odd], order_ref),
        (place_hbm.at[odd], place_ref), (cot_hbm, cot_ref), (select_hbm, select_ref),
    )
    copies = [pltpu.make_async_copy(src, dst, sems.at[k]) for k, (src, dst) in enumerate(moves)]
    for copy in copies:
        copy.start()
    copies[0].wait()
    for tap in range(27):
        k1_rows_ref[CIN * tap : CIN * (tap + 1), :] = k1_ref[tap].astype(jnp.float32)
    copies[1].wait()
    blank = jnp.zeros((C1, C2), jnp.bfloat16)

    def stacked(bc, pair):
        k = [blank] + [k2_ref[9 * a + bc] for a in range(3)] + [blank]
        lower = jnp.concatenate(k[1 + 2 * pair : 3 + 2 * pair], axis=0)
        upper = jnp.concatenate(k[2 * pair : 2 + 2 * pair], axis=0)
        return jnp.concatenate([lower, upper], axis=1)

    for pair in range(2):
        for bc in range(9):
            begin = (9 * pair + bc) * 2 * C1
            k2_rows_ref[begin : begin + 2 * C1, :] = stacked(bc, pair)
    copies[2].wait()
    ordered = jnp.dot(k2_rows_ref[...], order_ref[...], preferred_element_type=jnp.float32).astype(jnp.bfloat16)
    for pair in range(2):
        for b in range(3):
            for c in range(3):
                begin = (9 * pair + 3 * b + c) * 2 * C1
                w2_ref[pair, c * 2 * C1 : (c + 1) * 2 * C1, b * LANES : (b + 1) * LANES] = ordered[begin : begin + 2 * C1]
    copies[3].wait()
    spread = lax.dot_general(
        k1_rows_ref[...].astype(jnp.bfloat16), place_ref[...],
        (((0,), (0,)), ((), ())), preferred_element_type=jnp.float32,
    ).astype(jnp.bfloat16)
    for q in range(4):
        rows = slice(q % 2 * C1, (q % 2 + 1) * C1)
        w1_near_ref[q // 2, rows, :] = spread[:, CHUNK * q : CHUNK * q + 18 * ROWS]
        w1_far_ref[q // 2, rows, :] = spread[:, CHUNK * q + 18 * ROWS : CHUNK * q + 27 * ROWS]
    copies[4].wait()
    for n in range(4):
        planes = [cot_ref[0, 0, :, z * PLANE + 256 * n : z * PLANE + 256 * n + 256] for z in range(2)]
        turned = jnp.concatenate(planes, axis=0).T
        turned_ref[256 * n : 256 * n + 256, :] = jnp.dot(
            turned, order_ref[...], preferred_element_type=jnp.float32
        ).astype(jnp.bfloat16)
    copies[5].wait()


def near_kernel(
    own_ref, within_ref, select_ref, w1_ref, w2_ref, first_ref, columns_ref, pre_ref,
    parity_ref, taps_ref, act_ref, turned_ref, rowed_ref,
):
    odd = lax.axis_index("core")
    rows = jnp.concatenate([plane_rows(own_ref), plane_rows(within_ref)], axis=0)
    strided_taps(rows, select_ref, parity_ref, taps_ref)
    clear_margins(act_ref)
    for n in range(4):
        here = slice(256 * n, 256 * n + 256)
        first_ref[:, here] = jnp.dot(w1_ref[odd], taps_ref[:, here], preferred_element_type=jnp.float32)
        complete = jnp.dot(w1_ref[1 - odd], taps_ref[:, here], preferred_element_type=jnp.float32)
        act_ref[:, LANES + 256 * n : LANES + 256 * n + 256] = leaky_relu(complete).astype(jnp.bfloat16)
    shifted_columns(act_ref, columns_ref)
    second_layer(w2_ref[1 - odd], columns_ref, turned_ref, rowed_ref)
    for n in range(4):
        pre_ref[256 * n : 256 * n + 256, :] = row_sum(rowed_ref, n)


def slots():
    where = {}
    for a in range(3):
        for b in range(3):
            for c in range(3):
                slot, side = divmod(3 * a + c, 2)
                where[9 * a + 3 * b + c] = (2 * b + side, slot) if slot < 4 else (6, (0, 2, 1)[b])
    return where


def group_of_lane():
    return lax.broadcasted_iota(jnp.int32, (C1, LANES), 1) // C1


def paired_terms(sums_ref, tile):
    even = group_of_lane() % 2 == 0

    def plane(q, c):
        begin = 2 * C1 * c + C1 * (q % 2)
        return sums_ref[q // 2, begin : begin + C1, tile * LANES : (tile + 1) * LANES]

    terms = [plane(a, c) + pltpu.roll(plane(a + 1, c), 3 * C1, 1) for a in range(3) for c in range(3)]
    return [jnp.where(even, terms[k], pltpu.roll(terms[k + 1], C1, 1)) for k in range(0, 8, 2)] + [terms[8]]


def turned_groups(blocks, scale):
    flat = (jnp.concatenate(blocks, axis=0) * scale).T
    return [flat[g * C1 : (g + 1) * C1] for g in range(4)]


def first_two_rows(left_ref, right_ref):
    low = lax.broadcasted_iota(jnp.int32, (1, LANES), 1) < C2
    return jnp.where(low, left_ref[2 * HALF : 2 * HALF + PLANE, :], right_ref[HALF : HALF + PLANE, :])


def gradient_sums(odd, near_ref, far_ref, backs, sums_ref):
    columns = jnp.concatenate([near_ref[...], far_ref[...]], axis=0)
    sums = jnp.dot(columns, backs, preferred_element_type=jnp.float32)
    sums_ref[1 - odd] = sums[0 : 6 * C1]
    sums_ref[odd] = sums[6 * C1 :]


def far_kernel(
    chips, scale, across_ref, select_ref, w1_ref, w2_ref, cot_ref, first_ref, near_ref, near_pre_ref,
    pre_ref, give_ref, keep_ref, columns_ref, back_ref, swapped_ref,
    parity_ref, taps_ref, act_ref, turned_ref, rowed_ref, sums_ref,
):
    odd = lax.axis_index("core")
    last = (lax.axis_index("chip") == chips - 1) & (odd == 1)
    inside = jnp.where(last, 0.0, 1.0)
    strided_taps(plane_rows(across_ref), select_ref, parity_ref, taps_ref)
    clear_margins(act_ref)
    for n in range(4):
        here = slice(256 * n, 256 * n + 256)
        first_pre = first_ref[:, here] + jnp.dot(w1_ref[odd], taps_ref[:, here], preferred_element_type=jnp.float32)
        first_act = leaky_relu(first_pre)
        there = slice(LANES + 256 * n, LANES + 256 * n + 256)
        act_ref[0:C1, there] = first_act[0:C1].astype(jnp.bfloat16)
        act_ref[C1:, there] = (first_act[C1:] * inside).astype(jnp.bfloat16)
    shifted_columns(act_ref, columns_ref)
    second_layer(w2_ref[odd], columns_ref, turned_ref, rowed_ref)

    margin = jnp.zeros((HALF, LANES), jnp.bfloat16)
    for ref in (back_ref, swapped_ref):
        ref[0:HALF, :] = margin
        ref[HALF + PLANE :, :] = margin
    for n in range(4):
        cells = slice(256 * n, 256 * n + 256)
        pre = near_pre_ref[cells, :] + row_sum(rowed_ref, n)
        pre_ref[cells, :] = pre
        back = (cot_ref[cells, :].astype(jnp.float32) * jnp.where(pre > 0, 1.0, neg_slope)).astype(jnp.bfloat16)
        here = slice(HALF + 256 * n, HALF + 256 * n + 256)
        back_ref[here, :] = back
        swapped_ref[here, :] = jnp.concatenate([back[:, C2:], back[:, 0:C2]], axis=1)
    given = first_two_rows(back_ref, swapped_ref)
    mixed = back_ref[0:PLANE, :]
    gradient_sums(odd, near_ref, columns_ref, jnp.concatenate([given, mixed], axis=1), sums_ref)
    given, mixed = paired_terms(sums_ref, 0), paired_terms(sums_ref, 1)
    first = turned_groups(given[0:4], scale)
    second = turned_groups(mixed[0:4], scale)
    third = turned_groups([given[4], mixed[4], given[4], mixed[4]], scale)
    group = group_of_lane()
    tiles = first + second[0:2] + [jnp.where(group < 2, third[0], pltpu.roll(third[2], C2, 1))]
    for k, tile in enumerate(tiles):
        give_ref[:, k * LANES : (k + 1) * LANES] = tile.astype(jnp.bfloat16)
    for k, tile in enumerate((second[2], second[3], third[2])):
        keep_ref[:, k * LANES : (k + 1) * LANES] = tile


def rest_kernel(
    scale, pre_ref, order_ref, near_ref, far_ref, back_ref, swapped_ref, mixed_ref, out_hbm, keep_ref, sums_ref, out_ref, out_sem,
):
    for n in range(4):
        output = leaky_relu(pre_ref[256 * n : 256 * n + 256, :]).astype(jnp.bfloat16)
        ordered = lax.dot_general(
            order_ref[...], output, (((1,), (1,)), ((), ())), preferred_element_type=jnp.float32
        ).astype(jnp.bfloat16)
        for z in range(2):
            out_ref[0, 0, :, z * PLANE + 256 * n : z * PLANE + 256 * n + 256] = ordered[z * C2 : (z + 1) * C2]
    out_copy = pltpu.make_async_copy(out_ref, out_hbm, out_sem)
    out_copy.start()
    odd = lax.axis_index("core")
    gradient_sums(odd, near_ref, far_ref, first_two_rows(swapped_ref, back_ref), sums_ref)
    kept = paired_terms(sums_ref, 0)
    first = turned_groups(kept[0:4], scale)
    third = turned_groups([kept[4]] * 4, scale)
    group = group_of_lane()
    mixed = [mixed_ref[:, k * LANES : (k + 1) * LANES] for k in range(3)]
    ends = jnp.where(group == 1, mixed[2], jnp.where(group == 0, third[0], pltpu.roll(third[2], C2, 1)))
    for k, tile in enumerate(first + mixed[0:2] + [ends]):
        keep_ref[:, k * LANES : (k + 1) * LANES] = tile
    out_copy.wait()


def finish_kernel(total_ref, grad_hbm, grad_ref, sems):
    where = slots()
    copies = []
    for k in range(3):
        for tap in range(9 * k, 9 * k + 9):
            tile, slot = where[tap]
            begin = tile * LANES + slot * C1
            grad_ref[tap] = total_ref[:, begin : begin + C1]
        here = slice(9 * k, 9 * k + 9)
        copies.append(pltpu.make_async_copy(grad_ref.at[here], grad_hbm.at[here], sems.at[k]))
        copies[k].start()
    for copy in copies:
        copy.wait()


def body(volumes, first_kernel, second_kernel, cotangent):
    wide = lax.axis_size(WIDE)
    narrow = lax.axis_size("narrow")
    cells_out = cotangent.shape[3]
    scale = 1.0 / math.sqrt(wide * narrow * cells_out)
    across = lax.ppermute(volumes, WIDE, [p for k in range(1, wide - 1, 2) for p in ((k, k + 1), (k + 1, k))])
    pairs = [p for k in range(0, wide - 1, 2) for p in ((k, k + 1), (k + 1, k))]
    within = lax.ppermute(volumes, WIDE, pairs)
    pinned = pl.BlockSpec(memory_space=pltpu.HBM)
    fast = pl.BlockSpec(memory_space=pltpu.VMEM)
    bf16 = functools.partial(jax.ShapeDtypeStruct, dtype=jnp.bfloat16)
    f32 = functools.partial(jax.ShapeDtypeStruct, dtype=jnp.float32)
    stored = (
        first_kernel.transpose(0, 2, 1), jnp.asarray(placement(), jnp.bfloat16), second_kernel.transpose(0, 2, 1),
        jnp.asarray(selection(), jnp.bfloat16), cotangent, jnp.asarray(channel_order(narrow), jnp.bfloat16),
    )
    w1_near, w1_far, w2, select, cot, order = pl.pallas_call(
        prepare_kernel,
        in_specs=[pinned] * 6,
        out_specs=(fast,) * 6,
        out_shape=(
            bf16((2, 2 * C1, 18 * ROWS)), bf16((2, 2 * C1, 9 * ROWS)), bf16((2, 6 * C1, 6 * C2)),
            bf16((CHUNK, CHUNK)), bf16((PLANE, 2 * C2)), bf16((2 * C2, 2 * C2)),
        ),
        scratch_shapes=[
            pltpu.VMEM((27, CIN, C1), jnp.bfloat16),
            pltpu.VMEM((27 * CIN, 4 * CHUNK), jnp.bfloat16),
            pltpu.VMEM((27, C1, C2), jnp.bfloat16),
            pltpu.VMEM(cotangent.shape, jnp.bfloat16),
            pltpu.VMEM((27 * CIN, C1), jnp.float32),
            pltpu.VMEM((36 * C1, 2 * C2), jnp.bfloat16),
            pltpu.SemaphoreType.DMA((6,)),
        ],
        compiler_params=pltpu.CompilerParams(vmem_limit_bytes=12 * MIB),
        cost_estimate=pl.CostEstimate(flops=10**9, bytes_accessed=4 * MIB, transcendentals=0),
        name="prepare",
    )(*(pltpu.with_memory_space_constraint(x, pltpu.HBM) for x in stored))
    first, near, pre = pl.pallas_call(
        near_kernel,
        in_specs=[fast] * 5,
        out_specs=(fast,) * 3,
        out_shape=(f32((2 * C1, PLANE)), bf16((6 * C1, PLANE)), f32((PLANE, 2 * C2))),
        scratch_shapes=[
            pltpu.VMEM((4, 2 * ROWS, LANES + PLANE), jnp.bfloat16),
            pltpu.VMEM((18 * ROWS, PLANE), jnp.bfloat16),
            pltpu.VMEM((2 * C1, PLANE + 2 * LANES), jnp.bfloat16),
            pltpu.VMEM((PLANE, 6 * C1), jnp.bfloat16),
            pltpu.VMEM((3, PLANE + 2 * HALF, LANES), jnp.float32),
        ],
        compiler_params=pltpu.CompilerParams(vmem_limit_bytes=16 * MIB),
        cost_estimate=pl.CostEstimate(flops=10**9, bytes_accessed=4 * MIB, transcendentals=0),
        name="near",
    )(volumes, within, select, w1_near, w2)
    rows = C2 // narrow
    pre, give, mixed, far, back, swapped = pl.pallas_call(
        functools.partial(far_kernel, wide // 2, scale),
        in_specs=[fast] * 8,
        out_specs=(fast,) * 6,
        out_shape=(
            f32((PLANE, 2 * C2)), bf16((C2 // 2, PACKED)), f32((C2 // 2, 3 * LANES)),
            bf16((6 * C1, PLANE)), bf16((PLANE + 2 * HALF, LANES)), bf16((PLANE + 2 * HALF, LANES)),
        ),
        scratch_shapes=[
            pltpu.VMEM((4, ROWS, LANES + PLANE), jnp.bfloat16),
            pltpu.VMEM((9 * ROWS, PLANE), jnp.bfloat16),
            pltpu.VMEM((2 * C1, PLANE + 2 * LANES), jnp.bfloat16),
            pltpu.VMEM((PLANE, 6 * C1), jnp.bfloat16),
            pltpu.VMEM((3, PLANE + 2 * HALF, LANES), jnp.float32),
            pltpu.VMEM((2, 6 * C1, 2 * LANES), jnp.float32),
        ],
        compiler_params=pltpu.CompilerParams(vmem_limit_bytes=16 * MIB),
        cost_estimate=pl.CostEstimate(flops=10**9, bytes_accessed=4 * MIB, transcendentals=0),
        name="far",
    )(across, select, w1_far, w2, cot, first, near, pre)
    got = lax.ppermute(give, WIDE, pairs)
    output, keep = pl.pallas_call(
        functools.partial(rest_kernel, scale),
        in_specs=[fast] * 7,
        out_specs=(pl.BlockSpec(memory_space=pl.ANY), fast),
        out_shape=(bf16((1, 1, C2, cells_out)), f32((C2 // 2, PACKED))),
        scratch_shapes=[
            pltpu.VMEM((2, 6 * C1, LANES), jnp.float32),
            pltpu.VMEM((1, 1, C2, cells_out), jnp.bfloat16),
            pltpu.SemaphoreType.DMA,
        ],
        compiler_params=pltpu.CompilerParams(vmem_limit_bytes=8 * MIB),
        cost_estimate=pl.CostEstimate(flops=10**9, bytes_accessed=4 * MIB, transcendentals=0),
        name="rest",
    )(pre, order, near, far, back, swapped, mixed)
    half = rows // 2
    term = (keep + got.astype(jnp.float32)).astype(jnp.bfloat16)
    received = lax.all_to_all(term, "narrow", 0, 0, tiled=True)
    owned = jnp.sum(received.reshape(narrow, half, PACKED).astype(jnp.float32), axis=0).astype(jnp.bfloat16)
    parts = lax.all_to_all(jnp.broadcast_to(owned[None], (wide, half, PACKED)), WIDE, 0, 0, tiled=True)
    total = jnp.sum(parts.reshape(wide // 2, rows, PACKED).astype(jnp.float32), axis=0)
    weight_grad = pl.pallas_call(
        finish_kernel,
        in_specs=[fast],
        out_specs=pl.BlockSpec(memory_space=pl.ANY),
        out_shape=f32((27, rows, C1)),
        scratch_shapes=[pltpu.VMEM((27, rows, C1), jnp.float32), pltpu.SemaphoreType.DMA((3,))],
        compiler_params=pltpu.CompilerParams(vmem_limit_bytes=8 * MIB),
        name="finish",
    )(total)
    return (output, weight_grad)


def solution(mesh):
    wide, narrow = mesh.devices.shape
    split = jax.sharding.Mesh(mesh.devices.reshape(wide // 2, 2, narrow), ("chip", "core", "narrow"))
    return jax.shard_map(
        body,
        mesh=split,
        in_specs=(P("narrow", None, None, WIDE, None), P(), P(), P("narrow", None, None, WIDE)),
        out_specs=(P("narrow", None, None, WIDE), P(None, "narrow", None)),
        check_vma=False,
    )
```

```python
import functools
import math

import jax
import jax.numpy as jnp
import numpy as np
from jax import lax
from jax.experimental import pallas as pl
from jax.experimental.pallas import tpu as pltpu
from jax.sharding import PartitionSpec as P

CIN = 4
C1 = 32
C2 = 64
PLANES = 4
CELLS = 4096
HALF = 32
PLANE = 1024
LANES = 128
ROWS = CIN * PLANES
CHUNK = 512
PACKED = 7 * LANES
MIB = 2**20
WIDE = ("chip", "core")
neg_slope = 0.3


def selection():
    table = np.zeros((CHUNK, 2, 2, 4, HALF), np.float32)
    for py in range(2):
        for px in range(2):
            for row in range(4):
                for col in range(HALF):
                    table[(2 * row + py) * 64 + 2 * col + px, py, px, row, col] = 1
    return table.reshape(CHUNK, CHUNK)


def placement():
    table = np.zeros((2, 27, CIN, 4, CHUNK), np.float32)
    for odd in range(2):
        for a in range(3):
            for bc in range(9):
                for i in range(CIN):
                    for q in range(4):
                        slab, plane = divmod(2 * q + a + 1, PLANES)
                        inner = i * PLANES + plane
                        if slab == 1:
                            column = bc * 2 * ROWS + inner
                        elif (slab == 0) == (odd == 1):
                            column = bc * 2 * ROWS + ROWS + inner
                        else:
                            column = 18 * ROWS + bc * ROWS + inner
                        table[odd, 9 * a + bc, i, q, column] = 1
    return table.reshape(2, 27 * CIN, 4 * CHUNK)


def leaky_relu(value):
    return jnp.where(value > 0, value, neg_slope * value)


def plane_rows(volume_ref):
    return jnp.concatenate([volume_ref[0, 0, i] for i in range(CIN)], axis=0)


def column_masks():
    column = lax.broadcasted_iota(jnp.int32, (1, PLANE), 1) % HALF
    left_ok = jnp.where(column > 0, 1.0, 0.0).astype(jnp.bfloat16)
    right_ok = jnp.where(column < HALF - 1, 1.0, 0.0).astype(jnp.bfloat16)
    return left_ok, right_ok


def strided_taps(rows, select_ref, parity_ref, taps_ref):
    count = rows.shape[0]
    left_ok, _ = column_masks()
    chunks = jnp.concatenate([rows[:, CHUNK * j : CHUNK * (j + 1)] for j in range(8)], axis=0)
    for p in range(4):
        parity_ref[p, :, 0:LANES] = jnp.zeros((count, LANES), jnp.bfloat16)
    for py in range(2):
        parts = jnp.dot(
            chunks, select_ref[:, 256 * py : 256 * py + 256], preferred_element_type=jnp.float32
        ).astype(jnp.bfloat16)
        for px in range(2):
            for j in range(8):
                parity_ref[2 * py + px, :, LANES * (j + 1) : LANES * (j + 2)] = parts[
                    j * count : (j + 1) * count, px * LANES : (px + 1) * LANES
                ]
    for b in range(3):
        for c in range(3):
            begin = LANES - HALF * (b == 0) - (c == 0)
            part = parity_ref[2 * (b != 1) + (c != 1), :, begin : begin + PLANE]
            if c == 0:
                part = part * left_ok
            taps_ref[(3 * b + c) * count : (3 * b + c + 1) * count, :] = part


def shifted_columns(act_ref, columns_ref):
    left_ok, right_ok = column_masks()
    for c in range(3):
        begin = LANES + c - 1
        part = act_ref[:, begin : begin + PLANE]
        if c == 0:
            part = part * left_ok
        if c == 2:
            part = part * right_ok
        columns_ref[c * 2 * C1 : (c + 1) * 2 * C1, :] = part


def second_layer(w2, columns_ref, turned_ref, rowed_ref):
    blank = jnp.zeros((HALF, LANES), jnp.float32)
    for b in (0, 2):
        rowed_ref[b, 0:HALF, :] = blank
        rowed_ref[b, HALF + PLANE :, :] = blank
    for n in range(4):
        cells = slice(256 * n, 256 * n + 256)
        turned_ref[cells, :] = columns_ref[:, cells].T
    for n in range(4):
        sums = jnp.dot(turned_ref[256 * n : 256 * n + 256, :], w2, preferred_element_type=jnp.float32)
        for b in range(3):
            rowed_ref[b, HALF + 256 * n : HALF + 256 * n + 256, :] = sums[:, b * LANES : (b + 1) * LANES]


def row_sum(rowed_ref, n):
    begins = [HALF * b + 256 * n for b in range(3)]
    first, second, third = (rowed_ref[b, begin : begin + 256, :] for b, begin in enumerate(begins))
    return first + second + third


def clear_margins(act_ref):
    margin = jnp.zeros((2 * C1, LANES), jnp.bfloat16)
    act_ref[:, 0:LANES] = margin
    act_ref[:, LANES + PLANE :] = margin


def prepare_kernel(
    k1_hbm, place_hbm, k2_hbm, select_hbm, cot_hbm,
    w1_near_ref, w1_far_ref, w2_ref, select_ref, turned_ref,
    k1_ref, place_ref, k2_ref, cot_ref, k1_rows_ref, sems,
):
    odd = lax.axis_index("core")
    moves = (
        (k1_hbm, k1_ref), (k2_hbm, k2_ref), (place_hbm.at[odd], place_ref), (cot_hbm, cot_ref), (select_hbm, select_ref),
    )
    copies = [pltpu.make_async_copy(src, dst, sems.at[k]) for k, (src, dst) in enumerate(moves)]
    for copy in copies:
        copy.start()
    copies[0].wait()
    for tap in range(27):
        k1_rows_ref[CIN * tap : CIN * (tap + 1), :] = k1_ref[tap].astype(jnp.float32)
    copies[1].wait()
    blank = jnp.zeros((C1, C2), jnp.bfloat16)

    def stacked(bc, pair):
        k = [blank] + [k2_ref[9 * a + bc] for a in range(3)] + [blank]
        lower = jnp.concatenate(k[1 + 2 * pair : 3 + 2 * pair], axis=0)
        upper = jnp.concatenate(k[2 * pair : 2 + 2 * pair], axis=0)
        return jnp.concatenate([lower, upper], axis=1)

    for pair in range(2):
        for b in range(3):
            for c in range(3):
                w2_ref[pair, c * 2 * C1 : (c + 1) * 2 * C1, b * LANES : (b + 1) * LANES] = stacked(3 * b + c, pair)
    copies[2].wait()
    spread = lax.dot_general(
        k1_rows_ref[...].astype(jnp.bfloat16), place_ref[...],
        (((0,), (0,)), ((), ())), preferred_element_type=jnp.float32,
    ).astype(jnp.bfloat16)
    for q in range(4):
        rows = slice(q % 2 * C1, (q % 2 + 1) * C1)
        w1_near_ref[q // 2, rows, :] = spread[:, CHUNK * q : CHUNK * q + 18 * ROWS]
        w1_far_ref[q // 2, rows, :] = spread[:, CHUNK * q + 18 * ROWS : CHUNK * q + 27 * ROWS]
    copies[3].wait()
    for n in range(4):
        planes = [cot_ref[0, 0, :, z * PLANE + 256 * n : z * PLANE + 256 * n + 256] for z in range(2)]
        turned_ref[256 * n : 256 * n + 256, :] = jnp.concatenate(planes, axis=0).T
    copies[4].wait()


def near_kernel(
    own_ref, within_ref, select_ref, w1_ref, w2_ref, first_ref, columns_ref, pre_ref,
    parity_ref, taps_ref, act_ref, turned_ref, rowed_ref,
):
    odd = lax.axis_index("core")
    rows = jnp.concatenate([plane_rows(own_ref), plane_rows(within_ref)], axis=0)
    strided_taps(rows, select_ref, parity_ref, taps_ref)
    clear_margins(act_ref)
    for n in range(4):
        here = slice(256 * n, 256 * n + 256)
        first_ref[:, here] = jnp.dot(w1_ref[odd], taps_ref[:, here], preferred_element_type=jnp.float32)
        complete = jnp.dot(w1_ref[1 - odd], taps_ref[:, here], preferred_element_type=jnp.float32)
        act_ref[:, LANES + 256 * n : LANES + 256 * n + 256] = leaky_relu(complete).astype(jnp.bfloat16)
    shifted_columns(act_ref, columns_ref)
    second_layer(w2_ref[1 - odd], columns_ref, turned_ref, rowed_ref)
    for n in range(4):
        pre_ref[256 * n : 256 * n + 256, :] = row_sum(rowed_ref, n)


def far_kernel(
    chips, scale, across_ref, select_ref, w1_ref, w2_ref, cot_ref, first_ref, near_ref, near_pre_ref, out_hbm, grad_ref,
    parity_ref, taps_ref, act_ref, columns_ref, turned_ref, rowed_ref, back_ref, sums_ref, out_ref, out_sem,
):
    odd = lax.axis_index("core")
    last = (lax.axis_index("chip") == chips - 1) & (odd == 1)
    inside = jnp.where(last, 0.0, 1.0)
    strided_taps(plane_rows(across_ref), select_ref, parity_ref, taps_ref)
    clear_margins(act_ref)
    for n in range(4):
        here = slice(256 * n, 256 * n + 256)
        first_pre = first_ref[:, here] + jnp.dot(w1_ref[odd], taps_ref[:, here], preferred_element_type=jnp.float32)
        first_act = leaky_relu(first_pre)
        there = slice(LANES + 256 * n, LANES + 256 * n + 256)
        act_ref[0:C1, there] = first_act[0:C1].astype(jnp.bfloat16)
        act_ref[C1:, there] = (first_act[C1:] * inside).astype(jnp.bfloat16)
    shifted_columns(act_ref, columns_ref)
    second_layer(w2_ref[odd], columns_ref, turned_ref, rowed_ref)
    margin = jnp.zeros((HALF, LANES), jnp.bfloat16)
    back_ref[0:HALF, :] = margin
    back_ref[HALF + PLANE :, :] = margin
    for n in range(4):
        cells = slice(256 * n, 256 * n + 256)
        pre = near_pre_ref[cells, :] + row_sum(rowed_ref, n)
        back = cot_ref[cells, :].astype(jnp.float32) * jnp.where(pre > 0, 1.0, neg_slope)
        back_ref[HALF + 256 * n : HALF + 256 * n + 256, :] = back.astype(jnp.bfloat16)
        output = leaky_relu(pre).astype(jnp.bfloat16).T
        for z in range(2):
            out_ref[0, 0, :, z * PLANE + 256 * n : z * PLANE + 256 * n + 256] = output[z * C2 : (z + 1) * C2]
    out_copy = pltpu.make_async_copy(out_ref, out_hbm, out_sem)
    out_copy.start()
    columns = jnp.concatenate([near_ref[...], columns_ref[...]], axis=0)
    rowed_back = jnp.concatenate([back_ref[(2 - b) * HALF : (2 - b) * HALF + PLANE, :] for b in range(3)], axis=1)
    sums = jnp.dot(columns, rowed_back, preferred_element_type=jnp.float32)
    sums_ref[1 - odd] = sums[0 : 6 * C1]
    sums_ref[odd] = sums[6 * C1 :]
    low = lax.broadcasted_iota(jnp.int32, (C1, LANES), 1) < C2

    def plane_sums(bc, q):
        b, c = divmod(bc, 3)
        begin = 2 * C1 * c + C1 * (q % 2)
        return sums_ref[q // 2, begin : begin + C1, b * LANES : (b + 1) * LANES]

    def two_taps(first, second):
        a, bc = divmod(first, 9)
        here, above = plane_sums(bc, a), pltpu.roll(plane_sums(bc, a + 1), C2, 1)
        if second > 26:
            return here + above
        a, bc = divmod(second, 9)
        there, beyond = pltpu.roll(plane_sums(bc, a), C2, 1), plane_sums(bc, a + 1)
        return jnp.where(low, here, there) + jnp.where(low, above, beyond)

    for block in range(4):
        tall = jnp.concatenate([two_taps(min(8 * block + g, 26), 8 * block + 4 + g) for g in range(4)], axis=0)
        flat = (tall * scale).T.astype(jnp.bfloat16)
        grad_ref[:, 2 * block * LANES : (2 * block + 1) * LANES] = flat[0:C2]
        if block < 3:
            grad_ref[:, (2 * block + 1) * LANES : (2 * block + 2) * LANES] = flat[C2:]
    out_copy.wait()


def finish_kernel(total_ref, grad_hbm, grad_ref, sems):
    copies = []
    for k in range(3):
        for tap in range(9 * k, 9 * k + 9):
            grad_ref[tap] = total_ref[:, tap * C1 : (tap + 1) * C1]
        here = slice(9 * k, 9 * k + 9)
        copies.append(pltpu.make_async_copy(grad_ref.at[here], grad_hbm.at[here], sems.at[k]))
        copies[k].start()
    for copy in copies:
        copy.wait()


def body(volumes, first_kernel, second_kernel, cotangent):
    wide = lax.axis_size(WIDE)
    narrow = lax.axis_size("narrow")
    cells_out = cotangent.shape[3]
    scale = 1.0 / math.sqrt(wide * narrow * cells_out)
    across = lax.ppermute(volumes, WIDE, [p for k in range(1, wide - 1, 2) for p in ((k, k + 1), (k + 1, k))])
    pairs = [p for k in range(0, wide - 1, 2) for p in ((k, k + 1), (k + 1, k))]
    within = lax.ppermute(volumes, WIDE, pairs)
    pinned = pl.BlockSpec(memory_space=pltpu.HBM)
    fast = pl.BlockSpec(memory_space=pltpu.VMEM)
    bf16 = functools.partial(jax.ShapeDtypeStruct, dtype=jnp.bfloat16)
    f32 = functools.partial(jax.ShapeDtypeStruct, dtype=jnp.float32)
    stored = (
        first_kernel.transpose(0, 2, 1), jnp.asarray(placement(), jnp.bfloat16), second_kernel.transpose(0, 2, 1),
        jnp.asarray(selection(), jnp.bfloat16), cotangent,
    )
    w1_near, w1_far, w2, select, cot = pl.pallas_call(
        prepare_kernel,
        in_specs=[pinned] * 5,
        out_specs=(fast,) * 5,
        out_shape=(
            bf16((2, 2 * C1, 18 * ROWS)), bf16((2, 2 * C1, 9 * ROWS)), bf16((2, 6 * C1, 6 * C2)),
            bf16((CHUNK, CHUNK)), bf16((PLANE, 2 * C2)),
        ),
        scratch_shapes=[
            pltpu.VMEM((27, CIN, C1), jnp.bfloat16),
            pltpu.VMEM((27 * CIN, 4 * CHUNK), jnp.bfloat16),
            pltpu.VMEM((27, C1, C2), jnp.bfloat16),
            pltpu.VMEM(cotangent.shape, jnp.bfloat16),
            pltpu.VMEM((27 * CIN, C1), jnp.float32),
            pltpu.SemaphoreType.DMA((5,)),
        ],
        compiler_params=pltpu.CompilerParams(vmem_limit_bytes=12 * MIB),
        cost_estimate=pl.CostEstimate(flops=10**9, bytes_accessed=4 * MIB, transcendentals=0),
        name="prepare",
    )(*(pltpu.with_memory_space_constraint(x, pltpu.HBM) for x in stored))
    first, near, pre = pl.pallas_call(
        near_kernel,
        in_specs=[fast] * 5,
        out_specs=(fast,) * 3,
        out_shape=(f32((2 * C1, PLANE)), bf16((6 * C1, PLANE)), f32((PLANE, 2 * C2))),
        scratch_shapes=[
            pltpu.VMEM((4, 2 * ROWS, LANES + PLANE), jnp.bfloat16),
            pltpu.VMEM((18 * ROWS, PLANE), jnp.bfloat16),
            pltpu.VMEM((2 * C1, PLANE + 2 * LANES), jnp.bfloat16),
            pltpu.VMEM((PLANE, 6 * C1), jnp.bfloat16),
            pltpu.VMEM((3, PLANE + 2 * HALF, LANES), jnp.float32),
        ],
        compiler_params=pltpu.CompilerParams(vmem_limit_bytes=16 * MIB),
        cost_estimate=pl.CostEstimate(flops=10**9, bytes_accessed=4 * MIB, transcendentals=0),
        name="near",
    )(volumes, within, select, w1_near, w2)
    rows = C2 // narrow
    output, term = pl.pallas_call(
        functools.partial(far_kernel, wide // 2, scale),
        in_specs=[fast] * 8,
        out_specs=(pl.BlockSpec(memory_space=pl.ANY), fast),
        out_shape=(bf16((1, 1, C2, cells_out)), bf16((C2, PACKED))),
        scratch_shapes=[
            pltpu.VMEM((4, ROWS, LANES + PLANE), jnp.bfloat16),
            pltpu.VMEM((9 * ROWS, PLANE), jnp.bfloat16),
            pltpu.VMEM((2 * C1, PLANE + 2 * LANES), jnp.bfloat16),
            pltpu.VMEM((6 * C1, PLANE), jnp.bfloat16),
            pltpu.VMEM((PLANE, 6 * C1), jnp.bfloat16),
            pltpu.VMEM((3, PLANE + 2 * HALF, LANES), jnp.float32),
            pltpu.VMEM((PLANE + 2 * HALF, LANES), jnp.bfloat16),
            pltpu.VMEM((2, 6 * C1, 3 * LANES), jnp.float32),
            pltpu.VMEM((1, 1, C2, cells_out), jnp.bfloat16),
            pltpu.SemaphoreType.DMA,
        ],
        compiler_params=pltpu.CompilerParams(vmem_limit_bytes=16 * MIB),
        name="far",
    )(across, select, w1_far, w2, cot, first, near, pre)
    half = rows // 2
    received = lax.all_to_all(term, ("narrow", "core"), 0, 0, tiled=True)
    owned = jnp.sum(received.reshape(2 * narrow, half, PACKED).astype(jnp.float32), axis=0).astype(jnp.bfloat16)
    parts = lax.all_to_all(jnp.broadcast_to(owned[None], (wide, half, PACKED)), WIDE, 0, 0, tiled=True)
    total = jnp.sum(parts.reshape(wide // 2, rows, PACKED).astype(jnp.float32), axis=0)
    weight_grad = pl.pallas_call(
        finish_kernel,
        in_specs=[fast],
        out_specs=pl.BlockSpec(memory_space=pl.ANY),
        out_shape=f32((27, rows, C1)),
        scratch_shapes=[pltpu.VMEM((27, rows, C1), jnp.float32), pltpu.SemaphoreType.DMA((3,))],
        compiler_params=pltpu.CompilerParams(vmem_limit_bytes=8 * MIB),
        name="finish",
    )(total)
    return (output, weight_grad)


def solution(mesh):
    wide, narrow = mesh.devices.shape
    split = jax.sharding.Mesh(mesh.devices.reshape(wide // 2, 2, narrow), ("chip", "core", "narrow"))
    return jax.shard_map(
        body,
        mesh=split,
        in_specs=(P("narrow", None, None, WIDE, None), P(), P(), P("narrow", None, None, WIDE)),
        out_specs=(P("narrow", None, None, WIDE), P(None, "narrow", None)),
        check_vma=False,
    )
```

```python
import functools
import math

import jax
import jax.numpy as jnp
import numpy as np
from jax import lax
from jax.experimental import pallas as pl
from jax.experimental.pallas import tpu as pltpu
from jax.sharding import PartitionSpec as P

CIN = 4
C1 = 32
C2 = 64
PLANES = 4
CELLS = 4096
HALF = 32
PLANE = 1024
LANES = 128
ROWS = CIN * PLANES
CHUNK = 512
PACKED = 7 * LANES
MIB = 2**20
WIDE = ("chip", "core")
neg_slope = 0.3


def selection():
    table = np.zeros((CHUNK, 2, 2, 4, HALF), np.float32)
    for py in range(2):
        for px in range(2):
            for row in range(4):
                for col in range(HALF):
                    table[(2 * row + py) * 64 + 2 * col + px, py, px, row, col] = 1
    return table.reshape(CHUNK, CHUNK)


def placement():
    table = np.zeros((2, 27, CIN, 4, CHUNK), np.float32)
    for odd in range(2):
        for a in range(3):
            for bc in range(9):
                for i in range(CIN):
                    for q in range(4):
                        slab, plane = divmod(2 * q + a + 1, PLANES)
                        inner = i * PLANES + plane
                        if slab == 1:
                            column = bc * 2 * ROWS + inner
                        elif (slab == 0) == (odd == 1):
                            column = bc * 2 * ROWS + ROWS + inner
                        else:
                            column = 18 * ROWS + bc * ROWS + inner
                        table[odd, 9 * a + bc, i, q, column] = 1
    return table.reshape(2, 27 * CIN, 4 * CHUNK)


def leaky_relu(value):
    return jnp.where(value > 0, value, neg_slope * value)


def plane_rows(volume_ref):
    return jnp.concatenate([volume_ref[0, 0, i] for i in range(CIN)], axis=0)


def column_masks():
    column = lax.broadcasted_iota(jnp.int32, (1, PLANE), 1) % HALF
    left_ok = jnp.where(column > 0, 1.0, 0.0).astype(jnp.bfloat16)
    right_ok = jnp.where(column < HALF - 1, 1.0, 0.0).astype(jnp.bfloat16)
    return left_ok, right_ok


def strided_taps(rows, select_ref, parity_ref, taps_ref):
    count = rows.shape[0]
    left_ok, _ = column_masks()
    chunks = jnp.concatenate([rows[:, CHUNK * j : CHUNK * (j + 1)] for j in range(8)], axis=0)
    for p in range(4):
        parity_ref[p, :, 0:LANES] = jnp.zeros((count, LANES), jnp.bfloat16)
    for py in range(2):
        parts = jnp.dot(
            chunks, select_ref[:, 256 * py : 256 * py + 256], preferred_element_type=jnp.float32
        ).astype(jnp.bfloat16)
        for px in range(2):
            for j in range(8):
                parity_ref[2 * py + px, :, LANES * (j + 1) : LANES * (j + 2)] = parts[
                    j * count : (j + 1) * count, px * LANES : (px + 1) * LANES
                ]
    for b in range(3):
        for c in range(3):
            begin = LANES - HALF * (b == 0) - (c == 0)
            part = parity_ref[2 * (b != 1) + (c != 1), :, begin : begin + PLANE]
            if c == 0:
                part = part * left_ok
            taps_ref[(3 * b + c) * count : (3 * b + c + 1) * count, :] = part


def shifted_columns(act_ref, columns_ref):
    left_ok, right_ok = column_masks()
    for c in range(3):
        begin = LANES + c - 1
        part = act_ref[:, begin : begin + PLANE]
        if c == 0:
            part = part * left_ok
        if c == 2:
            part = part * right_ok
        columns_ref[c * 2 * C1 : (c + 1) * 2 * C1, :] = part


def second_layer(w2, columns_ref, turned_ref, rowed_ref):
    blank = jnp.zeros((HALF, LANES), jnp.float32)
    for b in (0, 2):
        rowed_ref[b, 0:HALF, :] = blank
        rowed_ref[b, HALF + PLANE :, :] = blank
    for n in range(4):
        cells = slice(256 * n, 256 * n + 256)
        turned_ref[cells, :] = columns_ref[:, cells].T
    for n in range(4):
        sums = jnp.dot(turned_ref[256 * n : 256 * n + 256, :], w2, preferred_element_type=jnp.float32)
        for b in range(3):
            rowed_ref[b, HALF + 256 * n : HALF + 256 * n + 256, :] = sums[:, b * LANES : (b + 1) * LANES]


def row_sum(rowed_ref, n):
    begins = [HALF * b + 256 * n for b in range(3)]
    first, second, third = (rowed_ref[b, begin : begin + 256, :] for b, begin in enumerate(begins))
    return first + second + third


def clear_margins(act_ref):
    margin = jnp.zeros((2 * C1, LANES), jnp.bfloat16)
    act_ref[:, 0:LANES] = margin
    act_ref[:, LANES + PLANE :] = margin


def fetch_kernel(slab_hbm, low_ref, high_ref, sems):
    copies = [pltpu.make_async_copy(slab_hbm.at[:, :, 2 * k : 2 * k + 2], ref, sems.at[k]) for k, ref in enumerate((low_ref, high_ref))]
    for copy in copies:
        copy.start()
    for copy in copies:
        copy.wait()


def prepare_kernel(
    k1_hbm, place_hbm, k2_hbm, select_hbm, cot_hbm,
    w1_near_ref, w1_far_ref, w2_ref, select_ref, turned_ref,
    k1_ref, place_ref, k2_ref, cot_ref, k1_rows_ref, sems,
):
    odd = lax.axis_index("core")
    moves = (
        (k1_hbm, k1_ref), (k2_hbm, k2_ref), (place_hbm.at[odd], place_ref), (cot_hbm, cot_ref), (select_hbm, select_ref),
    )
    copies = [pltpu.make_async_copy(src, dst, sems.at[k]) for k, (src, dst) in enumerate(moves)]
    for copy in copies:
        copy.start()
    copies[0].wait()
    for tap in range(27):
        k1_rows_ref[CIN * tap : CIN * (tap + 1), :] = k1_ref[tap].astype(jnp.float32)
    copies[1].wait()
    blank = jnp.zeros((C1, C2), jnp.bfloat16)

    def stacked(bc, pair):
        k = [blank] + [k2_ref[9 * a + bc] for a in range(3)] + [blank]
        lower = jnp.concatenate(k[1 + 2 * pair : 3 + 2 * pair], axis=0)
        upper = jnp.concatenate(k[2 * pair : 2 + 2 * pair], axis=0)
        return jnp.concatenate([lower, upper], axis=1)

    for pair in range(2):
        for b in range(3):
            for c in range(3):
                w2_ref[pair, c * 2 * C1 : (c + 1) * 2 * C1, b * LANES : (b + 1) * LANES] = stacked(3 * b + c, pair)
    copies[2].wait()
    spread = lax.dot_general(
        k1_rows_ref[...].astype(jnp.bfloat16), place_ref[...],
        (((0,), (0,)), ((), ())), preferred_element_type=jnp.float32,
    ).astype(jnp.bfloat16)
    for q in range(4):
        rows = slice(q % 2 * C1, (q % 2 + 1) * C1)
        w1_near_ref[q // 2, rows, :] = spread[:, CHUNK * q : CHUNK * q + 18 * ROWS]
        w1_far_ref[q // 2, rows, :] = spread[:, CHUNK * q + 18 * ROWS : CHUNK * q + 27 * ROWS]
    copies[3].wait()
    for n in range(4):
        planes = [cot_ref[0, 0, :, z * PLANE + 256 * n : z * PLANE + 256 * n + 256] for z in range(2)]
        turned_ref[256 * n : 256 * n + 256, :] = jnp.concatenate(planes, axis=0).T
    copies[4].wait()


def near_kernel(
    own_ref, own2_ref, within_ref, within2_ref, select_ref, w1_ref, w2_ref, first_ref, columns_ref, pre_ref,
    parity_ref, taps_ref, act_ref, turned_ref, rowed_ref,
):
    odd = lax.axis_index("core")
    slabs = (own_ref, own2_ref, within_ref, within2_ref)
    rows = jnp.concatenate([ref[0, 0, i] for ref in slabs for i in range(2)], axis=0)
    strided_taps(rows, select_ref, parity_ref, taps_ref)
    clear_margins(act_ref)
    for n in range(4):
        here = slice(256 * n, 256 * n + 256)
        first_ref[:, here] = jnp.dot(w1_ref[odd], taps_ref[:, here], preferred_element_type=jnp.float32)
        complete = jnp.dot(w1_ref[1 - odd], taps_ref[:, here], preferred_element_type=jnp.float32)
        act_ref[:, LANES + 256 * n : LANES + 256 * n + 256] = leaky_relu(complete).astype(jnp.bfloat16)
    shifted_columns(act_ref, columns_ref)
    second_layer(w2_ref[1 - odd], columns_ref, turned_ref, rowed_ref)
    for n in range(4):
        pre_ref[256 * n : 256 * n + 256, :] = row_sum(rowed_ref, n)


def far_kernel(
    chips, scale, across_ref, select_ref, w1_ref, w2_ref, cot_ref, first_ref, near_ref, near_pre_ref, out_hbm, grad_ref,
    parity_ref, taps_ref, act_ref, columns_ref, turned_ref, rowed_ref, back_ref, sums_ref, out_ref, out_sem,
):
    odd = lax.axis_index("core")
    last = (lax.axis_index("chip") == chips - 1) & (odd == 1)
    inside = jnp.where(last, 0.0, 1.0)
    strided_taps(plane_rows(across_ref), select_ref, parity_ref, taps_ref)
    clear_margins(act_ref)
    for n in range(4):
        here = slice(256 * n, 256 * n + 256)
        first_pre = first_ref[:, here] + jnp.dot(w1_ref[odd], taps_ref[:, here], preferred_element_type=jnp.float32)
        first_act = leaky_relu(first_pre)
        there = slice(LANES + 256 * n, LANES + 256 * n + 256)
        act_ref[0:C1, there] = first_act[0:C1].astype(jnp.bfloat16)
        act_ref[C1:, there] = (first_act[C1:] * inside).astype(jnp.bfloat16)
    shifted_columns(act_ref, columns_ref)
    second_layer(w2_ref[odd], columns_ref, turned_ref, rowed_ref)
    margin = jnp.zeros((HALF, LANES), jnp.bfloat16)
    back_ref[0:HALF, :] = margin
    back_ref[HALF + PLANE :, :] = margin
    for n in range(4):
        cells = slice(256 * n, 256 * n + 256)
        pre = near_pre_ref[cells, :] + row_sum(rowed_ref, n)
        back = cot_ref[cells, :].astype(jnp.float32) * jnp.where(pre > 0, 1.0, neg_slope)
        back_ref[HALF + 256 * n : HALF + 256 * n + 256, :] = back.astype(jnp.bfloat16)
        output = leaky_relu(pre).astype(jnp.bfloat16).T
        for z in range(2):
            out_ref[0, 0, :, z * PLANE + 256 * n : z * PLANE + 256 * n + 256] = output[z * C2 : (z + 1) * C2]
    out_copy = pltpu.make_async_copy(out_ref, out_hbm, out_sem)
    out_copy.start()
    columns = jnp.concatenate([near_ref[...], columns_ref[...]], axis=0)
    rowed_back = jnp.concatenate([back_ref[(2 - b) * HALF : (2 - b) * HALF + PLANE, :] for b in range(3)], axis=1)
    sums = jnp.dot(columns, rowed_back, preferred_element_type=jnp.float32)
    sums_ref[1 - odd] = sums[0 : 6 * C1]
    sums_ref[odd] = sums[6 * C1 :]
    low = lax.broadcasted_iota(jnp.int32, (C1, LANES), 1) < C2

    def plane_sums(bc, q):
        b, c = divmod(bc, 3)
        begin = 2 * C1 * c + C1 * (q % 2)
        return sums_ref[q // 2, begin : begin + C1, b * LANES : (b + 1) * LANES]

    def two_taps(first, second):
        a, bc = divmod(first, 9)
        here, above = plane_sums(bc, a), pltpu.roll(plane_sums(bc, a + 1), C2, 1)
        if second > 26:
            return here + above
        a, bc = divmod(second, 9)
        there, beyond = pltpu.roll(plane_sums(bc, a), C2, 1), plane_sums(bc, a + 1)
        return jnp.where(low, here, there) + jnp.where(low, above, beyond)

    for block in range(4):
        tall = jnp.concatenate([two_taps(min(8 * block + g, 26), 8 * block + 4 + g) for g in range(4)], axis=0)
        flat = (tall * scale).T.astype(jnp.bfloat16)
        grad_ref[:, 2 * block * LANES : (2 * block + 1) * LANES] = flat[0:C2]
        if block < 3:
            grad_ref[:, (2 * block + 1) * LANES : (2 * block + 2) * LANES] = flat[C2:]
    out_copy.wait()


def finish_kernel(total_ref, grad_hbm, grad_ref, sems):
    copies = []
    for k in range(3):
        for tap in range(9 * k, 9 * k + 9):
            grad_ref[tap] = total_ref[:, tap * C1 : (tap + 1) * C1]
        here = slice(9 * k, 9 * k + 9)
        copies.append(pltpu.make_async_copy(grad_ref.at[here], grad_hbm.at[here], sems.at[k]))
        copies[k].start()
    for copy in copies:
        copy.wait()


def body(volumes, first_kernel, second_kernel, cotangent):
    wide = lax.axis_size(WIDE)
    narrow = lax.axis_size("narrow")
    cells_out = cotangent.shape[3]
    scale = 1.0 / math.sqrt(wide * narrow * cells_out)
    across = lax.ppermute(volumes, WIDE, [p for k in range(1, wide - 1, 2) for p in ((k, k + 1), (k + 1, k))])
    pinned = pl.BlockSpec(memory_space=pltpu.HBM)
    fast = pl.BlockSpec(memory_space=pltpu.VMEM)
    bf16 = functools.partial(jax.ShapeDtypeStruct, dtype=jnp.bfloat16)
    f32 = functools.partial(jax.ShapeDtypeStruct, dtype=jnp.float32)
    slabs = pl.pallas_call(
        fetch_kernel,
        in_specs=[pinned],
        out_specs=(fast, fast),
        out_shape=(bf16((1, 1, 2, PLANES, CELLS)),) * 2,
        scratch_shapes=[pltpu.SemaphoreType.DMA((2,))],
        compiler_params=pltpu.CompilerParams(vmem_limit_bytes=4 * MIB),
        name="fetch",
    )(pltpu.with_memory_space_constraint(volumes, pltpu.HBM))
    pairs = [p for k in range(0, wide - 1, 2) for p in ((k, k + 1), (k + 1, k))]
    withins = [lax.ppermute(slab, WIDE, pairs) for slab in slabs]
    stored = (
        first_kernel.transpose(0, 2, 1), jnp.asarray(placement(), jnp.bfloat16), second_kernel.transpose(0, 2, 1),
        jnp.asarray(selection(), jnp.bfloat16), cotangent,
    )
    w1_near, w1_far, w2, select, cot = pl.pallas_call(
        prepare_kernel,
        in_specs=[pinned] * 5,
        out_specs=(fast,) * 5,
        out_shape=(
            bf16((2, 2 * C1, 18 * ROWS)), bf16((2, 2 * C1, 9 * ROWS)), bf16((2, 6 * C1, 6 * C2)),
            bf16((CHUNK, CHUNK)), bf16((PLANE, 2 * C2)),
        ),
        scratch_shapes=[
            pltpu.VMEM((27, CIN, C1), jnp.bfloat16),
            pltpu.VMEM((27 * CIN, 4 * CHUNK), jnp.bfloat16),
            pltpu.VMEM((27, C1, C2), jnp.bfloat16),
            pltpu.VMEM(cotangent.shape, jnp.bfloat16),
            pltpu.VMEM((27 * CIN, C1), jnp.float32),
            pltpu.SemaphoreType.DMA((5,)),
        ],
        compiler_params=pltpu.CompilerParams(vmem_limit_bytes=12 * MIB),
        cost_estimate=pl.CostEstimate(flops=10**9, bytes_accessed=4 * MIB, transcendentals=0),
        name="prepare",
    )(*(pltpu.with_memory_space_constraint(x, pltpu.HBM) for x in stored))
    first, near, pre = pl.pallas_call(
        near_kernel,
        in_specs=[fast] * 7,
        out_specs=(fast,) * 3,
        out_shape=(f32((2 * C1, PLANE)), bf16((6 * C1, PLANE)), f32((PLANE, 2 * C2))),
        scratch_shapes=[
            pltpu.VMEM((4, 2 * ROWS, LANES + PLANE), jnp.bfloat16),
            pltpu.VMEM((18 * ROWS, PLANE), jnp.bfloat16),
            pltpu.VMEM((2 * C1, PLANE + 2 * LANES), jnp.bfloat16),
            pltpu.VMEM((PLANE, 6 * C1), jnp.bfloat16),
            pltpu.VMEM((3, PLANE + 2 * HALF, LANES), jnp.float32),
        ],
        compiler_params=pltpu.CompilerParams(vmem_limit_bytes=16 * MIB),
        name="near",
    )(*slabs, *withins, select, w1_near, w2)
    rows = C2 // narrow
    output, term = pl.pallas_call(
        functools.partial(far_kernel, wide // 2, scale),
        in_specs=[fast] * 8,
        out_specs=(pl.BlockSpec(memory_space=pl.ANY), fast),
        out_shape=(bf16((1, 1, C2, cells_out)), bf16((C2, PACKED))),
        scratch_shapes=[
            pltpu.VMEM((4, ROWS, LANES + PLANE), jnp.bfloat16),
            pltpu.VMEM((9 * ROWS, PLANE), jnp.bfloat16),
            pltpu.VMEM((2 * C1, PLANE + 2 * LANES), jnp.bfloat16),
            pltpu.VMEM((6 * C1, PLANE), jnp.bfloat16),
            pltpu.VMEM((PLANE, 6 * C1), jnp.bfloat16),
            pltpu.VMEM((3, PLANE + 2 * HALF, LANES), jnp.float32),
            pltpu.VMEM((PLANE + 2 * HALF, LANES), jnp.bfloat16),
            pltpu.VMEM((2, 6 * C1, 3 * LANES), jnp.float32),
            pltpu.VMEM((1, 1, C2, cells_out), jnp.bfloat16),
            pltpu.SemaphoreType.DMA,
        ],
        compiler_params=pltpu.CompilerParams(vmem_limit_bytes=16 * MIB),
        name="far",
    )(across, select, w1_far, w2, cot, first, near, pre)
    half = rows // 2
    received = lax.all_to_all(term, ("narrow", "core"), 0, 0, tiled=True)
    owned = jnp.sum(received.reshape(2 * narrow, half, PACKED).astype(jnp.float32), axis=0).astype(jnp.bfloat16)
    parts = lax.all_to_all(jnp.broadcast_to(owned[None], (wide, half, PACKED)), WIDE, 0, 0, tiled=True)
    total = jnp.sum(parts.reshape(wide // 2, rows, PACKED).astype(jnp.float32), axis=0)
    weight_grad = pl.pallas_call(
        finish_kernel,
        in_specs=[fast],
        out_specs=pl.BlockSpec(memory_space=pl.ANY),
        out_shape=f32((27, rows, C1)),
        scratch_shapes=[pltpu.VMEM((27, rows, C1), jnp.float32), pltpu.SemaphoreType.DMA((3,))],
        compiler_params=pltpu.CompilerParams(vmem_limit_bytes=8 * MIB),
        name="finish",
    )(total)
    return (output, weight_grad)


def solution(mesh):
    wide, narrow = mesh.devices.shape
    split = jax.sharding.Mesh(mesh.devices.reshape(wide // 2, 2, narrow), ("chip", "core", "narrow"))
    return jax.shard_map(
        body,
        mesh=split,
        in_specs=(P("narrow", None, None, WIDE, None), P(), P(), P("narrow", None, None, WIDE)),
        out_specs=(P("narrow", None, None, WIDE), P(None, "narrow", None)),
        check_vma=False,
    )
```

```python
import functools
import math

import jax
import jax.numpy as jnp
import numpy as np
from jax import lax
from jax.experimental import pallas as pl
from jax.experimental.pallas import tpu as pltpu
from jax.sharding import PartitionSpec as P

CIN = 4
C1 = 32
C2 = 64
PLANES = 4
CELLS = 4096
HALF = 32
PLANE = 1024
LANES = 128
ROWS = CIN * PLANES
CHUNK = 512
PACKED = 7 * LANES
MIB = 2**20
WIDE = ("chip", "core")
neg_slope = 0.3


def selection():
    table = np.zeros((CHUNK, 2, 2, 4, HALF), np.float32)
    for py in range(2):
        for px in range(2):
            for row in range(4):
                for col in range(HALF):
                    table[(2 * row + py) * 64 + 2 * col + px, py, px, row, col] = 1
    return table.reshape(CHUNK, CHUNK)


def placement():
    table = np.zeros((2, 27, CIN, 4, CHUNK), np.float32)
    for odd in range(2):
        for a in range(3):
            for bc in range(9):
                for i in range(CIN):
                    for q in range(4):
                        slab, plane = divmod(2 * q + a + 1, PLANES)
                        inner = i * PLANES + plane
                        if slab == 1:
                            column = bc * 2 * ROWS + inner
                        elif (slab == 0) == (odd == 1):
                            column = bc * 2 * ROWS + ROWS + inner
                        else:
                            column = 18 * ROWS + bc * ROWS + inner
                        table[odd, 9 * a + bc, i, q, column] = 1
    return table.reshape(2, 27 * CIN, 4 * CHUNK)


def leaky_relu(value):
    return jnp.where(value > 0, value, neg_slope * value)


def plane_rows(volume_ref):
    return jnp.concatenate([volume_ref[0, 0, i] for i in range(CIN)], axis=0)


def column_masks():
    column = lax.broadcasted_iota(jnp.int32, (1, PLANE), 1) % HALF
    left_ok = jnp.where(column > 0, 1.0, 0.0).astype(jnp.bfloat16)
    right_ok = jnp.where(column < HALF - 1, 1.0, 0.0).astype(jnp.bfloat16)
    return left_ok, right_ok


def strided_taps(rows, select_ref, parity_ref, taps_ref):
    count = rows.shape[0]
    left_ok, _ = column_masks()
    chunks = jnp.concatenate([rows[:, CHUNK * j : CHUNK * (j + 1)] for j in range(8)], axis=0)
    for p in range(4):
        parity_ref[p, :, 0:LANES] = jnp.zeros((count, LANES), jnp.bfloat16)
    for py in range(2):
        parts = jnp.dot(
            chunks, select_ref[:, 256 * py : 256 * py + 256], preferred_element_type=jnp.float32
        ).astype(jnp.bfloat16)
        for px in range(2):
            for j in range(8):
                parity_ref[2 * py + px, :, LANES * (j + 1) : LANES * (j + 2)] = parts[
                    j * count : (j + 1) * count, px * LANES : (px + 1) * LANES
                ]
    for b in range(3):
        for c in range(3):
            begin = LANES - HALF * (b == 0) - (c == 0)
            part = parity_ref[2 * (b != 1) + (c != 1), :, begin : begin + PLANE]
            if c == 0:
                part = part * left_ok
            taps_ref[(3 * b + c) * count : (3 * b + c + 1) * count, :] = part


def shifted_columns(act_ref, columns_ref):
    left_ok, right_ok = column_masks()
    for c in range(3):
        begin = LANES + c - 1
        part = act_ref[:, begin : begin + PLANE]
        if c == 0:
            part = part * left_ok
        if c == 2:
            part = part * right_ok
        columns_ref[c * 2 * C1 : (c + 1) * 2 * C1, :] = part


def second_layer(w2, columns_ref, turned_ref, rowed_ref):
    blank = jnp.zeros((HALF, LANES), jnp.float32)
    for b in (0, 2):
        rowed_ref[b, 0:HALF, :] = blank
        rowed_ref[b, HALF + PLANE :, :] = blank
    for n in range(4):
        cells = slice(256 * n, 256 * n + 256)
        turned_ref[cells, :] = columns_ref[:, cells].T
    for n in range(4):
        sums = jnp.dot(turned_ref[256 * n : 256 * n + 256, :], w2, preferred_element_type=jnp.float32)
        for b in range(3):
            rowed_ref[b, HALF + 256 * n : HALF + 256 * n + 256, :] = sums[:, b * LANES : (b + 1) * LANES]


def row_sum(rowed_ref, n):
    begins = [HALF * b + 256 * n for b in range(3)]
    first, second, third = (rowed_ref[b, begin : begin + 256, :] for b, begin in enumerate(begins))
    return first + second + third


def clear_margins(act_ref):
    margin = jnp.zeros((2 * C1, LANES), jnp.bfloat16)
    act_ref[:, 0:LANES] = margin
    act_ref[:, LANES + PLANE :] = margin


def prepare_kernel(
    k1_hbm, place_hbm, k2_hbm, select_hbm, cot_hbm,
    w1_near_ref, w1_far_ref, w2_ref, select_ref, turned_ref,
    k1_ref, place_ref, k2_ref, cot_ref, k1_rows_ref, sems,
):
    odd = lax.axis_index("core")
    moves = (
        (k1_hbm, k1_ref), (k2_hbm, k2_ref), (place_hbm.at[odd], place_ref), (cot_hbm, cot_ref), (select_hbm, select_ref),
    )
    copies = [pltpu.make_async_copy(src, dst, sems.at[k]) for k, (src, dst) in enumerate(moves)]
    for copy in copies:
        copy.start()
    copies[0].wait()
    for tap in range(27):
        k1_rows_ref[CIN * tap : CIN * (tap + 1), :] = k1_ref[tap].astype(jnp.float32)
    copies[1].wait()
    blank = jnp.zeros((C1, C2), jnp.bfloat16)

    def stacked(bc, pair):
        k = [blank] + [k2_ref[9 * a + bc] for a in range(3)] + [blank]
        lower = jnp.concatenate(k[1 + 2 * pair : 3 + 2 * pair], axis=0)
        upper = jnp.concatenate(k[2 * pair : 2 + 2 * pair], axis=0)
        return jnp.concatenate([lower, upper], axis=1)

    for pair in range(2):
        for b in range(3):
            for c in range(3):
                w2_ref[pair, c * 2 * C1 : (c + 1) * 2 * C1, b * LANES : (b + 1) * LANES] = stacked(3 * b + c, pair)
    copies[2].wait()
    spread = lax.dot_general(
        k1_rows_ref[...].astype(jnp.bfloat16), place_ref[...],
        (((0,), (0,)), ((), ())), preferred_element_type=jnp.float32,
    ).astype(jnp.bfloat16)
    for q in range(4):
        rows = slice(q % 2 * C1, (q % 2 + 1) * C1)
        w1_near_ref[q // 2, rows, :] = spread[:, CHUNK * q : CHUNK * q + 18 * ROWS]
        w1_far_ref[q // 2, rows, :] = spread[:, CHUNK * q + 18 * ROWS : CHUNK * q + 27 * ROWS]
    copies[3].wait()
    for n in range(4):
        planes = [cot_ref[0, 0, :, z * PLANE + 256 * n : z * PLANE + 256 * n + 256] for z in range(2)]
        turned_ref[256 * n : 256 * n + 256, :] = jnp.concatenate(planes, axis=0).T
    copies[4].wait()


def near_kernel(
    own_ref, within_ref, select_ref, w1_ref, w2_ref, first_ref, columns_ref, pre_ref,
    parity_ref, taps_ref, act_ref, turned_ref, rowed_ref,
):
    odd = lax.axis_index("core")
    rows = jnp.concatenate([plane_rows(own_ref), plane_rows(within_ref)], axis=0)
    strided_taps(rows, select_ref, parity_ref, taps_ref)
    clear_margins(act_ref)
    for n in range(4):
        here = slice(256 * n, 256 * n + 256)
        first_ref[:, here] = jnp.dot(w1_ref[odd], taps_ref[:, here], preferred_element_type=jnp.float32)
        complete = jnp.dot(w1_ref[1 - odd], taps_ref[:, here], preferred_element_type=jnp.float32)
        act_ref[:, LANES + 256 * n : LANES + 256 * n + 256] = leaky_relu(complete).astype(jnp.bfloat16)
    shifted_columns(act_ref, columns_ref)
    second_layer(w2_ref[1 - odd], columns_ref, turned_ref, rowed_ref)
    for n in range(4):
        pre_ref[256 * n : 256 * n + 256, :] = row_sum(rowed_ref, n)


def emit_activations(pre_ref, out_ref, out_hbm, sem):
    for n in range(4):
        output = leaky_relu(pre_ref[256 * n : 256 * n + 256, :]).astype(jnp.bfloat16).T
        for z in range(2):
            out_ref[0, 0, :, z * PLANE + 256 * n : z * PLANE + 256 * n + 256] = output[z * C2 : (z + 1) * C2]
    copy = pltpu.make_async_copy(out_ref, out_hbm, sem)
    copy.start()
    copy.wait()


def far_kernel(
    chips, narrow, scale, across_ref, select_ref, w1_ref, w2_ref, cot_ref, first_ref, near_ref, near_pre_ref, out_hbm, grad_ref, pre_ref,
    parity_ref, taps_ref, act_ref, columns_ref, turned_ref, rowed_ref, back_ref, sums_ref, out_ref, out_sem,
):
    odd = lax.axis_index("core")
    last = (lax.axis_index("chip") == chips - 1) & (odd == 1)
    inside = jnp.where(last, 0.0, 1.0)
    strided_taps(plane_rows(across_ref), select_ref, parity_ref, taps_ref)
    clear_margins(act_ref)
    for n in range(4):
        here = slice(256 * n, 256 * n + 256)
        first_pre = first_ref[:, here] + jnp.dot(w1_ref[odd], taps_ref[:, here], preferred_element_type=jnp.float32)
        first_act = leaky_relu(first_pre)
        there = slice(LANES + 256 * n, LANES + 256 * n + 256)
        act_ref[0:C1, there] = first_act[0:C1].astype(jnp.bfloat16)
        act_ref[C1:, there] = (first_act[C1:] * inside).astype(jnp.bfloat16)
    shifted_columns(act_ref, columns_ref)
    second_layer(w2_ref[odd], columns_ref, turned_ref, rowed_ref)
    margin = jnp.zeros((HALF, LANES), jnp.bfloat16)
    back_ref[0:HALF, :] = margin
    back_ref[HALF + PLANE :, :] = margin
    for n in range(4):
        cells = slice(256 * n, 256 * n + 256)
        pre = near_pre_ref[cells, :] + row_sum(rowed_ref, n)
        pre_ref[cells, :] = pre
        back = cot_ref[cells, :].astype(jnp.float32) * jnp.where(pre > 0, 1.0, neg_slope)
        back_ref[HALF + 256 * n : HALF + 256 * n + 256, :] = back.astype(jnp.bfloat16)
    columns = jnp.concatenate([near_ref[...], columns_ref[...]], axis=0)
    rowed_back = jnp.concatenate([back_ref[(2 - b) * HALF : (2 - b) * HALF + PLANE, :] for b in range(3)], axis=1)
    sums = jnp.dot(columns, rowed_back, preferred_element_type=jnp.float32)
    sums_ref[1 - odd] = sums[0 : 6 * C1]
    sums_ref[odd] = sums[6 * C1 :]
    low = lax.broadcasted_iota(jnp.int32, (C1, LANES), 1) < C2

    def plane_sums(bc, q):
        b, c = divmod(bc, 3)
        begin = 2 * C1 * c + C1 * (q % 2)
        return sums_ref[q // 2, begin : begin + C1, b * LANES : (b + 1) * LANES]

    def two_taps(first, second):
        a, bc = divmod(first, 9)
        here, above = plane_sums(bc, a), pltpu.roll(plane_sums(bc, a + 1), C2, 1)
        if second > 26:
            return here + above
        a, bc = divmod(second, 9)
        there, beyond = pltpu.roll(plane_sums(bc, a), C2, 1), plane_sums(bc, a + 1)
        return jnp.where(low, here, there) + jnp.where(low, above, beyond)

    for block in range(4):
        tall = jnp.concatenate([two_taps(min(8 * block + g, 26), 8 * block + 4 + g) for g in range(4)], axis=0)
        flat = (tall * scale).T.astype(jnp.bfloat16)
        grad_ref[:, 2 * block * LANES : (2 * block + 1) * LANES] = flat[0:C2]
        if block < 3:
            grad_ref[:, (2 * block + 1) * LANES : (2 * block + 2) * LANES] = flat[C2:]
    early = lax.axis_index("narrow") < narrow - 1
    pl.when(early)(lambda: emit_activations(pre_ref, out_ref, out_hbm, out_sem))


def finish_kernel(narrow, total_ref, pre_ref, begun_hbm, grad_hbm, out_hbm, grad_ref, out_ref, sems, out_sem):
    del begun_hbm
    copies = []
    for k in range(3):
        for tap in range(9 * k, 9 * k + 9):
            grad_ref[tap] = total_ref[:, tap * C1 : (tap + 1) * C1]
        here = slice(9 * k, 9 * k + 9)
        copies.append(pltpu.make_async_copy(grad_ref.at[here], grad_hbm.at[here], sems.at[k]))
        copies[k].start()
    late = lax.axis_index("narrow") == narrow - 1
    pl.when(late)(lambda: emit_activations(pre_ref, out_ref, out_hbm, out_sem))
    for copy in copies:
        copy.wait()


def body(volumes, first_kernel, second_kernel, cotangent):
    wide = lax.axis_size(WIDE)
    narrow = lax.axis_size("narrow")
    cells_out = cotangent.shape[3]
    scale = 1.0 / math.sqrt(wide * narrow * cells_out)
    across = lax.ppermute(volumes, WIDE, [p for k in range(1, wide - 1, 2) for p in ((k, k + 1), (k + 1, k))])
    pairs = [p for k in range(0, wide - 1, 2) for p in ((k, k + 1), (k + 1, k))]
    within = lax.ppermute(volumes, WIDE, pairs)
    pinned = pl.BlockSpec(memory_space=pltpu.HBM)
    fast = pl.BlockSpec(memory_space=pltpu.VMEM)
    bf16 = functools.partial(jax.ShapeDtypeStruct, dtype=jnp.bfloat16)
    f32 = functools.partial(jax.ShapeDtypeStruct, dtype=jnp.float32)
    stored = (
        first_kernel.transpose(0, 2, 1), jnp.asarray(placement(), jnp.bfloat16), second_kernel.transpose(0, 2, 1),
        jnp.asarray(selection(), jnp.bfloat16), cotangent,
    )
    w1_near, w1_far, w2, select, cot = pl.pallas_call(
        prepare_kernel,
        in_specs=[pinned] * 5,
        out_specs=(fast,) * 5,
        out_shape=(
            bf16((2, 2 * C1, 18 * ROWS)), bf16((2, 2 * C1, 9 * ROWS)), bf16((2, 6 * C1, 6 * C2)),
            bf16((CHUNK, CHUNK)), bf16((PLANE, 2 * C2)),
        ),
        scratch_shapes=[
            pltpu.VMEM((27, CIN, C1), jnp.bfloat16),
            pltpu.VMEM((27 * CIN, 4 * CHUNK), jnp.bfloat16),
            pltpu.VMEM((27, C1, C2), jnp.bfloat16),
            pltpu.VMEM(cotangent.shape, jnp.bfloat16),
            pltpu.VMEM((27 * CIN, C1), jnp.float32),
            pltpu.SemaphoreType.DMA((5,)),
        ],
        compiler_params=pltpu.CompilerParams(vmem_limit_bytes=12 * MIB),
        cost_estimate=pl.CostEstimate(flops=10**9, bytes_accessed=4 * MIB, transcendentals=0),
        name="prepare",
    )(*(pltpu.with_memory_space_constraint(x, pltpu.HBM) for x in stored))
    first, near, pre = pl.pallas_call(
        near_kernel,
        in_specs=[fast] * 5,
        out_specs=(fast,) * 3,
        out_shape=(f32((2 * C1, PLANE)), bf16((6 * C1, PLANE)), f32((PLANE, 2 * C2))),
        scratch_shapes=[
            pltpu.VMEM((4, 2 * ROWS, LANES + PLANE), jnp.bfloat16),
            pltpu.VMEM((18 * ROWS, PLANE), jnp.bfloat16),
            pltpu.VMEM((2 * C1, PLANE + 2 * LANES), jnp.bfloat16),
            pltpu.VMEM((PLANE, 6 * C1), jnp.bfloat16),
            pltpu.VMEM((3, PLANE + 2 * HALF, LANES), jnp.float32),
        ],
        compiler_params=pltpu.CompilerParams(vmem_limit_bytes=16 * MIB),
        cost_estimate=pl.CostEstimate(flops=10**9, bytes_accessed=4 * MIB, transcendentals=0),
        name="near",
    )(volumes, within, select, w1_near, w2)
    rows = C2 // narrow
    begun, term, pre = pl.pallas_call(
        functools.partial(far_kernel, wide // 2, narrow, scale),
        in_specs=[fast] * 8,
        out_specs=(pl.BlockSpec(memory_space=pl.ANY), fast, fast),
        out_shape=(bf16((1, 1, C2, cells_out)), bf16((C2, PACKED)), f32((PLANE, 2 * C2))),
        scratch_shapes=[
            pltpu.VMEM((4, ROWS, LANES + PLANE), jnp.bfloat16),
            pltpu.VMEM((9 * ROWS, PLANE), jnp.bfloat16),
            pltpu.VMEM((2 * C1, PLANE + 2 * LANES), jnp.bfloat16),
            pltpu.VMEM((6 * C1, PLANE), jnp.bfloat16),
            pltpu.VMEM((PLANE, 6 * C1), jnp.bfloat16),
            pltpu.VMEM((3, PLANE + 2 * HALF, LANES), jnp.float32),
            pltpu.VMEM((PLANE + 2 * HALF, LANES), jnp.bfloat16),
            pltpu.VMEM((2, 6 * C1, 3 * LANES), jnp.float32),
            pltpu.VMEM((1, 1, C2, cells_out), jnp.bfloat16),
            pltpu.SemaphoreType.DMA,
        ],
        compiler_params=pltpu.CompilerParams(vmem_limit_bytes=16 * MIB),
        name="far",
    )(across, select, w1_far, w2, cot, first, near, pre)
    half = rows // 2
    received = lax.all_to_all(term, ("narrow", "core"), 0, 0, tiled=True)
    owned = jnp.sum(received.reshape(2 * narrow, half, PACKED).astype(jnp.float32), axis=0).astype(jnp.bfloat16)
    parts = lax.all_to_all(jnp.broadcast_to(owned[None], (wide, half, PACKED)), WIDE, 0, 0, tiled=True)
    total = jnp.sum(parts.reshape(wide // 2, rows, PACKED).astype(jnp.float32), axis=0)
    anywhere = pl.BlockSpec(memory_space=pl.ANY)
    weight_grad, output = pl.pallas_call(
        functools.partial(finish_kernel, narrow),
        in_specs=[fast, fast, anywhere],
        out_specs=(anywhere, anywhere),
        out_shape=(f32((27, rows, C1)), bf16((1, 1, C2, cells_out))),
        scratch_shapes=[
            pltpu.VMEM((27, rows, C1), jnp.float32),
            pltpu.VMEM((1, 1, C2, cells_out), jnp.bfloat16),
            pltpu.SemaphoreType.DMA((3,)),
            pltpu.SemaphoreType.DMA,
        ],
        input_output_aliases={2: 1},
        compiler_params=pltpu.CompilerParams(vmem_limit_bytes=8 * MIB),
        name="finish",
    )(total, pre, begun)
    return (output, weight_grad)


def solution(mesh):
    wide, narrow = mesh.devices.shape
    split = jax.sharding.Mesh(mesh.devices.reshape(wide // 2, 2, narrow), ("chip", "core", "narrow"))
    return jax.shard_map(
        body,
        mesh=split,
        in_specs=(P("narrow", None, None, WIDE, None), P(), P(), P("narrow", None, None, WIDE)),
        out_specs=(P("narrow", None, None, WIDE), P(None, "narrow", None)),
        check_vma=False,
    )
```

```python
import functools
import math

import jax
import jax.numpy as jnp
import numpy as np
from jax import lax
from jax.experimental import pallas as pl
from jax.experimental.pallas import tpu as pltpu
from jax.sharding import PartitionSpec as P

CIN = 4
C1 = 32
C2 = 64
PLANES = 4
CELLS = 4096
HALF = 32
PLANE = 1024
LANES = 128
ROWS = CIN * PLANES
CHUNK = 512
PACKED = 7 * LANES
MIB = 2**20
WIDE = ("chip", "core")
neg_slope = 0.3


def selection():
    table = np.zeros((CHUNK, 2, 2, 4, HALF), np.float32)
    for py in range(2):
        for px in range(2):
            for row in range(4):
                for col in range(HALF):
                    table[(2 * row + py) * 64 + 2 * col + px, py, px, row, col] = 1
    return table.reshape(CHUNK, CHUNK)


def placement():
    table = np.zeros((2, 27, CIN, 4, CHUNK), np.float32)
    for odd in range(2):
        for a in range(3):
            for bc in range(9):
                for i in range(CIN):
                    for q in range(4):
                        slab, plane = divmod(2 * q + a + 1, PLANES)
                        inner = i * PLANES + plane
                        if slab == 1:
                            column = bc * 2 * ROWS + inner
                        elif (slab == 0) == (odd == 1):
                            column = bc * 2 * ROWS + ROWS + inner
                        else:
                            column = 18 * ROWS + bc * ROWS + inner
                        table[odd, 9 * a + bc, i, q, column] = 1
    return table.reshape(2, 27 * CIN, 4 * CHUNK)


def leaky_relu(value):
    return jnp.where(value > 0, value, neg_slope * value)


def plane_rows(volume_ref):
    return jnp.concatenate([volume_ref[0, 0, i] for i in range(CIN)], axis=0)


def column_masks():
    column = lax.broadcasted_iota(jnp.int32, (1, PLANE), 1) % HALF
    left_ok = jnp.where(column > 0, 1.0, 0.0).astype(jnp.bfloat16)
    right_ok = jnp.where(column < HALF - 1, 1.0, 0.0).astype(jnp.bfloat16)
    return left_ok, right_ok


def strided_taps(rows, select_ref, parity_ref, taps_ref):
    count = rows.shape[0]
    left_ok, _ = column_masks()
    chunks = jnp.concatenate([rows[:, CHUNK * j : CHUNK * (j + 1)] for j in range(8)], axis=0)
    for p in range(4):
        parity_ref[p, :, 0:LANES] = jnp.zeros((count, LANES), jnp.bfloat16)
    for py in range(2):
        parts = jnp.dot(
            chunks, select_ref[:, 256 * py : 256 * py + 256], preferred_element_type=jnp.float32
        ).astype(jnp.bfloat16)
        for px in range(2):
            for j in range(8):
                parity_ref[2 * py + px, :, LANES * (j + 1) : LANES * (j + 2)] = parts[
                    j * count : (j + 1) * count, px * LANES : (px + 1) * LANES
                ]
    for b in range(3):
        for c in range(3):
            begin = LANES - HALF * (b == 0) - (c == 0)
            part = parity_ref[2 * (b != 1) + (c != 1), :, begin : begin + PLANE]
            if c == 0:
                part = part * left_ok
            taps_ref[(3 * b + c) * count : (3 * b + c + 1) * count, :] = part


def shifted_columns(act_ref, columns_ref):
    left_ok, right_ok = column_masks()
    for c in range(3):
        begin = LANES + c - 1
        part = act_ref[:, begin : begin + PLANE]
        if c == 0:
            part = part * left_ok
        if c == 2:
            part = part * right_ok
        columns_ref[c * 2 * C1 : (c + 1) * 2 * C1, :] = part


def second_layer(w2, columns_ref, turned_ref, rowed_ref):
    blank = jnp.zeros((HALF, LANES), jnp.float32)
    for b in (0, 2):
        rowed_ref[b, 0:HALF, :] = blank
        rowed_ref[b, HALF + PLANE :, :] = blank
    for n in range(4):
        cells = slice(256 * n, 256 * n + 256)
        turned_ref[cells, :] = columns_ref[:, cells].T
    for n in range(4):
        sums = jnp.dot(turned_ref[256 * n : 256 * n + 256, :], w2, preferred_element_type=jnp.float32)
        for b in range(3):
            rowed_ref[b, HALF + 256 * n : HALF + 256 * n + 256, :] = sums[:, b * LANES : (b + 1) * LANES]


def row_sum(rowed_ref, n):
    begins = [HALF * b + 256 * n for b in range(3)]
    first, second, third = (rowed_ref[b, begin : begin + 256, :] for b, begin in enumerate(begins))
    return first + second + third


def clear_margins(act_ref):
    margin = jnp.zeros((2 * C1, LANES), jnp.bfloat16)
    act_ref[:, 0:LANES] = margin
    act_ref[:, LANES + PLANE :] = margin


def prepare_kernel(
    k1_hbm, place_hbm, k2_hbm, select_hbm, cot_hbm,
    w1_near_ref, w1_far_ref, w2_ref, select_ref, turned_ref,
    k1_ref, place_ref, k2_ref, cot_ref, k1_rows_ref, sems,
):
    odd = lax.axis_index("core")
    moves = (
        (k1_hbm, k1_ref), (k2_hbm, k2_ref), (place_hbm.at[odd], place_ref), (cot_hbm, cot_ref), (select_hbm, select_ref),
    )
    copies = [pltpu.make_async_copy(src, dst, sems.at[k]) for k, (src, dst) in enumerate(moves)]
    for copy in copies:
        copy.start()
    copies[0].wait()
    for tap in range(27):
        k1_rows_ref[CIN * tap : CIN * (tap + 1), :] = k1_ref[tap].astype(jnp.float32)
    copies[1].wait()
    blank = jnp.zeros((C1, C2), jnp.bfloat16)

    def stacked(bc, pair):
        k = [blank] + [k2_ref[9 * a + bc] for a in range(3)] + [blank]
        lower = jnp.concatenate(k[1 + 2 * pair : 3 + 2 * pair], axis=0)
        upper = jnp.concatenate(k[2 * pair : 2 + 2 * pair], axis=0)
        return jnp.concatenate([lower, upper], axis=1)

    for pair in range(2):
        for b in range(3):
            for c in range(3):
                w2_ref[pair, c * 2 * C1 : (c + 1) * 2 * C1, b * LANES : (b + 1) * LANES] = stacked(3 * b + c, pair)
    copies[2].wait()
    spread = lax.dot_general(
        k1_rows_ref[...].astype(jnp.bfloat16), place_ref[...],
        (((0,), (0,)), ((), ())), preferred_element_type=jnp.float32,
    ).astype(jnp.bfloat16)
    for q in range(4):
        rows = slice(q % 2 * C1, (q % 2 + 1) * C1)
        w1_near_ref[q // 2, rows, :] = spread[:, CHUNK * q : CHUNK * q + 18 * ROWS]
        w1_far_ref[q // 2, rows, :] = spread[:, CHUNK * q + 18 * ROWS : CHUNK * q + 27 * ROWS]
    copies[3].wait()
    for n in range(4):
        planes = [cot_ref[0, 0, :, z * PLANE + 256 * n : z * PLANE + 256 * n + 256] for z in range(2)]
        turned_ref[256 * n : 256 * n + 256, :] = jnp.concatenate(planes, axis=0).T
    copies[4].wait()


def near_kernel(
    own_ref, within_ref, select_ref, w1_ref, w2_ref, first_ref, columns_ref, pre_ref,
    parity_ref, taps_ref, act_ref, turned_ref, rowed_ref,
):
    odd = lax.axis_index("core")
    rows = jnp.concatenate([plane_rows(own_ref), plane_rows(within_ref)], axis=0)
    strided_taps(rows, select_ref, parity_ref, taps_ref)
    clear_margins(act_ref)
    for n in range(4):
        here = slice(256 * n, 256 * n + 256)
        first_ref[:, here] = jnp.dot(w1_ref[odd], taps_ref[:, here], preferred_element_type=jnp.float32)
        complete = jnp.dot(w1_ref[1 - odd], taps_ref[:, here], preferred_element_type=jnp.float32)
        act_ref[:, LANES + 256 * n : LANES + 256 * n + 256] = leaky_relu(complete).astype(jnp.bfloat16)
    shifted_columns(act_ref, columns_ref)
    second_layer(w2_ref[1 - odd], columns_ref, turned_ref, rowed_ref)
    for n in range(4):
        pre_ref[256 * n : 256 * n + 256, :] = row_sum(rowed_ref, n)


def emit_activations(pre_ref, out_ref, out_hbm, sem):
    for n in range(4):
        output = leaky_relu(pre_ref[256 * n : 256 * n + 256, :]).astype(jnp.bfloat16).T
        for z in range(2):
            out_ref[0, 0, :, z * PLANE + 256 * n : z * PLANE + 256 * n + 256] = output[z * C2 : (z + 1) * C2]
    copy = pltpu.make_async_copy(out_ref, out_hbm, sem)
    copy.start()
    copy.wait()


def far_kernel(
    chips, scale, across_ref, select_ref, w1_ref, w2_ref, cot_ref, first_ref, near_ref, near_pre_ref, out_hbm, grad_ref, pre_ref,
    parity_ref, taps_ref, act_ref, columns_ref, turned_ref, rowed_ref, back_ref, sums_ref, out_ref, out_sem,
):
    odd = lax.axis_index("core")
    last = (lax.axis_index("chip") == chips - 1) & (odd == 1)
    inside = jnp.where(last, 0.0, 1.0)
    strided_taps(plane_rows(across_ref), select_ref, parity_ref, taps_ref)
    clear_margins(act_ref)
    for n in range(4):
        here = slice(256 * n, 256 * n + 256)
        first_pre = first_ref[:, here] + jnp.dot(w1_ref[odd], taps_ref[:, here], preferred_element_type=jnp.float32)
        first_act = leaky_relu(first_pre)
        there = slice(LANES + 256 * n, LANES + 256 * n + 256)
        act_ref[0:C1, there] = first_act[0:C1].astype(jnp.bfloat16)
        act_ref[C1:, there] = (first_act[C1:] * inside).astype(jnp.bfloat16)
    shifted_columns(act_ref, columns_ref)
    second_layer(w2_ref[odd], columns_ref, turned_ref, rowed_ref)
    margin = jnp.zeros((HALF, LANES), jnp.bfloat16)
    back_ref[0:HALF, :] = margin
    back_ref[HALF + PLANE :, :] = margin
    for n in range(4):
        cells = slice(256 * n, 256 * n + 256)
        pre = near_pre_ref[cells, :] + row_sum(rowed_ref, n)
        pre_ref[cells, :] = pre
        back = cot_ref[cells, :].astype(jnp.float32) * jnp.where(pre > 0, 1.0, neg_slope)
        back_ref[HALF + 256 * n : HALF + 256 * n + 256, :] = back.astype(jnp.bfloat16)
    columns = jnp.concatenate([near_ref[...], columns_ref[...]], axis=0)
    rowed_back = jnp.concatenate([back_ref[(2 - b) * HALF : (2 - b) * HALF + PLANE, :] for b in range(3)], axis=1)
    sums = jnp.dot(columns, rowed_back, preferred_element_type=jnp.float32)
    sums_ref[1 - odd] = sums[0 : 6 * C1]
    sums_ref[odd] = sums[6 * C1 :]
    low = lax.broadcasted_iota(jnp.int32, (C1, LANES), 1) < C2

    def plane_sums(bc, q):
        b, c = divmod(bc, 3)
        begin = 2 * C1 * c + C1 * (q % 2)
        return sums_ref[q // 2, begin : begin + C1, b * LANES : (b + 1) * LANES]

    def two_taps(first, second):
        a, bc = divmod(first, 9)
        here, above = plane_sums(bc, a), pltpu.roll(plane_sums(bc, a + 1), C2, 1)
        if second > 26:
            return here + above
        a, bc = divmod(second, 9)
        there, beyond = pltpu.roll(plane_sums(bc, a), C2, 1), plane_sums(bc, a + 1)
        return jnp.where(low, here, there) + jnp.where(low, above, beyond)

    for block in range(4):
        tall = jnp.concatenate([two_taps(min(8 * block + g, 26), 8 * block + 4 + g) for g in range(4)], axis=0)
        flat = (tall * scale).T.astype(jnp.bfloat16)
        grad_ref[:, 2 * block * LANES : (2 * block + 1) * LANES] = flat[0:C2]
        if block < 3:
            grad_ref[:, (2 * block + 1) * LANES : (2 * block + 2) * LANES] = flat[C2:]
    early = lax.axis_index("narrow") == 0
    pl.when(early)(lambda: emit_activations(pre_ref, out_ref, out_hbm, out_sem))


def finish_kernel(total_ref, pre_ref, begun_hbm, grad_hbm, out_hbm, grad_ref, out_ref, sems, out_sem):
    del begun_hbm
    copies = []
    for k in range(3):
        for tap in range(9 * k, 9 * k + 9):
            grad_ref[tap] = total_ref[:, tap * C1 : (tap + 1) * C1]
        here = slice(9 * k, 9 * k + 9)
        copies.append(pltpu.make_async_copy(grad_ref.at[here], grad_hbm.at[here], sems.at[k]))
        copies[k].start()
    late = lax.axis_index("narrow") > 0
    pl.when(late)(lambda: emit_activations(pre_ref, out_ref, out_hbm, out_sem))
    for copy in copies:
        copy.wait()


def body(volumes, first_kernel, second_kernel, cotangent):
    wide = lax.axis_size(WIDE)
    narrow = lax.axis_size("narrow")
    cells_out = cotangent.shape[3]
    scale = 1.0 / math.sqrt(wide * narrow * cells_out)
    across = lax.ppermute(volumes, WIDE, [p for k in range(1, wide - 1, 2) for p in ((k, k + 1), (k + 1, k))])
    pairs = [p for k in range(0, wide - 1, 2) for p in ((k, k + 1), (k + 1, k))]
    within = lax.ppermute(volumes, WIDE, pairs)
    pinned = pl.BlockSpec(memory_space=pltpu.HBM)
    fast = pl.BlockSpec(memory_space=pltpu.VMEM)
    bf16 = functools.partial(jax.ShapeDtypeStruct, dtype=jnp.bfloat16)
    f32 = functools.partial(jax.ShapeDtypeStruct, dtype=jnp.float32)
    stored = (
        first_kernel.transpose(0, 2, 1), jnp.asarray(placement(), jnp.bfloat16), second_kernel.transpose(0, 2, 1),
        jnp.asarray(selection(), jnp.bfloat16), cotangent,
    )
    w1_near, w1_far, w2, select, cot = pl.pallas_call(
        prepare_kernel,
        in_specs=[pinned] * 5,
        out_specs=(fast,) * 5,
        out_shape=(
            bf16((2, 2 * C1, 18 * ROWS)), bf16((2, 2 * C1, 9 * ROWS)), bf16((2, 6 * C1, 6 * C2)),
            bf16((CHUNK, CHUNK)), bf16((PLANE, 2 * C2)),
        ),
        scratch_shapes=[
            pltpu.VMEM((27, CIN, C1), jnp.bfloat16),
            pltpu.VMEM((27 * CIN, 4 * CHUNK), jnp.bfloat16),
            pltpu.VMEM((27, C1, C2), jnp.bfloat16),
            pltpu.VMEM(cotangent.shape, jnp.bfloat16),
            pltpu.VMEM((27 * CIN, C1), jnp.float32),
            pltpu.SemaphoreType.DMA((5,)),
        ],
        compiler_params=pltpu.CompilerParams(vmem_limit_bytes=12 * MIB),
        cost_estimate=pl.CostEstimate(flops=10**9, bytes_accessed=4 * MIB, transcendentals=0),
        name="prepare",
    )(*(pltpu.with_memory_space_constraint(x, pltpu.HBM) for x in stored))
    first, near, pre = pl.pallas_call(
        near_kernel,
        in_specs=[fast] * 5,
        out_specs=(fast,) * 3,
        out_shape=(f32((2 * C1, PLANE)), bf16((6 * C1, PLANE)), f32((PLANE, 2 * C2))),
        scratch_shapes=[
            pltpu.VMEM((4, 2 * ROWS, LANES + PLANE), jnp.bfloat16),
            pltpu.VMEM((18 * ROWS, PLANE), jnp.bfloat16),
            pltpu.VMEM((2 * C1, PLANE + 2 * LANES), jnp.bfloat16),
            pltpu.VMEM((PLANE, 6 * C1), jnp.bfloat16),
            pltpu.VMEM((3, PLANE + 2 * HALF, LANES), jnp.float32),
        ],
        compiler_params=pltpu.CompilerParams(vmem_limit_bytes=16 * MIB),
        cost_estimate=pl.CostEstimate(flops=10**9, bytes_accessed=4 * MIB, transcendentals=0),
        name="near",
    )(volumes, within, select, w1_near, w2)
    rows = C2 // narrow
    begun, term, pre = pl.pallas_call(
        functools.partial(far_kernel, wide // 2, scale),
        in_specs=[fast] * 8,
        out_specs=(pl.BlockSpec(memory_space=pl.ANY), fast, fast),
        out_shape=(bf16((1, 1, C2, cells_out)), bf16((C2, PACKED)), f32((PLANE, 2 * C2))),
        scratch_shapes=[
            pltpu.VMEM((4, ROWS, LANES + PLANE), jnp.bfloat16),
            pltpu.VMEM((9 * ROWS, PLANE), jnp.bfloat16),
            pltpu.VMEM((2 * C1, PLANE + 2 * LANES), jnp.bfloat16),
            pltpu.VMEM((6 * C1, PLANE), jnp.bfloat16),
            pltpu.VMEM((PLANE, 6 * C1), jnp.bfloat16),
            pltpu.VMEM((3, PLANE + 2 * HALF, LANES), jnp.float32),
            pltpu.VMEM((PLANE + 2 * HALF, LANES), jnp.bfloat16),
            pltpu.VMEM((2, 6 * C1, 3 * LANES), jnp.float32),
            pltpu.VMEM((1, 1, C2, cells_out), jnp.bfloat16),
            pltpu.SemaphoreType.DMA,
        ],
        compiler_params=pltpu.CompilerParams(vmem_limit_bytes=16 * MIB),
        name="far",
    )(across, select, w1_far, w2, cot, first, near, pre)
    half = rows // 2
    received = lax.all_to_all(term, ("narrow", "core"), 0, 0, tiled=True)
    owned = jnp.sum(received.reshape(2 * narrow, half, PACKED).astype(jnp.float32), axis=0).astype(jnp.bfloat16)
    parts = lax.all_to_all(jnp.broadcast_to(owned[None], (wide, half, PACKED)), WIDE, 0, 0, tiled=True)
    total = jnp.sum(parts.reshape(wide // 2, rows, PACKED).astype(jnp.float32), axis=0)
    anywhere = pl.BlockSpec(memory_space=pl.ANY)
    weight_grad, output = pl.pallas_call(
        finish_kernel,
        in_specs=[fast, fast, anywhere],
        out_specs=(anywhere, anywhere),
        out_shape=(f32((27, rows, C1)), bf16((1, 1, C2, cells_out))),
        scratch_shapes=[
            pltpu.VMEM((27, rows, C1), jnp.float32),
            pltpu.VMEM((1, 1, C2, cells_out), jnp.bfloat16),
            pltpu.SemaphoreType.DMA((3,)),
            pltpu.SemaphoreType.DMA,
        ],
        input_output_aliases={2: 1},
        compiler_params=pltpu.CompilerParams(vmem_limit_bytes=8 * MIB),
        name="finish",
    )(total, pre, begun)
    return (output, weight_grad)


def solution(mesh):
    wide, narrow = mesh.devices.shape
    split = jax.sharding.Mesh(mesh.devices.reshape(wide // 2, 2, narrow), ("chip", "core", "narrow"))
    return jax.shard_map(
        body,
        mesh=split,
        in_specs=(P("narrow", None, None, WIDE, None), P(), P(), P("narrow", None, None, WIDE)),
        out_specs=(P("narrow", None, None, WIDE), P(None, "narrow", None)),
        check_vma=False,
    )
```

```python
import functools
import math

import jax
import jax.numpy as jnp
import numpy as np
from jax import lax
from jax.experimental import pallas as pl
from jax.experimental.pallas import tpu as pltpu
from jax.sharding import PartitionSpec as P

CIN = 4
C1 = 32
C2 = 64
PLANES = 4
CELLS = 4096
HALF = 32
PLANE = 1024
LANES = 128
ROWS = CIN * PLANES
CHUNK = 512
PACKED = 7 * LANES
MIB = 2**20
WIDE = ("chip", "core")
neg_slope = 0.3


def selection():
    table = np.zeros((CHUNK, 2, 2, 4, HALF), np.float32)
    for py in range(2):
        for px in range(2):
            for row in range(4):
                for col in range(HALF):
                    table[(2 * row + py) * 64 + 2 * col + px, py, px, row, col] = 1
    return table.reshape(CHUNK, CHUNK)


def placement():
    table = np.zeros((2, 27, CIN, 4, CHUNK), np.float32)
    for odd in range(2):
        for a in range(3):
            for bc in range(9):
                for i in range(CIN):
                    for q in range(4):
                        slab, plane = divmod(2 * q + a + 1, PLANES)
                        inner = i * PLANES + plane
                        if slab == 1:
                            column = bc * 2 * ROWS + inner
                        elif (slab == 0) == (odd == 1):
                            column = bc * 2 * ROWS + ROWS + inner
                        else:
                            column = 18 * ROWS + bc * ROWS + inner
                        table[odd, 9 * a + bc, i, q, column] = 1
    return table.reshape(2, 27 * CIN, 4 * CHUNK)


def leaky_relu(value):
    return jnp.where(value > 0, value, neg_slope * value)


def plane_rows(volume_ref):
    return jnp.concatenate([volume_ref[0, 0, i] for i in range(CIN)], axis=0)


def column_masks():
    column = lax.broadcasted_iota(jnp.int32, (1, PLANE), 1) % HALF
    left_ok = jnp.where(column > 0, 1.0, 0.0).astype(jnp.bfloat16)
    right_ok = jnp.where(column < HALF - 1, 1.0, 0.0).astype(jnp.bfloat16)
    return left_ok, right_ok


def strided_taps(rows, select_ref, parity_ref, taps_ref):
    count = rows.shape[0]
    left_ok, _ = column_masks()
    chunks = jnp.concatenate([rows[:, CHUNK * j : CHUNK * (j + 1)] for j in range(8)], axis=0)
    for p in range(4):
        parity_ref[p, :, 0:LANES] = jnp.zeros((count, LANES), jnp.bfloat16)
    for py in range(2):
        parts = jnp.dot(
            chunks, select_ref[:, 256 * py : 256 * py + 256], preferred_element_type=jnp.float32
        ).astype(jnp.bfloat16)
        for px in range(2):
            for j in range(8):
                parity_ref[2 * py + px, :, LANES * (j + 1) : LANES * (j + 2)] = parts[
                    j * count : (j + 1) * count, px * LANES : (px + 1) * LANES
                ]
    for b in range(3):
        for c in range(3):
            begin = LANES - HALF * (b == 0) - (c == 0)
            part = parity_ref[2 * (b != 1) + (c != 1), :, begin : begin + PLANE]
            if c == 0:
                part = part * left_ok
            taps_ref[(3 * b + c) * count : (3 * b + c + 1) * count, :] = part


def shifted_columns(act_ref, columns_ref):
    left_ok, right_ok = column_masks()
    for c in range(3):
        begin = LANES + c - 1
        part = act_ref[:, begin : begin + PLANE]
        if c == 0:
            part = part * left_ok
        if c == 2:
            part = part * right_ok
        columns_ref[c * 2 * C1 : (c + 1) * 2 * C1, :] = part


def second_layer(w2, columns_ref, turned_ref, rowed_ref):
    blank = jnp.zeros((HALF, LANES), jnp.float32)
    for b in (0, 2):
        rowed_ref[b, 0:HALF, :] = blank
        rowed_ref[b, HALF + PLANE :, :] = blank
    for n in range(4):
        cells = slice(256 * n, 256 * n + 256)
        turned_ref[cells, :] = columns_ref[:, cells].T
    for n in range(4):
        sums = jnp.dot(turned_ref[256 * n : 256 * n + 256, :], w2, preferred_element_type=jnp.float32)
        for b in range(3):
            rowed_ref[b, HALF + 256 * n : HALF + 256 * n + 256, :] = sums[:, b * LANES : (b + 1) * LANES]


def row_sum(rowed_ref, n):
    begins = [HALF * b + 256 * n for b in range(3)]
    first, second, third = (rowed_ref[b, begin : begin + 256, :] for b, begin in enumerate(begins))
    return first + second + third


def clear_margins(act_ref):
    margin = jnp.zeros((2 * C1, LANES), jnp.bfloat16)
    act_ref[:, 0:LANES] = margin
    act_ref[:, LANES + PLANE :] = margin


def prepare_kernel(
    k1_hbm, place_hbm, k2_hbm, select_hbm, cot_hbm,
    w1_near_ref, w1_far_ref, w2_ref, select_ref, turned_ref,
    k1_ref, place_ref, k2_ref, cot_ref, k1_rows_ref, sems,
):
    odd = lax.axis_index("core")
    moves = (
        (k1_hbm, k1_ref), (k2_hbm, k2_ref), (place_hbm.at[odd], place_ref), (cot_hbm, cot_ref), (select_hbm, select_ref),
    )
    copies = [pltpu.make_async_copy(src, dst, sems.at[k]) for k, (src, dst) in enumerate(moves)]
    for copy in copies:
        copy.start()
    copies[0].wait()
    for tap in range(27):
        k1_rows_ref[CIN * tap : CIN * (tap + 1), :] = k1_ref[tap].astype(jnp.float32)
    copies[1].wait()
    blank = jnp.zeros((C1, C2), jnp.bfloat16)

    def stacked(bc, pair):
        k = [blank] + [k2_ref[9 * a + bc] for a in range(3)] + [blank]
        lower = jnp.concatenate(k[1 + 2 * pair : 3 + 2 * pair], axis=0)
        upper = jnp.concatenate(k[2 * pair : 2 + 2 * pair], axis=0)
        return jnp.concatenate([lower, upper], axis=1)

    for pair in range(2):
        for b in range(3):
            for c in range(3):
                w2_ref[pair, c * 2 * C1 : (c + 1) * 2 * C1, b * LANES : (b + 1) * LANES] = stacked(3 * b + c, pair)
    copies[2].wait()
    spread = lax.dot_general(
        k1_rows_ref[...].astype(jnp.bfloat16), place_ref[...],
        (((0,), (0,)), ((), ())), preferred_element_type=jnp.float32,
    ).astype(jnp.bfloat16)
    for q in range(4):
        rows = slice(q % 2 * C1, (q % 2 + 1) * C1)
        w1_near_ref[q // 2, rows, :] = spread[:, CHUNK * q : CHUNK * q + 18 * ROWS]
        w1_far_ref[q // 2, rows, :] = spread[:, CHUNK * q + 18 * ROWS : CHUNK * q + 27 * ROWS]
    copies[3].wait()
    for n in range(4):
        planes = [cot_ref[0, 0, :, z * PLANE + 256 * n : z * PLANE + 256 * n + 256] for z in range(2)]
        turned_ref[256 * n : 256 * n + 256, :] = jnp.concatenate(planes, axis=0).T
    copies[4].wait()


def near_kernel(
    own_ref, within_ref, select_ref, w1_ref, w2_ref, first_ref, columns_ref, pre_ref,
    parity_ref, taps_ref, act_ref, turned_ref, rowed_ref,
):
    odd = lax.axis_index("core")
    rows = jnp.concatenate([plane_rows(own_ref), plane_rows(within_ref)], axis=0)
    strided_taps(rows, select_ref, parity_ref, taps_ref)
    clear_margins(act_ref)
    for n in range(4):
        here = slice(256 * n, 256 * n + 256)
        first_ref[:, here] = jnp.dot(w1_ref[odd], taps_ref[:, here], preferred_element_type=jnp.float32)
        complete = jnp.dot(w1_ref[1 - odd], taps_ref[:, here], preferred_element_type=jnp.float32)
        act_ref[:, LANES + 256 * n : LANES + 256 * n + 256] = leaky_relu(complete).astype(jnp.bfloat16)
    shifted_columns(act_ref, columns_ref)
    second_layer(w2_ref[1 - odd], columns_ref, turned_ref, rowed_ref)
    for n in range(4):
        pre_ref[256 * n : 256 * n + 256, :] = row_sum(rowed_ref, n)


def emit_activations(pre_ref, out_ref, out_hbm, sem):
    for n in range(4):
        output = leaky_relu(pre_ref[256 * n : 256 * n + 256, :]).astype(jnp.bfloat16).T
        for z in range(2):
            out_ref[0, 0, :, z * PLANE + 256 * n : z * PLANE + 256 * n + 256] = output[z * C2 : (z + 1) * C2]
    copy = pltpu.make_async_copy(out_ref, out_hbm, sem)
    copy.start()
    copy.wait()


def far_kernel(
    chips, scale, across_ref, select_ref, w1_ref, w2_ref, cot_ref, first_ref, near_ref, near_pre_ref, out_hbm, grad_ref, pre_ref,
    parity_ref, taps_ref, act_ref, columns_ref, turned_ref, rowed_ref, back_ref, swapped_ref, out_ref, out_sem,
):
    odd = lax.axis_index("core")
    last = (lax.axis_index("chip") == chips - 1) & (odd == 1)
    inside = jnp.where(last, 0.0, 1.0)
    strided_taps(plane_rows(across_ref), select_ref, parity_ref, taps_ref)
    clear_margins(act_ref)
    for n in range(4):
        here = slice(256 * n, 256 * n + 256)
        first_pre = first_ref[:, here] + jnp.dot(w1_ref[odd], taps_ref[:, here], preferred_element_type=jnp.float32)
        first_act = leaky_relu(first_pre)
        there = slice(LANES + 256 * n, LANES + 256 * n + 256)
        act_ref[0:C1, there] = first_act[0:C1].astype(jnp.bfloat16)
        act_ref[C1:, there] = (first_act[C1:] * inside).astype(jnp.bfloat16)
    columns_ref[1 - odd] = near_ref[...]
    shifted_columns(act_ref, columns_ref.at[odd])
    second_layer(w2_ref[odd], columns_ref.at[odd], turned_ref, rowed_ref)
    margin = jnp.zeros((HALF, LANES), jnp.bfloat16)
    for ref in (back_ref, swapped_ref):
        ref[0:HALF, :] = margin
        ref[HALF + PLANE :, :] = margin
    for n in range(4):
        cells = slice(256 * n, 256 * n + 256)
        pre = near_pre_ref[cells, :] + row_sum(rowed_ref, n)
        pre_ref[cells, :] = pre
        back = (cot_ref[cells, :].astype(jnp.float32) * jnp.where(pre > 0, 1.0, neg_slope)).astype(jnp.bfloat16)
        here = slice(HALF + 256 * n, HALF + 256 * n + 256)
        back_ref[here, :] = back
        swapped_ref[here, :] = jnp.concatenate([back[:, C2:], back[:, 0:C2]], axis=1)
    low = lax.broadcasted_iota(jnp.int32, (1, LANES), 1) < C2
    rows_of = [slice((2 - b) * HALF, (2 - b) * HALF + PLANE) for b in range(3)]
    operands = []
    for left_ref, right_ref in ((back_ref, swapped_ref), (swapped_ref, back_ref)):
        first_two = jnp.where(low, left_ref[rows_of[0], :], right_ref[rows_of[1], :])
        operands.append(jnp.concatenate([first_two, left_ref[rows_of[2], :]], axis=1))

    def plane_columns(q, c):
        begin = 2 * C1 * c + C1 * (q % 2)
        return columns_ref[q // 2, begin : begin + C1, :]

    columns = [jnp.concatenate([plane_columns(a + z, c) for a in range(3) for c in range(3)], axis=0) for z in range(2)]
    sums = scale * jnp.dot(
        jnp.concatenate(columns, axis=1), jnp.concatenate(operands, axis=0), preferred_element_type=jnp.float32
    )
    left, right, ends = sums[0:256, 0:LANES], sums[0:256, LANES:], sums[256:]
    turned = [left[0:LANES].T, left[LANES:].T]
    third = jnp.where(low, right[0:LANES], pltpu.roll(right[LANES:], C2, 1)).T
    fourth = jnp.concatenate([ends[:, 0:LANES], ends[:, LANES:]] * 2, axis=0).T
    group = lax.broadcasted_iota(jnp.int32, (1, LANES), 1) // C1
    tiles = [turned[0][0:C2], turned[1][0:C2], turned[0][C2:], turned[1][C2:], third[0:C2], third[C2:]]
    tiles.append(jnp.where(group < 2, fourth[0:C2], pltpu.roll(fourth[C2:], C2, 1)))
    for k, tile in enumerate(tiles):
        grad_ref[:, k * LANES : (k + 1) * LANES] = tile.astype(jnp.bfloat16)
    early = lax.axis_index("narrow") == 0
    pl.when(early)(lambda: emit_activations(pre_ref, out_ref, out_hbm, out_sem))


def slots():
    where = []
    for a in range(3):
        for b in range(3):
            for c in range(3):
                tile, group = divmod(3 * a + c, 4)
                where.append((2 * b + tile, group) if tile < 2 else (6, (0, 2, 1)[b]))
    return where


def finish_kernel(total_ref, pre_ref, begun_hbm, grad_hbm, out_hbm, grad_ref, out_ref, sems, out_sem):
    del begun_hbm
    copies = []
    for k in range(3):
        for tap in range(9 * k, 9 * k + 9):
            tile, slot = slots()[tap]
            begin = tile * LANES + slot * C1
            grad_ref[tap] = total_ref[:, begin : begin + C1]
        here = slice(9 * k, 9 * k + 9)
        copies.append(pltpu.make_async_copy(grad_ref.at[here], grad_hbm.at[here], sems.at[k]))
        copies[k].start()
    late = lax.axis_index("narrow") > 0
    pl.when(late)(lambda: emit_activations(pre_ref, out_ref, out_hbm, out_sem))
    for copy in copies:
        copy.wait()


def body(volumes, first_kernel, second_kernel, cotangent):
    wide = lax.axis_size(WIDE)
    narrow = lax.axis_size("narrow")
    cells_out = cotangent.shape[3]
    scale = 1.0 / math.sqrt(wide * narrow * cells_out)
    across = lax.ppermute(volumes, WIDE, [p for k in range(1, wide - 1, 2) for p in ((k, k + 1), (k + 1, k))])
    pairs = [p for k in range(0, wide - 1, 2) for p in ((k, k + 1), (k + 1, k))]
    within = lax.ppermute(volumes, WIDE, pairs)
    pinned = pl.BlockSpec(memory_space=pltpu.HBM)
    fast = pl.BlockSpec(memory_space=pltpu.VMEM)
    bf16 = functools.partial(jax.ShapeDtypeStruct, dtype=jnp.bfloat16)
    f32 = functools.partial(jax.ShapeDtypeStruct, dtype=jnp.float32)
    stored = (
        first_kernel.transpose(0, 2, 1), jnp.asarray(placement(), jnp.bfloat16), second_kernel.transpose(0, 2, 1),
        jnp.asarray(selection(), jnp.bfloat16), cotangent,
    )
    w1_near, w1_far, w2, select, cot = pl.pallas_call(
        prepare_kernel,
        in_specs=[pinned] * 5,
        out_specs=(fast,) * 5,
        out_shape=(
            bf16((2, 2 * C1, 18 * ROWS)), bf16((2, 2 * C1, 9 * ROWS)), bf16((2, 6 * C1, 6 * C2)),
            bf16((CHUNK, CHUNK)), bf16((PLANE, 2 * C2)),
        ),
        scratch_shapes=[
            pltpu.VMEM((27, CIN, C1), jnp.bfloat16),
            pltpu.VMEM((27 * CIN, 4 * CHUNK), jnp.bfloat16),
            pltpu.VMEM((27, C1, C2), jnp.bfloat16),
            pltpu.VMEM(cotangent.shape, jnp.bfloat16),
            pltpu.VMEM((27 * CIN, C1), jnp.float32),
            pltpu.SemaphoreType.DMA((5,)),
        ],
        compiler_params=pltpu.CompilerParams(vmem_limit_bytes=12 * MIB),
        cost_estimate=pl.CostEstimate(flops=10**9, bytes_accessed=4 * MIB, transcendentals=0),
        name="prepare",
    )(*(pltpu.with_memory_space_constraint(x, pltpu.HBM) for x in stored))
    first, near, pre = pl.pallas_call(
        near_kernel,
        in_specs=[fast] * 5,
        out_specs=(fast,) * 3,
        out_shape=(f32((2 * C1, PLANE)), bf16((6 * C1, PLANE)), f32((PLANE, 2 * C2))),
        scratch_shapes=[
            pltpu.VMEM((4, 2 * ROWS, LANES + PLANE), jnp.bfloat16),
            pltpu.VMEM((18 * ROWS, PLANE), jnp.bfloat16),
            pltpu.VMEM((2 * C1, PLANE + 2 * LANES), jnp.bfloat16),
            pltpu.VMEM((PLANE, 6 * C1), jnp.bfloat16),
            pltpu.VMEM((3, PLANE + 2 * HALF, LANES), jnp.float32),
        ],
        compiler_params=pltpu.CompilerParams(vmem_limit_bytes=16 * MIB),
        cost_estimate=pl.CostEstimate(flops=10**9, bytes_accessed=4 * MIB, transcendentals=0),
        name="near",
    )(volumes, within, select, w1_near, w2)
    rows = C2 // narrow
    begun, term, pre = pl.pallas_call(
        functools.partial(far_kernel, wide // 2, scale),
        in_specs=[fast] * 8,
        out_specs=(pl.BlockSpec(memory_space=pl.ANY), fast, fast),
        out_shape=(bf16((1, 1, C2, cells_out)), bf16((C2, PACKED)), f32((PLANE, 2 * C2))),
        scratch_shapes=[
            pltpu.VMEM((4, ROWS, LANES + PLANE), jnp.bfloat16),
            pltpu.VMEM((9 * ROWS, PLANE), jnp.bfloat16),
            pltpu.VMEM((2 * C1, PLANE + 2 * LANES), jnp.bfloat16),
            pltpu.VMEM((2, 6 * C1, PLANE), jnp.bfloat16),
            pltpu.VMEM((PLANE, 6 * C1), jnp.bfloat16),
            pltpu.VMEM((3, PLANE + 2 * HALF, LANES), jnp.float32),
            pltpu.VMEM((PLANE + 2 * HALF, LANES), jnp.bfloat16),
            pltpu.VMEM((PLANE + 2 * HALF, LANES), jnp.bfloat16),
            pltpu.VMEM((1, 1, C2, cells_out), jnp.bfloat16),
            pltpu.SemaphoreType.DMA,
        ],
        compiler_params=pltpu.CompilerParams(vmem_limit_bytes=16 * MIB),
        name="far",
    )(across, select, w1_far, w2, cot, first, near, pre)
    half = rows // 2
    received = lax.all_to_all(term, ("narrow", "core"), 0, 0, tiled=True)
    owned = jnp.sum(received.reshape(2 * narrow, half, PACKED).astype(jnp.float32), axis=0).astype(jnp.bfloat16)
    parts = lax.all_to_all(jnp.broadcast_to(owned[None], (wide, half, PACKED)), WIDE, 0, 0, tiled=True)
    total = jnp.sum(parts.reshape(wide // 2, rows, PACKED).astype(jnp.float32), axis=0)
    anywhere = pl.BlockSpec(memory_space=pl.ANY)
    weight_grad, output = pl.pallas_call(
        finish_kernel,
        in_specs=[fast, fast, anywhere],
        out_specs=(anywhere, anywhere),
        out_shape=(f32((27, rows, C1)), bf16((1, 1, C2, cells_out))),
        scratch_shapes=[
            pltpu.VMEM((27, rows, C1), jnp.float32),
            pltpu.VMEM((1, 1, C2, cells_out), jnp.bfloat16),
            pltpu.SemaphoreType.DMA((3,)),
            pltpu.SemaphoreType.DMA,
        ],
        input_output_aliases={2: 1},
        compiler_params=pltpu.CompilerParams(vmem_limit_bytes=8 * MIB),
        name="finish",
    )(total, pre, begun)
    return (output, weight_grad)


def solution(mesh):
    wide, narrow = mesh.devices.shape
    split = jax.sharding.Mesh(mesh.devices.reshape(wide // 2, 2, narrow), ("chip", "core", "narrow"))
    return jax.shard_map(
        body,
        mesh=split,
        in_specs=(P("narrow", None, None, WIDE, None), P(), P(), P("narrow", None, None, WIDE)),
        out_specs=(P("narrow", None, None, WIDE), P(None, "narrow", None)),
        check_vma=False,
    )
```

```python
import functools
import math

import jax
import jax.numpy as jnp
import numpy as np
from jax import lax
from jax.experimental import pallas as pl
from jax.experimental.pallas import tpu as pltpu
from jax.sharding import PartitionSpec as P

CIN = 4
C1 = 32
C2 = 64
PLANES = 4
CELLS = 4096
HALF = 32
PLANE = 1024
LANES = 128
ROWS = CIN * PLANES
CHUNK = 512
PACKED = 8 * LANES
MIB = 2**20
WIDE = ("row", "column", "core")
PART = 256
neg_slope = 0.3


def selection():
    table = np.zeros((CHUNK, 2, 2, 4, HALF), np.float32)
    for py in range(2):
        for px in range(2):
            for row in range(4):
                for col in range(HALF):
                    table[(2 * row + py) * 64 + 2 * col + px, py, px, row, col] = 1
    return table.reshape(CHUNK, CHUNK)


def placement():
    table = np.zeros((2, 27, CIN, 4, CHUNK), np.float32)
    for odd in range(2):
        for a in range(3):
            for bc in range(9):
                for i in range(CIN):
                    for q in range(4):
                        slab, plane = divmod(2 * q + a + 1, PLANES)
                        inner = i * PLANES + plane
                        if slab == 1:
                            column = bc * 2 * ROWS + inner
                        elif (slab == 0) == (odd == 1):
                            column = bc * 2 * ROWS + ROWS + inner
                        else:
                            column = 18 * ROWS + bc * ROWS + inner
                        table[odd, 9 * a + bc, i, q, column] = 1
    return table.reshape(2, 27 * CIN, 4 * CHUNK)


def chip_index():
    return 2 * lax.axis_index("row") + lax.axis_index("column")


def leaky_relu(value):
    return jnp.where(value > 0, value, neg_slope * value)


def plane_rows(volume_ref):
    return jnp.concatenate([volume_ref[0, 0, i] for i in range(CIN)], axis=0)


def column_masks():
    column = lax.broadcasted_iota(jnp.int32, (1, PLANE), 1) % HALF
    left_ok = jnp.where(column > 0, 1.0, 0.0).astype(jnp.bfloat16)
    right_ok = jnp.where(column < HALF - 1, 1.0, 0.0).astype(jnp.bfloat16)
    return left_ok, right_ok


def strided_taps(rows, select_ref, parity_ref, taps_ref):
    count = rows.shape[0]
    left_ok, _ = column_masks()
    chunks = jnp.concatenate([rows[:, CHUNK * j : CHUNK * (j + 1)] for j in range(8)], axis=0)
    for p in range(4):
        parity_ref[p, :, 0:LANES] = jnp.zeros((count, LANES), jnp.bfloat16)
    for py in range(2):
        parts = jnp.dot(
            chunks, select_ref[:, 256 * py : 256 * py + 256], preferred_element_type=jnp.float32
        ).astype(jnp.bfloat16)
        for px in range(2):
            for j in range(8):
                parity_ref[2 * py + px, :, LANES * (j + 1) : LANES * (j + 2)] = parts[
                    j * count : (j + 1) * count, px * LANES : (px + 1) * LANES
                ]
    for b in range(3):
        for c in range(3):
            begin = LANES - HALF * (b == 0) - (c == 0)
            part = parity_ref[2 * (b != 1) + (c != 1), :, begin : begin + PLANE]
            if c == 0:
                part = part * left_ok
            taps_ref[(3 * b + c) * count : (3 * b + c + 1) * count, :] = part


def shifted_columns(act_ref, columns_ref):
    left_ok, right_ok = column_masks()
    for c in range(3):
        begin = LANES + c - 1
        part = act_ref[:, begin : begin + PLANE]
        if c == 0:
            part = part * left_ok
        if c == 2:
            part = part * right_ok
        columns_ref[c * 2 * C1 : (c + 1) * 2 * C1, :] = part


def second_layer(w2, columns_ref, turned_ref, rowed_ref):
    blank = jnp.zeros((HALF, LANES), jnp.float32)
    for b in (0, 2):
        rowed_ref[b, 0:HALF, :] = blank
        rowed_ref[b, HALF + PLANE :, :] = blank
    for n in range(4):
        cells = slice(256 * n, 256 * n + 256)
        turned_ref[cells, :] = columns_ref[:, cells].T
    for n in range(4):
        sums = jnp.dot(turned_ref[256 * n : 256 * n + 256, :], w2, preferred_element_type=jnp.float32)
        for b in range(3):
            rowed_ref[b, HALF + 256 * n : HALF + 256 * n + 256, :] = sums[:, b * LANES : (b + 1) * LANES]


def row_sum(rowed_ref, n):
    begins = [HALF * b + 256 * n for b in range(3)]
    first, second, third = (rowed_ref[b, begin : begin + 256, :] for b, begin in enumerate(begins))
    return first + second + third


def clear_margins(act_ref):
    margin = jnp.zeros((2 * C1, LANES), jnp.bfloat16)
    act_ref[:, 0:LANES] = margin
    act_ref[:, LANES + PLANE :] = margin


def prepare_kernel(
    k1_hbm, place_hbm, k2_hbm, select_hbm, cot_hbm,
    w1_near_ref, w1_far_ref, w2_ref, select_ref, turned_ref,
    k1_ref, place_ref, k2_ref, cot_ref, k1_rows_ref, sems,
):
    odd = lax.axis_index("core")
    moves = (
        (k1_hbm, k1_ref), (k2_hbm, k2_ref), (place_hbm.at[odd], place_ref), (cot_hbm, cot_ref), (select_hbm, select_ref),
    )
    copies = [pltpu.make_async_copy(src, dst, sems.at[k]) for k, (src, dst) in enumerate(moves)]
    for copy in copies:
        copy.start()
    copies[0].wait()
    for tap in range(27):
        k1_rows_ref[CIN * tap : CIN * (tap + 1), :] = k1_ref[tap].astype(jnp.float32)
    copies[1].wait()
    blank = jnp.zeros((C1, C2), jnp.bfloat16)

    def stacked(bc, pair):
        k = [blank] + [k2_ref[9 * a + bc] for a in range(3)] + [blank]
        lower = jnp.concatenate(k[1 + 2 * pair : 3 + 2 * pair], axis=0)
        upper = jnp.concatenate(k[2 * pair : 2 + 2 * pair], axis=0)
        return jnp.concatenate([lower, upper], axis=1)

    for pair in range(2):
        for b in range(3):
            for c in range(3):
                w2_ref[pair, c * 2 * C1 : (c + 1) * 2 * C1, b * LANES : (b + 1) * LANES] = stacked(3 * b + c, pair)
    copies[2].wait()
    spread = lax.dot_general(
        k1_rows_ref[...].astype(jnp.bfloat16), place_ref[...],
        (((0,), (0,)), ((), ())), preferred_element_type=jnp.float32,
    ).astype(jnp.bfloat16)
    for q in range(4):
        rows = slice(q % 2 * C1, (q % 2 + 1) * C1)
        w1_near_ref[q // 2, rows, :] = spread[:, CHUNK * q : CHUNK * q + 18 * ROWS]
        w1_far_ref[q // 2, rows, :] = spread[:, CHUNK * q + 18 * ROWS : CHUNK * q + 27 * ROWS]
    copies[3].wait()
    for n in range(4):
        planes = [cot_ref[0, 0, :, z * PLANE + 256 * n : z * PLANE + 256 * n + 256] for z in range(2)]
        turned_ref[256 * n : 256 * n + 256, :] = jnp.concatenate(planes, axis=0).T
    copies[4].wait()


def near_kernel(
    own_ref, within_ref, select_ref, w1_ref, w2_ref, first_ref, columns_ref, pre_ref,
    parity_ref, taps_ref, act_ref, turned_ref, rowed_ref,
):
    odd = lax.axis_index("core")
    rows = jnp.concatenate([plane_rows(own_ref), plane_rows(within_ref)], axis=0)
    strided_taps(rows, select_ref, parity_ref, taps_ref)
    clear_margins(act_ref)
    for n in range(4):
        here = slice(256 * n, 256 * n + 256)
        first_ref[:, here] = jnp.dot(w1_ref[odd], taps_ref[:, here], preferred_element_type=jnp.float32)
        complete = jnp.dot(w1_ref[1 - odd], taps_ref[:, here], preferred_element_type=jnp.float32)
        act_ref[:, LANES + 256 * n : LANES + 256 * n + 256] = leaky_relu(complete).astype(jnp.bfloat16)
    shifted_columns(act_ref, columns_ref)
    second_layer(w2_ref[1 - odd], columns_ref, turned_ref, rowed_ref)
    for n in range(4):
        pre_ref[256 * n : 256 * n + 256, :] = row_sum(rowed_ref, n)


def emit_activations(pre_ref, out_ref, out_hbm, sem):
    for n in range(4):
        output = leaky_relu(pre_ref[256 * n : 256 * n + 256, :]).astype(jnp.bfloat16).T
        for z in range(2):
            out_ref[0, 0, :, z * PLANE + 256 * n : z * PLANE + 256 * n + 256] = output[z * C2 : (z + 1) * C2]
    copy = pltpu.make_async_copy(out_ref, out_hbm, sem)
    copy.start()
    copy.wait()


def far_kernel(
    chips, scale, across_ref, select_ref, w1_ref, w2_ref, cot_ref, first_ref, near_ref, near_pre_ref, out_hbm, grad_ref, pre_ref,
    parity_ref, taps_ref, act_ref, columns_ref, turned_ref, rowed_ref, back_ref, swapped_ref, out_ref, out_sem,
):
    odd = lax.axis_index("core")
    last = (chip_index() == chips - 1) & (odd == 1)
    inside = jnp.where(last, 0.0, 1.0)
    strided_taps(plane_rows(across_ref), select_ref, parity_ref, taps_ref)
    clear_margins(act_ref)
    for n in range(4):
        here = slice(256 * n, 256 * n + 256)
        first_pre = first_ref[:, here] + jnp.dot(w1_ref[odd], taps_ref[:, here], preferred_element_type=jnp.float32)
        first_act = leaky_relu(first_pre)
        there = slice(LANES + 256 * n, LANES + 256 * n + 256)
        act_ref[0:C1, there] = first_act[0:C1].astype(jnp.bfloat16)
        act_ref[C1:, there] = (first_act[C1:] * inside).astype(jnp.bfloat16)
    columns_ref[1 - odd] = near_ref[...]
    shifted_columns(act_ref, columns_ref.at[odd])
    second_layer(w2_ref[odd], columns_ref.at[odd], turned_ref, rowed_ref)
    margin = jnp.zeros((HALF, LANES), jnp.bfloat16)
    for ref in (back_ref, swapped_ref):
        ref[0:HALF, :] = margin
        ref[HALF + PLANE :, :] = margin
    for n in range(4):
        cells = slice(256 * n, 256 * n + 256)
        pre = near_pre_ref[cells, :] + row_sum(rowed_ref, n)
        pre_ref[cells, :] = pre
        back = (cot_ref[cells, :].astype(jnp.float32) * jnp.where(pre > 0, 1.0, neg_slope)).astype(jnp.bfloat16)
        here = slice(HALF + 256 * n, HALF + 256 * n + 256)
        back_ref[here, :] = back
        swapped_ref[here, :] = jnp.concatenate([back[:, C2:], back[:, 0:C2]], axis=1)
    low = lax.broadcasted_iota(jnp.int32, (1, LANES), 1) < C2
    rows_of = [slice((2 - b) * HALF, (2 - b) * HALF + PLANE) for b in range(3)]
    operands = []
    for left_ref, right_ref in ((back_ref, swapped_ref), (swapped_ref, back_ref)):
        first_two = jnp.where(low, left_ref[rows_of[0], :], right_ref[rows_of[1], :])
        operands.append(jnp.concatenate([first_two, left_ref[rows_of[2], :]], axis=1))

    def plane_columns(q, c):
        begin = 2 * C1 * c + C1 * (q % 2)
        return columns_ref[q // 2, begin : begin + C1, :]

    columns = [jnp.concatenate([plane_columns(a + z, c) for a in range(3) for c in range(3)], axis=0) for z in range(2)]
    sums = scale * jnp.dot(
        jnp.concatenate(columns, axis=1), jnp.concatenate(operands, axis=0), preferred_element_type=jnp.float32
    )
    left, right, ends = sums[0:256, 0:LANES], sums[0:256, LANES:], sums[256:]
    turned = [left[0:LANES].T, left[LANES:].T]
    third = jnp.where(low, right[0:LANES], pltpu.roll(right[LANES:], C2, 1)).T
    fourth = jnp.concatenate([ends[:, 0:LANES], ends[:, LANES:]] * 2, axis=0).T
    group = lax.broadcasted_iota(jnp.int32, (1, LANES), 1) // C1
    tiles = [turned[0][0:C2], turned[1][0:C2], turned[0][C2:], turned[1][C2:], third[0:C2], third[C2:]]
    tiles.append(jnp.where(group < 2, fourth[0:C2], pltpu.roll(fourth[C2:], C2, 1)))
    tiles.append(tiles[-1])
    owners = grad_ref.shape[0] // 4
    rows = C2 // owners
    for n in range(owners):
        for k, tile in enumerate(tiles):
            lanes = slice(k % 2 * LANES, k % 2 * LANES + LANES)
            grad_ref[4 * n + k // 2, :, lanes] = tile[n * rows : (n + 1) * rows].astype(jnp.bfloat16)
    early = lax.axis_index("narrow") == 0
    pl.when(early)(lambda: emit_activations(pre_ref, out_ref, out_hbm, out_sem))


def slots():
    where = []
    for a in range(3):
        for b in range(3):
            for c in range(3):
                tile, group = divmod(3 * a + c, 4)
                where.append((2 * b + tile, group) if tile < 2 else (6, (0, 2, 1)[b]))
    return where


def finish_kernel(total_ref, pre_ref, begun_hbm, grad_hbm, out_hbm, grad_ref, out_ref, sems, out_sem):
    del begun_hbm
    copies = []
    for k in range(3):
        for tap in range(9 * k, 9 * k + 9):
            tile, slot = slots()[tap]
            begin = tile % 2 * LANES + slot * C1
            grad_ref[tap] = total_ref[tile // 2, :, begin : begin + C1]
        here = slice(9 * k, 9 * k + 9)
        copies.append(pltpu.make_async_copy(grad_ref.at[here], grad_hbm.at[here], sems.at[k]))
        copies[k].start()
    late = lax.axis_index("narrow") > 0
    pl.when(late)(lambda: emit_activations(pre_ref, out_ref, out_hbm, out_sem))
    for copy in copies:
        copy.wait()


def body(volumes, first_kernel, second_kernel, cotangent):
    wide = lax.axis_size(WIDE)
    narrow = lax.axis_size("narrow")
    cells_out = cotangent.shape[3]
    scale = 1.0 / math.sqrt(wide * narrow * cells_out)
    across = lax.ppermute(volumes, WIDE, [p for k in range(1, wide - 1, 2) for p in ((k, k + 1), (k + 1, k))])
    pairs = [p for k in range(0, wide - 1, 2) for p in ((k, k + 1), (k + 1, k))]
    within = lax.ppermute(volumes, WIDE, pairs)
    pinned = pl.BlockSpec(memory_space=pltpu.HBM)
    fast = pl.BlockSpec(memory_space=pltpu.VMEM)
    bf16 = functools.partial(jax.ShapeDtypeStruct, dtype=jnp.bfloat16)
    f32 = functools.partial(jax.ShapeDtypeStruct, dtype=jnp.float32)
    stored = (
        first_kernel.transpose(0, 2, 1), jnp.asarray(placement(), jnp.bfloat16), second_kernel.transpose(0, 2, 1),
        jnp.asarray(selection(), jnp.bfloat16), cotangent,
    )
    w1_near, w1_far, w2, select, cot = pl.pallas_call(
        prepare_kernel,
        in_specs=[pinned] * 5,
        out_specs=(fast,) * 5,
        out_shape=(
            bf16((2, 2 * C1, 18 * ROWS)), bf16((2, 2 * C1, 9 * ROWS)), bf16((2, 6 * C1, 6 * C2)),
            bf16((CHUNK, CHUNK)), bf16((PLANE, 2 * C2)),
        ),
        scratch_shapes=[
            pltpu.VMEM((27, CIN, C1), jnp.bfloat16),
            pltpu.VMEM((27 * CIN, 4 * CHUNK), jnp.bfloat16),
            pltpu.VMEM((27, C1, C2), jnp.bfloat16),
            pltpu.VMEM(cotangent.shape, jnp.bfloat16),
            pltpu.VMEM((27 * CIN, C1), jnp.float32),
            pltpu.SemaphoreType.DMA((5,)),
        ],
        compiler_params=pltpu.CompilerParams(vmem_limit_bytes=12 * MIB),
        cost_estimate=pl.CostEstimate(flops=10**9, bytes_accessed=4 * MIB, transcendentals=0),
        name="prepare",
    )(*(pltpu.with_memory_space_constraint(x, pltpu.HBM) for x in stored))
    first, near, pre = pl.pallas_call(
        near_kernel,
        in_specs=[fast] * 5,
        out_specs=(fast,) * 3,
        out_shape=(f32((2 * C1, PLANE)), bf16((6 * C1, PLANE)), f32((PLANE, 2 * C2))),
        scratch_shapes=[
            pltpu.VMEM((4, 2 * ROWS, LANES + PLANE), jnp.bfloat16),
            pltpu.VMEM((18 * ROWS, PLANE), jnp.bfloat16),
            pltpu.VMEM((2 * C1, PLANE + 2 * LANES), jnp.bfloat16),
            pltpu.VMEM((PLANE, 6 * C1), jnp.bfloat16),
            pltpu.VMEM((3, PLANE + 2 * HALF, LANES), jnp.float32),
        ],
        compiler_params=pltpu.CompilerParams(vmem_limit_bytes=16 * MIB),
        cost_estimate=pl.CostEstimate(flops=10**9, bytes_accessed=4 * MIB, transcendentals=0),
        name="near",
    )(volumes, within, select, w1_near, w2)
    rows = C2 // narrow
    begun, term, pre = pl.pallas_call(
        functools.partial(far_kernel, wide // 2, scale),
        in_specs=[fast] * 8,
        out_specs=(pl.BlockSpec(memory_space=pl.ANY), fast, fast),
        out_shape=(bf16((1, 1, C2, cells_out)), bf16((4 * narrow, rows, PART)), f32((PLANE, 2 * C2))),
        scratch_shapes=[
            pltpu.VMEM((4, ROWS, LANES + PLANE), jnp.bfloat16),
            pltpu.VMEM((9 * ROWS, PLANE), jnp.bfloat16),
            pltpu.VMEM((2 * C1, PLANE + 2 * LANES), jnp.bfloat16),
            pltpu.VMEM((2, 6 * C1, PLANE), jnp.bfloat16),
            pltpu.VMEM((PLANE, 6 * C1), jnp.bfloat16),
            pltpu.VMEM((3, PLANE + 2 * HALF, LANES), jnp.float32),
            pltpu.VMEM((PLANE + 2 * HALF, LANES), jnp.bfloat16),
            pltpu.VMEM((PLANE + 2 * HALF, LANES), jnp.bfloat16),
            pltpu.VMEM((1, 1, C2, cells_out), jnp.bfloat16),
            pltpu.SemaphoreType.DMA,
        ],
        compiler_params=pltpu.CompilerParams(vmem_limit_bytes=16 * MIB),
        name="far",
    )(across, select, w1_far, w2, cot, first, near, pre)
    received = lax.all_to_all(term, ("narrow", "column", "core"), 0, 0, tiled=True)
    owned = jnp.sum(received.astype(jnp.float32), axis=0).astype(jnp.bfloat16)
    parts = lax.all_to_all(jnp.broadcast_to(owned[None], (wide, rows, PART)), WIDE, 0, 0, tiled=True)
    total = jnp.sum(parts.reshape(wide // 4, 4, rows, PART).astype(jnp.float32), axis=0)
    anywhere = pl.BlockSpec(memory_space=pl.ANY)
    weight_grad, output = pl.pallas_call(
        finish_kernel,
        in_specs=[fast, fast, anywhere],
        out_specs=(anywhere, anywhere),
        out_shape=(f32((27, rows, C1)), bf16((1, 1, C2, cells_out))),
        scratch_shapes=[
            pltpu.VMEM((27, rows, C1), jnp.float32),
            pltpu.VMEM((1, 1, C2, cells_out), jnp.bfloat16),
            pltpu.SemaphoreType.DMA((3,)),
            pltpu.SemaphoreType.DMA,
        ],
        input_output_aliases={2: 1},
        compiler_params=pltpu.CompilerParams(vmem_limit_bytes=8 * MIB),
        name="finish",
    )(total, pre, begun)
    return (output, weight_grad)


def solution(mesh):
    wide, narrow = mesh.devices.shape
    split = jax.sharding.Mesh(mesh.devices.reshape(wide // 4, 2, 2, narrow), WIDE + ("narrow",))
    return jax.shard_map(
        body,
        mesh=split,
        in_specs=(P("narrow", None, None, WIDE, None), P(), P(), P("narrow", None, None, WIDE)),
        out_specs=(P("narrow", None, None, WIDE), P(None, "narrow", None)),
        check_vma=False,
    )
```

```python
import functools
import math

import jax
import jax.numpy as jnp
import numpy as np
from jax import lax
from jax.experimental import pallas as pl
from jax.experimental.pallas import tpu as pltpu
from jax.sharding import PartitionSpec as P

CIN = 4
C1 = 32
C2 = 64
PLANES = 4
CELLS = 4096
HALF = 32
PLANE = 1024
LANES = 128
ROWS = CIN * PLANES
CHUNK = 512
PACKED = 7 * LANES
MIB = 2**20
WIDE = ("chip", "core")
neg_slope = 0.3


def selection():
    table = np.zeros((CHUNK, 2, 2, 4, HALF), np.float32)
    for py in range(2):
        for px in range(2):
            for row in range(4):
                for col in range(HALF):
                    table[(2 * row + py) * 64 + 2 * col + px, py, px, row, col] = 1
    return table.reshape(CHUNK, CHUNK)


def placement():
    table = np.zeros((2, 27, CIN, 4, CHUNK), np.float32)
    for odd in range(2):
        for a in range(3):
            for bc in range(9):
                for i in range(CIN):
                    for q in range(4):
                        slab, plane = divmod(2 * q + a + 1, PLANES)
                        inner = (plane - (slab == 0)) * CIN + i
                        if slab == 1:
                            column = bc * 2 * ROWS + inner
                        elif (slab == 0) == (odd == 1):
                            column = bc * 2 * ROWS + ROWS + inner
                        else:
                            column = 18 * ROWS + bc * ROWS + inner
                        table[odd, 9 * a + bc, i, q, column] = 1
    return table.reshape(2, 27 * CIN, 4 * CHUNK)


def leaky_relu(value):
    return jnp.where(value > 0, value, neg_slope * value)


def padded_rows(planes):
    return jnp.concatenate(planes + [jnp.zeros((CIN, CELLS), jnp.bfloat16)], axis=0)


def column_masks():
    column = lax.broadcasted_iota(jnp.int32, (1, PLANE), 1) % HALF
    left_ok = jnp.where(column > 0, 1.0, 0.0).astype(jnp.bfloat16)
    right_ok = jnp.where(column < HALF - 1, 1.0, 0.0).astype(jnp.bfloat16)
    return left_ok, right_ok


def strided_taps(rows, select_ref, parity_ref, taps_ref):
    count = rows.shape[0]
    left_ok, _ = column_masks()
    chunks = jnp.concatenate([rows[:, CHUNK * j : CHUNK * (j + 1)] for j in range(8)], axis=0)
    for p in range(4):
        parity_ref[p, :, 0:LANES] = jnp.zeros((count, LANES), jnp.bfloat16)
    for py in range(2):
        parts = jnp.dot(
            chunks, select_ref[:, 256 * py : 256 * py + 256], preferred_element_type=jnp.float32
        ).astype(jnp.bfloat16)
        for px in range(2):
            for j in range(8):
                parity_ref[2 * py + px, :, LANES * (j + 1) : LANES * (j + 2)] = parts[
                    j * count : (j + 1) * count, px * LANES : (px + 1) * LANES
                ]
    for b in range(3):
        for c in range(3):
            begin = LANES - HALF * (b == 0) - (c == 0)
            part = parity_ref[2 * (b != 1) + (c != 1), :, begin : begin + PLANE]
            if c == 0:
                part = part * left_ok
            taps_ref[(3 * b + c) * count : (3 * b + c + 1) * count, :] = part


def shifted_columns(act_ref, columns_ref):
    left_ok, right_ok = column_masks()
    for c in range(3):
        begin = LANES + c - 1
        part = act_ref[:, begin : begin + PLANE]
        if c == 0:
            part = part * left_ok
        if c == 2:
            part = part * right_ok
        columns_ref[c * 2 * C1 : (c + 1) * 2 * C1, :] = part


def second_layer(w2, columns_ref, turned_ref, rowed_ref):
    blank = jnp.zeros((HALF, LANES), jnp.float32)
    for b in (0, 2):
        rowed_ref[b, 0:HALF, :] = blank
        rowed_ref[b, HALF + PLANE :, :] = blank
    for n in range(4):
        cells = slice(256 * n, 256 * n + 256)
        turned_ref[cells, :] = columns_ref[:, cells].T
    for n in range(4):
        sums = jnp.dot(turned_ref[256 * n : 256 * n + 256, :], w2, preferred_element_type=jnp.float32)
        for b in range(3):
            rowed_ref[b, HALF + 256 * n : HALF + 256 * n + 256, :] = sums[:, b * LANES : (b + 1) * LANES]


def row_sum(rowed_ref, n):
    begins = [HALF * b + 256 * n for b in range(3)]
    first, second, third = (rowed_ref[b, begin : begin + 256, :] for b, begin in enumerate(begins))
    return first + second + third


def clear_margins(act_ref):
    margin = jnp.zeros((2 * C1, LANES), jnp.bfloat16)
    act_ref[:, 0:LANES] = margin
    act_ref[:, LANES + PLANE :] = margin


def pack_kernel(slab_hbm, own_ref, across_ref, within_ref, within_last_ref, slab_ref, sem):
    copy = pltpu.make_async_copy(slab_hbm, slab_ref, sem)
    copy.start()
    copy.wait()
    odd = lax.axis_index("core")
    channels = [slab_ref[0, 0, i].astype(jnp.float32) for i in range(CIN)]
    for p in range(PLANES):
        own_ref[p] = jnp.concatenate([x[p : p + 1] for x in channels], axis=0).astype(jnp.bfloat16)
    for k in range(3):
        across_ref[k] = own_ref[k + odd]
    for k in range(2):
        within_ref[k] = own_ref[k + 1 - odd]
    within_last_ref[0] = own_ref[3 - odd]


def prepare_kernel(
    k1_hbm, place_hbm, k2_hbm, select_hbm, cot_hbm,
    w1_near_ref, w1_far_ref, w2_ref, select_ref, turned_ref,
    k1_ref, place_ref, k2_ref, cot_ref, k1_rows_ref, sems,
):
    odd = lax.axis_index("core")
    moves = (
        (k1_hbm, k1_ref), (k2_hbm, k2_ref), (place_hbm.at[odd], place_ref), (cot_hbm, cot_ref), (select_hbm, select_ref),
    )
    copies = [pltpu.make_async_copy(src, dst, sems.at[k]) for k, (src, dst) in enumerate(moves)]
    for copy in copies:
        copy.start()
    copies[0].wait()
    for tap in range(27):
        k1_rows_ref[CIN * tap : CIN * (tap + 1), :] = k1_ref[tap].astype(jnp.float32)
    copies[1].wait()
    blank = jnp.zeros((C1, C2), jnp.bfloat16)

    def stacked(bc, pair):
        k = [blank] + [k2_ref[9 * a + bc] for a in range(3)] + [blank]
        lower = jnp.concatenate(k[1 + 2 * pair : 3 + 2 * pair], axis=0)
        upper = jnp.concatenate(k[2 * pair : 2 + 2 * pair], axis=0)
        return jnp.concatenate([lower, upper], axis=1)

    for pair in range(2):
        for b in range(3):
            for c in range(3):
                w2_ref[pair, c * 2 * C1 : (c + 1) * 2 * C1, b * LANES : (b + 1) * LANES] = stacked(3 * b + c, pair)
    copies[2].wait()
    spread = lax.dot_general(
        k1_rows_ref[...].astype(jnp.bfloat16), place_ref[...],
        (((0,), (0,)), ((), ())), preferred_element_type=jnp.float32,
    ).astype(jnp.bfloat16)
    for q in range(4):
        rows = slice(q % 2 * C1, (q % 2 + 1) * C1)
        w1_near_ref[q // 2, rows, :] = spread[:, CHUNK * q : CHUNK * q + 18 * ROWS]
        w1_far_ref[q // 2, rows, :] = spread[:, CHUNK * q + 18 * ROWS : CHUNK * q + 27 * ROWS]
    copies[3].wait()
    for n in range(4):
        planes = [cot_ref[0, 0, :, z * PLANE + 256 * n : z * PLANE + 256 * n + 256] for z in range(2)]
        turned_ref[256 * n : 256 * n + 256, :] = jnp.concatenate(planes, axis=0).T
    copies[4].wait()


def near_kernel(
    own_ref, within_ref, within_last_ref, select_ref, w1_ref, w2_ref, first_ref, columns_ref, pre_ref,
    parity_ref, taps_ref, act_ref, turned_ref, rowed_ref,
):
    odd = lax.axis_index("core")
    rows = padded_rows([own_ref[p] for p in range(PLANES)] + [within_ref[0], within_ref[1], within_last_ref[0]])
    strided_taps(rows, select_ref, parity_ref, taps_ref)
    clear_margins(act_ref)
    for n in range(4):
        here = slice(256 * n, 256 * n + 256)
        first_ref[:, here] = jnp.dot(w1_ref[odd], taps_ref[:, here], preferred_element_type=jnp.float32)
        complete = jnp.dot(w1_ref[1 - odd], taps_ref[:, here], preferred_element_type=jnp.float32)
        act_ref[:, LANES + 256 * n : LANES + 256 * n + 256] = leaky_relu(complete).astype(jnp.bfloat16)
    shifted_columns(act_ref, columns_ref)
    second_layer(w2_ref[1 - odd], columns_ref, turned_ref, rowed_ref)
    for n in range(4):
        pre_ref[256 * n : 256 * n + 256, :] = row_sum(rowed_ref, n)


def emit_activations(pre_ref, out_ref, out_hbm, sem):
    for n in range(4):
        output = leaky_relu(pre_ref[256 * n : 256 * n + 256, :]).astype(jnp.bfloat16).T
        for z in range(2):
            out_ref[0, 0, :, z * PLANE + 256 * n : z * PLANE + 256 * n + 256] = output[z * C2 : (z + 1) * C2]
    copy = pltpu.make_async_copy(out_ref, out_hbm, sem)
    copy.start()
    copy.wait()


def far_kernel(
    chips, scale, across_ref, select_ref, w1_ref, w2_ref, cot_ref, first_ref, near_ref, near_pre_ref, out_hbm, grad_ref, pre_ref,
    parity_ref, taps_ref, act_ref, columns_ref, turned_ref, rowed_ref, back_ref, swapped_ref, out_ref, out_sem,
):
    odd = lax.axis_index("core")
    last = (lax.axis_index("chip") == chips - 1) & (odd == 1)
    inside = jnp.where(last, 0.0, 1.0)
    strided_taps(padded_rows([across_ref[k] for k in range(3)]), select_ref, parity_ref, taps_ref)
    clear_margins(act_ref)
    for n in range(4):
        here = slice(256 * n, 256 * n + 256)
        first_pre = first_ref[:, here] + jnp.dot(w1_ref[odd], taps_ref[:, here], preferred_element_type=jnp.float32)
        first_act = leaky_relu(first_pre)
        there = slice(LANES + 256 * n, LANES + 256 * n + 256)
        act_ref[0:C1, there] = first_act[0:C1].astype(jnp.bfloat16)
        act_ref[C1:, there] = (first_act[C1:] * inside).astype(jnp.bfloat16)
    columns_ref[1 - odd] = near_ref[...]
    shifted_columns(act_ref, columns_ref.at[odd])
    second_layer(w2_ref[odd], columns_ref.at[odd], turned_ref, rowed_ref)
    margin = jnp.zeros((HALF, LANES), jnp.bfloat16)
    for ref in (back_ref, swapped_ref):
        ref[0:HALF, :] = margin
        ref[HALF + PLANE :, :] = margin
    for n in range(4):
        cells = slice(256 * n, 256 * n + 256)
        pre = near_pre_ref[cells, :] + row_sum(rowed_ref, n)
        pre_ref[cells, :] = pre
        back = (cot_ref[cells, :].astype(jnp.float32) * jnp.where(pre > 0, 1.0, neg_slope)).astype(jnp.bfloat16)
        here = slice(HALF + 256 * n, HALF + 256 * n + 256)
        back_ref[here, :] = back
        swapped_ref[here, :] = jnp.concatenate([back[:, C2:], back[:, 0:C2]], axis=1)
    low = lax.broadcasted_iota(jnp.int32, (1, LANES), 1) < C2
    rows_of = [slice((2 - b) * HALF, (2 - b) * HALF + PLANE) for b in range(3)]
    operands = []
    for left_ref, right_ref in ((back_ref, swapped_ref), (swapped_ref, back_ref)):
        first_two = jnp.where(low, left_ref[rows_of[0], :], right_ref[rows_of[1], :])
        operands.append(jnp.concatenate([first_two, left_ref[rows_of[2], :]], axis=1))

    def plane_columns(q, c):
        begin = 2 * C1 * c + C1 * (q % 2)
        return columns_ref[q // 2, begin : begin + C1, :]

    columns = [jnp.concatenate([plane_columns(a + z, c) for a in range(3) for c in range(3)], axis=0) for z in range(2)]
    sums = scale * jnp.dot(
        jnp.concatenate(columns, axis=1), jnp.concatenate(operands, axis=0), preferred_element_type=jnp.float32
    )
    left, right, ends = sums[0:256, 0:LANES], sums[0:256, LANES:], sums[256:]
    turned = [left[0:LANES].T, left[LANES:].T]
    third = jnp.where(low, right[0:LANES], pltpu.roll(right[LANES:], C2, 1)).T
    fourth = jnp.concatenate([ends[:, 0:LANES], ends[:, LANES:]] * 2, axis=0).T
    group = lax.broadcasted_iota(jnp.int32, (1, LANES), 1) // C1
    tiles = [turned[0][0:C2], turned[1][0:C2], turned[0][C2:], turned[1][C2:], third[0:C2], third[C2:]]
    tiles.append(jnp.where(group < 2, fourth[0:C2], pltpu.roll(fourth[C2:], C2, 1)))
    for k, tile in enumerate(tiles):
        grad_ref[:, k * LANES : (k + 1) * LANES] = tile.astype(jnp.bfloat16)
    early = lax.axis_index("narrow") == 0
    pl.when(early)(lambda: emit_activations(pre_ref, out_ref, out_hbm, out_sem))


def slots():
    where = []
    for a in range(3):
        for b in range(3):
            for c in range(3):
                tile, group = divmod(3 * a + c, 4)
                where.append((2 * b + tile, group) if tile < 2 else (6, (0, 2, 1)[b]))
    return where


def finish_kernel(total_ref, pre_ref, begun_hbm, grad_hbm, out_hbm, grad_ref, out_ref, sems, out_sem):
    del begun_hbm
    copies = []
    for k in range(3):
        for tap in range(9 * k, 9 * k + 9):
            tile, slot = slots()[tap]
            begin = tile * LANES + slot * C1
            grad_ref[tap] = total_ref[:, begin : begin + C1]
        here = slice(9 * k, 9 * k + 9)
        copies.append(pltpu.make_async_copy(grad_ref.at[here], grad_hbm.at[here], sems.at[k]))
        copies[k].start()
    late = lax.axis_index("narrow") > 0
    pl.when(late)(lambda: emit_activations(pre_ref, out_ref, out_hbm, out_sem))
    for copy in copies:
        copy.wait()


def body(volumes, first_kernel, second_kernel, cotangent):
    wide = lax.axis_size(WIDE)
    narrow = lax.axis_size("narrow")
    cells_out = cotangent.shape[3]
    scale = 1.0 / math.sqrt(wide * narrow * cells_out)
    pinned = pl.BlockSpec(memory_space=pltpu.HBM)
    fast = pl.BlockSpec(memory_space=pltpu.VMEM)
    bf16 = functools.partial(jax.ShapeDtypeStruct, dtype=jnp.bfloat16)
    f32 = functools.partial(jax.ShapeDtypeStruct, dtype=jnp.float32)
    own, across, within, within_last = pl.pallas_call(
        pack_kernel,
        in_specs=[pinned],
        out_specs=(fast,) * 4,
        out_shape=tuple(bf16((planes, CIN, CELLS)) for planes in (PLANES, 3, 2, 1)),
        scratch_shapes=[pltpu.VMEM(volumes.shape, jnp.bfloat16), pltpu.SemaphoreType.DMA],
        compiler_params=pltpu.CompilerParams(vmem_limit_bytes=8 * MIB),
        name="pack",
    )(pltpu.with_memory_space_constraint(volumes, pltpu.HBM))
    across = lax.ppermute(across, WIDE, [p for k in range(1, wide - 1, 2) for p in ((k, k + 1), (k + 1, k))])
    pairs = [p for k in range(0, wide - 1, 2) for p in ((k, k + 1), (k + 1, k))]
    within = lax.ppermute(within, WIDE, pairs)
    within_last = lax.ppermute(within_last, WIDE, pairs)
    stored = (
        first_kernel.transpose(0, 2, 1), jnp.asarray(placement(), jnp.bfloat16), second_kernel.transpose(0, 2, 1),
        jnp.asarray(selection(), jnp.bfloat16), cotangent,
    )
    w1_near, w1_far, w2, select, cot = pl.pallas_call(
        prepare_kernel,
        in_specs=[pinned] * 5,
        out_specs=(fast,) * 5,
        out_shape=(
            bf16((2, 2 * C1, 18 * ROWS)), bf16((2, 2 * C1, 9 * ROWS)), bf16((2, 6 * C1, 6 * C2)),
            bf16((CHUNK, CHUNK)), bf16((PLANE, 2 * C2)),
        ),
        scratch_shapes=[
            pltpu.VMEM((27, CIN, C1), jnp.bfloat16),
            pltpu.VMEM((27 * CIN, 4 * CHUNK), jnp.bfloat16),
            pltpu.VMEM((27, C1, C2), jnp.bfloat16),
            pltpu.VMEM(cotangent.shape, jnp.bfloat16),
            pltpu.VMEM((27 * CIN, C1), jnp.float32),
            pltpu.SemaphoreType.DMA((5,)),
        ],
        compiler_params=pltpu.CompilerParams(vmem_limit_bytes=12 * MIB),
        cost_estimate=pl.CostEstimate(flops=10**9, bytes_accessed=4 * MIB, transcendentals=0),
        name="prepare",
    )(*(pltpu.with_memory_space_constraint(x, pltpu.HBM) for x in stored))
    first, near, pre = pl.pallas_call(
        near_kernel,
        in_specs=[fast] * 6,
        out_specs=(fast,) * 3,
        out_shape=(f32((2 * C1, PLANE)), bf16((6 * C1, PLANE)), f32((PLANE, 2 * C2))),
        scratch_shapes=[
            pltpu.VMEM((4, 2 * ROWS, LANES + PLANE), jnp.bfloat16),
            pltpu.VMEM((18 * ROWS, PLANE), jnp.bfloat16),
            pltpu.VMEM((2 * C1, PLANE + 2 * LANES), jnp.bfloat16),
            pltpu.VMEM((PLANE, 6 * C1), jnp.bfloat16),
            pltpu.VMEM((3, PLANE + 2 * HALF, LANES), jnp.float32),
        ],
        compiler_params=pltpu.CompilerParams(vmem_limit_bytes=16 * MIB),
        name="near",
    )(own, within, within_last, select, w1_near, w2)
    rows = C2 // narrow
    begun, term, pre = pl.pallas_call(
        functools.partial(far_kernel, wide // 2, scale),
        in_specs=[fast] * 8,
        out_specs=(pl.BlockSpec(memory_space=pl.ANY), fast, fast),
        out_shape=(bf16((1, 1, C2, cells_out)), bf16((C2, PACKED)), f32((PLANE, 2 * C2))),
        scratch_shapes=[
            pltpu.VMEM((4, ROWS, LANES + PLANE), jnp.bfloat16),
            pltpu.VMEM((9 * ROWS, PLANE), jnp.bfloat16),
            pltpu.VMEM((2 * C1, PLANE + 2 * LANES), jnp.bfloat16),
            pltpu.VMEM((2, 6 * C1, PLANE), jnp.bfloat16),
            pltpu.VMEM((PLANE, 6 * C1), jnp.bfloat16),
            pltpu.VMEM((3, PLANE + 2 * HALF, LANES), jnp.float32),
            pltpu.VMEM((PLANE + 2 * HALF, LANES), jnp.bfloat16),
            pltpu.VMEM((PLANE + 2 * HALF, LANES), jnp.bfloat16),
            pltpu.VMEM((1, 1, C2, cells_out), jnp.bfloat16),
            pltpu.SemaphoreType.DMA,
        ],
        compiler_params=pltpu.CompilerParams(vmem_limit_bytes=16 * MIB),
        name="far",
    )(across, select, w1_far, w2, cot, first, near, pre)
    half = rows // 2
    received = lax.all_to_all(term, ("narrow", "core"), 0, 0, tiled=True)
    owned = jnp.sum(received.reshape(2 * narrow, half, PACKED).astype(jnp.float32), axis=0).astype(jnp.bfloat16)
    parts = lax.all_to_all(jnp.broadcast_to(owned[None], (wide, half, PACKED)), WIDE, 0, 0, tiled=True)
    total = jnp.sum(parts.reshape(wide // 2, rows, PACKED).astype(jnp.float32), axis=0)
    anywhere = pl.BlockSpec(memory_space=pl.ANY)
    weight_grad, output = pl.pallas_call(
        finish_kernel,
        in_specs=[fast, fast, anywhere],
        out_specs=(anywhere, anywhere),
        out_shape=(f32((27, rows, C1)), bf16((1, 1, C2, cells_out))),
        scratch_shapes=[
            pltpu.VMEM((27, rows, C1), jnp.float32),
            pltpu.VMEM((1, 1, C2, cells_out), jnp.bfloat16),
            pltpu.SemaphoreType.DMA((3,)),
            pltpu.SemaphoreType.DMA,
        ],
        input_output_aliases={2: 1},
        compiler_params=pltpu.CompilerParams(vmem_limit_bytes=8 * MIB),
        name="finish",
    )(total, pre, begun)
    return (output, weight_grad)


def solution(mesh):
    wide, narrow = mesh.devices.shape
    split = jax.sharding.Mesh(mesh.devices.reshape(wide // 2, 2, narrow), ("chip", "core", "narrow"))
    return jax.shard_map(
        body,
        mesh=split,
        in_specs=(P("narrow", None, None, WIDE, None), P(), P(), P("narrow", None, None, WIDE)),
        out_specs=(P("narrow", None, None, WIDE), P(None, "narrow", None)),
        check_vma=False,
    )
```

```python
import functools
import math

import jax
import jax.numpy as jnp
import numpy as np
from jax import lax
from jax.experimental import pallas as pl
from jax.experimental.pallas import tpu as pltpu
from jax.sharding import PartitionSpec as P

CIN = 4
C1 = 32
C2 = 64
PLANES = 4
CELLS = 4096
HALF = 32
PLANE = 1024
LANES = 128
ROWS = CIN * PLANES
CHUNK = 512
PACKED = 7 * LANES
MIB = 2**20
WIDE = ("chip", "core")
neg_slope = 0.3


def selection():
    table = np.zeros((CHUNK, 2, 2, 4, HALF), np.float32)
    for py in range(2):
        for px in range(2):
            for row in range(4):
                for col in range(HALF):
                    table[(2 * row + py) * 64 + 2 * col + px, py, px, row, col] = 1
    return table.reshape(CHUNK, CHUNK)


def placement():
    table = np.zeros((2, 27, CIN, 4, CHUNK), np.float32)
    for odd in range(2):
        for a in range(3):
            for bc in range(9):
                for i in range(CIN):
                    for q in range(4):
                        slab, plane = divmod(2 * q + a + 1, PLANES)
                        inner = i * PLANES + plane
                        if slab == 1:
                            column = bc * 2 * ROWS + inner
                        elif (slab == 0) == (odd == 1):
                            column = bc * 2 * ROWS + ROWS + inner
                        else:
                            column = 18 * ROWS + bc * ROWS + (plane - (slab == 0)) * CIN + i
                        table[odd, 9 * a + bc, i, q, column] = 1
    return table.reshape(2, 27 * CIN, 4 * CHUNK)


def leaky_relu(value):
    return jnp.where(value > 0, value, neg_slope * value)


def column_masks():
    column = lax.broadcasted_iota(jnp.int32, (1, PLANE), 1) % HALF
    left_ok = jnp.where(column > 0, 1.0, 0.0).astype(jnp.bfloat16)
    right_ok = jnp.where(column < HALF - 1, 1.0, 0.0).astype(jnp.bfloat16)
    return left_ok, right_ok


def strided_taps(rows, select_ref, parity_ref, taps_ref):
    count = rows.shape[0]
    left_ok, _ = column_masks()
    chunks = jnp.concatenate([rows[:, CHUNK * j : CHUNK * (j + 1)] for j in range(8)], axis=0)
    for p in range(4):
        parity_ref[p, :, 0:LANES] = jnp.zeros((count, LANES), jnp.bfloat16)
    for py in range(2):
        parts = jnp.dot(
            chunks, select_ref[:, 256 * py : 256 * py + 256], preferred_element_type=jnp.float32
        ).astype(jnp.bfloat16)
        for px in range(2):
            for j in range(8):
                parity_ref[2 * py + px, :, LANES * (j + 1) : LANES * (j + 2)] = parts[
                    j * count : (j + 1) * count, px * LANES : (px + 1) * LANES
                ]
    for b in range(3):
        for c in range(3):
            begin = LANES - HALF * (b == 0) - (c == 0)
            part = parity_ref[2 * (b != 1) + (c != 1), :, begin : begin + PLANE]
            if c == 0:
                part = part * left_ok
            taps_ref[(3 * b + c) * count : (3 * b + c + 1) * count, :] = part


def shifted_columns(act_ref, columns_ref):
    left_ok, right_ok = column_masks()
    for c in range(3):
        begin = LANES + c - 1
        part = act_ref[:, begin : begin + PLANE]
        if c == 0:
            part = part * left_ok
        if c == 2:
            part = part * right_ok
        columns_ref[c * 2 * C1 : (c + 1) * 2 * C1, :] = part


def second_layer(w2, columns_ref, turned_ref, rowed_ref):
    blank = jnp.zeros((HALF, LANES), jnp.float32)
    for b in (0, 2):
        rowed_ref[b, 0:HALF, :] = blank
        rowed_ref[b, HALF + PLANE :, :] = blank
    for n in range(4):
        cells = slice(256 * n, 256 * n + 256)
        turned_ref[cells, :] = columns_ref[:, cells].T
    for n in range(4):
        sums = jnp.dot(turned_ref[256 * n : 256 * n + 256, :], w2, preferred_element_type=jnp.float32)
        for b in range(3):
            rowed_ref[b, HALF + 256 * n : HALF + 256 * n + 256, :] = sums[:, b * LANES : (b + 1) * LANES]


def row_sum(rowed_ref, n):
    begins = [HALF * b + 256 * n for b in range(3)]
    first, second, third = (rowed_ref[b, begin : begin + 256, :] for b, begin in enumerate(begins))
    return first + second + third


def clear_margins(act_ref):
    margin = jnp.zeros((2 * C1, LANES), jnp.bfloat16)
    act_ref[:, 0:LANES] = margin
    act_ref[:, LANES + PLANE :] = margin


def pack_kernel(slab_hbm, across_ref, low_ref, high_ref, rows_ref, sems):
    odd = lax.axis_index("core")
    places = [(ref, k) for ref in (low_ref, high_ref) for k in range(CIN // 2)]
    copies = [pltpu.make_async_copy(slab_hbm.at[0, 0, i], ref.at[k], sems.at[i]) for i, (ref, k) in enumerate(places)]
    for copy in copies:
        copy.start()
    for i, (ref, k) in enumerate(places):
        copies[i].wait()
        planes = ref[k].astype(jnp.float32)
        for j in range(CELLS // LANES):
            begin = j * ROWS + PLANES * i
            rows_ref[begin : begin + PLANES, :] = planes[:, j * LANES : (j + 1) * LANES]
    for k in range(3):
        for j in range(CELLS // LANES):
            channels = rows_ref[pl.ds(j * ROWS + k + odd, CIN, stride=PLANES), :]
            across_ref[k, :, j * LANES : (j + 1) * LANES] = channels.astype(jnp.bfloat16)


def prepare_kernel(
    k1_hbm, place_hbm, k2_hbm, select_hbm, cot_hbm,
    w1_near_ref, w1_far_ref, w2_ref, select_ref, turned_ref,
    k1_ref, place_ref, k2_ref, cot_ref, k1_rows_ref, sems,
):
    odd = lax.axis_index("core")
    moves = (
        (k1_hbm, k1_ref), (k2_hbm, k2_ref), (place_hbm.at[odd], place_ref), (cot_hbm, cot_ref), (select_hbm, select_ref),
    )
    copies = [pltpu.make_async_copy(src, dst, sems.at[k]) for k, (src, dst) in enumerate(moves)]
    for copy in copies:
        copy.start()
    copies[0].wait()
    for tap in range(27):
        k1_rows_ref[CIN * tap : CIN * (tap + 1), :] = k1_ref[tap].astype(jnp.float32)
    copies[1].wait()
    blank = jnp.zeros((C1, C2), jnp.bfloat16)

    def stacked(bc, pair):
        k = [blank] + [k2_ref[9 * a + bc] for a in range(3)] + [blank]
        lower = jnp.concatenate(k[1 + 2 * pair : 3 + 2 * pair], axis=0)
        upper = jnp.concatenate(k[2 * pair : 2 + 2 * pair], axis=0)
        return jnp.concatenate([lower, upper], axis=1)

    for pair in range(2):
        for b in range(3):
            for c in range(3):
                w2_ref[pair, c * 2 * C1 : (c + 1) * 2 * C1, b * LANES : (b + 1) * LANES] = stacked(3 * b + c, pair)
    copies[2].wait()
    spread = lax.dot_general(
        k1_rows_ref[...].astype(jnp.bfloat16), place_ref[...],
        (((0,), (0,)), ((), ())), preferred_element_type=jnp.float32,
    ).astype(jnp.bfloat16)
    for q in range(4):
        rows = slice(q % 2 * C1, (q % 2 + 1) * C1)
        w1_near_ref[q // 2, rows, :] = spread[:, CHUNK * q : CHUNK * q + 18 * ROWS]
        w1_far_ref[q // 2, rows, :] = spread[:, CHUNK * q + 18 * ROWS : CHUNK * q + 27 * ROWS]
    copies[3].wait()
    for n in range(4):
        planes = [cot_ref[0, 0, :, z * PLANE + 256 * n : z * PLANE + 256 * n + 256] for z in range(2)]
        turned_ref[256 * n : 256 * n + 256, :] = jnp.concatenate(planes, axis=0).T
    copies[4].wait()


def near_kernel(
    own_low_ref, own_high_ref, low_ref, high_ref, select_ref, w1_ref, w2_ref, first_ref, columns_ref, pre_ref,
    parity_ref, taps_ref, act_ref, turned_ref, rowed_ref,
):
    odd = lax.axis_index("core")
    slabs = (own_low_ref, own_high_ref, low_ref, high_ref)
    rows = jnp.concatenate([ref[k] for ref in slabs for k in range(CIN // 2)], axis=0)
    strided_taps(rows, select_ref, parity_ref, taps_ref)
    clear_margins(act_ref)
    for n in range(4):
        here = slice(256 * n, 256 * n + 256)
        first_ref[:, here] = jnp.dot(w1_ref[odd], taps_ref[:, here], preferred_element_type=jnp.float32)
        complete = jnp.dot(w1_ref[1 - odd], taps_ref[:, here], preferred_element_type=jnp.float32)
        act_ref[:, LANES + 256 * n : LANES + 256 * n + 256] = leaky_relu(complete).astype(jnp.bfloat16)
    shifted_columns(act_ref, columns_ref)
    second_layer(w2_ref[1 - odd], columns_ref, turned_ref, rowed_ref)
    for n in range(4):
        pre_ref[256 * n : 256 * n + 256, :] = row_sum(rowed_ref, n)


def emit_activations(pre_ref, out_ref, out_hbm, sem):
    for n in range(4):
        output = leaky_relu(pre_ref[256 * n : 256 * n + 256, :]).astype(jnp.bfloat16).T
        for z in range(2):
            out_ref[0, 0, :, z * PLANE + 256 * n : z * PLANE + 256 * n + 256] = output[z * C2 : (z + 1) * C2]
    copy = pltpu.make_async_copy(out_ref, out_hbm, sem)
    copy.start()
    copy.wait()


def far_kernel(
    chips, scale, across_ref, select_ref, w1_ref, w2_ref, cot_ref, first_ref, near_ref, near_pre_ref, out_hbm, grad_ref, pre_ref,
    parity_ref, taps_ref, act_ref, columns_ref, turned_ref, rowed_ref, back_ref, swapped_ref, out_ref, out_sem,
):
    odd = lax.axis_index("core")
    last = (lax.axis_index("chip") == chips - 1) & (odd == 1)
    inside = jnp.where(last, 0.0, 1.0)
    blank = jnp.zeros((CIN, CELLS), jnp.bfloat16)
    rows = jnp.concatenate([across_ref[k] for k in range(3)] + [blank], axis=0)
    strided_taps(rows, select_ref, parity_ref, taps_ref)
    clear_margins(act_ref)
    for n in range(4):
        here = slice(256 * n, 256 * n + 256)
        first_pre = first_ref[:, here] + jnp.dot(w1_ref[odd], taps_ref[:, here], preferred_element_type=jnp.float32)
        first_act = leaky_relu(first_pre)
        there = slice(LANES + 256 * n, LANES + 256 * n + 256)
        act_ref[0:C1, there] = first_act[0:C1].astype(jnp.bfloat16)
        act_ref[C1:, there] = (first_act[C1:] * inside).astype(jnp.bfloat16)
    columns_ref[1 - odd] = near_ref[...]
    shifted_columns(act_ref, columns_ref.at[odd])
    second_layer(w2_ref[odd], columns_ref.at[odd], turned_ref, rowed_ref)
    margin = jnp.zeros((HALF, LANES), jnp.bfloat16)
    for ref in (back_ref, swapped_ref):
        ref[0:HALF, :] = margin
        ref[HALF + PLANE :, :] = margin
    for n in range(4):
        cells = slice(256 * n, 256 * n + 256)
        pre = near_pre_ref[cells, :] + row_sum(rowed_ref, n)
        pre_ref[cells, :] = pre
        back = (cot_ref[cells, :].astype(jnp.float32) * jnp.where(pre > 0, 1.0, neg_slope)).astype(jnp.bfloat16)
        here = slice(HALF + 256 * n, HALF + 256 * n + 256)
        back_ref[here, :] = back
        swapped_ref[here, :] = jnp.concatenate([back[:, C2:], back[:, 0:C2]], axis=1)
    low = lax.broadcasted_iota(jnp.int32, (1, LANES), 1) < C2
    rows_of = [slice((2 - b) * HALF, (2 - b) * HALF + PLANE) for b in range(3)]
    operands = []
    for left_ref, right_ref in ((back_ref, swapped_ref), (swapped_ref, back_ref)):
        first_two = jnp.where(low, left_ref[rows_of[0], :], right_ref[rows_of[1], :])
        operands.append(jnp.concatenate([first_two, left_ref[rows_of[2], :]], axis=1))

    def plane_columns(q, c):
        begin = 2 * C1 * c + C1 * (q % 2)
        return columns_ref[q // 2, begin : begin + C1, :]

    columns = [jnp.concatenate([plane_columns(a + z, c) for a in range(3) for c in range(3)], axis=0) for z in range(2)]
    sums = scale * jnp.dot(
        jnp.concatenate(columns, axis=1), jnp.concatenate(operands, axis=0), preferred_element_type=jnp.float32
    )
    left, right, ends = sums[0:256, 0:LANES], sums[0:256, LANES:], sums[256:]
    turned = [left[0:LANES].T, left[LANES:].T]
    third = jnp.where(low, right[0:LANES], pltpu.roll(right[LANES:], C2, 1)).T
    fourth = jnp.concatenate([ends[:, 0:LANES], ends[:, LANES:]] * 2, axis=0).T
    group = lax.broadcasted_iota(jnp.int32, (1, LANES), 1) // C1
    tiles = [turned[0][0:C2], turned[1][0:C2], turned[0][C2:], turned[1][C2:], third[0:C2], third[C2:]]
    tiles.append(jnp.where(group < 2, fourth[0:C2], pltpu.roll(fourth[C2:], C2, 1)))
    for k, tile in enumerate(tiles):
        grad_ref[:, k * LANES : (k + 1) * LANES] = tile.astype(jnp.bfloat16)
    early = lax.axis_index("narrow") == 0
    pl.when(early)(lambda: emit_activations(pre_ref, out_ref, out_hbm, out_sem))


def slots():
    where = []
    for a in range(3):
        for b in range(3):
            for c in range(3):
                tile, group = divmod(3 * a + c, 4)
                where.append((2 * b + tile, group) if tile < 2 else (6, (0, 2, 1)[b]))
    return where


def finish_kernel(total_ref, pre_ref, begun_hbm, grad_hbm, out_hbm, grad_ref, out_ref, sems, out_sem):
    del begun_hbm
    copies = []
    for k in range(3):
        for tap in range(9 * k, 9 * k + 9):
            tile, slot = slots()[tap]
            begin = tile * LANES + slot * C1
            grad_ref[tap] = total_ref[:, begin : begin + C1]
        here = slice(9 * k, 9 * k + 9)
        copies.append(pltpu.make_async_copy(grad_ref.at[here], grad_hbm.at[here], sems.at[k]))
        copies[k].start()
    late = lax.axis_index("narrow") > 0
    pl.when(late)(lambda: emit_activations(pre_ref, out_ref, out_hbm, out_sem))
    for copy in copies:
        copy.wait()


def body(volumes, first_kernel, second_kernel, cotangent):
    wide = lax.axis_size(WIDE)
    narrow = lax.axis_size("narrow")
    cells_out = cotangent.shape[3]
    scale = 1.0 / math.sqrt(wide * narrow * cells_out)
    pinned = pl.BlockSpec(memory_space=pltpu.HBM)
    fast = pl.BlockSpec(memory_space=pltpu.VMEM)
    bf16 = functools.partial(jax.ShapeDtypeStruct, dtype=jnp.bfloat16)
    f32 = functools.partial(jax.ShapeDtypeStruct, dtype=jnp.float32)
    halves = bf16((CIN // 2, PLANES, CELLS))
    across, low, high = pl.pallas_call(
        pack_kernel,
        in_specs=[pinned],
        out_specs=(fast,) * 3,
        out_shape=(bf16((3, CIN, CELLS)), halves, halves),
        scratch_shapes=[pltpu.VMEM((CELLS // LANES * ROWS, LANES), jnp.float32), pltpu.SemaphoreType.DMA((CIN,))],
        compiler_params=pltpu.CompilerParams(vmem_limit_bytes=8 * MIB),
        name="pack",
    )(pltpu.with_memory_space_constraint(volumes, pltpu.HBM))
    across = lax.ppermute(across, WIDE, [p for k in range(1, wide - 1, 2) for p in ((k, k + 1), (k + 1, k))])
    pairs = [p for k in range(0, wide - 1, 2) for p in ((k, k + 1), (k + 1, k))]
    within = [lax.ppermute(half, WIDE, pairs) for half in (low, high)]
    stored = (
        first_kernel.transpose(0, 2, 1), jnp.asarray(placement(), jnp.bfloat16), second_kernel.transpose(0, 2, 1),
        jnp.asarray(selection(), jnp.bfloat16), cotangent,
    )
    w1_near, w1_far, w2, select, cot = pl.pallas_call(
        prepare_kernel,
        in_specs=[pinned] * 5,
        out_specs=(fast,) * 5,
        out_shape=(
            bf16((2, 2 * C1, 18 * ROWS)), bf16((2, 2 * C1, 9 * ROWS)), bf16((2, 6 * C1, 6 * C2)),
            bf16((CHUNK, CHUNK)), bf16((PLANE, 2 * C2)),
        ),
        scratch_shapes=[
            pltpu.VMEM((27, CIN, C1), jnp.bfloat16),
            pltpu.VMEM((27 * CIN, 4 * CHUNK), jnp.bfloat16),
            pltpu.VMEM((27, C1, C2), jnp.bfloat16),
            pltpu.VMEM(cotangent.shape, jnp.bfloat16),
            pltpu.VMEM((27 * CIN, C1), jnp.float32),
            pltpu.SemaphoreType.DMA((5,)),
        ],
        compiler_params=pltpu.CompilerParams(vmem_limit_bytes=12 * MIB),
        cost_estimate=pl.CostEstimate(flops=10**9, bytes_accessed=4 * MIB, transcendentals=0),
        name="prepare",
    )(*(pltpu.with_memory_space_constraint(x, pltpu.HBM) for x in stored))
    first, near, pre = pl.pallas_call(
        near_kernel,
        in_specs=[fast] * 7,
        out_specs=(fast,) * 3,
        out_shape=(f32((2 * C1, PLANE)), bf16((6 * C1, PLANE)), f32((PLANE, 2 * C2))),
        scratch_shapes=[
            pltpu.VMEM((4, 2 * ROWS, LANES + PLANE), jnp.bfloat16),
            pltpu.VMEM((18 * ROWS, PLANE), jnp.bfloat16),
            pltpu.VMEM((2 * C1, PLANE + 2 * LANES), jnp.bfloat16),
            pltpu.VMEM((PLANE, 6 * C1), jnp.bfloat16),
            pltpu.VMEM((3, PLANE + 2 * HALF, LANES), jnp.float32),
        ],
        compiler_params=pltpu.CompilerParams(vmem_limit_bytes=16 * MIB),
        name="near",
    )(low, high, *within, select, w1_near, w2)
    rows = C2 // narrow
    begun, term, pre = pl.pallas_call(
        functools.partial(far_kernel, wide // 2, scale),
        in_specs=[fast] * 8,
        out_specs=(pl.BlockSpec(memory_space=pl.ANY), fast, fast),
        out_shape=(bf16((1, 1, C2, cells_out)), bf16((C2, PACKED)), f32((PLANE, 2 * C2))),
        scratch_shapes=[
            pltpu.VMEM((4, ROWS, LANES + PLANE), jnp.bfloat16),
            pltpu.VMEM((9 * ROWS, PLANE), jnp.bfloat16),
            pltpu.VMEM((2 * C1, PLANE + 2 * LANES), jnp.bfloat16),
            pltpu.VMEM((2, 6 * C1, PLANE), jnp.bfloat16),
            pltpu.VMEM((PLANE, 6 * C1), jnp.bfloat16),
            pltpu.VMEM((3, PLANE + 2 * HALF, LANES), jnp.float32),
            pltpu.VMEM((PLANE + 2 * HALF, LANES), jnp.bfloat16),
            pltpu.VMEM((PLANE + 2 * HALF, LANES), jnp.bfloat16),
            pltpu.VMEM((1, 1, C2, cells_out), jnp.bfloat16),
            pltpu.SemaphoreType.DMA,
        ],
        compiler_params=pltpu.CompilerParams(vmem_limit_bytes=16 * MIB),
        name="far",
    )(across, select, w1_far, w2, cot, first, near, pre)
    half = rows // 2
    received = lax.all_to_all(term, ("narrow", "core"), 0, 0, tiled=True)
    owned = jnp.sum(received.reshape(2 * narrow, half, PACKED).astype(jnp.float32), axis=0).astype(jnp.bfloat16)
    parts = lax.all_to_all(jnp.broadcast_to(owned[None], (wide, half, PACKED)), WIDE, 0, 0, tiled=True)
    total = jnp.sum(parts.reshape(wide // 2, rows, PACKED).astype(jnp.float32), axis=0)
    anywhere = pl.BlockSpec(memory_space=pl.ANY)
    weight_grad, output = pl.pallas_call(
        finish_kernel,
        in_specs=[fast, fast, anywhere],
        out_specs=(anywhere, anywhere),
        out_shape=(f32((27, rows, C1)), bf16((1, 1, C2, cells_out))),
        scratch_shapes=[
            pltpu.VMEM((27, rows, C1), jnp.float32),
            pltpu.VMEM((1, 1, C2, cells_out), jnp.bfloat16),
            pltpu.SemaphoreType.DMA((3,)),
            pltpu.SemaphoreType.DMA,
        ],
        input_output_aliases={2: 1},
        compiler_params=pltpu.CompilerParams(vmem_limit_bytes=8 * MIB),
        name="finish",
    )(total, pre, begun)
    return (output, weight_grad)


def solution(mesh):
    wide, narrow = mesh.devices.shape
    split = jax.sharding.Mesh(mesh.devices.reshape(wide // 2, 2, narrow), ("chip", "core", "narrow"))
    return jax.shard_map(
        body,
        mesh=split,
        in_specs=(P("narrow", None, None, WIDE, None), P(), P(), P("narrow", None, None, WIDE)),
        out_specs=(P("narrow", None, None, WIDE), P(None, "narrow", None)),
        check_vma=False,
    )
```

```python
import functools
import math

import jax
import jax.numpy as jnp
import numpy as np
from jax import lax
from jax.experimental import pallas as pl
from jax.experimental.pallas import tpu as pltpu
from jax.sharding import PartitionSpec as P

CIN = 4
C1 = 32
C2 = 64
PLANES = 4
CELLS = 4096
HALF = 32
PLANE = 1024
LANES = 128
ROWS = CIN * PLANES
CHUNK = 512
PACKED = 7 * LANES
MIB = 2**20
WIDE = ("chip", "core")
neg_slope = 0.3


def selection():
    table = np.zeros((CHUNK, 2, 2, 4, HALF), np.float32)
    for py in range(2):
        for px in range(2):
            for row in range(4):
                for col in range(HALF):
                    table[(2 * row + py) * 64 + 2 * col + px, py, px, row, col] = 1
    return table.reshape(CHUNK, CHUNK)


def placement():
    table = np.zeros((2, 27, CIN, 4, CHUNK), np.float32)
    for odd in range(2):
        for a in range(3):
            for bc in range(9):
                for i in range(CIN):
                    for q in range(4):
                        slab, plane = divmod(2 * q + a + 1, PLANES)
                        inner = i * PLANES + plane
                        if slab == 1:
                            column = bc * 2 * ROWS + inner
                        elif (slab == 0) == (odd == 1):
                            column = bc * 2 * ROWS + ROWS + inner
                        else:
                            column = 18 * ROWS + bc * ROWS + (plane - (slab == 0)) * CIN + i
                        table[odd, 9 * a + bc, i, q, column] = 1
    return table.reshape(2, 27 * CIN, 4 * CHUNK)


def leaky_relu(value):
    return jnp.where(value > 0, value, neg_slope * value)


def column_masks():
    column = lax.broadcasted_iota(jnp.int32, (1, PLANE), 1) % HALF
    left_ok = jnp.where(column > 0, 1.0, 0.0).astype(jnp.bfloat16)
    right_ok = jnp.where(column < HALF - 1, 1.0, 0.0).astype(jnp.bfloat16)
    return left_ok, right_ok


def strided_taps(rows, select_ref, parity_ref, taps_ref):
    count = rows.shape[0]
    left_ok, _ = column_masks()
    chunks = jnp.concatenate([rows[:, CHUNK * j : CHUNK * (j + 1)] for j in range(8)], axis=0)
    for p in range(4):
        parity_ref[p, :, 0:LANES] = jnp.zeros((count, LANES), jnp.bfloat16)
    for py in range(2):
        parts = jnp.dot(
            chunks, select_ref[:, 256 * py : 256 * py + 256], preferred_element_type=jnp.float32
        ).astype(jnp.bfloat16)
        for px in range(2):
            for j in range(8):
                parity_ref[2 * py + px, :, LANES * (j + 1) : LANES * (j + 2)] = parts[
                    j * count : (j + 1) * count, px * LANES : (px + 1) * LANES
                ]
    for b in range(3):
        for c in range(3):
            begin = LANES - HALF * (b == 0) - (c == 0)
            part = parity_ref[2 * (b != 1) + (c != 1), :, begin : begin + PLANE]
            if c == 0:
                part = part * left_ok
            taps_ref[(3 * b + c) * count : (3 * b + c + 1) * count, :] = part


def shifted_columns(act_ref, columns_ref):
    left_ok, right_ok = column_masks()
    for c in range(3):
        begin = LANES + c - 1
        part = act_ref[:, begin : begin + PLANE]
        if c == 0:
            part = part * left_ok
        if c == 2:
            part = part * right_ok
        columns_ref[c * 2 * C1 : (c + 1) * 2 * C1, :] = part


def second_layer(w2, columns_ref, turned_ref, rowed_ref):
    blank = jnp.zeros((HALF, LANES), jnp.float32)
    for b in (0, 2):
        rowed_ref[b, 0:HALF, :] = blank
        rowed_ref[b, HALF + PLANE :, :] = blank
    for n in range(4):
        cells = slice(256 * n, 256 * n + 256)
        turned_ref[cells, :] = columns_ref[:, cells].T
    for n in range(4):
        sums = jnp.dot(turned_ref[256 * n : 256 * n + 256, :], w2, preferred_element_type=jnp.float32)
        for b in range(3):
            rowed_ref[b, HALF + 256 * n : HALF + 256 * n + 256, :] = sums[:, b * LANES : (b + 1) * LANES]


def row_sum(rowed_ref, n):
    begins = [HALF * b + 256 * n for b in range(3)]
    first, second, third = (rowed_ref[b, begin : begin + 256, :] for b, begin in enumerate(begins))
    return first + second + third


def clear_margins(act_ref):
    margin = jnp.zeros((2 * C1, LANES), jnp.bfloat16)
    act_ref[:, 0:LANES] = margin
    act_ref[:, LANES + PLANE :] = margin


def pack_kernel(slab_hbm, across_ref, slab_ref, rows_ref, sems):
    odd = lax.axis_index("core")
    copies = [pltpu.make_async_copy(slab_hbm.at[0, 0, i], slab_ref.at[i], sems.at[i]) for i in range(CIN)]
    for copy in copies:
        copy.start()
    for i in range(CIN):
        copies[i].wait()
        planes = slab_ref[i].astype(jnp.float32)
        for j in range(CELLS // LANES):
            begin = j * ROWS + PLANES * i
            rows_ref[begin : begin + PLANES, :] = planes[:, j * LANES : (j + 1) * LANES]
    for k in range(3):
        for j in range(CELLS // LANES):
            channels = rows_ref[pl.ds(j * ROWS + k + odd, CIN, stride=PLANES), :]
            across_ref[k, :, j * LANES : (j + 1) * LANES] = channels.astype(jnp.bfloat16)


def prepare_kernel(
    k1_hbm, place_hbm, k2_hbm, select_hbm, cot_hbm,
    w1_near_ref, w1_far_ref, w2_ref, select_ref, turned_ref,
    k1_ref, place_ref, k2_ref, cot_ref, k1_rows_ref, sems,
):
    odd = lax.axis_index("core")
    moves = (
        (k1_hbm, k1_ref), (k2_hbm, k2_ref), (place_hbm.at[odd], place_ref), (cot_hbm, cot_ref), (select_hbm, select_ref),
    )
    copies = [pltpu.make_async_copy(src, dst, sems.at[k]) for k, (src, dst) in enumerate(moves)]
    for copy in copies:
        copy.start()
    copies[0].wait()
    for tap in range(27):
        k1_rows_ref[CIN * tap : CIN * (tap + 1), :] = k1_ref[tap].astype(jnp.float32)
    copies[1].wait()
    blank = jnp.zeros((C1, C2), jnp.bfloat16)

    def stacked(bc, pair):
        k = [blank] + [k2_ref[9 * a + bc] for a in range(3)] + [blank]
        lower = jnp.concatenate(k[1 + 2 * pair : 3 + 2 * pair], axis=0)
        upper = jnp.concatenate(k[2 * pair : 2 + 2 * pair], axis=0)
        return jnp.concatenate([lower, upper], axis=1)

    for pair in range(2):
        for b in range(3):
            for c in range(3):
                w2_ref[pair, c * 2 * C1 : (c + 1) * 2 * C1, b * LANES : (b + 1) * LANES] = stacked(3 * b + c, pair)
    copies[2].wait()
    spread = lax.dot_general(
        k1_rows_ref[...].astype(jnp.bfloat16), place_ref[...],
        (((0,), (0,)), ((), ())), preferred_element_type=jnp.float32,
    ).astype(jnp.bfloat16)
    for q in range(4):
        rows = slice(q % 2 * C1, (q % 2 + 1) * C1)
        w1_near_ref[q // 2, rows, :] = spread[:, CHUNK * q : CHUNK * q + 18 * ROWS]
        w1_far_ref[q // 2, rows, :] = spread[:, CHUNK * q + 18 * ROWS : CHUNK * q + 27 * ROWS]
    copies[3].wait()
    for n in range(4):
        planes = [cot_ref[0, 0, :, z * PLANE + 256 * n : z * PLANE + 256 * n + 256] for z in range(2)]
        turned_ref[256 * n : 256 * n + 256, :] = jnp.concatenate(planes, axis=0).T
    copies[4].wait()


def near_kernel(
    own_ref, within_ref, select_ref, w1_ref, w2_ref, first_ref, columns_ref, pre_ref,
    parity_ref, taps_ref, act_ref, turned_ref, rowed_ref,
):
    odd = lax.axis_index("core")
    rows = jnp.concatenate([ref[i] for ref in (own_ref, within_ref) for i in range(CIN)], axis=0)
    strided_taps(rows, select_ref, parity_ref, taps_ref)
    clear_margins(act_ref)
    for n in range(4):
        here = slice(256 * n, 256 * n + 256)
        first_ref[:, here] = jnp.dot(w1_ref[odd], taps_ref[:, here], preferred_element_type=jnp.float32)
        complete = jnp.dot(w1_ref[1 - odd], taps_ref[:, here], preferred_element_type=jnp.float32)
        act_ref[:, LANES + 256 * n : LANES + 256 * n + 256] = leaky_relu(complete).astype(jnp.bfloat16)
    shifted_columns(act_ref, columns_ref)
    second_layer(w2_ref[1 - odd], columns_ref, turned_ref, rowed_ref)
    for n in range(4):
        pre_ref[256 * n : 256 * n + 256, :] = row_sum(rowed_ref, n)


def emit_activations(pre_ref, out_ref, out_hbm, sem):
    for n in range(4):
        output = leaky_relu(pre_ref[256 * n : 256 * n + 256, :]).astype(jnp.bfloat16).T
        for z in range(2):
            out_ref[0, 0, :, z * PLANE + 256 * n : z * PLANE + 256 * n + 256] = output[z * C2 : (z + 1) * C2]
    copy = pltpu.make_async_copy(out_ref, out_hbm, sem)
    copy.start()
    copy.wait()


def far_kernel(
    chips, scale, across_ref, select_ref, w1_ref, w2_ref, cot_ref, first_ref, near_ref, near_pre_ref, out_hbm, grad_ref, pre_ref,
    parity_ref, taps_ref, act_ref, columns_ref, turned_ref, rowed_ref, back_ref, swapped_ref, out_ref, out_sem,
):
    odd = lax.axis_index("core")
    last = (lax.axis_index("chip") == chips - 1) & (odd == 1)
    inside = jnp.where(last, 0.0, 1.0)
    blank = jnp.zeros((CIN, CELLS), jnp.bfloat16)
    rows = jnp.concatenate([across_ref[k] for k in range(3)] + [blank], axis=0)
    strided_taps(rows, select_ref, parity_ref, taps_ref)
    clear_margins(act_ref)
    for n in range(4):
        here = slice(256 * n, 256 * n + 256)
        first_pre = first_ref[:, here] + jnp.dot(w1_ref[odd], taps_ref[:, here], preferred_element_type=jnp.float32)
        first_act = leaky_relu(first_pre)
        there = slice(LANES + 256 * n, LANES + 256 * n + 256)
        act_ref[0:C1, there] = first_act[0:C1].astype(jnp.bfloat16)
        act_ref[C1:, there] = (first_act[C1:] * inside).astype(jnp.bfloat16)
    columns_ref[1 - odd] = near_ref[...]
    shifted_columns(act_ref, columns_ref.at[odd])
    second_layer(w2_ref[odd], columns_ref.at[odd], turned_ref, rowed_ref)
    margin = jnp.zeros((HALF, LANES), jnp.bfloat16)
    for ref in (back_ref, swapped_ref):
        ref[0:HALF, :] = margin
        ref[HALF + PLANE :, :] = margin
    for n in range(4):
        cells = slice(256 * n, 256 * n + 256)
        pre = near_pre_ref[cells, :] + row_sum(rowed_ref, n)
        pre_ref[cells, :] = pre
        back = (cot_ref[cells, :].astype(jnp.float32) * jnp.where(pre > 0, 1.0, neg_slope)).astype(jnp.bfloat16)
        here = slice(HALF + 256 * n, HALF + 256 * n + 256)
        back_ref[here, :] = back
        swapped_ref[here, :] = jnp.concatenate([back[:, C2:], back[:, 0:C2]], axis=1)
    low = lax.broadcasted_iota(jnp.int32, (1, LANES), 1) < C2
    rows_of = [slice((2 - b) * HALF, (2 - b) * HALF + PLANE) for b in range(3)]
    operands = []
    for left_ref, right_ref in ((back_ref, swapped_ref), (swapped_ref, back_ref)):
        first_two = jnp.where(low, left_ref[rows_of[0], :], right_ref[rows_of[1], :])
        operands.append(jnp.concatenate([first_two, left_ref[rows_of[2], :]], axis=1))

    def plane_columns(q, c):
        begin = 2 * C1 * c + C1 * (q % 2)
        return columns_ref[q // 2, begin : begin + C1, :]

    columns = [jnp.concatenate([plane_columns(a + z, c) for a in range(3) for c in range(3)], axis=0) for z in range(2)]
    sums = scale * jnp.dot(
        jnp.concatenate(columns, axis=1), jnp.concatenate(operands, axis=0), preferred_element_type=jnp.float32
    )
    left, right, ends = sums[0:256, 0:LANES], sums[0:256, LANES:], sums[256:]
    turned = [left[0:LANES].T, left[LANES:].T]
    third = jnp.where(low, right[0:LANES], pltpu.roll(right[LANES:], C2, 1)).T
    fourth = jnp.concatenate([ends[:, 0:LANES], ends[:, LANES:]] * 2, axis=0).T
    group = lax.broadcasted_iota(jnp.int32, (1, LANES), 1) // C1
    tiles = [turned[0][0:C2], turned[1][0:C2], turned[0][C2:], turned[1][C2:], third[0:C2], third[C2:]]
    tiles.append(jnp.where(group < 2, fourth[0:C2], pltpu.roll(fourth[C2:], C2, 1)))
    for k, tile in enumerate(tiles):
        grad_ref[:, k * LANES : (k + 1) * LANES] = tile.astype(jnp.bfloat16)
    early = lax.axis_index("narrow") == 0
    pl.when(early)(lambda: emit_activations(pre_ref, out_ref, out_hbm, out_sem))


def slots():
    where = []
    for a in range(3):
        for b in range(3):
            for c in range(3):
                tile, group = divmod(3 * a + c, 4)
                where.append((2 * b + tile, group) if tile < 2 else (6, (0, 2, 1)[b]))
    return where


def finish_kernel(total_ref, pre_ref, begun_hbm, grad_hbm, out_hbm, grad_ref, out_ref, sems, out_sem):
    del begun_hbm
    copies = []
    for k in range(3):
        for tap in range(9 * k, 9 * k + 9):
            tile, slot = slots()[tap]
            begin = tile * LANES + slot * C1
            grad_ref[tap] = total_ref[:, begin : begin + C1]
        here = slice(9 * k, 9 * k + 9)
        copies.append(pltpu.make_async_copy(grad_ref.at[here], grad_hbm.at[here], sems.at[k]))
        copies[k].start()
    late = lax.axis_index("narrow") > 0
    pl.when(late)(lambda: emit_activations(pre_ref, out_ref, out_hbm, out_sem))
    for copy in copies:
        copy.wait()


def body(volumes, first_kernel, second_kernel, cotangent):
    wide = lax.axis_size(WIDE)
    narrow = lax.axis_size("narrow")
    cells_out = cotangent.shape[3]
    scale = 1.0 / math.sqrt(wide * narrow * cells_out)
    pinned = pl.BlockSpec(memory_space=pltpu.HBM)
    fast = pl.BlockSpec(memory_space=pltpu.VMEM)
    bf16 = functools.partial(jax.ShapeDtypeStruct, dtype=jnp.bfloat16)
    f32 = functools.partial(jax.ShapeDtypeStruct, dtype=jnp.float32)
    across, slab = pl.pallas_call(
        pack_kernel,
        in_specs=[pinned],
        out_specs=(fast,) * 2,
        out_shape=(bf16((3, CIN, CELLS)), bf16((CIN, PLANES, CELLS))),
        scratch_shapes=[pltpu.VMEM((CELLS // LANES * ROWS, LANES), jnp.float32), pltpu.SemaphoreType.DMA((CIN,))],
        compiler_params=pltpu.CompilerParams(vmem_limit_bytes=8 * MIB),
        name="pack",
    )(pltpu.with_memory_space_constraint(volumes, pltpu.HBM))
    across = lax.ppermute(across, WIDE, [p for k in range(1, wide - 1, 2) for p in ((k, k + 1), (k + 1, k))])
    within = lax.ppermute(slab, WIDE, [p for k in range(0, wide - 1, 2) for p in ((k, k + 1), (k + 1, k))])
    stored = (
        first_kernel.transpose(0, 2, 1), jnp.asarray(placement(), jnp.bfloat16), second_kernel.transpose(0, 2, 1),
        jnp.asarray(selection(), jnp.bfloat16), cotangent,
    )
    w1_near, w1_far, w2, select, cot = pl.pallas_call(
        prepare_kernel,
        in_specs=[pinned] * 5,
        out_specs=(fast,) * 5,
        out_shape=(
            bf16((2, 2 * C1, 18 * ROWS)), bf16((2, 2 * C1, 9 * ROWS)), bf16((2, 6 * C1, 6 * C2)),
            bf16((CHUNK, CHUNK)), bf16((PLANE, 2 * C2)),
        ),
        scratch_shapes=[
            pltpu.VMEM((27, CIN, C1), jnp.bfloat16),
            pltpu.VMEM((27 * CIN, 4 * CHUNK), jnp.bfloat16),
            pltpu.VMEM((27, C1, C2), jnp.bfloat16),
            pltpu.VMEM(cotangent.shape, jnp.bfloat16),
            pltpu.VMEM((27 * CIN, C1), jnp.float32),
            pltpu.SemaphoreType.DMA((5,)),
        ],
        compiler_params=pltpu.CompilerParams(vmem_limit_bytes=12 * MIB),
        cost_estimate=pl.CostEstimate(flops=10**9, bytes_accessed=4 * MIB, transcendentals=0),
        name="prepare",
    )(*(pltpu.with_memory_space_constraint(x, pltpu.HBM) for x in stored))
    first, near, pre = pl.pallas_call(
        near_kernel,
        in_specs=[fast] * 5,
        out_specs=(fast,) * 3,
        out_shape=(f32((2 * C1, PLANE)), bf16((6 * C1, PLANE)), f32((PLANE, 2 * C2))),
        scratch_shapes=[
            pltpu.VMEM((4, 2 * ROWS, LANES + PLANE), jnp.bfloat16),
            pltpu.VMEM((18 * ROWS, PLANE), jnp.bfloat16),
            pltpu.VMEM((2 * C1, PLANE + 2 * LANES), jnp.bfloat16),
            pltpu.VMEM((PLANE, 6 * C1), jnp.bfloat16),
            pltpu.VMEM((3, PLANE + 2 * HALF, LANES), jnp.float32),
        ],
        compiler_params=pltpu.CompilerParams(vmem_limit_bytes=16 * MIB),
        name="near",
    )(slab, within, select, w1_near, w2)
    rows = C2 // narrow
    begun, term, pre = pl.pallas_call(
        functools.partial(far_kernel, wide // 2, scale),
        in_specs=[fast] * 8,
        out_specs=(pl.BlockSpec(memory_space=pl.ANY), fast, fast),
        out_shape=(bf16((1, 1, C2, cells_out)), bf16((C2, PACKED)), f32((PLANE, 2 * C2))),
        scratch_shapes=[
            pltpu.VMEM((4, ROWS, LANES + PLANE), jnp.bfloat16),
            pltpu.VMEM((9 * ROWS, PLANE), jnp.bfloat16),
            pltpu.VMEM((2 * C1, PLANE + 2 * LANES), jnp.bfloat16),
            pltpu.VMEM((2, 6 * C1, PLANE), jnp.bfloat16),
            pltpu.VMEM((PLANE, 6 * C1), jnp.bfloat16),
            pltpu.VMEM((3, PLANE + 2 * HALF, LANES), jnp.float32),
            pltpu.VMEM((PLANE + 2 * HALF, LANES), jnp.bfloat16),
            pltpu.VMEM((PLANE + 2 * HALF, LANES), jnp.bfloat16),
            pltpu.VMEM((1, 1, C2, cells_out), jnp.bfloat16),
            pltpu.SemaphoreType.DMA,
        ],
        compiler_params=pltpu.CompilerParams(vmem_limit_bytes=16 * MIB),
        name="far",
    )(across, select, w1_far, w2, cot, first, near, pre)
    half = rows // 2
    received = lax.all_to_all(term, ("narrow", "core"), 0, 0, tiled=True)
    owned = jnp.sum(received.reshape(2 * narrow, half, PACKED).astype(jnp.float32), axis=0).astype(jnp.bfloat16)
    parts = lax.all_to_all(jnp.broadcast_to(owned[None], (wide, half, PACKED)), WIDE, 0, 0, tiled=True)
    total = jnp.sum(parts.reshape(wide // 2, rows, PACKED).astype(jnp.float32), axis=0)
    anywhere = pl.BlockSpec(memory_space=pl.ANY)
    weight_grad, output = pl.pallas_call(
        finish_kernel,
        in_specs=[fast, fast, anywhere],
        out_specs=(anywhere, anywhere),
        out_shape=(f32((27, rows, C1)), bf16((1, 1, C2, cells_out))),
        scratch_shapes=[
            pltpu.VMEM((27, rows, C1), jnp.float32),
            pltpu.VMEM((1, 1, C2, cells_out), jnp.bfloat16),
            pltpu.SemaphoreType.DMA((3,)),
            pltpu.SemaphoreType.DMA,
        ],
        input_output_aliases={2: 1},
        compiler_params=pltpu.CompilerParams(vmem_limit_bytes=8 * MIB),
        name="finish",
    )(total, pre, begun)
    return (output, weight_grad)


def solution(mesh):
    wide, narrow = mesh.devices.shape
    split = jax.sharding.Mesh(mesh.devices.reshape(wide // 2, 2, narrow), ("chip", "core", "narrow"))
    return jax.shard_map(
        body,
        mesh=split,
        in_specs=(P("narrow", None, None, WIDE, None), P(), P(), P("narrow", None, None, WIDE)),
        out_specs=(P("narrow", None, None, WIDE), P(None, "narrow", None)),
        check_vma=False,
    )
```

```python
import functools
import math

import jax
import jax.numpy as jnp
import numpy as np
from jax import lax
from jax.experimental import pallas as pl
from jax.experimental.pallas import tpu as pltpu
from jax.sharding import PartitionSpec as P

CIN = 4
C1 = 32
C2 = 64
PLANES = 4
CELLS = 4096
HALF = 32
PLANE = 1024
LANES = 128
ROWS = CIN * PLANES
CHUNK = 512
PACKED = 7 * LANES
MIB = 2**20
WIDE = ("chip", "core")
neg_slope = 0.3


def selection():
    table = np.zeros((CHUNK, 2, 2, 4, HALF), np.float32)
    for py in range(2):
        for px in range(2):
            for row in range(4):
                for col in range(HALF):
                    table[(2 * row + py) * 64 + 2 * col + px, py, px, row, col] = 1
    return table.reshape(CHUNK, CHUNK)


def placement():
    table = np.zeros((2, 27, CIN, 4, CHUNK), np.float32)
    for odd in range(2):
        for a in range(3):
            for bc in range(9):
                for i in range(CIN):
                    for q in range(4):
                        slab, plane = divmod(2 * q + a + 1, PLANES)
                        inner = i * PLANES + plane
                        if slab == 1:
                            column = bc * 2 * ROWS + inner
                        elif (slab == 0) == (odd == 1):
                            column = bc * 2 * ROWS + ROWS + inner
                        else:
                            column = 18 * ROWS + bc * ROWS + (plane - (slab == 0)) * CIN + i
                        table[odd, 9 * a + bc, i, q, column] = 1
    return table.reshape(2, 27 * CIN, 4 * CHUNK)


def leaky_relu(value):
    return jnp.where(value > 0, value, neg_slope * value)


def column_masks():
    column = lax.broadcasted_iota(jnp.int32, (1, PLANE), 1) % HALF
    left_ok = jnp.where(column > 0, 1.0, 0.0).astype(jnp.bfloat16)
    right_ok = jnp.where(column < HALF - 1, 1.0, 0.0).astype(jnp.bfloat16)
    return left_ok, right_ok


def strided_taps(rows, select_ref, parity_ref, taps_ref):
    count = rows.shape[0]
    left_ok, _ = column_masks()
    chunks = jnp.concatenate([rows[:, CHUNK * j : CHUNK * (j + 1)] for j in range(8)], axis=0)
    for p in range(4):
        parity_ref[p, :, 0:LANES] = jnp.zeros((count, LANES), jnp.bfloat16)
    for py in range(2):
        parts = jnp.dot(
            chunks, select_ref[:, 256 * py : 256 * py + 256], preferred_element_type=jnp.float32
        ).astype(jnp.bfloat16)
        for px in range(2):
            for j in range(8):
                parity_ref[2 * py + px, :, LANES * (j + 1) : LANES * (j + 2)] = parts[
                    j * count : (j + 1) * count, px * LANES : (px + 1) * LANES
                ]
    for b in range(3):
        for c in range(3):
            begin = LANES - HALF * (b == 0) - (c == 0)
            part = parity_ref[2 * (b != 1) + (c != 1), :, begin : begin + PLANE]
            if c == 0:
                part = part * left_ok
            taps_ref[(3 * b + c) * count : (3 * b + c + 1) * count, :] = part


def shifted_columns(act_ref, columns_ref):
    left_ok, right_ok = column_masks()
    for c in range(3):
        begin = LANES + c - 1
        part = act_ref[:, begin : begin + PLANE]
        if c == 0:
            part = part * left_ok
        if c == 2:
            part = part * right_ok
        columns_ref[c * 2 * C1 : (c + 1) * 2 * C1, :] = part


def second_layer(w2, columns_ref, turned_ref, rowed_ref):
    blank = jnp.zeros((HALF, LANES), jnp.float32)
    for b in (0, 2):
        rowed_ref[b, 0:HALF, :] = blank
        rowed_ref[b, HALF + PLANE :, :] = blank
    for n in range(4):
        cells = slice(256 * n, 256 * n + 256)
        turned_ref[cells, :] = columns_ref[:, cells].T
    for n in range(4):
        sums = jnp.dot(turned_ref[256 * n : 256 * n + 256, :], w2, preferred_element_type=jnp.float32)
        for b in range(3):
            rowed_ref[b, HALF + 256 * n : HALF + 256 * n + 256, :] = sums[:, b * LANES : (b + 1) * LANES]


def row_sum(rowed_ref, n):
    begins = [HALF * b + 256 * n for b in range(3)]
    first, second, third = (rowed_ref[b, begin : begin + 256, :] for b, begin in enumerate(begins))
    return first + second + third


def clear_margins(act_ref):
    margin = jnp.zeros((2 * C1, LANES), jnp.bfloat16)
    act_ref[:, 0:LANES] = margin
    act_ref[:, LANES + PLANE :] = margin


def pack_kernel(slab_hbm, across_ref, slab_ref, rows_ref, sems):
    odd = lax.axis_index("core")
    quarter = CELLS // 4
    parts = [(i, slice(n * quarter, (n + 1) * quarter)) for n in range(4) for i in range(CIN)]
    copies = [
        pltpu.make_async_copy(slab_hbm.at[0, 0, i, :, cells], slab_ref.at[i, :, cells], sems.at[k])
        for k, (i, cells) in enumerate(parts)
    ]
    for copy in copies:
        copy.start()
    for n in range(4):
        tiles = range(n * quarter // LANES, (n + 1) * quarter // LANES)
        for i in range(CIN):
            copies[CIN * n + i].wait()
            for j in tiles:
                begin = j * ROWS + PLANES * i
                rows_ref[begin : begin + PLANES, :] = slab_ref[i, :, j * LANES : (j + 1) * LANES].astype(jnp.float32)
        for k in range(3):
            for j in tiles:
                channels = rows_ref[pl.ds(j * ROWS + k + odd, CIN, stride=PLANES), :]
                across_ref[k, :, j * LANES : (j + 1) * LANES] = channels.astype(jnp.bfloat16)


def prepare_kernel(
    k1_hbm, place_hbm, k2_hbm, select_hbm, cot_hbm,
    w1_near_ref, w1_far_ref, w2_ref, select_ref, turned_ref,
    k1_ref, place_ref, k2_ref, cot_ref, k1_rows_ref, sems,
):
    odd = lax.axis_index("core")
    moves = (
        (k1_hbm, k1_ref), (k2_hbm, k2_ref), (place_hbm.at[odd], place_ref), (cot_hbm, cot_ref), (select_hbm, select_ref),
    )
    copies = [pltpu.make_async_copy(src, dst, sems.at[k]) for k, (src, dst) in enumerate(moves)]
    for copy in copies:
        copy.start()
    copies[0].wait()
    for tap in range(27):
        k1_rows_ref[CIN * tap : CIN * (tap + 1), :] = k1_ref[tap].astype(jnp.float32)
    copies[1].wait()
    blank = jnp.zeros((C1, C2), jnp.bfloat16)

    def stacked(bc, pair):
        k = [blank] + [k2_ref[9 * a + bc] for a in range(3)] + [blank]
        lower = jnp.concatenate(k[1 + 2 * pair : 3 + 2 * pair], axis=0)
        upper = jnp.concatenate(k[2 * pair : 2 + 2 * pair], axis=0)
        return jnp.concatenate([lower, upper], axis=1)

    for pair in range(2):
        for b in range(3):
            for c in range(3):
                w2_ref[pair, c * 2 * C1 : (c + 1) * 2 * C1, b * LANES : (b + 1) * LANES] = stacked(3 * b + c, pair)
    copies[2].wait()
    spread = lax.dot_general(
        k1_rows_ref[...].astype(jnp.bfloat16), place_ref[...],
        (((0,), (0,)), ((), ())), preferred_element_type=jnp.float32,
    ).astype(jnp.bfloat16)
    for q in range(4):
        rows = slice(q % 2 * C1, (q % 2 + 1) * C1)
        w1_near_ref[q // 2, rows, :] = spread[:, CHUNK * q : CHUNK * q + 18 * ROWS]
        w1_far_ref[q // 2, rows, :] = spread[:, CHUNK * q + 18 * ROWS : CHUNK * q + 27 * ROWS]
    copies[3].wait()
    for n in range(4):
        planes = [cot_ref[0, 0, :, z * PLANE + 256 * n : z * PLANE + 256 * n + 256] for z in range(2)]
        turned_ref[256 * n : 256 * n + 256, :] = jnp.concatenate(planes, axis=0).T
    copies[4].wait()


def near_kernel(
    own_ref, within_ref, select_ref, w1_ref, w2_ref, first_ref, columns_ref, pre_ref,
    parity_ref, taps_ref, act_ref, turned_ref, rowed_ref,
):
    odd = lax.axis_index("core")
    rows = jnp.concatenate([ref[i] for ref in (own_ref, within_ref) for i in range(CIN)], axis=0)
    strided_taps(rows, select_ref, parity_ref, taps_ref)
    clear_margins(act_ref)
    for n in range(4):
        here = slice(256 * n, 256 * n + 256)
        first_ref[:, here] = jnp.dot(w1_ref[odd], taps_ref[:, here], preferred_element_type=jnp.float32)
        complete = jnp.dot(w1_ref[1 - odd], taps_ref[:, here], preferred_element_type=jnp.float32)
        act_ref[:, LANES + 256 * n : LANES + 256 * n + 256] = leaky_relu(complete).astype(jnp.bfloat16)
    shifted_columns(act_ref, columns_ref)
    second_layer(w2_ref[1 - odd], columns_ref, turned_ref, rowed_ref)
    for n in range(4):
        pre_ref[256 * n : 256 * n + 256, :] = row_sum(rowed_ref, n)


def emit_activations(pre_ref, out_ref, out_hbm, sem):
    for n in range(4):
        output = leaky_relu(pre_ref[256 * n : 256 * n + 256, :]).astype(jnp.bfloat16).T
        for z in range(2):
            out_ref[0, 0, :, z * PLANE + 256 * n : z * PLANE + 256 * n + 256] = output[z * C2 : (z + 1) * C2]
    copy = pltpu.make_async_copy(out_ref, out_hbm, sem)
    copy.start()
    copy.wait()


def far_kernel(
    chips, scale, across_ref, select_ref, w1_ref, w2_ref, cot_ref, first_ref, near_ref, near_pre_ref, out_hbm, grad_ref, pre_ref,
    parity_ref, taps_ref, act_ref, columns_ref, turned_ref, rowed_ref, back_ref, swapped_ref, out_ref, out_sem,
):
    odd = lax.axis_index("core")
    last = (lax.axis_index("chip") == chips - 1) & (odd == 1)
    inside = jnp.where(last, 0.0, 1.0)
    blank = jnp.zeros((CIN, CELLS), jnp.bfloat16)
    rows = jnp.concatenate([across_ref[k] for k in range(3)] + [blank], axis=0)
    strided_taps(rows, select_ref, parity_ref, taps_ref)
    clear_margins(act_ref)
    for n in range(4):
        here = slice(256 * n, 256 * n + 256)
        first_pre = first_ref[:, here] + jnp.dot(w1_ref[odd], taps_ref[:, here], preferred_element_type=jnp.float32)
        first_act = leaky_relu(first_pre)
        there = slice(LANES + 256 * n, LANES + 256 * n + 256)
        act_ref[0:C1, there] = first_act[0:C1].astype(jnp.bfloat16)
        act_ref[C1:, there] = (first_act[C1:] * inside).astype(jnp.bfloat16)
    columns_ref[1 - odd] = near_ref[...]
    shifted_columns(act_ref, columns_ref.at[odd])
    second_layer(w2_ref[odd], columns_ref.at[odd], turned_ref, rowed_ref)
    margin = jnp.zeros((HALF, LANES), jnp.bfloat16)
    for ref in (back_ref, swapped_ref):
        ref[0:HALF, :] = margin
        ref[HALF + PLANE :, :] = margin
    for n in range(4):
        cells = slice(256 * n, 256 * n + 256)
        pre = near_pre_ref[cells, :] + row_sum(rowed_ref, n)
        pre_ref[cells, :] = pre
        back = (cot_ref[cells, :].astype(jnp.float32) * jnp.where(pre > 0, 1.0, neg_slope)).astype(jnp.bfloat16)
        here = slice(HALF + 256 * n, HALF + 256 * n + 256)
        back_ref[here, :] = back
        swapped_ref[here, :] = jnp.concatenate([back[:, C2:], back[:, 0:C2]], axis=1)
    low = lax.broadcasted_iota(jnp.int32, (1, LANES), 1) < C2
    rows_of = [slice((2 - b) * HALF, (2 - b) * HALF + PLANE) for b in range(3)]
    operands = []
    for left_ref, right_ref in ((back_ref, swapped_ref), (swapped_ref, back_ref)):
        first_two = jnp.where(low, left_ref[rows_of[0], :], right_ref[rows_of[1], :])
        operands.append(jnp.concatenate([first_two, left_ref[rows_of[2], :]], axis=1))

    def plane_columns(q, c):
        begin = 2 * C1 * c + C1 * (q % 2)
        return columns_ref[q // 2, begin : begin + C1, :]

    columns = [jnp.concatenate([plane_columns(a + z, c) for a in range(3) for c in range(3)], axis=0) for z in range(2)]
    sums = scale * jnp.dot(
        jnp.concatenate(columns, axis=1), jnp.concatenate(operands, axis=0), preferred_element_type=jnp.float32
    )
    left, right, ends = sums[0:256, 0:LANES], sums[0:256, LANES:], sums[256:]
    turned = [left[0:LANES].T, left[LANES:].T]
    third = jnp.where(low, right[0:LANES], pltpu.roll(right[LANES:], C2, 1)).T
    fourth = jnp.concatenate([ends[:, 0:LANES], ends[:, LANES:]] * 2, axis=0).T
    group = lax.broadcasted_iota(jnp.int32, (1, LANES), 1) // C1
    tiles = [turned[0][0:C2], turned[1][0:C2], turned[0][C2:], turned[1][C2:], third[0:C2], third[C2:]]
    tiles.append(jnp.where(group < 2, fourth[0:C2], pltpu.roll(fourth[C2:], C2, 1)))
    for k, tile in enumerate(tiles):
        grad_ref[:, k * LANES : (k + 1) * LANES] = tile.astype(jnp.bfloat16)
    early = lax.axis_index("narrow") == 0
    pl.when(early)(lambda: emit_activations(pre_ref, out_ref, out_hbm, out_sem))


def slots():
    where = []
    for a in range(3):
        for b in range(3):
            for c in range(3):
                tile, group = divmod(3 * a + c, 4)
                where.append((2 * b + tile, group) if tile < 2 else (6, (0, 2, 1)[b]))
    return where


def finish_kernel(total_ref, pre_ref, begun_hbm, grad_hbm, out_hbm, grad_ref, out_ref, sems, out_sem):
    del begun_hbm
    copies = []
    for k in range(3):
        for tap in range(9 * k, 9 * k + 9):
            tile, slot = slots()[tap]
            begin = tile * LANES + slot * C1
            grad_ref[tap] = total_ref[:, begin : begin + C1]
        here = slice(9 * k, 9 * k + 9)
        copies.append(pltpu.make_async_copy(grad_ref.at[here], grad_hbm.at[here], sems.at[k]))
        copies[k].start()
    late = lax.axis_index("narrow") > 0
    pl.when(late)(lambda: emit_activations(pre_ref, out_ref, out_hbm, out_sem))
    for copy in copies:
        copy.wait()


def body(volumes, first_kernel, second_kernel, cotangent):
    wide = lax.axis_size(WIDE)
    narrow = lax.axis_size("narrow")
    cells_out = cotangent.shape[3]
    scale = 1.0 / math.sqrt(wide * narrow * cells_out)
    pinned = pl.BlockSpec(memory_space=pltpu.HBM)
    fast = pl.BlockSpec(memory_space=pltpu.VMEM)
    bf16 = functools.partial(jax.ShapeDtypeStruct, dtype=jnp.bfloat16)
    f32 = functools.partial(jax.ShapeDtypeStruct, dtype=jnp.float32)
    across, slab = pl.pallas_call(
        pack_kernel,
        in_specs=[pinned],
        out_specs=(fast,) * 2,
        out_shape=(bf16((3, CIN, CELLS)), bf16((CIN, PLANES, CELLS))),
        scratch_shapes=[pltpu.VMEM((CELLS // LANES * ROWS, LANES), jnp.float32), pltpu.SemaphoreType.DMA((4 * CIN,))],
        compiler_params=pltpu.CompilerParams(vmem_limit_bytes=8 * MIB),
        name="pack",
    )(pltpu.with_memory_space_constraint(volumes, pltpu.HBM))
    across = lax.ppermute(across, WIDE, [p for k in range(1, wide - 1, 2) for p in ((k, k + 1), (k + 1, k))])
    within = lax.ppermute(slab, WIDE, [p for k in range(0, wide - 1, 2) for p in ((k, k + 1), (k + 1, k))])
    stored = (
        first_kernel.transpose(0, 2, 1), jnp.asarray(placement(), jnp.bfloat16), second_kernel.transpose(0, 2, 1),
        jnp.asarray(selection(), jnp.bfloat16), cotangent,
    )
    w1_near, w1_far, w2, select, cot = pl.pallas_call(
        prepare_kernel,
        in_specs=[pinned] * 5,
        out_specs=(fast,) * 5,
        out_shape=(
            bf16((2, 2 * C1, 18 * ROWS)), bf16((2, 2 * C1, 9 * ROWS)), bf16((2, 6 * C1, 6 * C2)),
            bf16((CHUNK, CHUNK)), bf16((PLANE, 2 * C2)),
        ),
        scratch_shapes=[
            pltpu.VMEM((27, CIN, C1), jnp.bfloat16),
            pltpu.VMEM((27 * CIN, 4 * CHUNK), jnp.bfloat16),
            pltpu.VMEM((27, C1, C2), jnp.bfloat16),
            pltpu.VMEM(cotangent.shape, jnp.bfloat16),
            pltpu.VMEM((27 * CIN, C1), jnp.float32),
            pltpu.SemaphoreType.DMA((5,)),
        ],
        compiler_params=pltpu.CompilerParams(vmem_limit_bytes=12 * MIB),
        cost_estimate=pl.CostEstimate(flops=10**9, bytes_accessed=4 * MIB, transcendentals=0),
        name="prepare",
    )(*(pltpu.with_memory_space_constraint(x, pltpu.HBM) for x in stored))
    first, near, pre = pl.pallas_call(
        near_kernel,
        in_specs=[fast] * 5,
        out_specs=(fast,) * 3,
        out_shape=(f32((2 * C1, PLANE)), bf16((6 * C1, PLANE)), f32((PLANE, 2 * C2))),
        scratch_shapes=[
            pltpu.VMEM((4, 2 * ROWS, LANES + PLANE), jnp.bfloat16),
            pltpu.VMEM((18 * ROWS, PLANE), jnp.bfloat16),
            pltpu.VMEM((2 * C1, PLANE + 2 * LANES), jnp.bfloat16),
            pltpu.VMEM((PLANE, 6 * C1), jnp.bfloat16),
            pltpu.VMEM((3, PLANE + 2 * HALF, LANES), jnp.float32),
        ],
        compiler_params=pltpu.CompilerParams(vmem_limit_bytes=16 * MIB),
        name="near",
    )(slab, within, select, w1_near, w2)
    rows = C2 // narrow
    begun, term, pre = pl.pallas_call(
        functools.partial(far_kernel, wide // 2, scale),
        in_specs=[fast] * 8,
        out_specs=(pl.BlockSpec(memory_space=pl.ANY), fast, fast),
        out_shape=(bf16((1, 1, C2, cells_out)), bf16((C2, PACKED)), f32((PLANE, 2 * C2))),
        scratch_shapes=[
            pltpu.VMEM((4, ROWS, LANES + PLANE), jnp.bfloat16),
            pltpu.VMEM((9 * ROWS, PLANE), jnp.bfloat16),
            pltpu.VMEM((2 * C1, PLANE + 2 * LANES), jnp.bfloat16),
            pltpu.VMEM((2, 6 * C1, PLANE), jnp.bfloat16),
            pltpu.VMEM((PLANE, 6 * C1), jnp.bfloat16),
            pltpu.VMEM((3, PLANE + 2 * HALF, LANES), jnp.float32),
            pltpu.VMEM((PLANE + 2 * HALF, LANES), jnp.bfloat16),
            pltpu.VMEM((PLANE + 2 * HALF, LANES), jnp.bfloat16),
            pltpu.VMEM((1, 1, C2, cells_out), jnp.bfloat16),
            pltpu.SemaphoreType.DMA,
        ],
        compiler_params=pltpu.CompilerParams(vmem_limit_bytes=16 * MIB),
        name="far",
    )(across, select, w1_far, w2, cot, first, near, pre)
    half = rows // 2
    received = lax.all_to_all(term, ("narrow", "core"), 0, 0, tiled=True)
    owned = jnp.sum(received.reshape(2 * narrow, half, PACKED).astype(jnp.float32), axis=0).astype(jnp.bfloat16)
    parts = lax.all_to_all(jnp.broadcast_to(owned[None], (wide, half, PACKED)), WIDE, 0, 0, tiled=True)
    total = jnp.sum(parts.reshape(wide // 2, rows, PACKED).astype(jnp.float32), axis=0)
    anywhere = pl.BlockSpec(memory_space=pl.ANY)
    weight_grad, output = pl.pallas_call(
        finish_kernel,
        in_specs=[fast, fast, anywhere],
        out_specs=(anywhere, anywhere),
        out_shape=(f32((27, rows, C1)), bf16((1, 1, C2, cells_out))),
        scratch_shapes=[
            pltpu.VMEM((27, rows, C1), jnp.float32),
            pltpu.VMEM((1, 1, C2, cells_out), jnp.bfloat16),
            pltpu.SemaphoreType.DMA((3,)),
            pltpu.SemaphoreType.DMA,
        ],
        input_output_aliases={2: 1},
        compiler_params=pltpu.CompilerParams(vmem_limit_bytes=8 * MIB),
        name="finish",
    )(total, pre, begun)
    return (output, weight_grad)


def solution(mesh):
    wide, narrow = mesh.devices.shape
    split = jax.sharding.Mesh(mesh.devices.reshape(wide // 2, 2, narrow), ("chip", "core", "narrow"))
    return jax.shard_map(
        body,
        mesh=split,
        in_specs=(P("narrow", None, None, WIDE, None), P(), P(), P("narrow", None, None, WIDE)),
        out_specs=(P("narrow", None, None, WIDE), P(None, "narrow", None)),
        check_vma=False,
    )
```

```python
import functools
import math

import jax
import jax.numpy as jnp
import numpy as np
from jax import lax
from jax.experimental import pallas as pl
from jax.experimental.pallas import tpu as pltpu
from jax.sharding import PartitionSpec as P

CIN = 4
C1 = 32
C2 = 64
PLANES = 4
CELLS = 4096
HALF = 32
PLANE = 1024
LANES = 128
ROWS = CIN * PLANES
CHUNK = 512
PACKED = 7 * LANES
MIB = 2**20
WIDE = ("chip", "core")
neg_slope = 0.3


def selection():
    table = np.zeros((CHUNK, 2, 2, 4, HALF), np.float32)
    for py in range(2):
        for px in range(2):
            for row in range(4):
                for col in range(HALF):
                    table[(2 * row + py) * 64 + 2 * col + px, py, px, row, col] = 1
    return table.reshape(CHUNK, CHUNK)


def placement():
    table = np.zeros((2, 27, CIN, 4, CHUNK), np.float32)
    for odd in range(2):
        for a in range(3):
            for bc in range(9):
                for i in range(CIN):
                    for q in range(4):
                        slab, plane = divmod(2 * q + a + 1, PLANES)
                        inner = i * PLANES + plane
                        if slab == 1:
                            column = bc * 2 * ROWS + inner
                        elif (slab == 0) == (odd == 1):
                            column = bc * 2 * ROWS + ROWS + inner
                        else:
                            column = 18 * ROWS + bc * ROWS + inner
                        table[odd, 9 * a + bc, i, q, column] = 1
    return table.reshape(2, 27 * CIN, 4 * CHUNK)


def leaky_relu(value):
    return jnp.maximum(value, neg_slope * value)


def plane_rows(volume_ref):
    return jnp.concatenate([volume_ref[0, 0, i] for i in range(CIN)], axis=0)


def column_masks():
    column = lax.broadcasted_iota(jnp.int32, (1, PLANE), 1) % HALF
    left_ok = jnp.where(column > 0, 1.0, 0.0).astype(jnp.bfloat16)
    right_ok = jnp.where(column < HALF - 1, 1.0, 0.0).astype(jnp.bfloat16)
    return left_ok, right_ok


def strided_taps(rows, select_ref, parity_ref, taps_ref):
    count = rows.shape[0]
    left_ok, _ = column_masks()
    chunks = jnp.concatenate([rows[:, CHUNK * j : CHUNK * (j + 1)] for j in range(8)], axis=0)
    for p in range(4):
        parity_ref[p, :, 0:LANES] = jnp.zeros((count, LANES), jnp.bfloat16)
    for py in range(2):
        parts = jnp.dot(
            chunks, select_ref[:, 256 * py : 256 * py + 256], preferred_element_type=jnp.float32
        ).astype(jnp.bfloat16)
        for px in range(2):
            for j in range(8):
                parity_ref[2 * py + px, :, LANES * (j + 1) : LANES * (j + 2)] = parts[
                    j * count : (j + 1) * count, px * LANES : (px + 1) * LANES
                ]
    for b in range(3):
        for c in range(3):
            begin = LANES - HALF * (b == 0) - (c == 0)
            part = parity_ref[2 * (b != 1) + (c != 1), :, begin : begin + PLANE]
            if c == 0:
                part = part * left_ok
            taps_ref[(3 * b + c) * count : (3 * b + c + 1) * count, :] = part


def shifted_columns(act_ref, columns_ref):
    left_ok, right_ok = column_masks()
    for c in range(3):
        begin = LANES + c - 1
        part = act_ref[:, begin : begin + PLANE]
        if c == 0:
            part = part * left_ok
        if c == 2:
            part = part * right_ok
        columns_ref[c * 2 * C1 : (c + 1) * 2 * C1, :] = part


def turn_columns(columns_ref, turned_ref):
    margin = jnp.zeros((HALF, 2 * LANES), jnp.bfloat16)
    turned_ref[0:HALF, :] = margin
    turned_ref[HALF + PLANE :, :] = margin
    blank = jnp.zeros((2 * C1, 256), jnp.bfloat16)
    for n in range(4):
        channels = jnp.concatenate([columns_ref[:, 256 * n : 256 * n + 256], blank], axis=0)
        turned_ref[HALF + 256 * n : HALF + 256 * n + 256, :] = channels.T


def second_layer(w2, turned_ref, n):
    views = [turned_ref[HALF * b + 256 * n : HALF * b + 256 * n + 256, :] for b in range(3)]
    return jnp.dot(jnp.concatenate(views, axis=1), w2, preferred_element_type=jnp.float32)


def clear_margins(act_ref):
    margin = jnp.zeros((2 * C1, LANES), jnp.bfloat16)
    act_ref[:, 0:LANES] = margin
    act_ref[:, LANES + PLANE :] = margin


def prepare_kernel(
    k1_hbm, place_hbm, k2_hbm, select_hbm, cot_hbm,
    w1_near_ref, w1_far_ref, w2_ref, select_ref, turned_ref,
    k1_ref, place_ref, k2_ref, cot_ref, k1_rows_ref, sems,
):
    odd = lax.axis_index("core")
    moves = (
        (k1_hbm, k1_ref), (k2_hbm, k2_ref), (place_hbm.at[odd], place_ref), (cot_hbm, cot_ref), (select_hbm, select_ref),
    )
    copies = [pltpu.make_async_copy(src, dst, sems.at[k]) for k, (src, dst) in enumerate(moves)]
    for copy in copies:
        copy.start()
    copies[0].wait()
    for tap in range(27):
        k1_rows_ref[CIN * tap : CIN * (tap + 1), :] = k1_ref[tap].astype(jnp.float32)
    copies[1].wait()
    blank = jnp.zeros((C1, C2), jnp.bfloat16)

    def stacked(bc, pair):
        k = [blank] + [k2_ref[9 * a + bc] for a in range(3)] + [blank]
        lower = jnp.concatenate(k[1 + 2 * pair : 3 + 2 * pair], axis=0)
        upper = jnp.concatenate(k[2 * pair : 2 + 2 * pair], axis=0)
        return jnp.concatenate([lower, upper], axis=1)

    for pair in range(2):
        for b in range(3):
            begin = 2 * LANES * b
            for c in range(3):
                w2_ref[pair, begin + c * 2 * C1 : begin + (c + 1) * 2 * C1, :] = stacked(3 * b + c, pair)
            w2_ref[pair, begin + 6 * C1 : begin + 2 * LANES, :] = jnp.zeros((2 * C1, LANES), jnp.bfloat16)
    copies[2].wait()
    spread = lax.dot_general(
        k1_rows_ref[...].astype(jnp.bfloat16), place_ref[...],
        (((0,), (0,)), ((), ())), preferred_element_type=jnp.float32,
    ).astype(jnp.bfloat16)
    for q in range(4):
        rows = slice(q % 2 * C1, (q % 2 + 1) * C1)
        w1_near_ref[q // 2, rows, :] = spread[:, CHUNK * q : CHUNK * q + 18 * ROWS]
        w1_far_ref[q // 2, rows, :] = spread[:, CHUNK * q + 18 * ROWS : CHUNK * q + 27 * ROWS]
    copies[3].wait()
    for n in range(4):
        planes = [cot_ref[0, 0, :, z * PLANE + 256 * n : z * PLANE + 256 * n + 256] for z in range(2)]
        turned_ref[256 * n : 256 * n + 256, :] = jnp.concatenate(planes, axis=0).T
    copies[4].wait()


def near_kernel(
    own_ref, within_ref, select_ref, w1_ref, w2_ref, first_ref, columns_ref, pre_ref,
    parity_ref, taps_ref, act_ref, turned_ref,
):
    odd = lax.axis_index("core")
    rows = jnp.concatenate([plane_rows(own_ref), plane_rows(within_ref)], axis=0)
    strided_taps(rows, select_ref, parity_ref, taps_ref)
    clear_margins(act_ref)
    for n in range(4):
        here = slice(256 * n, 256 * n + 256)
        first_ref[:, here] = jnp.dot(w1_ref[odd], taps_ref[:, here], preferred_element_type=jnp.float32)
        complete = jnp.dot(w1_ref[1 - odd], taps_ref[:, here], preferred_element_type=jnp.float32)
        act_ref[:, LANES + 256 * n : LANES + 256 * n + 256] = leaky_relu(complete).astype(jnp.bfloat16)
    shifted_columns(act_ref, columns_ref)
    turn_columns(columns_ref, turned_ref)
    for n in range(4):
        pre_ref[256 * n : 256 * n + 256, :] = second_layer(w2_ref[1 - odd], turned_ref, n)


def emit_activations(pre_ref, out_ref, out_hbm, sem):
    for n in range(4):
        output = leaky_relu(pre_ref[256 * n : 256 * n + 256, :]).astype(jnp.bfloat16).T
        for z in range(2):
            out_ref[0, 0, :, z * PLANE + 256 * n : z * PLANE + 256 * n + 256] = output[z * C2 : (z + 1) * C2]
    copy = pltpu.make_async_copy(out_ref, out_hbm, sem)
    copy.start()
    copy.wait()


def far_kernel(
    chips, scale, across_ref, select_ref, w1_ref, w2_ref, cot_ref, first_ref, near_ref, near_pre_ref, out_hbm, grad_ref, pre_ref,
    parity_ref, taps_ref, act_ref, columns_ref, turned_ref, back_ref, swapped_ref, out_ref, out_sem,
):
    odd = lax.axis_index("core")
    last = (lax.axis_index("chip") == chips - 1) & (odd == 1)
    inside = jnp.where(last, 0.0, 1.0)
    strided_taps(plane_rows(across_ref), select_ref, parity_ref, taps_ref)
    clear_margins(act_ref)
    for n in range(4):
        here = slice(256 * n, 256 * n + 256)
        first_pre = first_ref[:, here] + jnp.dot(w1_ref[odd], taps_ref[:, here], preferred_element_type=jnp.float32)
        first_act = leaky_relu(first_pre)
        there = slice(LANES + 256 * n, LANES + 256 * n + 256)
        act_ref[0:C1, there] = first_act[0:C1].astype(jnp.bfloat16)
        act_ref[C1:, there] = (first_act[C1:] * inside).astype(jnp.bfloat16)
    columns_ref[1 - odd] = near_ref[...]
    shifted_columns(act_ref, columns_ref.at[odd])
    turn_columns(columns_ref.at[odd], turned_ref)
    margin = jnp.zeros((HALF, LANES), jnp.bfloat16)
    for ref in (back_ref, swapped_ref):
        ref[0:HALF, :] = margin
        ref[HALF + PLANE :, :] = margin
    for n in range(4):
        cells = slice(256 * n, 256 * n + 256)
        pre = near_pre_ref[cells, :] + second_layer(w2_ref[odd], turned_ref, n)
        pre_ref[cells, :] = pre
        back = (cot_ref[cells, :].astype(jnp.float32) * jnp.where(pre > 0, 1.0, neg_slope)).astype(jnp.bfloat16)
        here = slice(HALF + 256 * n, HALF + 256 * n + 256)
        back_ref[here, :] = back
        swapped_ref[here, :] = jnp.concatenate([back[:, C2:], back[:, 0:C2]], axis=1)
    low = lax.broadcasted_iota(jnp.int32, (1, LANES), 1) < C2
    rows_of = [slice((2 - b) * HALF, (2 - b) * HALF + PLANE) for b in range(3)]
    operands = []
    for left_ref, right_ref in ((back_ref, swapped_ref), (swapped_ref, back_ref)):
        first_two = jnp.where(low, left_ref[rows_of[0], :], right_ref[rows_of[1], :])
        operands.append(jnp.concatenate([first_two, left_ref[rows_of[2], :]], axis=1))

    def plane_columns(q, c):
        begin = 2 * C1 * c + C1 * (q % 2)
        return columns_ref[q // 2, begin : begin + C1, :]

    columns = [jnp.concatenate([plane_columns(a + z, c) for a in range(3) for c in range(3)], axis=0) for z in range(2)]
    sums = scale * jnp.dot(
        jnp.concatenate(columns, axis=1), jnp.concatenate(operands, axis=0), preferred_element_type=jnp.float32
    )
    left, right, ends = sums[0:256, 0:LANES], sums[0:256, LANES:], sums[256:]
    turned = [left[0:LANES].T, left[LANES:].T]
    third = jnp.where(low, right[0:LANES], pltpu.roll(right[LANES:], C2, 1)).T
    fourth = jnp.concatenate([ends[:, 0:LANES], ends[:, LANES:]] * 2, axis=0).T
    group = lax.broadcasted_iota(jnp.int32, (1, LANES), 1) // C1
    tiles = [turned[0][0:C2], turned[1][0:C2], turned[0][C2:], turned[1][C2:], third[0:C2], third[C2:]]
    tiles.append(jnp.where(group < 2, fourth[0:C2], pltpu.roll(fourth[C2:], C2, 1)))
    for k, tile in enumerate(tiles):
        grad_ref[:, k * LANES : (k + 1) * LANES] = tile.astype(jnp.bfloat16)
    early = lax.axis_index("narrow") == 0
    pl.when(early)(lambda: emit_activations(pre_ref, out_ref, out_hbm, out_sem))


def slots():
    where = []
    for a in range(3):
        for b in range(3):
            for c in range(3):
                tile, group = divmod(3 * a + c, 4)
                where.append((2 * b + tile, group) if tile < 2 else (6, (0, 2, 1)[b]))
    return where


def finish_kernel(total_ref, pre_ref, begun_hbm, grad_hbm, out_hbm, grad_ref, out_ref, sems, out_sem):
    del begun_hbm
    copies = []
    for k in range(3):
        for tap in range(9 * k, 9 * k + 9):
            tile, slot = slots()[tap]
            begin = tile * LANES + slot * C1
            grad_ref[tap] = total_ref[:, begin : begin + C1]
        here = slice(9 * k, 9 * k + 9)
        copies.append(pltpu.make_async_copy(grad_ref.at[here], grad_hbm.at[here], sems.at[k]))
        copies[k].start()
    late = lax.axis_index("narrow") > 0
    pl.when(late)(lambda: emit_activations(pre_ref, out_ref, out_hbm, out_sem))
    for copy in copies:
        copy.wait()


def body(volumes, first_kernel, second_kernel, cotangent):
    wide = lax.axis_size(WIDE)
    narrow = lax.axis_size("narrow")
    cells_out = cotangent.shape[3]
    scale = 1.0 / math.sqrt(wide * narrow * cells_out)
    across = lax.ppermute(volumes, WIDE, [p for k in range(1, wide - 1, 2) for p in ((k, k + 1), (k + 1, k))])
    pairs = [p for k in range(0, wide - 1, 2) for p in ((k, k + 1), (k + 1, k))]
    within = lax.ppermute(volumes, WIDE, pairs)
    pinned = pl.BlockSpec(memory_space=pltpu.HBM)
    fast = pl.BlockSpec(memory_space=pltpu.VMEM)
    bf16 = functools.partial(jax.ShapeDtypeStruct, dtype=jnp.bfloat16)
    f32 = functools.partial(jax.ShapeDtypeStruct, dtype=jnp.float32)
    stored = (
        first_kernel.transpose(0, 2, 1), jnp.asarray(placement(), jnp.bfloat16), second_kernel.transpose(0, 2, 1),
        jnp.asarray(selection(), jnp.bfloat16), cotangent,
    )
    w1_near, w1_far, w2, select, cot = pl.pallas_call(
        prepare_kernel,
        in_specs=[pinned] * 5,
        out_specs=(fast,) * 5,
        out_shape=(
            bf16((2, 2 * C1, 18 * ROWS)), bf16((2, 2 * C1, 9 * ROWS)), bf16((2, 6 * LANES, 2 * C2)),
            bf16((CHUNK, CHUNK)), bf16((PLANE, 2 * C2)),
        ),
        scratch_shapes=[
            pltpu.VMEM((27, CIN, C1), jnp.bfloat16),
            pltpu.VMEM((27 * CIN, 4 * CHUNK), jnp.bfloat16),
            pltpu.VMEM((27, C1, C2), jnp.bfloat16),
            pltpu.VMEM(cotangent.shape, jnp.bfloat16),
            pltpu.VMEM((27 * CIN, C1), jnp.float32),
            pltpu.SemaphoreType.DMA((5,)),
        ],
        compiler_params=pltpu.CompilerParams(vmem_limit_bytes=12 * MIB),
        cost_estimate=pl.CostEstimate(flops=10**9, bytes_accessed=4 * MIB, transcendentals=0),
        name="prepare",
    )(*(pltpu.with_memory_space_constraint(x, pltpu.HBM) for x in stored))
    first, near, pre = pl.pallas_call(
        near_kernel,
        in_specs=[fast] * 5,
        out_specs=(fast,) * 3,
        out_shape=(f32((2 * C1, PLANE)), bf16((6 * C1, PLANE)), f32((PLANE, 2 * C2))),
        scratch_shapes=[
            pltpu.VMEM((4, 2 * ROWS, LANES + PLANE), jnp.bfloat16),
            pltpu.VMEM((18 * ROWS, PLANE), jnp.bfloat16),
            pltpu.VMEM((2 * C1, PLANE + 2 * LANES), jnp.bfloat16),
            pltpu.VMEM((PLANE + 2 * HALF, 2 * LANES), jnp.bfloat16),
        ],
        compiler_params=pltpu.CompilerParams(vmem_limit_bytes=16 * MIB),
        cost_estimate=pl.CostEstimate(flops=10**9, bytes_accessed=4 * MIB, transcendentals=0),
        name="near",
    )(volumes, within, select, w1_near, w2)
    rows = C2 // narrow
    begun, term, pre = pl.pallas_call(
        functools.partial(far_kernel, wide // 2, scale),
        in_specs=[fast] * 8,
        out_specs=(pl.BlockSpec(memory_space=pl.ANY), fast, fast),
        out_shape=(bf16((1, 1, C2, cells_out)), bf16((C2, PACKED)), f32((PLANE, 2 * C2))),
        scratch_shapes=[
            pltpu.VMEM((4, ROWS, LANES + PLANE), jnp.bfloat16),
            pltpu.VMEM((9 * ROWS, PLANE), jnp.bfloat16),
            pltpu.VMEM((2 * C1, PLANE + 2 * LANES), jnp.bfloat16),
            pltpu.VMEM((2, 6 * C1, PLANE), jnp.bfloat16),
            pltpu.VMEM((PLANE + 2 * HALF, 2 * LANES), jnp.bfloat16),
            pltpu.VMEM((PLANE + 2 * HALF, LANES), jnp.bfloat16),
            pltpu.VMEM((PLANE + 2 * HALF, LANES), jnp.bfloat16),
            pltpu.VMEM((1, 1, C2, cells_out), jnp.bfloat16),
            pltpu.SemaphoreType.DMA,
        ],
        compiler_params=pltpu.CompilerParams(vmem_limit_bytes=16 * MIB),
        name="far",
    )(across, select, w1_far, w2, cot, first, near, pre)
    half = rows // 2
    received = lax.all_to_all(term, ("narrow", "core"), 0, 0, tiled=True)
    owned = jnp.sum(received.reshape(2 * narrow, half, PACKED).astype(jnp.float32), axis=0).astype(jnp.bfloat16)
    parts = lax.all_to_all(jnp.broadcast_to(owned[None], (wide, half, PACKED)), WIDE, 0, 0, tiled=True)
    total = jnp.sum(parts.reshape(wide // 2, rows, PACKED).astype(jnp.float32), axis=0)
    anywhere = pl.BlockSpec(memory_space=pl.ANY)
    weight_grad, output = pl.pallas_call(
        finish_kernel,
        in_specs=[fast, fast, anywhere],
        out_specs=(anywhere, anywhere),
        out_shape=(f32((27, rows, C1)), bf16((1, 1, C2, cells_out))),
        scratch_shapes=[
            pltpu.VMEM((27, rows, C1), jnp.float32),
            pltpu.VMEM((1, 1, C2, cells_out), jnp.bfloat16),
            pltpu.SemaphoreType.DMA((3,)),
            pltpu.SemaphoreType.DMA,
        ],
        input_output_aliases={2: 1},
        compiler_params=pltpu.CompilerParams(vmem_limit_bytes=8 * MIB),
        name="finish",
    )(total, pre, begun)
    return (output, weight_grad)


def solution(mesh):
    wide, narrow = mesh.devices.shape
    split = jax.sharding.Mesh(mesh.devices.reshape(wide // 2, 2, narrow), ("chip", "core", "narrow"))
    return jax.shard_map(
        body,
        mesh=split,
        in_specs=(P("narrow", None, None, WIDE, None), P(), P(), P("narrow", None, None, WIDE)),
        out_specs=(P("narrow", None, None, WIDE), P(None, "narrow", None)),
        check_vma=False,
    )
```

```python
import functools
import math

import jax
import jax.numpy as jnp
import numpy as np
from jax import lax
from jax.experimental import pallas as pl
from jax.experimental.pallas import tpu as pltpu
from jax.sharding import PartitionSpec as P

CIN = 4
C1 = 32
C2 = 64
PLANES = 4
CELLS = 4096
HALF = 32
PLANE = 1024
LANES = 128
ROWS = CIN * PLANES
CHUNK = 512
PACKED = 7 * LANES
MIB = 2**20
WIDE = ("chip", "core")
neg_slope = 0.3


def selection():
    table = np.zeros((CHUNK, 2, 2, 4, HALF), np.float32)
    for py in range(2):
        for px in range(2):
            for row in range(4):
                for col in range(HALF):
                    table[(2 * row + py) * 64 + 2 * col + px, py, px, row, col] = 1
    return table.reshape(CHUNK, CHUNK)


def placement():
    table = np.zeros((2, 27, CIN, 4, CHUNK), np.float32)
    for odd in range(2):
        for a in range(3):
            for bc in range(9):
                for i in range(CIN):
                    for q in range(4):
                        slab, plane = divmod(2 * q + a + 1, PLANES)
                        inner = i * PLANES + plane
                        if slab == 1:
                            column = bc * 2 * ROWS + inner
                        elif (slab == 0) == (odd == 1):
                            column = bc * 2 * ROWS + ROWS + inner
                        else:
                            column = 18 * ROWS + bc * ROWS + (plane - (slab == 0)) * CIN + i
                        table[odd, 9 * a + bc, i, q, column] = 1
    return table.reshape(2, 27 * CIN, 4 * CHUNK)


def leaky_relu(value):
    return jnp.maximum(value, neg_slope * value)


def column_masks():
    column = lax.broadcasted_iota(jnp.int32, (1, PLANE), 1) % HALF
    left_ok = jnp.where(column > 0, 1.0, 0.0).astype(jnp.bfloat16)
    right_ok = jnp.where(column < HALF - 1, 1.0, 0.0).astype(jnp.bfloat16)
    return left_ok, right_ok


def strided_taps(rows, select_ref, parity_ref, taps_ref):
    count = rows.shape[0]
    left_ok, _ = column_masks()
    chunks = jnp.concatenate([rows[:, CHUNK * j : CHUNK * (j + 1)] for j in range(8)], axis=0)
    for p in range(4):
        parity_ref[p, :, 0:LANES] = jnp.zeros((count, LANES), jnp.bfloat16)
    for py in range(2):
        parts = jnp.dot(
            chunks, select_ref[:, 256 * py : 256 * py + 256], preferred_element_type=jnp.float32
        ).astype(jnp.bfloat16)
        for px in range(2):
            for j in range(8):
                parity_ref[2 * py + px, :, LANES * (j + 1) : LANES * (j + 2)] = parts[
                    j * count : (j + 1) * count, px * LANES : (px + 1) * LANES
                ]
    for b in range(3):
        for c in range(3):
            begin = LANES - HALF * (b == 0) - (c == 0)
            part = parity_ref[2 * (b != 1) + (c != 1), :, begin : begin + PLANE]
            if c == 0:
                part = part * left_ok
            taps_ref[(3 * b + c) * count : (3 * b + c + 1) * count, :] = part


def shifted_columns(act_ref, columns_ref):
    left_ok, right_ok = column_masks()
    for c in range(3):
        begin = LANES + c - 1
        part = act_ref[:, begin : begin + PLANE]
        if c == 0:
            part = part * left_ok
        if c == 2:
            part = part * right_ok
        columns_ref[c * 2 * C1 : (c + 1) * 2 * C1, :] = part


def second_layer(w2, columns_ref, turned_ref, rowed_ref):
    blank = jnp.zeros((HALF, LANES), jnp.float32)
    for b in (0, 2):
        rowed_ref[b, 0:HALF, :] = blank
        rowed_ref[b, HALF + PLANE :, :] = blank
    for n in range(4):
        cells = slice(256 * n, 256 * n + 256)
        turned_ref[cells, :] = columns_ref[:, cells].T
    for n in range(4):
        sums = jnp.dot(turned_ref[256 * n : 256 * n + 256, :], w2, preferred_element_type=jnp.float32)
        for b in range(3):
            rowed_ref[b, HALF + 256 * n : HALF + 256 * n + 256, :] = sums[:, b * LANES : (b + 1) * LANES]


def row_sum(rowed_ref, n):
    begins = [HALF * b + 256 * n for b in range(3)]
    first, second, third = (rowed_ref[b, begin : begin + 256, :] for b, begin in enumerate(begins))
    return first + second + third


def clear_margins(act_ref):
    margin = jnp.zeros((2 * C1, LANES), jnp.bfloat16)
    act_ref[:, 0:LANES] = margin
    act_ref[:, LANES + PLANE :] = margin


def pack_kernel(slab_hbm, across_ref, slab_ref, rows_ref, sems):
    odd = lax.axis_index("core")
    copies = [pltpu.make_async_copy(slab_hbm.at[0, 0, i], slab_ref.at[i], sems.at[i]) for i in range(CIN)]
    for copy in copies:
        copy.start()
    for i in range(CIN):
        copies[i].wait()
        planes = slab_ref[i].astype(jnp.float32)
        for j in range(CELLS // LANES):
            begin = j * ROWS + PLANES * i
            rows_ref[begin : begin + PLANES, :] = planes[:, j * LANES : (j + 1) * LANES]
    for k in range(3):
        for j in range(CELLS // LANES):
            channels = rows_ref[pl.ds(j * ROWS + k + odd, CIN, stride=PLANES), :]
            across_ref[k, :, j * LANES : (j + 1) * LANES] = channels.astype(jnp.bfloat16)


def prepare_kernel(
    k1_hbm, place_hbm, k2_hbm, select_hbm, cot_hbm,
    w1_near_ref, w1_far_ref, w2_ref, select_ref, turned_ref,
    k1_ref, place_ref, k2_ref, cot_ref, k1_rows_ref, sems,
):
    odd = lax.axis_index("core")
    moves = (
        (k1_hbm, k1_ref), (k2_hbm, k2_ref), (place_hbm.at[odd], place_ref), (cot_hbm, cot_ref), (select_hbm, select_ref),
    )
    copies = [pltpu.make_async_copy(src, dst, sems.at[k]) for k, (src, dst) in enumerate(moves)]
    for copy in copies:
        copy.start()
    copies[0].wait()
    for tap in range(27):
        k1_rows_ref[CIN * tap : CIN * (tap + 1), :] = k1_ref[tap].astype(jnp.float32)
    copies[1].wait()
    blank = jnp.zeros((C1, C2), jnp.bfloat16)

    def stacked(bc, pair):
        k = [blank] + [k2_ref[9 * a + bc] for a in range(3)] + [blank]
        lower = jnp.concatenate(k[1 + 2 * pair : 3 + 2 * pair], axis=0)
        upper = jnp.concatenate(k[2 * pair : 2 + 2 * pair], axis=0)
        return jnp.concatenate([lower, upper], axis=1)

    for pair in range(2):
        for b in range(3):
            for c in range(3):
                w2_ref[pair, c * 2 * C1 : (c + 1) * 2 * C1, b * LANES : (b + 1) * LANES] = stacked(3 * b + c, pair)
    copies[2].wait()
    spread = lax.dot_general(
        k1_rows_ref[...].astype(jnp.bfloat16), place_ref[...],
        (((0,), (0,)), ((), ())), preferred_element_type=jnp.float32,
    ).astype(jnp.bfloat16)
    for q in range(4):
        rows = slice(q % 2 * C1, (q % 2 + 1) * C1)
        w1_near_ref[q // 2, rows, :] = spread[:, CHUNK * q : CHUNK * q + 18 * ROWS]
        w1_far_ref[q // 2, rows, :] = spread[:, CHUNK * q + 18 * ROWS : CHUNK * q + 27 * ROWS]
    copies[3].wait()
    for n in range(4):
        planes = [cot_ref[0, 0, :, z * PLANE + 256 * n : z * PLANE + 256 * n + 256] for z in range(2)]
        turned_ref[256 * n : 256 * n + 256, :] = jnp.concatenate(planes, axis=0).T
    copies[4].wait()


def near_kernel(
    own_ref, within_ref, select_ref, w1_ref, w2_ref, first_ref, columns_ref, pre_ref,
    parity_ref, taps_ref, act_ref, turned_ref, rowed_ref,
):
    odd = lax.axis_index("core")
    rows = jnp.concatenate([ref[i] for ref in (own_ref, within_ref) for i in range(CIN)], axis=0)
    strided_taps(rows, select_ref, parity_ref, taps_ref)
    clear_margins(act_ref)
    for n in range(4):
        here = slice(256 * n, 256 * n + 256)
        first_ref[:, here] = jnp.dot(w1_ref[odd], taps_ref[:, here], preferred_element_type=jnp.float32)
        complete = jnp.dot(w1_ref[1 - odd], taps_ref[:, here], preferred_element_type=jnp.float32)
        act_ref[:, LANES + 256 * n : LANES + 256 * n + 256] = leaky_relu(complete).astype(jnp.bfloat16)
    shifted_columns(act_ref, columns_ref)
    second_layer(w2_ref[1 - odd], columns_ref, turned_ref, rowed_ref)
    for n in range(4):
        pre_ref[256 * n : 256 * n + 256, :] = row_sum(rowed_ref, n)


def emit_activations(pre_ref, out_ref, out_hbm, sem):
    for n in range(4):
        output = leaky_relu(pre_ref[256 * n : 256 * n + 256, :]).astype(jnp.bfloat16).T
        for z in range(2):
            out_ref[0, 0, :, z * PLANE + 256 * n : z * PLANE + 256 * n + 256] = output[z * C2 : (z + 1) * C2]
    copy = pltpu.make_async_copy(out_ref, out_hbm, sem)
    copy.start()
    copy.wait()


def far_kernel(
    chips, scale, across_ref, select_ref, w1_ref, w2_ref, cot_ref, first_ref, near_ref, near_pre_ref, out_hbm, grad_ref, pre_ref,
    parity_ref, taps_ref, act_ref, columns_ref, turned_ref, rowed_ref, back_ref, swapped_ref, out_ref, out_sem,
):
    odd = lax.axis_index("core")
    last = (lax.axis_index("chip") == chips - 1) & (odd == 1)
    inside = jnp.where(last, 0.0, 1.0)
    blank = jnp.zeros((CIN, CELLS), jnp.bfloat16)
    rows = jnp.concatenate([across_ref[k] for k in range(3)] + [blank], axis=0)
    strided_taps(rows, select_ref, parity_ref, taps_ref)
    clear_margins(act_ref)
    for n in range(4):
        here = slice(256 * n, 256 * n + 256)
        first_pre = first_ref[:, here] + jnp.dot(w1_ref[odd], taps_ref[:, here], preferred_element_type=jnp.float32)
        first_act = leaky_relu(first_pre)
        there = slice(LANES + 256 * n, LANES + 256 * n + 256)
        act_ref[0:C1, there] = first_act[0:C1].astype(jnp.bfloat16)
        act_ref[C1:, there] = (first_act[C1:] * inside).astype(jnp.bfloat16)
    columns_ref[1 - odd] = near_ref[...]
    shifted_columns(act_ref, columns_ref.at[odd])
    second_layer(w2_ref[odd], columns_ref.at[odd], turned_ref, rowed_ref)
    margin = jnp.zeros((HALF, LANES), jnp.bfloat16)
    for ref in (back_ref, swapped_ref):
        ref[0:HALF, :] = margin
        ref[HALF + PLANE :, :] = margin
    for n in range(4):
        cells = slice(256 * n, 256 * n + 256)
        pre = near_pre_ref[cells, :] + row_sum(rowed_ref, n)
        pre_ref[cells, :] = pre
        back = (cot_ref[cells, :].astype(jnp.float32) * jnp.where(pre > 0, 1.0, neg_slope)).astype(jnp.bfloat16)
        here = slice(HALF + 256 * n, HALF + 256 * n + 256)
        back_ref[here, :] = back
        swapped_ref[here, :] = jnp.concatenate([back[:, C2:], back[:, 0:C2]], axis=1)
    low = lax.broadcasted_iota(jnp.int32, (1, LANES), 1) < C2
    rows_of = [slice((2 - b) * HALF, (2 - b) * HALF + PLANE) for b in range(3)]
    operands = []
    for left_ref, right_ref in ((back_ref, swapped_ref), (swapped_ref, back_ref)):
        first_two = jnp.where(low, left_ref[rows_of[0], :], right_ref[rows_of[1], :])
        operands.append(jnp.concatenate([first_two, left_ref[rows_of[2], :]], axis=1))

    def plane_columns(q, c):
        begin = 2 * C1 * c + C1 * (q % 2)
        return columns_ref[q // 2, begin : begin + C1, :]

    columns = [jnp.concatenate([plane_columns(a + z, c) for a in range(3) for c in range(3)], axis=0) for z in range(2)]
    sums = scale * jnp.dot(
        jnp.concatenate(columns, axis=1), jnp.concatenate(operands, axis=0), preferred_element_type=jnp.float32
    )
    left, right, ends = sums[0:256, 0:LANES], sums[0:256, LANES:], sums[256:]
    turned = [left[0:LANES].T, left[LANES:].T]
    third = jnp.where(low, right[0:LANES], pltpu.roll(right[LANES:], C2, 1)).T
    fourth = jnp.concatenate([ends[:, 0:LANES], ends[:, LANES:]] * 2, axis=0).T
    group = lax.broadcasted_iota(jnp.int32, (1, LANES), 1) // C1
    tiles = [turned[0][0:C2], turned[1][0:C2], turned[0][C2:], turned[1][C2:], third[0:C2], third[C2:]]
    tiles.append(jnp.where(group < 2, fourth[0:C2], pltpu.roll(fourth[C2:], C2, 1)))
    for k, tile in enumerate(tiles):
        grad_ref[:, k * LANES : (k + 1) * LANES] = tile.astype(jnp.bfloat16)
    early = lax.axis_index("narrow") == 0
    pl.when(early)(lambda: emit_activations(pre_ref, out_ref, out_hbm, out_sem))


def slots():
    where = []
    for a in range(3):
        for b in range(3):
            for c in range(3):
                tile, group = divmod(3 * a + c, 4)
                where.append((2 * b + tile, group) if tile < 2 else (6, (0, 2, 1)[b]))
    return where


def finish_kernel(total_ref, pre_ref, begun_hbm, grad_hbm, out_hbm, grad_ref, out_ref, sems, out_sem):
    del begun_hbm
    copies = []
    for k in range(3):
        for tap in range(9 * k, 9 * k + 9):
            tile, slot = slots()[tap]
            begin = tile * LANES + slot * C1
            grad_ref[tap] = total_ref[:, begin : begin + C1]
        here = slice(9 * k, 9 * k + 9)
        copies.append(pltpu.make_async_copy(grad_ref.at[here], grad_hbm.at[here], sems.at[k]))
        copies[k].start()
    late = lax.axis_index("narrow") > 0
    pl.when(late)(lambda: emit_activations(pre_ref, out_ref, out_hbm, out_sem))
    for copy in copies:
        copy.wait()


def body(volumes, first_kernel, second_kernel, cotangent):
    wide = lax.axis_size(WIDE)
    narrow = lax.axis_size("narrow")
    cells_out = cotangent.shape[3]
    scale = 1.0 / math.sqrt(wide * narrow * cells_out)
    pinned = pl.BlockSpec(memory_space=pltpu.HBM)
    fast = pl.BlockSpec(memory_space=pltpu.VMEM)
    bf16 = functools.partial(jax.ShapeDtypeStruct, dtype=jnp.bfloat16)
    f32 = functools.partial(jax.ShapeDtypeStruct, dtype=jnp.float32)
    across, slab = pl.pallas_call(
        pack_kernel,
        in_specs=[pinned],
        out_specs=(fast,) * 2,
        out_shape=(bf16((3, CIN, CELLS)), bf16((CIN, PLANES, CELLS))),
        scratch_shapes=[pltpu.VMEM((CELLS // LANES * ROWS, LANES), jnp.float32), pltpu.SemaphoreType.DMA((CIN,))],
        compiler_params=pltpu.CompilerParams(vmem_limit_bytes=8 * MIB),
        name="pack",
    )(pltpu.with_memory_space_constraint(volumes, pltpu.HBM))
    across = lax.ppermute(across, WIDE, [p for k in range(1, wide - 1, 2) for p in ((k, k + 1), (k + 1, k))])
    within = lax.ppermute(slab, WIDE, [p for k in range(0, wide - 1, 2) for p in ((k, k + 1), (k + 1, k))])
    stored = (
        first_kernel.transpose(0, 2, 1), jnp.asarray(placement(), jnp.bfloat16), second_kernel.transpose(0, 2, 1),
        jnp.asarray(selection(), jnp.bfloat16), cotangent,
    )
    w1_near, w1_far, w2, select, cot = pl.pallas_call(
        prepare_kernel,
        in_specs=[pinned] * 5,
        out_specs=(fast,) * 5,
        out_shape=(
            bf16((2, 2 * C1, 18 * ROWS)), bf16((2, 2 * C1, 9 * ROWS)), bf16((2, 6 * C1, 6 * C2)),
            bf16((CHUNK, CHUNK)), bf16((PLANE, 2 * C2)),
        ),
        scratch_shapes=[
            pltpu.VMEM((27, CIN, C1), jnp.bfloat16),
            pltpu.VMEM((27 * CIN, 4 * CHUNK), jnp.bfloat16),
            pltpu.VMEM((27, C1, C2), jnp.bfloat16),
            pltpu.VMEM(cotangent.shape, jnp.bfloat16),
            pltpu.VMEM((27 * CIN, C1), jnp.float32),
            pltpu.SemaphoreType.DMA((5,)),
        ],
        compiler_params=pltpu.CompilerParams(vmem_limit_bytes=12 * MIB),
        cost_estimate=pl.CostEstimate(flops=10**9, bytes_accessed=4 * MIB, transcendentals=0),
        name="prepare",
    )(*(pltpu.with_memory_space_constraint(x, pltpu.HBM) for x in stored))
    first, near, pre = pl.pallas_call(
        near_kernel,
        in_specs=[fast] * 5,
        out_specs=(fast,) * 3,
        out_shape=(f32((2 * C1, PLANE)), bf16((6 * C1, PLANE)), f32((PLANE, 2 * C2))),
        scratch_shapes=[
            pltpu.VMEM((4, 2 * ROWS, LANES + PLANE), jnp.bfloat16),
            pltpu.VMEM((18 * ROWS, PLANE), jnp.bfloat16),
            pltpu.VMEM((2 * C1, PLANE + 2 * LANES), jnp.bfloat16),
            pltpu.VMEM((PLANE, 6 * C1), jnp.bfloat16),
            pltpu.VMEM((3, PLANE + 2 * HALF, LANES), jnp.float32),
        ],
        compiler_params=pltpu.CompilerParams(vmem_limit_bytes=16 * MIB),
        name="near",
    )(slab, within, select, w1_near, w2)
    rows = C2 // narrow
    begun, term, pre = pl.pallas_call(
        functools.partial(far_kernel, wide // 2, scale),
        in_specs=[fast] * 8,
        out_specs=(pl.BlockSpec(memory_space=pl.ANY), fast, fast),
        out_shape=(bf16((1, 1, C2, cells_out)), bf16((C2, PACKED)), f32((PLANE, 2 * C2))),
        scratch_shapes=[
            pltpu.VMEM((4, ROWS, LANES + PLANE), jnp.bfloat16),
            pltpu.VMEM((9 * ROWS, PLANE), jnp.bfloat16),
            pltpu.VMEM((2 * C1, PLANE + 2 * LANES), jnp.bfloat16),
            pltpu.VMEM((2, 6 * C1, PLANE), jnp.bfloat16),
            pltpu.VMEM((PLANE, 6 * C1), jnp.bfloat16),
            pltpu.VMEM((3, PLANE + 2 * HALF, LANES), jnp.float32),
            pltpu.VMEM((PLANE + 2 * HALF, LANES), jnp.bfloat16),
            pltpu.VMEM((PLANE + 2 * HALF, LANES), jnp.bfloat16),
            pltpu.VMEM((1, 1, C2, cells_out), jnp.bfloat16),
            pltpu.SemaphoreType.DMA,
        ],
        compiler_params=pltpu.CompilerParams(vmem_limit_bytes=16 * MIB),
        name="far",
    )(across, select, w1_far, w2, cot, first, near, pre)
    half = rows // 2
    received = lax.all_to_all(term, ("narrow", "core"), 0, 0, tiled=True)
    owned = jnp.sum(received.reshape(2 * narrow, half, PACKED).astype(jnp.float32), axis=0).astype(jnp.bfloat16)
    parts = lax.all_to_all(jnp.broadcast_to(owned[None], (wide, half, PACKED)), WIDE, 0, 0, tiled=True)
    total = jnp.sum(parts.reshape(wide // 2, rows, PACKED).astype(jnp.float32), axis=0)
    anywhere = pl.BlockSpec(memory_space=pl.ANY)
    weight_grad, output = pl.pallas_call(
        finish_kernel,
        in_specs=[fast, fast, anywhere],
        out_specs=(anywhere, anywhere),
        out_shape=(f32((27, rows, C1)), bf16((1, 1, C2, cells_out))),
        scratch_shapes=[
            pltpu.VMEM((27, rows, C1), jnp.float32),
            pltpu.VMEM((1, 1, C2, cells_out), jnp.bfloat16),
            pltpu.SemaphoreType.DMA((3,)),
            pltpu.SemaphoreType.DMA,
        ],
        input_output_aliases={2: 1},
        compiler_params=pltpu.CompilerParams(vmem_limit_bytes=8 * MIB),
        name="finish",
    )(total, pre, begun)
    return (output, weight_grad)


def solution(mesh):
    wide, narrow = mesh.devices.shape
    split = jax.sharding.Mesh(mesh.devices.reshape(wide // 2, 2, narrow), ("chip", "core", "narrow"))
    return jax.shard_map(
        body,
        mesh=split,
        in_specs=(P("narrow", None, None, WIDE, None), P(), P(), P("narrow", None, None, WIDE)),
        out_specs=(P("narrow", None, None, WIDE), P(None, "narrow", None)),
        check_vma=False,
    )
```

```python
import functools
import math

import jax
import jax.numpy as jnp
import numpy as np
from jax import lax
from jax.experimental import pallas as pl
from jax.experimental.pallas import tpu as pltpu
from jax.sharding import PartitionSpec as P

CIN = 4
C1 = 32
C2 = 64
PLANES = 4
CELLS = 4096
HALF = 32
PLANE = 1024
LANES = 128
ROWS = CIN * PLANES
CHUNK = 512
PACKED = 7 * LANES
MIB = 2**20
WIDE = ("chip", "core")
neg_slope = 0.3


def selection():
    table = np.zeros((CHUNK, 2, 2, 4, HALF), np.float32)
    for py in range(2):
        for px in range(2):
            for row in range(4):
                for col in range(HALF):
                    table[(2 * row + py) * 64 + 2 * col + px, py, px, row, col] = 1
    return table.reshape(CHUNK, CHUNK)


def placement():
    table = np.zeros((2, 27, CIN, 4, CHUNK), np.float32)
    for odd in range(2):
        for a in range(3):
            for bc in range(9):
                for i in range(CIN):
                    for q in range(4):
                        slab, plane = divmod(2 * q + a + 1, PLANES)
                        inner = i * PLANES + plane
                        if slab == 1:
                            column = bc * 2 * ROWS + inner
                        elif (slab == 0) == (odd == 1):
                            column = bc * 2 * ROWS + ROWS + inner
                        else:
                            column = 18 * ROWS + bc * ROWS + inner
                        table[odd, 9 * a + bc, i, q, column] = 1
    return table.reshape(2, 27 * CIN, 4 * CHUNK)


def leaky_relu(value):
    return jnp.maximum(value, neg_slope * value)


def plane_rows(volume_ref):
    return jnp.concatenate([volume_ref[0, 0, i] for i in range(CIN)], axis=0)


def column_masks():
    column = lax.broadcasted_iota(jnp.int32, (1, PLANE), 1) % HALF
    left_ok = jnp.where(column > 0, 1.0, 0.0).astype(jnp.bfloat16)
    right_ok = jnp.where(column < HALF - 1, 1.0, 0.0).astype(jnp.bfloat16)
    return left_ok, right_ok


def strided_taps(rows, select_ref, parity_ref, taps_ref):
    count = rows.shape[0]
    left_ok, _ = column_masks()
    chunks = jnp.concatenate([rows[:, CHUNK * j : CHUNK * (j + 1)] for j in range(8)], axis=0)
    for p in range(4):
        parity_ref[p, :, 0:LANES] = jnp.zeros((count, LANES), jnp.bfloat16)
    for py in range(2):
        parts = jnp.dot(
            chunks, select_ref[:, 256 * py : 256 * py + 256], preferred_element_type=jnp.float32
        ).astype(jnp.bfloat16)
        for px in range(2):
            for j in range(8):
                parity_ref[2 * py + px, :, LANES * (j + 1) : LANES * (j + 2)] = parts[
                    j * count : (j + 1) * count, px * LANES : (px + 1) * LANES
                ]
    for b in range(3):
        for c in range(3):
            begin = LANES - HALF * (b == 0) - (c == 0)
            part = parity_ref[2 * (b != 1) + (c != 1), :, begin : begin + PLANE]
            if c == 0:
                part = part * left_ok
            taps_ref[(3 * b + c) * count : (3 * b + c + 1) * count, :] = part


def shifted_columns(act_ref, columns_ref):
    left_ok, right_ok = column_masks()
    for c in range(3):
        begin = LANES + c - 1
        part = act_ref[:, begin : begin + PLANE]
        if c == 0:
            part = part * left_ok
        if c == 2:
            part = part * right_ok
        columns_ref[c * 2 * C1 : (c + 1) * 2 * C1, :] = part


def second_layer(w2, columns_ref, turned_ref, rowed_ref):
    blank = jnp.zeros((HALF, LANES), jnp.float32)
    for b in (0, 2):
        rowed_ref[b, 0:HALF, :] = blank
        rowed_ref[b, HALF + PLANE :, :] = blank
    for n in range(4):
        cells = slice(256 * n, 256 * n + 256)
        turned_ref[cells, :] = columns_ref[:, cells].T
    for n in range(4):
        sums = jnp.dot(turned_ref[256 * n : 256 * n + 256, :], w2, preferred_element_type=jnp.float32)
        for b in range(3):
            rowed_ref[b, HALF + 256 * n : HALF + 256 * n + 256, :] = sums[:, b * LANES : (b + 1) * LANES]


def row_sum(rowed_ref, n):
    begins = [HALF * b + 256 * n for b in range(3)]
    first, second, third = (rowed_ref[b, begin : begin + 256, :] for b, begin in enumerate(begins))
    return first + second + third


def clear_margins(act_ref):
    margin = jnp.zeros((2 * C1, LANES), jnp.bfloat16)
    act_ref[:, 0:LANES] = margin
    act_ref[:, LANES + PLANE :] = margin


def prepare_kernel(
    k1_hbm, place_hbm, k2_hbm, select_hbm, cot_hbm,
    w1_near_ref, w1_far_ref, w2_ref, select_ref, turned_ref,
    k1_ref, place_ref, k2_ref, cot_ref, k1_rows_ref, sems,
):
    odd = lax.axis_index("core")
    moves = (
        (k1_hbm, k1_ref), (k2_hbm, k2_ref), (place_hbm.at[odd], place_ref), (cot_hbm, cot_ref), (select_hbm, select_ref),
    )
    copies = [pltpu.make_async_copy(src, dst, sems.at[k]) for k, (src, dst) in enumerate(moves)]
    for copy in copies:
        copy.start()
    copies[0].wait()
    for tap in range(27):
        k1_rows_ref[CIN * tap : CIN * (tap + 1), :] = k1_ref[tap].astype(jnp.float32)
    copies[1].wait()
    blank = jnp.zeros((C1, C2), jnp.bfloat16)

    def stacked(bc, pair):
        k = [blank] + [k2_ref[9 * a + bc] for a in range(3)] + [blank]
        lower = jnp.concatenate(k[1 + 2 * pair : 3 + 2 * pair], axis=0)
        upper = jnp.concatenate(k[2 * pair : 2 + 2 * pair], axis=0)
        return jnp.concatenate([lower, upper], axis=1)

    for pair in range(2):
        for b in range(3):
            for c in range(3):
                w2_ref[pair, c * 2 * C1 : (c + 1) * 2 * C1, b * LANES : (b + 1) * LANES] = stacked(3 * b + c, pair)
    copies[2].wait()
    spread = lax.dot_general(
        k1_rows_ref[...].astype(jnp.bfloat16), place_ref[...],
        (((0,), (0,)), ((), ())), preferred_element_type=jnp.float32,
    ).astype(jnp.bfloat16)
    for q in range(4):
        rows = slice(q % 2 * C1, (q % 2 + 1) * C1)
        w1_near_ref[q // 2, rows, :] = spread[:, CHUNK * q : CHUNK * q + 18 * ROWS]
        w1_far_ref[q // 2, rows, :] = spread[:, CHUNK * q + 18 * ROWS : CHUNK * q + 27 * ROWS]
    copies[3].wait()
    for n in range(4):
        planes = [cot_ref[0, 0, :, z * PLANE + 256 * n : z * PLANE + 256 * n + 256] for z in range(2)]
        turned_ref[256 * n : 256 * n + 256, :] = jnp.concatenate(planes, axis=0).T
    copies[4].wait()


def near_kernel(
    own_ref, within_ref, select_ref, w1_ref, w2_ref, first_ref, columns_ref, pre_ref,
    parity_ref, taps_ref, act_ref, turned_ref, rowed_ref,
):
    odd = lax.axis_index("core")
    rows = jnp.concatenate([plane_rows(own_ref), plane_rows(within_ref)], axis=0)
    strided_taps(rows, select_ref, parity_ref, taps_ref)
    clear_margins(act_ref)
    for n in range(4):
        here = slice(256 * n, 256 * n + 256)
        first_ref[:, here] = jnp.dot(w1_ref[odd], taps_ref[:, here], preferred_element_type=jnp.float32)
        complete = jnp.dot(w1_ref[1 - odd], taps_ref[:, here], preferred_element_type=jnp.float32)
        act_ref[:, LANES + 256 * n : LANES + 256 * n + 256] = leaky_relu(complete).astype(jnp.bfloat16)
    shifted_columns(act_ref, columns_ref)
    second_layer(w2_ref[1 - odd], columns_ref, turned_ref, rowed_ref)
    for n in range(4):
        pre_ref[256 * n : 256 * n + 256, :] = row_sum(rowed_ref, n)


def emit_activations(pre_ref, out_ref, out_hbm, sem):
    for n in range(4):
        output = leaky_relu(pre_ref[256 * n : 256 * n + 256, :]).astype(jnp.bfloat16).T
        for z in range(2):
            out_ref[0, 0, :, z * PLANE + 256 * n : z * PLANE + 256 * n + 256] = output[z * C2 : (z + 1) * C2]
    copy = pltpu.make_async_copy(out_ref, out_hbm, sem)
    copy.start()
    copy.wait()


def far_kernel(
    chips, scale, across_ref, select_ref, w1_ref, w2_ref, cot_ref, first_ref, near_ref, near_pre_ref, out_hbm, grad_ref, pre_ref,
    parity_ref, taps_ref, act_ref, columns_ref, turned_ref, rowed_ref, back_ref, swapped_ref, out_ref, out_sem,
):
    odd = lax.axis_index("core")
    last = (lax.axis_index("chip") == chips - 1) & (odd == 1)
    inside = jnp.where(last, 0.0, 1.0)
    strided_taps(plane_rows(across_ref), select_ref, parity_ref, taps_ref)
    clear_margins(act_ref)
    for n in range(4):
        here = slice(256 * n, 256 * n + 256)
        first_pre = first_ref[:, here] + jnp.dot(w1_ref[odd], taps_ref[:, here], preferred_element_type=jnp.float32)
        first_act = leaky_relu(first_pre)
        there = slice(LANES + 256 * n, LANES + 256 * n + 256)
        act_ref[0:C1, there] = first_act[0:C1].astype(jnp.bfloat16)
        act_ref[C1:, there] = (first_act[C1:] * inside).astype(jnp.bfloat16)
    columns_ref[1 - odd] = near_ref[...]
    shifted_columns(act_ref, columns_ref.at[odd])
    second_layer(w2_ref[odd], columns_ref.at[odd], turned_ref, rowed_ref)
    margin = jnp.zeros((HALF, LANES), jnp.bfloat16)
    for ref in (back_ref, swapped_ref):
        ref[0:HALF, :] = margin
        ref[HALF + PLANE :, :] = margin
    for n in range(4):
        cells = slice(256 * n, 256 * n + 256)
        pre = near_pre_ref[cells, :] + row_sum(rowed_ref, n)
        pre_ref[cells, :] = pre
        back = (cot_ref[cells, :].astype(jnp.float32) * jnp.where(pre > 0, 1.0, neg_slope)).astype(jnp.bfloat16)
        here = slice(HALF + 256 * n, HALF + 256 * n + 256)
        back_ref[here, :] = back
        swapped_ref[here, :] = jnp.concatenate([back[:, C2:], back[:, 0:C2]], axis=1)
    low = lax.broadcasted_iota(jnp.int32, (1, LANES), 1) < C2
    rows_of = [slice((2 - b) * HALF, (2 - b) * HALF + PLANE) for b in range(3)]
    operands = []
    for left_ref, right_ref in ((back_ref, swapped_ref), (swapped_ref, back_ref)):
        first_two = jnp.where(low, left_ref[rows_of[0], :], right_ref[rows_of[1], :])
        operands.append(jnp.concatenate([first_two, left_ref[rows_of[2], :]], axis=1))

    def plane_columns(q, c):
        begin = 2 * C1 * c + C1 * (q % 2)
        return columns_ref[q // 2, begin : begin + C1, :]

    columns = [jnp.concatenate([plane_columns(a + z, c) for a in range(3) for c in range(3)], axis=0) for z in range(2)]
    sums = scale * jnp.dot(
        jnp.concatenate(columns, axis=1), jnp.concatenate(operands, axis=0), preferred_element_type=jnp.float32
    )
    left, right, ends = sums[0:256, 0:LANES], sums[0:256, LANES:], sums[256:]
    turned = [left[0:LANES].T, left[LANES:].T]
    third = jnp.where(low, right[0:LANES], pltpu.roll(right[LANES:], C2, 1)).T
    fourth = jnp.concatenate([ends[:, 0:LANES], ends[:, LANES:]] * 2, axis=0).T
    group = lax.broadcasted_iota(jnp.int32, (1, LANES), 1) // C1
    tiles = [turned[0][0:C2], turned[1][0:C2], turned[0][C2:], turned[1][C2:], third[0:C2], third[C2:]]
    tiles.append(jnp.where(group < 2, fourth[0:C2], pltpu.roll(fourth[C2:], C2, 1)))
    for k, tile in enumerate(tiles):
        grad_ref[:, k * LANES : (k + 1) * LANES] = tile.astype(jnp.bfloat16)
    early = lax.axis_index("narrow") == 0
    pl.when(early)(lambda: emit_activations(pre_ref, out_ref, out_hbm, out_sem))


def slots():
    where = []
    for a in range(3):
        for b in range(3):
            for c in range(3):
                tile, group = divmod(3 * a + c, 4)
                where.append((2 * b + tile, group) if tile < 2 else (6, (0, 2, 1)[b]))
    return where


def finish_kernel(total_ref, pre_ref, begun_hbm, grad_hbm, out_hbm, grad_ref, out_ref, sems, out_sem):
    del begun_hbm
    copies = []
    for k in range(3):
        for tap in range(9 * k, 9 * k + 9):
            tile, slot = slots()[tap]
            begin = tile * LANES + slot * C1
            grad_ref[tap] = total_ref[:, begin : begin + C1]
        here = slice(9 * k, 9 * k + 9)
        copies.append(pltpu.make_async_copy(grad_ref.at[here], grad_hbm.at[here], sems.at[k]))
        copies[k].start()
    late = lax.axis_index("narrow") > 0
    pl.when(late)(lambda: emit_activations(pre_ref, out_ref, out_hbm, out_sem))
    for copy in copies:
        copy.wait()


def body(volumes, first_kernel, second_kernel, cotangent):
    wide = lax.axis_size(WIDE)
    narrow = lax.axis_size("narrow")
    cells_out = cotangent.shape[3]
    scale = 1.0 / math.sqrt(wide * narrow * cells_out)
    across = lax.ppermute(volumes, WIDE, [p for k in range(1, wide - 1, 2) for p in ((k, k + 1), (k + 1, k))])
    pairs = [p for k in range(0, wide - 1, 2) for p in ((k, k + 1), (k + 1, k))]
    within = lax.ppermute(volumes, WIDE, pairs)
    pinned = pl.BlockSpec(memory_space=pltpu.HBM)
    fast = pl.BlockSpec(memory_space=pltpu.VMEM)
    bf16 = functools.partial(jax.ShapeDtypeStruct, dtype=jnp.bfloat16)
    f32 = functools.partial(jax.ShapeDtypeStruct, dtype=jnp.float32)
    stored = (
        first_kernel.transpose(0, 2, 1), jnp.asarray(placement(), jnp.bfloat16), second_kernel.transpose(0, 2, 1),
        jnp.asarray(selection(), jnp.bfloat16), cotangent,
    )
    w1_near, w1_far, w2, select, cot = pl.pallas_call(
        prepare_kernel,
        in_specs=[pinned] * 5,
        out_specs=(fast,) * 5,
        out_shape=(
            bf16((2, 2 * C1, 18 * ROWS)), bf16((2, 2 * C1, 9 * ROWS)), bf16((2, 6 * C1, 6 * C2)),
            bf16((CHUNK, CHUNK)), bf16((PLANE, 2 * C2)),
        ),
        scratch_shapes=[
            pltpu.VMEM((27, CIN, C1), jnp.bfloat16),
            pltpu.VMEM((27 * CIN, 4 * CHUNK), jnp.bfloat16),
            pltpu.VMEM((27, C1, C2), jnp.bfloat16),
            pltpu.VMEM(cotangent.shape, jnp.bfloat16),
            pltpu.VMEM((27 * CIN, C1), jnp.float32),
            pltpu.SemaphoreType.DMA((5,)),
        ],
        compiler_params=pltpu.CompilerParams(vmem_limit_bytes=12 * MIB),
        cost_estimate=pl.CostEstimate(flops=10**9, bytes_accessed=4 * MIB, transcendentals=0),
        name="prepare",
    )(*(pltpu.with_memory_space_constraint(x, pltpu.HBM) for x in stored))
    first, near, pre = pl.pallas_call(
        near_kernel,
        in_specs=[fast] * 5,
        out_specs=(fast,) * 3,
        out_shape=(f32((2 * C1, PLANE)), bf16((6 * C1, PLANE)), f32((PLANE, 2 * C2))),
        scratch_shapes=[
            pltpu.VMEM((4, 2 * ROWS, LANES + PLANE), jnp.bfloat16),
            pltpu.VMEM((18 * ROWS, PLANE), jnp.bfloat16),
            pltpu.VMEM((2 * C1, PLANE + 2 * LANES), jnp.bfloat16),
            pltpu.VMEM((PLANE, 6 * C1), jnp.bfloat16),
            pltpu.VMEM((3, PLANE + 2 * HALF, LANES), jnp.float32),
        ],
        compiler_params=pltpu.CompilerParams(vmem_limit_bytes=16 * MIB),
        cost_estimate=pl.CostEstimate(flops=10**9, bytes_accessed=4 * MIB, transcendentals=0),
        name="near",
    )(volumes, within, select, w1_near, w2)
    rows = C2 // narrow
    begun, term, pre = pl.pallas_call(
        functools.partial(far_kernel, wide // 2, scale),
        in_specs=[fast] * 8,
        out_specs=(pl.BlockSpec(memory_space=pl.ANY), fast, fast),
        out_shape=(bf16((1, 1, C2, cells_out)), bf16((C2, PACKED)), f32((PLANE, 2 * C2))),
        scratch_shapes=[
            pltpu.VMEM((4, ROWS, LANES + PLANE), jnp.bfloat16),
            pltpu.VMEM((9 * ROWS, PLANE), jnp.bfloat16),
            pltpu.VMEM((2 * C1, PLANE + 2 * LANES), jnp.bfloat16),
            pltpu.VMEM((2, 6 * C1, PLANE), jnp.bfloat16),
            pltpu.VMEM((PLANE, 6 * C1), jnp.bfloat16),
            pltpu.VMEM((3, PLANE + 2 * HALF, LANES), jnp.float32),
            pltpu.VMEM((PLANE + 2 * HALF, LANES), jnp.bfloat16),
            pltpu.VMEM((PLANE + 2 * HALF, LANES), jnp.bfloat16),
            pltpu.VMEM((1, 1, C2, cells_out), jnp.bfloat16),
            pltpu.SemaphoreType.DMA,
        ],
        compiler_params=pltpu.CompilerParams(vmem_limit_bytes=16 * MIB),
        name="far",
    )(across, select, w1_far, w2, cot, first, near, pre)
    half = rows // 2
    received = lax.all_to_all(term, ("narrow", "core"), 0, 0, tiled=True)
    owned = jnp.sum(received.reshape(2 * narrow, half, PACKED).astype(jnp.float32), axis=0).astype(jnp.bfloat16)
    parts = lax.all_to_all(jnp.broadcast_to(owned[None], (wide, half, PACKED)), WIDE, 0, 0, tiled=True)
    total = jnp.sum(parts.reshape(wide // 2, rows, PACKED).astype(jnp.float32), axis=0)
    anywhere = pl.BlockSpec(memory_space=pl.ANY)
    weight_grad, output = pl.pallas_call(
        finish_kernel,
        in_specs=[fast, fast, anywhere],
        out_specs=(anywhere, anywhere),
        out_shape=(f32((27, rows, C1)), bf16((1, 1, C2, cells_out))),
        scratch_shapes=[
            pltpu.VMEM((27, rows, C1), jnp.float32),
            pltpu.VMEM((1, 1, C2, cells_out), jnp.bfloat16),
            pltpu.SemaphoreType.DMA((3,)),
            pltpu.SemaphoreType.DMA,
        ],
        input_output_aliases={2: 1},
        compiler_params=pltpu.CompilerParams(vmem_limit_bytes=8 * MIB),
        name="finish",
    )(total, pre, begun)
    return (output, weight_grad)


def solution(mesh):
    wide, narrow = mesh.devices.shape
    split = jax.sharding.Mesh(mesh.devices.reshape(wide // 2, 2, narrow), ("chip", "core", "narrow"))
    return jax.shard_map(
        body,
        mesh=split,
        in_specs=(P("narrow", None, None, WIDE, None), P(), P(), P("narrow", None, None, WIDE)),
        out_specs=(P("narrow", None, None, WIDE), P(None, "narrow", None)),
        check_vma=False,
    )
```

```python
import functools
import math

import jax
import jax.numpy as jnp
import numpy as np
from jax import lax
from jax.experimental import pallas as pl
from jax.experimental.pallas import tpu as pltpu
from jax.sharding import PartitionSpec as P

CIN = 4
C1 = 32
C2 = 64
PLANES = 4
CELLS = 4096
HALF = 32
PLANE = 1024
LANES = 128
ROWS = CIN * PLANES
CHUNK = 512
PACKED = 7 * LANES
MIB = 2**20
WIDE = ("chip", "core")
neg_slope = 0.3


def selection():
    table = np.zeros((CHUNK, 2, 2, 4, HALF), np.float32)
    for py in range(2):
        for px in range(2):
            for row in range(4):
                for col in range(HALF):
                    table[(2 * row + py) * 64 + 2 * col + px, py, px, row, col] = 1
    return table.reshape(CHUNK, CHUNK)


def placement():
    table = np.zeros((2, 27, CIN, 4, CHUNK), np.float32)
    for odd in range(2):
        for a in range(3):
            for bc in range(9):
                for i in range(CIN):
                    for q in range(4):
                        slab, plane = divmod(2 * q + a + 1, PLANES)
                        inner = i * PLANES + plane
                        if slab == 1:
                            column = bc * 2 * ROWS + inner
                        elif (slab == 0) == (odd == 1):
                            column = bc * 2 * ROWS + ROWS + inner
                        else:
                            column = 18 * ROWS + bc * ROWS + inner
                        table[odd, 9 * a + bc, i, q, column] = 1
    return table.reshape(2, 27 * CIN, 4 * CHUNK)


def leaky_relu(value):
    return jnp.maximum(value, neg_slope * value)


def plane_rows(volume_ref):
    return jnp.concatenate([volume_ref[0, 0, i] for i in range(CIN)], axis=0)


def column_masks():
    column = lax.broadcasted_iota(jnp.int32, (1, PLANE), 1) % HALF
    left_ok = jnp.where(column > 0, 1.0, 0.0).astype(jnp.bfloat16)
    right_ok = jnp.where(column < HALF - 1, 1.0, 0.0).astype(jnp.bfloat16)
    return left_ok, right_ok


def strided_taps(rows, select_ref, parity_ref, taps_ref):
    count = rows.shape[0]
    left_ok, _ = column_masks()
    chunks = jnp.concatenate([rows[:, CHUNK * j : CHUNK * (j + 1)] for j in range(8)], axis=0)
    for p in range(4):
        parity_ref[p, :, 0:LANES] = jnp.zeros((count, LANES), jnp.bfloat16)
    for py in range(2):
        parts = jnp.dot(
            chunks, select_ref[:, 256 * py : 256 * py + 256], preferred_element_type=jnp.float32
        ).astype(jnp.bfloat16)
        for px in range(2):
            for j in range(8):
                parity_ref[2 * py + px, :, LANES * (j + 1) : LANES * (j + 2)] = parts[
                    j * count : (j + 1) * count, px * LANES : (px + 1) * LANES
                ]
    for b in range(3):
        for c in range(3):
            begin = LANES - HALF * (b == 0) - (c == 0)
            part = parity_ref[2 * (b != 1) + (c != 1), :, begin : begin + PLANE]
            if c == 0:
                part = part * left_ok
            taps_ref[(3 * b + c) * count : (3 * b + c + 1) * count, :] = part


def shifted_columns(act_ref, columns_ref):
    left_ok, right_ok = column_masks()
    for c in range(3):
        begin = LANES + c - 1
        part = act_ref[:, begin : begin + PLANE]
        if c == 0:
            part = part * left_ok
        if c == 2:
            part = part * right_ok
        columns_ref[c * 2 * C1 : (c + 1) * 2 * C1, :] = part


def second_layer(w2, columns_ref, turned_ref, rowed_ref):
    blank = jnp.zeros((HALF, LANES), jnp.float32)
    for b in (0, 2):
        rowed_ref[b, 0:HALF, :] = blank
        rowed_ref[b, HALF + PLANE :, :] = blank
    for n in range(4):
        cells = slice(256 * n, 256 * n + 256)
        turned_ref[cells, :] = columns_ref[:, cells].T
    for n in range(4):
        sums = jnp.dot(turned_ref[256 * n : 256 * n + 256, :], w2, preferred_element_type=jnp.float32)
        for b in range(3):
            rowed_ref[b, HALF + 256 * n : HALF + 256 * n + 256, :] = sums[:, b * LANES : (b + 1) * LANES]


def row_sum(rowed_ref, n):
    begins = [HALF * b + 256 * n for b in range(3)]
    first, second, third = (rowed_ref[b, begin : begin + 256, :] for b, begin in enumerate(begins))
    return first + second + third


def clear_margins(act_ref):
    margin = jnp.zeros((2 * C1, LANES), jnp.bfloat16)
    act_ref[:, 0:LANES] = margin
    act_ref[:, LANES + PLANE :] = margin


def prepare_kernel(
    k1_hbm, place_hbm, k2_hbm, select_hbm, cot_hbm,
    w1_near_ref, w1_far_ref, w2_ref, select_ref, turned_ref,
    k1_ref, place_ref, k2_ref, cot_ref, k1_rows_ref, sems,
):
    odd = lax.axis_index("core")
    moves = (
        (k1_hbm, k1_ref), (k2_hbm, k2_ref), (place_hbm.at[odd], place_ref), (cot_hbm, cot_ref), (select_hbm, select_ref),
    )
    copies = [pltpu.make_async_copy(src, dst, sems.at[k]) for k, (src, dst) in enumerate(moves)]
    for copy in copies:
        copy.start()
    copies[0].wait()
    for tap in range(27):
        k1_rows_ref[CIN * tap : CIN * (tap + 1), :] = k1_ref[tap].astype(jnp.float32)
    copies[1].wait()
    blank = jnp.zeros((C1, C2), jnp.bfloat16)

    def stacked(bc, pair):
        k = [blank] + [k2_ref[9 * a + bc] for a in range(3)] + [blank]
        lower = jnp.concatenate(k[1 + 2 * pair : 3 + 2 * pair], axis=0)
        upper = jnp.concatenate(k[2 * pair : 2 + 2 * pair], axis=0)
        return jnp.concatenate([lower, upper], axis=1)

    for pair in range(2):
        for b in range(3):
            for c in range(3):
                w2_ref[pair, c * 2 * C1 : (c + 1) * 2 * C1, b * LANES : (b + 1) * LANES] = stacked(3 * b + c, pair)
    copies[2].wait()
    spread = lax.dot_general(
        k1_rows_ref[...].astype(jnp.bfloat16), place_ref[...],
        (((0,), (0,)), ((), ())), preferred_element_type=jnp.float32,
    ).astype(jnp.bfloat16)
    for q in range(4):
        rows = slice(q % 2 * C1, (q % 2 + 1) * C1)
        w1_near_ref[q // 2, rows, :] = spread[:, CHUNK * q : CHUNK * q + 18 * ROWS]
        w1_far_ref[q // 2, rows, :] = spread[:, CHUNK * q + 18 * ROWS : CHUNK * q + 27 * ROWS]
    copies[3].wait()
    for n in range(4):
        planes = [cot_ref[0, 0, :, z * PLANE + 256 * n : z * PLANE + 256 * n + 256] for z in range(2)]
        turned_ref[256 * n : 256 * n + 256, :] = jnp.concatenate(planes, axis=0).T
    copies[4].wait()


def near_kernel(
    own_ref, within_ref, select_ref, w1_ref, w2_ref, first_ref, columns_ref, pre_ref,
    parity_ref, taps_ref, act_ref, turned_ref, rowed_ref,
):
    odd = lax.axis_index("core")
    rows = jnp.concatenate([plane_rows(own_ref), plane_rows(within_ref)], axis=0)
    strided_taps(rows, select_ref, parity_ref, taps_ref)
    clear_margins(act_ref)
    for n in range(4):
        here = slice(256 * n, 256 * n + 256)
        first_ref[:, here] = jnp.dot(w1_ref[odd], taps_ref[:, here], preferred_element_type=jnp.float32)
        complete = jnp.dot(w1_ref[1 - odd], taps_ref[:, here], preferred_element_type=jnp.float32)
        act_ref[:, LANES + 256 * n : LANES + 256 * n + 256] = leaky_relu(complete).astype(jnp.bfloat16)
    shifted_columns(act_ref, columns_ref)
    second_layer(w2_ref[1 - odd], columns_ref, turned_ref, rowed_ref)
    for n in range(4):
        pre_ref[256 * n : 256 * n + 256, :] = row_sum(rowed_ref, n)


def emit_activations(pre_ref, out_ref, out_hbm, sem):
    for n in range(4):
        output = leaky_relu(pre_ref[256 * n : 256 * n + 256, :]).astype(jnp.bfloat16).T
        for z in range(2):
            out_ref[0, 0, :, z * PLANE + 256 * n : z * PLANE + 256 * n + 256] = output[z * C2 : (z + 1) * C2]
    copy = pltpu.make_async_copy(out_ref, out_hbm, sem)
    copy.start()
    copy.wait()


def far_kernel(
    chips, across_ref, select_ref, w1_ref, w2_ref, cot_ref, first_ref, near_ref, near_pre_ref, out_hbm, grad_ref, pre_ref,
    parity_ref, taps_ref, act_ref, columns_ref, turned_ref, rowed_ref, back_ref, swapped_ref, out_ref, out_sem,
):
    odd = lax.axis_index("core")
    last = (lax.axis_index("chip") == chips - 1) & (odd == 1)
    inside = jnp.where(last, 0.0, 1.0)
    strided_taps(plane_rows(across_ref), select_ref, parity_ref, taps_ref)
    clear_margins(act_ref)
    for n in range(4):
        here = slice(256 * n, 256 * n + 256)
        first_pre = first_ref[:, here] + jnp.dot(w1_ref[odd], taps_ref[:, here], preferred_element_type=jnp.float32)
        first_act = leaky_relu(first_pre)
        there = slice(LANES + 256 * n, LANES + 256 * n + 256)
        act_ref[0:C1, there] = first_act[0:C1].astype(jnp.bfloat16)
        act_ref[C1:, there] = (first_act[C1:] * inside).astype(jnp.bfloat16)
    columns_ref[1 - odd] = near_ref[...]
    shifted_columns(act_ref, columns_ref.at[odd])
    second_layer(w2_ref[odd], columns_ref.at[odd], turned_ref, rowed_ref)
    margin = jnp.zeros((HALF, LANES), jnp.bfloat16)
    for ref in (back_ref, swapped_ref):
        ref[0:HALF, :] = margin
        ref[HALF + PLANE :, :] = margin
    for n in range(4):
        cells = slice(256 * n, 256 * n + 256)
        pre = near_pre_ref[cells, :] + row_sum(rowed_ref, n)
        pre_ref[cells, :] = pre
        back = (cot_ref[cells, :].astype(jnp.float32) * jnp.where(pre > 0, 1.0, neg_slope)).astype(jnp.bfloat16)
        here = slice(HALF + 256 * n, HALF + 256 * n + 256)
        back_ref[here, :] = back
        swapped_ref[here, :] = jnp.concatenate([back[:, C2:], back[:, 0:C2]], axis=1)
    low = lax.broadcasted_iota(jnp.int32, (1, LANES), 1) < C2
    rows_of = [slice((2 - b) * HALF, (2 - b) * HALF + PLANE) for b in range(3)]
    operands = []
    for left_ref, right_ref in ((back_ref, swapped_ref), (swapped_ref, back_ref)):
        first_two = jnp.where(low, left_ref[rows_of[0], :], right_ref[rows_of[1], :])
        operands.append(jnp.concatenate([first_two, left_ref[rows_of[2], :]], axis=1))

    def plane_columns(q, c):
        begin = 2 * C1 * c + C1 * (q % 2)
        return columns_ref[q // 2, begin : begin + C1, :]

    columns = [jnp.concatenate([plane_columns(a + z, c) for a in range(3) for c in range(3)], axis=0) for z in range(2)]
    sums = jnp.dot(
        jnp.concatenate(columns, axis=1), jnp.concatenate(operands, axis=0), preferred_element_type=jnp.float32
    )
    left, right, ends = sums[0:256, 0:LANES], sums[0:256, LANES:], sums[256:]
    turned = [left[0:LANES].T, left[LANES:].T]
    third = jnp.where(low, right[0:LANES], pltpu.roll(right[LANES:], C2, 1)).T
    fourth = jnp.concatenate([ends[:, 0:LANES], ends[:, LANES:]] * 2, axis=0).T
    group = lax.broadcasted_iota(jnp.int32, (1, LANES), 1) // C1
    tiles = [turned[0][0:C2], turned[1][0:C2], turned[0][C2:], turned[1][C2:], third[0:C2], third[C2:]]
    tiles.append(jnp.where(group < 2, fourth[0:C2], pltpu.roll(fourth[C2:], C2, 1)))
    for k, tile in enumerate(tiles):
        grad_ref[:, k * LANES : (k + 1) * LANES] = tile.astype(jnp.bfloat16)
    early = lax.axis_index("narrow") == 0
    pl.when(early)(lambda: emit_activations(pre_ref, out_ref, out_hbm, out_sem))


def slots():
    where = []
    for a in range(3):
        for b in range(3):
            for c in range(3):
                tile, group = divmod(3 * a + c, 4)
                where.append((2 * b + tile, group) if tile < 2 else (6, (0, 2, 1)[b]))
    return where


def finish_kernel(total_ref, pre_ref, begun_hbm, grad_hbm, out_hbm, grad_ref, out_ref, sems, out_sem):
    del begun_hbm
    copies = []
    for k in range(3):
        for tap in range(9 * k, 9 * k + 9):
            tile, slot = slots()[tap]
            begin = tile * LANES + slot * C1
            grad_ref[tap] = total_ref[:, begin : begin + C1]
        here = slice(9 * k, 9 * k + 9)
        copies.append(pltpu.make_async_copy(grad_ref.at[here], grad_hbm.at[here], sems.at[k]))
        copies[k].start()
    late = lax.axis_index("narrow") > 0
    pl.when(late)(lambda: emit_activations(pre_ref, out_ref, out_hbm, out_sem))
    for copy in copies:
        copy.wait()


def body(volumes, first_kernel, second_kernel, cotangent):
    wide = lax.axis_size(WIDE)
    narrow = lax.axis_size("narrow")
    cells_out = cotangent.shape[3]
    scale = 1.0 / math.sqrt(wide * narrow * cells_out)
    across = lax.ppermute(volumes, WIDE, [p for k in range(1, wide - 1, 2) for p in ((k, k + 1), (k + 1, k))])
    pairs = [p for k in range(0, wide - 1, 2) for p in ((k, k + 1), (k + 1, k))]
    within = lax.ppermute(volumes, WIDE, pairs)
    pinned = pl.BlockSpec(memory_space=pltpu.HBM)
    fast = pl.BlockSpec(memory_space=pltpu.VMEM)
    bf16 = functools.partial(jax.ShapeDtypeStruct, dtype=jnp.bfloat16)
    f32 = functools.partial(jax.ShapeDtypeStruct, dtype=jnp.float32)
    stored = (
        first_kernel.transpose(0, 2, 1), jnp.asarray(placement(), jnp.bfloat16), second_kernel.transpose(0, 2, 1),
        jnp.asarray(selection(), jnp.bfloat16), cotangent,
    )
    w1_near, w1_far, w2, select, cot = pl.pallas_call(
        prepare_kernel,
        in_specs=[pinned] * 5,
        out_specs=(fast,) * 5,
        out_shape=(
            bf16((2, 2 * C1, 18 * ROWS)), bf16((2, 2 * C1, 9 * ROWS)), bf16((2, 6 * C1, 6 * C2)),
            bf16((CHUNK, CHUNK)), bf16((PLANE, 2 * C2)),
        ),
        scratch_shapes=[
            pltpu.VMEM((27, CIN, C1), jnp.bfloat16),
            pltpu.VMEM((27 * CIN, 4 * CHUNK), jnp.bfloat16),
            pltpu.VMEM((27, C1, C2), jnp.bfloat16),
            pltpu.VMEM(cotangent.shape, jnp.bfloat16),
            pltpu.VMEM((27 * CIN, C1), jnp.float32),
            pltpu.SemaphoreType.DMA((5,)),
        ],
        compiler_params=pltpu.CompilerParams(vmem_limit_bytes=12 * MIB),
        cost_estimate=pl.CostEstimate(flops=10**9, bytes_accessed=4 * MIB, transcendentals=0),
        name="prepare",
    )(*(pltpu.with_memory_space_constraint(x, pltpu.HBM) for x in stored))
    first, near, pre = pl.pallas_call(
        near_kernel,
        in_specs=[fast] * 5,
        out_specs=(fast,) * 3,
        out_shape=(f32((2 * C1, PLANE)), bf16((6 * C1, PLANE)), f32((PLANE, 2 * C2))),
        scratch_shapes=[
            pltpu.VMEM((4, 2 * ROWS, LANES + PLANE), jnp.bfloat16),
            pltpu.VMEM((18 * ROWS, PLANE), jnp.bfloat16),
            pltpu.VMEM((2 * C1, PLANE + 2 * LANES), jnp.bfloat16),
            pltpu.VMEM((PLANE, 6 * C1), jnp.bfloat16),
            pltpu.VMEM((3, PLANE + 2 * HALF, LANES), jnp.float32),
        ],
        compiler_params=pltpu.CompilerParams(vmem_limit_bytes=16 * MIB),
        cost_estimate=pl.CostEstimate(flops=10**9, bytes_accessed=4 * MIB, transcendentals=0),
        name="near",
    )(volumes, within, select, w1_near, w2)
    rows = C2 // narrow
    begun, term, pre = pl.pallas_call(
        functools.partial(far_kernel, wide // 2),
        in_specs=[fast] * 8,
        out_specs=(pl.BlockSpec(memory_space=pl.ANY), fast, fast),
        out_shape=(bf16((1, 1, C2, cells_out)), bf16((C2, PACKED)), f32((PLANE, 2 * C2))),
        scratch_shapes=[
            pltpu.VMEM((4, ROWS, LANES + PLANE), jnp.bfloat16),
            pltpu.VMEM((9 * ROWS, PLANE), jnp.bfloat16),
            pltpu.VMEM((2 * C1, PLANE + 2 * LANES), jnp.bfloat16),
            pltpu.VMEM((2, 6 * C1, PLANE), jnp.bfloat16),
            pltpu.VMEM((PLANE, 6 * C1), jnp.bfloat16),
            pltpu.VMEM((3, PLANE + 2 * HALF, LANES), jnp.float32),
            pltpu.VMEM((PLANE + 2 * HALF, LANES), jnp.bfloat16),
            pltpu.VMEM((PLANE + 2 * HALF, LANES), jnp.bfloat16),
            pltpu.VMEM((1, 1, C2, cells_out), jnp.bfloat16),
            pltpu.SemaphoreType.DMA,
        ],
        compiler_params=pltpu.CompilerParams(vmem_limit_bytes=16 * MIB),
        name="far",
    )(across, select, w1_far, w2, cot, first, near, pre)
    half = rows // 2
    received = lax.all_to_all(term, ("narrow", "core"), 0, 0, tiled=True)
    owned = jnp.sum(received.reshape(2 * narrow, half, PACKED).astype(jnp.float32), axis=0).astype(jnp.bfloat16)
    parts = lax.all_to_all(jnp.broadcast_to(owned[None], (wide, half, PACKED)), WIDE, 0, 0, tiled=True)
    total = scale * jnp.sum(parts.reshape(wide // 2, rows, PACKED).astype(jnp.float32), axis=0)
    anywhere = pl.BlockSpec(memory_space=pl.ANY)
    weight_grad, output = pl.pallas_call(
        finish_kernel,
        in_specs=[fast, fast, anywhere],
        out_specs=(anywhere, anywhere),
        out_shape=(f32((27, rows, C1)), bf16((1, 1, C2, cells_out))),
        scratch_shapes=[
            pltpu.VMEM((27, rows, C1), jnp.float32),
            pltpu.VMEM((1, 1, C2, cells_out), jnp.bfloat16),
            pltpu.SemaphoreType.DMA((3,)),
            pltpu.SemaphoreType.DMA,
        ],
        input_output_aliases={2: 1},
        compiler_params=pltpu.CompilerParams(vmem_limit_bytes=8 * MIB),
        name="finish",
    )(total, pre, begun)
    return (output, weight_grad)


def solution(mesh):
    wide, narrow = mesh.devices.shape
    split = jax.sharding.Mesh(mesh.devices.reshape(wide // 2, 2, narrow), ("chip", "core", "narrow"))
    return jax.shard_map(
        body,
        mesh=split,
        in_specs=(P("narrow", None, None, WIDE, None), P(), P(), P("narrow", None, None, WIDE)),
        out_specs=(P("narrow", None, None, WIDE), P(None, "narrow", None)),
        check_vma=False,
    )
```
